32 devices in a mesh: groups: 2 (over y), lists: 8 (over z, x), rep: 2 (over core).
Axes of the slice: x: 2, y: 2, z: 4, core: 2. Of those that a mesh axis runs over, the one named last changes fastest.
Arguments:
- queries: bfloat16 [512, 1024], P(('groups', 'lists', 'rep')), parts along dimension 0
- corpus: bfloat16 [64, 1024, 1024], P(('groups', 'lists')), parts along dimension 0
- list_slot: int32 [64], P('groups'), parts along dimension 0, may hold values from 0 to 31, each once
- probes: int32 [512, 8], P(('groups', 'lists', 'rep')), parts along dimension 0, may hold values from 0 to 31, all different within a row; in each aligned block of 16 rows (0 to 15, 16 to 31, ...) at most 8 rows name the same one
- cand: int32 [512, 8, 2], P(('groups', 'lists', 'rep')), parts along dimension 0, may hold values from 0 to 7
Outputs:
- scores: bfloat16 [512, 8, 2, 128], P(('groups', 'lists', 'rep')), parts along dimension 0
The draws below stay inside these ranges and needn't reach their ends.
There are 2 independent parts, one for each index of `groups`. The reference program is written for one: setup_inputs(seed, part) draws one part's arguments, and reference() takes and returns one part's arrays. A program takes and returns all parts, laid end to end along the dimension named above; each array names one. Nothing has to cross between parts.
Inputs may be any that keep to these rules, and one draw needn't show every extreme that they name: A permutation: list L is stored at position list_slot[L] of corpus. `probes`: each row names 8 different lists; in the 16 rows of one device no list is named by more than 8 rows, and in some device's rows one list is named by exactly 8. `cand`: index of a block of 128 consecutive rows within the probed list.
All inputs are finite; a program needn't handle non-finite values.
Results may differ from the reference program's by a relative error of at most 0.001.
Values may be sent and summed in bfloat16 or wider, within the bound.
No kernel may reach another device: no remote copies, remote signals or barrier semaphores. Data moves between devices by JAX's collectives and lax.ppermute only.
A program may use at most 64 MiB of HBM per device.

```python
import math
import jax
import jax.numpy as jnp
import numpy as np
from jax import lax

D = 1024
LIST_ROWS = 1024
Q_DEV = 16
PROBES = 8
CAND = 2
BLOCK = 128
LISTS = 32
QUERIES = 256
MOST = 8
NBLK = 8
N_LISTS = 8
N_REP = 2


def scaled_normal(key, array_shape):
    key_base = jax.random.fold_in(key, 11)
    key_rows = jax.random.fold_in(key, 23)
    key_cols = jax.random.fold_in(key, 37)
    row_scale = jnp.exp(jax.random.uniform(key_rows, array_shape[:-1] + (1,), jnp.float32) * math.log(10.0))
    col_scale = jnp.exp(jax.random.uniform(key_cols, (array_shape[-1],), jnp.float32) * math.log(10.0))
    entries = jax.random.normal(key_base, array_shape, jnp.float32)
    return (entries * row_scale * col_scale).astype(jnp.bfloat16)


def draw_queries(key, part):
    return scaled_normal(jax.random.fold_in(key, 101), (QUERIES, D))


def draw_corpus(key, part):
    return scaled_normal(jax.random.fold_in(key, 202), (LISTS, LIST_ROWS, D))


def set_ends(values, rng, least, top_value):
    place = [jax.random.randint(jax.random.fold_in(rng, axis), (), 0, length) for axis, length in enumerate(values.shape)]
    main_axis = values.shape.index(max(values.shape))
    neighbour = place[:main_axis] + [(place[main_axis] + 1) % values.shape[main_axis]] + place[main_axis + 1:]
    return values.at[tuple(place)].set(least).at[tuple(neighbour)].set(top_value)


def assign_block(key, own, number, rows, amount, top, reach, slope):
    sequence = jax.random.permutation(key, amount)
    packed, usual = shares(amount, rows * top, reach, slope, True), shares(amount, rows * top, reach, slope, False)
    places = jnp.arange(amount)

    def named(lengths, rotation):
        used = int((lengths > 0).sum())
        fixed = max(1, used // 4)
        passed = fixed + (places - fixed + rotation * (used - fixed)) % max(1, amount - fixed)
        return jnp.zeros((amount,), jnp.int32).at[sequence[jnp.where(places < fixed, places, passed)]].set(jnp.asarray(lengths, jnp.int32))

    lengths = jnp.where(number % 4 == 0, named(packed, number // 4), named(usual, number - number // 4 - 1))
    mixed = jax.random.permutation(jax.random.fold_in(own, 3), amount)
    source_of, receiver = mixed[0:amount // 2 * 2:2], mixed[1:amount // 2 * 2:2]
    room = jnp.minimum(lengths[source_of] - 1, reach - lengths[receiver]) // 2
    room = jnp.where((source_of == sequence[0]) | (receiver == sequence[0]) | (lengths[receiver] == 0), 0, jnp.maximum(room, 0))
    passed = jax.random.randint(jax.random.fold_in(own, 4), (amount // 2,), 0, 1 << 20) % (room + 1)
    lengths = lengths.at[source_of].add(-passed).at[receiver].add(passed)
    members = jnp.searchsorted(jnp.cumsum(lengths), jnp.arange(rows * top), side="right").astype(jnp.int32)
    grid = members.reshape(top, rows).T
    grid = grid[jax.random.permutation(jax.random.fold_in(own, 1), rows)]
    rotation = jax.random.randint(jax.random.fold_in(own, 2), (rows, 1), 0, top)
    return jnp.take_along_axis(grid, (jnp.arange(top)[None, :] + rotation) % top, axis=1)


def shares(number_of, total, reach, skew, full):
    weights = [(1 << 20) // math.isqrt(rank ** skew) + 1 for rank in range(1, number_of + 1)]
    largest = reach if full else min(reach, max(-(-total // number_of), total * weights[0] // sum(weights)))
    least = 1 if total - largest >= number_of - 1 else 0
    holding, spare = [largest] + [least] * (number_of - 1), total - largest - least * (number_of - 1)
    while spare > 0:
        movable = [i for i in range(1, number_of) if holding[i] < largest] or [i for i in range(1, number_of) if holding[i] < reach]
        mass, left = sum([weights[i] for i in movable]), spare
        for i in movable:
            extra = min(reach - holding[i], max(1, left * weights[i] // mass), spare)
            holding[i] = holding[i] + extra
            spare = spare - extra
    return np.array(holding)


def setup_inputs(seed: int = 0, part: int = 0) -> dict:
    key_list = jax.random.split(jax.random.key(seed), 6)
    part_splits = jax.random.split(jax.random.fold_in(key_list[5], part), 6)
    queries = draw_queries(jax.random.fold_in(jax.random.fold_in(key_list[5], part), 71), part)
    corpus = draw_corpus(jax.random.fold_in(jax.random.fold_in(key_list[5], part), 71), part)
    list_slot = jax.random.permutation(part_splits[2], LISTS).astype(jnp.int32)
    probes_keys = jax.random.split(jax.random.fold_in(part_splits[3], 1), QUERIES // Q_DEV)
    probes_turns = jax.random.permutation(jax.random.fold_in(part_splits[3], 3), QUERIES // Q_DEV)
    probes = jax.vmap(lambda own, number: assign_block(jax.random.fold_in(part_splits[3], 2), own, number, Q_DEV, LISTS, PROBES, MOST, 2))(probes_keys, probes_turns).reshape((QUERIES, PROBES))
    cand = set_ends(jax.random.randint(part_splits[4], (QUERIES, PROBES, CAND), 0, NBLK), jax.random.fold_in(part_splits[4], 1), 0, NBLK - 1).astype(jnp.int32)
    return dict(queries=queries, corpus=corpus, list_slot=list_slot, probes=probes, cand=cand)


epsilon = 1e-06

def inverse_norm(values):
    squares = jnp.einsum('...d,...d->...', values, values, preferred_element_type=jnp.float32)
    return lax.rsqrt(squares / values.shape[-1] + epsilon)

def reference(queries, corpus, list_slot, probes, cand):
    pair_count = QUERIES * PROBES
    list_room = N_LISTS * N_REP * MOST
    inv_rows = inverse_norm(corpus)
    inv_queries = inverse_norm(queries)
    pair_slot = list_slot[probes.reshape(pair_count)].astype(jnp.int32)
    pair_query = jnp.arange(pair_count, dtype=jnp.int32) // PROBES
    pair_cand = cand.reshape(pair_count, CAND).astype(jnp.int32)

    def one_list(totals, slot_id):
        pair_order = jnp.argsort((pair_slot != slot_id).astype(jnp.int32), stable=True)[:list_room].astype(jnp.int32)
        chosen = pair_slot[pair_order] == slot_id
        owners = pair_query[pair_order]
        vectors = queries[owners]
        listed = lax.dynamic_index_in_dim(corpus, slot_id, 0, keepdims=False)
        list_inv = lax.dynamic_index_in_dim(inv_rows, slot_id, 0, keepdims=False)
        products = jnp.dot(vectors, listed.T, preferred_element_type=jnp.float32)
        scaled = products * inv_queries[owners][:, None] * list_inv[None, :] * D ** (-0.5)
        blocks = scaled.astype(jnp.bfloat16).reshape(list_room, NBLK, BLOCK)
        selected = blocks[jnp.arange(list_room, dtype=jnp.int32)[:, None], pair_cand[pair_order]]
        target = jnp.where(chosen, pair_order, pair_count)
        totals = totals.at[target].set(selected, mode='drop')
        return (totals, None)
    blank_scores = jnp.zeros((pair_count, CAND, BLOCK), jnp.bfloat16)
    result, _ = lax.scan(one_list, blank_scores, jnp.arange(LISTS, dtype=jnp.int32))
    return result.reshape(QUERIES, PROBES, CAND, BLOCK)
```

```python
import functools

import jax
import jax.numpy as jnp
from jax import lax
from jax.experimental import pallas as pl
from jax.experimental.pallas import tpu as pltpu
from jax.sharding import PartitionSpec as P

BLOCK = 128
LANES = 128

epsilon = 1e-06


def contract(a, b, dims, precision=None):
    return lax.dot_general(
        a, b, (dims, ((), ())), precision=precision, preferred_element_type=jnp.float32
    )


def score_kernel(
    sizes, me_ref, slot_ref, message_ref, corpus_ref, out_ref, held, sems
):
    owners, query_count, probe_count, cand_count, capacity, chunk = sizes
    local_lists, list_length, features = held.shape
    total = owners * query_count
    per_list = list_length // chunk

    def copy(i):
        l, h = divmod(i, per_list)
        rows = pl.ds(h * chunk, chunk)
        return pltpu.make_async_copy(corpus_ref.at[l, rows], held.at[l, rows], sems.at[i])

    for i in range(local_lists * per_list):
        copy(i).start()

    width = probe_count * (1 + cand_count)
    padded = -(-width // 16) * 16
    indices = message_ref[:, features:]
    eye = lax.broadcasted_iota(jnp.int32, (padded, LANES), 0) == lax.broadcasted_iota(
        jnp.int32, (padded, LANES), 1
    )
    turned = contract(eye.astype(jnp.float32).astype(jnp.bfloat16), indices, ((1,), (1,)))
    probes = turned[:probe_count]
    cands = [
        turned[probe_count * (1 + c) : probe_count * (2 + c)] for c in range(cand_count)
    ]

    slots = slot_ref[...]
    names = lax.broadcasted_iota(jnp.int32, slots.shape, 1).astype(jnp.float32)
    first = me_ref[0] * local_lists
    hits, wanted = [], []
    for l in range(local_lists):
        name = jnp.sum(jnp.where(slots == first + l, names, 0.0), axis=1, keepdims=True)
        named = probes == name
        hits.append(jnp.sum(named.astype(jnp.float32), axis=0, keepdims=True))
        wanted.append(
            [jnp.sum(jnp.where(named, c, 0.0), axis=0, keepdims=True) for c in cands]
        )
    hit = jnp.concatenate(hits, axis=0)

    span = min(total, LANES)
    earlier = lax.broadcasted_iota(jnp.int32, (span, span), 0)
    later = lax.broadcasted_iota(jnp.int32, (span, span), 1)
    before = (earlier < later) & (earlier // query_count == later // query_count)
    before = before.astype(jnp.float32).astype(jnp.bfloat16)
    hit_low = hit.astype(jnp.bfloat16)
    rank = jnp.concatenate(
        [
            contract(hit_low[:, j : j + span], before, ((1,), (0,)))
            for j in range(0, total, span)
        ],
        axis=1,
    )
    source = (lax.broadcasted_iota(jnp.int32, (1, total), 1) // query_count) * capacity
    target = jnp.where(hit > 0.5, rank.astype(jnp.int32) + source, -1)

    room = owners * capacity
    places = lax.broadcasted_iota(jnp.int32, (room, total), 0)
    queries = message_ref[:, :features]
    for l in range(local_lists):
        pick = (places == target[l : l + 1]).astype(jnp.float32)
        blocks = [jnp.sum(pick * w, axis=1, keepdims=True) for w in wanted[l]]
        rows = contract(pick.astype(jnp.bfloat16), queries, ((1,), (0,)))
        inv_query = lax.rsqrt(jnp.sum(rows * rows, axis=1, keepdims=True) / features + epsilon)
        rows = rows.astype(jnp.bfloat16)
        chosen = [jnp.zeros((room, BLOCK), jnp.float32) for _ in range(cand_count)]
        for h in range(per_list):
            copy(l * per_list + h).wait()
            part = held[l, h * chunk : (h + 1) * chunk, :]
            products = contract(rows, part, ((1,), (1,)))
            wide = part.astype(jnp.float32)
            squares = functools.reduce(
                jnp.add,
                [wide[:, j : j + LANES] ** 2 for j in range(0, features, LANES)],
            )
            sums = contract(
                jnp.ones((8, LANES), jnp.float32), squares, ((1,), (1,)), lax.Precision.HIGHEST
            )[:1]
            inv_row = lax.rsqrt(sums / features + epsilon) * features ** (-0.5)
            scaled = products * inv_query * inv_row
            for j in range(chunk // BLOCK):
                number = (h * chunk + j * BLOCK) // BLOCK
                piece = scaled[:, j * BLOCK : (j + 1) * BLOCK]
                chosen = [
                    jnp.where(block == number, piece, old)
                    for block, old in zip(blocks, chosen)
                ]
        chosen = [c.reshape(owners, capacity, BLOCK) for c in chosen]
        step = capacity * cand_count
        out_ref[:, l * step : (l + 1) * step, :] = jnp.concatenate(chosen, axis=1).astype(
            jnp.bfloat16
        )


def block_scores(me, list_slot, message, corpus, owners, query_count, probe_count, cand_count, capacity):
    local_lists, list_length, features = corpus.shape
    chunk = min(list_length, 512)
    sizes = (owners, query_count, probe_count, cand_count, capacity, chunk)
    return pl.pallas_call(
        functools.partial(score_kernel, sizes),
        out_shape=jax.ShapeDtypeStruct(
            (owners, local_lists * cand_count * capacity, BLOCK), jnp.bfloat16
        ),
        in_specs=[
            pl.BlockSpec(memory_space=pltpu.SMEM),
            pl.BlockSpec(memory_space=pltpu.VMEM),
            pl.BlockSpec(memory_space=pltpu.VMEM),
            pl.BlockSpec(memory_space=pl.ANY),
        ],
        out_specs=pl.BlockSpec(memory_space=pltpu.VMEM),
        scratch_shapes=[
            pltpu.VMEM(corpus.shape, jnp.bfloat16),
            pltpu.SemaphoreType.DMA((local_lists * (list_length // chunk),)),
        ],
        compiler_params=pltpu.CompilerParams(vmem_limit_bytes=40 * 2**20),
        cost_estimate=pl.CostEstimate(
            flops=2 * owners * capacity * corpus.size,
            bytes_accessed=2 * corpus.size,
            transcendentals=0,
        ),
    )(me, list_slot, message, corpus)


def on_device(queries, corpus, list_slot, probes, cand):
    owners = lax.axis_size("lists")
    query_count, features = queries.shape
    probe_count = probes.shape[1]
    cand_count = cand.shape[2]
    local_lists, list_length, _ = corpus.shape
    total_lists = list_slot.shape[0]
    pair_count = query_count * probe_count
    capacity = min(query_count, max(2, (2 * pair_count + total_lists - 1) // total_lists))

    indices = jnp.concatenate([probes] + [cand[:, :, c] for c in range(cand_count)], axis=1)
    indices = jnp.pad(indices, ((0, 0), (0, LANES - indices.shape[1])))
    message = jnp.concatenate([queries, indices.astype(jnp.bfloat16)], axis=1)
    gathered = lax.all_gather(message, "lists", axis=0, tiled=True)

    me = lax.axis_index("lists").astype(jnp.int32).reshape(1)
    scores = block_scores(
        me, list_slot[None, :], gathered, corpus, owners, query_count, probe_count, cand_count, capacity
    )
    returned = lax.all_to_all(scores, "lists", split_axis=0, concat_axis=0, tiled=True)

    position = jnp.sum(
        jnp.where(
            probes[:, :, None] == jnp.arange(total_lists, dtype=jnp.int32), list_slot, 0
        ),
        axis=2,
    )
    named = position[:, :, None] == jnp.arange(total_lists, dtype=jnp.int32)
    counts = jnp.cumsum(jnp.any(named, axis=1).astype(jnp.int32), axis=0)
    rank = jnp.sum(jnp.where(named, counts[:, None, :], 0), axis=2) - 1
    column = position[:, :, None] * (cand_count * capacity) + rank[:, :, None]
    column = column + capacity * jnp.arange(cand_count, dtype=jnp.int32)
    places = returned.shape[0] * returned.shape[1]
    pick = column.reshape(-1)[:, None] == jnp.arange(places, dtype=jnp.int32)[None, :]
    chosen = jnp.dot(
        pick.astype(jnp.bfloat16),
        returned.reshape(places, BLOCK),
        preferred_element_type=jnp.float32,
    ).astype(jnp.bfloat16)
    return chosen.reshape(query_count, probe_count, cand_count, BLOCK)


def solution(mesh):
    placed = (
        P(("groups", "lists", "rep"), None),
        P(("groups", "lists"), None, None),
        P("groups"),
        P(("groups", "lists", "rep"), None),
        P(("groups", "lists", "rep"), None, None),
    )
    return jax.shard_map(
        on_device,
        mesh=mesh,
        in_specs=placed,
        out_specs=P(("groups", "lists", "rep"), None, None, None),
        check_vma=False,
    )
```

```python
import functools

import jax
import jax.numpy as jnp
from jax import lax
from jax.experimental import pallas as pl
from jax.experimental.pallas import tpu as pltpu
from jax.sharding import PartitionSpec as P

BLOCK = 128
LANES = 128
MIB = 2**20

epsilon = 1e-06


def contract(a, b, dims, precision=None):
    return lax.dot_general(
        a, b, (dims, ((), ())), precision=precision, preferred_element_type=jnp.float32
    )


def stage_kernel(chunk, corpus_ref, held_ref, inv_ref, sems):
    local_lists, list_length, features = held_ref.shape
    per_list = list_length // chunk

    def copy(i):
        l, h = divmod(i, per_list)
        rows = pl.ds(h * chunk, chunk)
        return pltpu.make_async_copy(corpus_ref.at[l, rows], held_ref.at[l, rows], sems.at[i])

    for i in range(local_lists * per_list):
        copy(i).start()
    ones = jnp.ones((8, LANES), jnp.float32)
    for i in range(local_lists * per_list):
        l, h = divmod(i, per_list)
        copy(i).wait()
        wide = held_ref[l, h * chunk : (h + 1) * chunk, :].astype(jnp.float32)
        squares = functools.reduce(
            jnp.add, [wide[:, j : j + LANES] ** 2 for j in range(0, features, LANES)]
        )
        sums = contract(ones, squares, ((1,), (1,)), lax.Precision.HIGHEST)[:1]
        inv_ref[l : l + 1, h * chunk : (h + 1) * chunk] = (
            lax.rsqrt(sums / features + epsilon) * features ** (-0.5)
        )


def stage_corpus(corpus):
    local_lists, list_length, features = corpus.shape
    chunk = min(list_length, 256)
    return pl.pallas_call(
        functools.partial(stage_kernel, chunk),
        out_shape=(
            pltpu.VMEM(corpus.shape, corpus.dtype),
            jax.ShapeDtypeStruct((local_lists, list_length), jnp.float32),
        ),
        in_specs=[pl.BlockSpec(memory_space=pl.ANY)],
        out_specs=(
            pl.BlockSpec(memory_space=pltpu.VMEM),
            pl.BlockSpec(memory_space=pltpu.VMEM),
        ),
        scratch_shapes=[
            pltpu.SemaphoreType.DMA((local_lists * (list_length // chunk),)),
        ],
        compiler_params=pltpu.CompilerParams(vmem_limit_bytes=24 * MIB),
        cost_estimate=pl.CostEstimate(
            flops=2 * corpus.size, bytes_accessed=2 * corpus.size, transcendentals=0
        ),
    )(corpus)


def score_kernel(sizes, me_ref, slot_ref, corpus_ref, inv_ref, *refs):
    owners, query_count, probe_count, cand_count, capacity, chunk = sizes
    message_refs, out_refs = refs[: len(refs) // 2], refs[len(refs) // 2 :]
    local_lists, list_length, features = corpus_ref.shape
    total = owners * query_count
    per_list = list_length // chunk
    message = jnp.concatenate([r[...].reshape(-1, r.shape[-1]) for r in message_refs], axis=0)

    width = probe_count * (1 + cand_count)
    padded = -(-width // 16) * 16
    eye = lax.broadcasted_iota(jnp.int32, (padded, LANES), 0) == lax.broadcasted_iota(
        jnp.int32, (padded, LANES), 1
    )
    turned = contract(
        eye.astype(jnp.float32).astype(jnp.bfloat16), message[:, features:], ((1,), (1,))
    )
    probes = turned[:probe_count]
    cands = [
        turned[probe_count * (1 + c) : probe_count * (2 + c)] for c in range(cand_count)
    ]

    slots = slot_ref[...]
    names = lax.broadcasted_iota(jnp.int32, slots.shape, 1).astype(jnp.float32)
    first = me_ref[0] * local_lists
    hits, wanted = [], []
    for l in range(local_lists):
        name = jnp.sum(jnp.where(slots == first + l, names, 0.0), axis=1, keepdims=True)
        named = probes == name
        hits.append(jnp.sum(named.astype(jnp.float32), axis=0, keepdims=True))
        wanted.append(
            [jnp.sum(jnp.where(named, c, 0.0), axis=0, keepdims=True) for c in cands]
        )
    hit = jnp.concatenate(hits, axis=0)

    span = min(total, LANES)
    earlier = lax.broadcasted_iota(jnp.int32, (span, span), 0)
    later = lax.broadcasted_iota(jnp.int32, (span, span), 1)
    before = (earlier < later) & (earlier // query_count == later // query_count)
    before = before.astype(jnp.float32).astype(jnp.bfloat16)
    hit_low = hit.astype(jnp.bfloat16)
    rank = jnp.concatenate(
        [
            contract(hit_low[:, j : j + span], before, ((1,), (0,)))
            for j in range(0, total, span)
        ],
        axis=1,
    )
    source = (lax.broadcasted_iota(jnp.int32, (1, total), 1) // query_count) * capacity
    target = jnp.where(hit > 0.5, rank.astype(jnp.int32) + source, -1)

    room = owners * capacity
    step = capacity * cand_count
    places = lax.broadcasted_iota(jnp.int32, (room, total), 0)
    queries = message[:, :features]
    for l in range(local_lists):
        pick = (places == target[l : l + 1]).astype(jnp.float32)
        blocks = [jnp.sum(pick * w, axis=1, keepdims=True) for w in wanted[l]]
        rows = contract(pick.astype(jnp.bfloat16), queries, ((1,), (0,)))
        inv_query = lax.rsqrt(jnp.sum(rows * rows, axis=1, keepdims=True) / features + epsilon)
        rows = rows.astype(jnp.bfloat16)
        chosen = [jnp.zeros((room, BLOCK), jnp.float32) for _ in range(cand_count)]
        for h in range(per_list):
            span_rows = slice(h * chunk, (h + 1) * chunk)
            products = contract(rows, corpus_ref[l, span_rows, :], ((1,), (1,)))
            scaled = products * inv_query * inv_ref[l : l + 1, span_rows]
            for j in range(chunk // BLOCK):
                number = (h * chunk + j * BLOCK) // BLOCK
                piece = scaled[:, j * BLOCK : (j + 1) * BLOCK]
                chosen = [
                    jnp.where(block == number, piece, old)
                    for block, old in zip(blocks, chosen)
                ]
        chosen = jnp.concatenate(
            [c.reshape(owners, capacity, BLOCK) for c in chosen], axis=1
        ).astype(jnp.bfloat16)
        each = owners // len(out_refs)
        for k, out_ref in enumerate(out_refs):
            out_ref[:, l * step : (l + 1) * step, :] = chosen[k * each : (k + 1) * each]


def block_scores(sizes, me, list_slot, corpus, inv_rows, messages):
    owners, query_count, probe_count, cand_count, capacity, chunk = sizes
    local_lists = corpus.shape[0]
    shape = (owners // len(messages), local_lists * cand_count * capacity, BLOCK)
    whole = pl.BlockSpec(memory_space=pltpu.VMEM)
    return pl.pallas_call(
        functools.partial(score_kernel, sizes),
        out_shape=[jax.ShapeDtypeStruct(shape, jnp.bfloat16) for _ in messages],
        in_specs=[pl.BlockSpec(memory_space=pltpu.SMEM)] + [whole] * (3 + len(messages)),
        out_specs=[whole] * len(messages),
        compiler_params=pltpu.CompilerParams(vmem_limit_bytes=40 * MIB),
        cost_estimate=pl.CostEstimate(
            flops=2 * owners * capacity * corpus.size,
            bytes_accessed=2 * corpus.size,
            transcendentals=0,
        ),
    )(me, list_slot, corpus, inv_rows, *messages)


def place_kernel(column_ref, *refs):
    pieces, out_ref = refs[:-1], refs[-1]
    returned = jnp.concatenate([r[...].reshape(-1, r.shape[-1]) for r in pieces], axis=0)
    lanes = lax.broadcasted_iota(jnp.int32, (out_ref.shape[0], returned.shape[0]), 1)
    pick = (lanes == column_ref[...]).astype(jnp.float32).astype(jnp.bfloat16)
    out_ref[...] = contract(pick, returned, ((1,), (0,))).astype(jnp.bfloat16)


def place(column, pieces):
    whole = pl.BlockSpec(memory_space=pltpu.VMEM)
    return pl.pallas_call(
        place_kernel,
        out_shape=jax.ShapeDtypeStruct((column.shape[0], BLOCK), jnp.bfloat16),
        in_specs=[whole] * (1 + len(pieces)),
        out_specs=whole,
        compiler_params=pltpu.CompilerParams(vmem_limit_bytes=24 * MIB),
    )(column, *pieces)


def swap(value, distance):
    owners = lax.axis_size("lists")
    return lax.ppermute(value, "lists", [(i, i ^ distance) for i in range(owners)])


def on_device(queries, corpus, list_slot, probes, cand):
    owners = lax.axis_size("lists")
    query_count, features = queries.shape
    probe_count = probes.shape[1]
    cand_count = cand.shape[2]
    local_lists, list_length, _ = corpus.shape
    total_lists = list_slot.shape[0]
    pair_count = query_count * probe_count
    capacity = min(query_count, max(2, (2 * pair_count + total_lists - 1) // total_lists))
    sizes = (owners, query_count, probe_count, cand_count, capacity, min(list_length, 512))
    pairwise = owners <= 16 and owners & (owners - 1) == 0
    me = lax.axis_index("lists").astype(jnp.int32)

    indices = jnp.concatenate([probes] + [cand[:, :, c] for c in range(cand_count)], axis=1)
    indices = jnp.pad(indices, ((0, 0), (0, LANES - indices.shape[1])))
    message = jnp.concatenate([queries, indices.astype(jnp.bfloat16)], axis=1)[None]
    if pairwise:
        messages = [message] + [swap(message, k) for k in range(1, owners)]
    else:
        messages = [lax.all_gather(message, "lists", axis=0, tiled=True)]

    held, inv_rows = stage_corpus(corpus)
    scores = block_scores(sizes, me.reshape(1), list_slot[None, :], held, inv_rows, messages)
    if pairwise:
        pieces = [scores[0]] + [swap(scores[k], k) for k in range(1, owners)]
    else:
        pieces = [lax.all_to_all(scores[0], "lists", split_axis=0, concat_axis=0, tiled=True)]

    position = jnp.sum(
        jnp.where(
            probes[:, :, None] == jnp.arange(total_lists, dtype=jnp.int32), list_slot, 0
        ),
        axis=2,
    )
    named = position[:, :, None] == jnp.arange(total_lists, dtype=jnp.int32)
    counts = jnp.cumsum(jnp.any(named, axis=1).astype(jnp.int32), axis=0)
    rank = jnp.sum(jnp.where(named, counts[:, None, :], 0), axis=2) - 1
    if pairwise:
        position = (position // local_lists ^ me) * local_lists + position % local_lists
    column = position[:, :, None] * (cand_count * capacity) + rank[:, :, None]
    column = column + capacity * jnp.arange(cand_count, dtype=jnp.int32)
    chosen = place(column.reshape(-1, 1), pieces)
    return chosen.reshape(query_count, probe_count, cand_count, BLOCK)


def solution(mesh):
    placed = (
        P(("groups", "lists", "rep"), None),
        P(("groups", "lists"), None, None),
        P("groups"),
        P(("groups", "lists", "rep"), None),
        P(("groups", "lists", "rep"), None, None),
    )
    return jax.shard_map(
        on_device,
        mesh=mesh,
        in_specs=placed,
        out_specs=P(("groups", "lists", "rep"), None, None, None),
        check_vma=False,
    )
```

```python
import functools

import jax
import jax.numpy as jnp
from jax import lax
from jax.experimental import pallas as pl
from jax.experimental.pallas import tpu as pltpu
from jax.sharding import PartitionSpec as P

BLOCK = 128
LANES = 128
MIB = 2**20

epsilon = 1e-06


def contract(a, b, dims, precision=None):
    return lax.dot_general(
        a, b, (dims, ((), ())), precision=precision, preferred_element_type=jnp.float32
    )


def in_hbm(value):
    return pltpu.with_memory_space_constraint(value, pltpu.HBM)


def stage_kernel(chunk, corpus_ref, held_ref, inv_ref, sems):
    local_lists, list_length, features = held_ref.shape
    per_list = list_length // chunk

    def copy(i):
        l, h = divmod(i, per_list)
        rows = pl.ds(h * chunk, chunk)
        return pltpu.make_async_copy(corpus_ref.at[l, rows], held_ref.at[l, rows], sems.at[i])

    for i in range(local_lists * per_list):
        copy(i).start()
    ones = jnp.ones((8, LANES), jnp.float32)
    for i in range(local_lists * per_list):
        l, h = divmod(i, per_list)
        copy(i).wait()
        wide = held_ref[l, h * chunk : (h + 1) * chunk, :].astype(jnp.float32)
        squares = functools.reduce(
            jnp.add, [wide[:, j : j + LANES] ** 2 for j in range(0, features, LANES)]
        )
        sums = contract(ones, squares, ((1,), (1,)), lax.Precision.HIGHEST)[:1]
        inv_ref[l : l + 1, h * chunk : (h + 1) * chunk] = (
            lax.rsqrt(sums / features + epsilon) * features ** (-0.5)
        )


def stage_corpus(corpus):
    local_lists, list_length, features = corpus.shape
    chunk = min(list_length, 256)
    return pl.pallas_call(
        functools.partial(stage_kernel, chunk),
        out_shape=(
            pltpu.VMEM(corpus.shape, corpus.dtype),
            jax.ShapeDtypeStruct((local_lists, list_length), jnp.float32),
        ),
        in_specs=[pl.BlockSpec(memory_space=pltpu.HBM)],
        out_specs=(
            pl.BlockSpec(memory_space=pltpu.VMEM),
            pl.BlockSpec(memory_space=pltpu.VMEM),
        ),
        scratch_shapes=[
            pltpu.SemaphoreType.DMA((local_lists * (list_length // chunk),)),
        ],
        compiler_params=pltpu.CompilerParams(vmem_limit_bytes=24 * MIB),
        cost_estimate=pl.CostEstimate(
            flops=2 * corpus.size, bytes_accessed=2 * corpus.size, transcendentals=0
        ),
    )(in_hbm(corpus))


def score_kernel(sizes, me_ref, slot_ref, corpus_ref, inv_ref, *refs):
    owners, query_count, probe_count, cand_count, capacity, chunk = sizes
    message_refs, out_refs = refs[: len(refs) // 2], refs[len(refs) // 2 :]
    local_lists, list_length, features = corpus_ref.shape
    total = owners * query_count
    per_list = list_length // chunk
    message = jnp.concatenate([r[...].reshape(-1, r.shape[-1]) for r in message_refs], axis=0)

    width = probe_count * (1 + cand_count)
    padded = -(-width // 16) * 16
    eye = lax.broadcasted_iota(jnp.int32, (padded, LANES), 0) == lax.broadcasted_iota(
        jnp.int32, (padded, LANES), 1
    )
    turned = contract(
        eye.astype(jnp.float32).astype(jnp.bfloat16), message[:, features:], ((1,), (1,))
    )
    probes = turned[:probe_count]
    cands = [
        turned[probe_count * (1 + c) : probe_count * (2 + c)] for c in range(cand_count)
    ]

    slots = slot_ref[...]
    names = lax.broadcasted_iota(jnp.int32, slots.shape, 1).astype(jnp.float32)
    first = me_ref[0] * local_lists
    hits, wanted = [], []
    for l in range(local_lists):
        name = jnp.sum(jnp.where(slots == first + l, names, 0.0), axis=1, keepdims=True)
        named = probes == name
        hits.append(jnp.sum(named.astype(jnp.float32), axis=0, keepdims=True))
        wanted.append(
            [jnp.sum(jnp.where(named, c, 0.0), axis=0, keepdims=True) for c in cands]
        )
    hit = jnp.concatenate(hits, axis=0)

    span = min(total, LANES)
    earlier = lax.broadcasted_iota(jnp.int32, (span, span), 0)
    later = lax.broadcasted_iota(jnp.int32, (span, span), 1)
    before = (earlier < later) & (earlier // query_count == later // query_count)
    before = before.astype(jnp.float32).astype(jnp.bfloat16)
    hit_low = hit.astype(jnp.bfloat16)
    rank = jnp.concatenate(
        [
            contract(hit_low[:, j : j + span], before, ((1,), (0,)))
            for j in range(0, total, span)
        ],
        axis=1,
    )
    source = (lax.broadcasted_iota(jnp.int32, (1, total), 1) // query_count) * capacity
    target = jnp.where(hit > 0.5, rank.astype(jnp.int32) + source, -1)

    room = owners * capacity
    step = capacity * cand_count
    places = lax.broadcasted_iota(jnp.int32, (room, total), 0)
    queries = message[:, :features]
    for l in range(local_lists):
        pick = (places == target[l : l + 1]).astype(jnp.float32)
        blocks = [jnp.sum(pick * w, axis=1, keepdims=True) for w in wanted[l]]
        rows = contract(pick.astype(jnp.bfloat16), queries, ((1,), (0,)))
        inv_query = lax.rsqrt(jnp.sum(rows * rows, axis=1, keepdims=True) / features + epsilon)
        rows = rows.astype(jnp.bfloat16)
        chosen = [jnp.zeros((room, BLOCK), jnp.float32) for _ in range(cand_count)]
        for h in range(per_list):
            span_rows = slice(h * chunk, (h + 1) * chunk)
            products = contract(rows, corpus_ref[l, span_rows, :], ((1,), (1,)))
            scaled = products * inv_query * inv_ref[l : l + 1, span_rows]
            for j in range(chunk // BLOCK):
                number = (h * chunk + j * BLOCK) // BLOCK
                piece = scaled[:, j * BLOCK : (j + 1) * BLOCK]
                chosen = [
                    jnp.where(block == number, piece, old)
                    for block, old in zip(blocks, chosen)
                ]
        chosen = jnp.concatenate(
            [c.reshape(owners, capacity, BLOCK) for c in chosen], axis=1
        ).astype(jnp.bfloat16)
        each = owners // len(out_refs)
        for k, out_ref in enumerate(out_refs):
            out_ref[:, l * step : (l + 1) * step, :] = chosen[k * each : (k + 1) * each]


def block_scores(sizes, me, list_slot, corpus, inv_rows, messages):
    owners, query_count, probe_count, cand_count, capacity, chunk = sizes
    local_lists = corpus.shape[0]
    shape = (owners // len(messages), local_lists * cand_count * capacity, BLOCK)
    whole = pl.BlockSpec(memory_space=pltpu.VMEM)
    return pl.pallas_call(
        functools.partial(score_kernel, sizes),
        out_shape=[jax.ShapeDtypeStruct(shape, jnp.bfloat16) for _ in messages],
        in_specs=[pl.BlockSpec(memory_space=pltpu.SMEM)] + [whole] * (3 + len(messages)),
        out_specs=[whole] * len(messages),
        compiler_params=pltpu.CompilerParams(vmem_limit_bytes=40 * MIB),
        cost_estimate=pl.CostEstimate(
            flops=2 * owners * capacity * corpus.size,
            bytes_accessed=2 * corpus.size,
            transcendentals=0,
        ),
    )(me, list_slot, corpus, inv_rows, *messages)


def place_kernel(column_ref, *refs):
    pieces, out_ref = refs[:-1], refs[-1]
    returned = jnp.concatenate([r[...].reshape(-1, r.shape[-1]) for r in pieces], axis=0)
    lanes = lax.broadcasted_iota(jnp.int32, (out_ref.shape[0], returned.shape[0]), 1)
    pick = (lanes == column_ref[...]).astype(jnp.float32).astype(jnp.bfloat16)
    out_ref[...] = contract(pick, returned, ((1,), (0,))).astype(jnp.bfloat16)


def place(column, pieces):
    whole = pl.BlockSpec(memory_space=pltpu.VMEM)
    return pl.pallas_call(
        place_kernel,
        out_shape=jax.ShapeDtypeStruct((column.shape[0], BLOCK), jnp.bfloat16),
        in_specs=[whole] * (1 + len(pieces)),
        out_specs=whole,
        compiler_params=pltpu.CompilerParams(vmem_limit_bytes=24 * MIB),
    )(column, *pieces)


def message_kernel(queries_ref, probes_ref, cand_ref, out_ref):
    owners, query_count, width = out_ref.shape
    features = queries_ref.shape[1]
    cand_count = cand_ref.shape[1]
    rows = jnp.concatenate(
        [probes_ref[...]] + [cand_ref[:, c, :] for c in range(cand_count)], axis=0
    ).astype(jnp.float32)
    eye = lax.broadcasted_iota(jnp.int32, (rows.shape[0], LANES), 0) == lax.broadcasted_iota(
        jnp.int32, (rows.shape[0], LANES), 1
    )
    indices = contract(
        rows.astype(jnp.bfloat16),
        eye.astype(jnp.float32).astype(jnp.bfloat16),
        ((0,), (0,)),
    ).astype(jnp.bfloat16)
    for k in range(owners):
        out_ref[k, :, :features] = queries_ref[...]
        out_ref[k, :, features:] = indices


def make_message(queries, probes, cand, owners):
    query_count, features = queries.shape
    whole = pl.BlockSpec(memory_space=pltpu.VMEM)
    return pl.pallas_call(
        message_kernel,
        out_shape=jax.ShapeDtypeStruct((owners, query_count, features + LANES), queries.dtype),
        in_specs=[whole] * 3,
        out_specs=whole,
        compiler_params=pltpu.CompilerParams(vmem_limit_bytes=24 * MIB),
    )(in_hbm(queries), in_hbm(probes.T), in_hbm(cand.transpose(1, 2, 0)))


def on_device(queries, corpus, list_slot, probes, cand):
    owners = lax.axis_size("lists")
    query_count, features = queries.shape
    probe_count = probes.shape[1]
    cand_count = cand.shape[2]
    local_lists, list_length, _ = corpus.shape
    total_lists = list_slot.shape[0]
    pair_count = query_count * probe_count
    capacity = min(query_count, max(2, (2 * pair_count + total_lists - 1) // total_lists))
    sizes = (owners, query_count, probe_count, cand_count, capacity, min(list_length, 512))
    me = lax.axis_index("lists").astype(jnp.int32)

    message = make_message(queries, probes, cand, owners)
    messages = lax.all_to_all(message, "lists", split_axis=0, concat_axis=0, tiled=True)
    held, inv_rows = stage_corpus(corpus)
    scores = block_scores(sizes, me.reshape(1), list_slot[None, :], held, inv_rows, [messages])
    pieces = lax.all_to_all(scores[0], "lists", split_axis=0, concat_axis=0, tiled=True)

    position = jnp.sum(
        jnp.where(
            probes[:, :, None] == jnp.arange(total_lists, dtype=jnp.int32), list_slot, 0
        ),
        axis=2,
    )
    named = position[:, :, None] == jnp.arange(total_lists, dtype=jnp.int32)
    counts = jnp.cumsum(jnp.any(named, axis=1).astype(jnp.int32), axis=0)
    rank = jnp.sum(jnp.where(named, counts[:, None, :], 0), axis=2) - 1
    column = position[:, :, None] * (cand_count * capacity) + rank[:, :, None]
    column = column + capacity * jnp.arange(cand_count, dtype=jnp.int32)
    chosen = place(column.reshape(-1, 1), [pieces])
    return chosen.reshape(query_count, probe_count, cand_count, BLOCK)


def solution(mesh):
    placed = (
        P(("groups", "lists", "rep"), None),
        P(("groups", "lists"), None, None),
        P("groups"),
        P(("groups", "lists", "rep"), None),
        P(("groups", "lists", "rep"), None, None),
    )
    return jax.shard_map(
        on_device,
        mesh=mesh,
        in_specs=placed,
        out_specs=P(("groups", "lists", "rep"), None, None, None),
        check_vma=False,
    )
```

```python
import functools

import jax
import jax.numpy as jnp
from jax import lax
from jax.experimental import pallas as pl
from jax.experimental.pallas import tpu as pltpu
from jax.sharding import PartitionSpec as P

BLOCK = 128
LANES = 128
MIB = 2**20

epsilon = 1e-06


def contract(a, b, dims, precision=None):
    return lax.dot_general(
        a, b, (dims, ((), ())), precision=precision, preferred_element_type=jnp.float32
    )


def in_hbm(value):
    return pltpu.with_memory_space_constraint(value, pltpu.HBM)


def stage_kernel(sizes, slot_ref, probes_ref, corpus_ref, held_ref, inv_ref, column_ref, sems):
    cand_count, capacity, chunk = sizes
    local_lists, list_length, features = held_ref.shape
    per_list = list_length // chunk

    def copy(i):
        l, h = divmod(i, per_list)
        rows = pl.ds(h * chunk, chunk)
        return pltpu.make_async_copy(corpus_ref.at[l, rows], held_ref.at[l, rows], sems.at[i])

    for i in range(local_lists * per_list):
        copy(i).start()
    column_ref[...] = result_columns(cand_count, capacity, slot_ref, probes_ref[...])
    ones = jnp.ones((8, 2 * LANES), jnp.bfloat16)
    for i in range(local_lists * per_list):
        l, h = divmod(i, per_list)
        copy(i).wait()
        wide = held_ref[l, h * chunk : (h + 1) * chunk, :].astype(jnp.float32)
        squares = functools.reduce(
            jnp.add, [wide[:, j : j + LANES] ** 2 for j in range(0, features, LANES)]
        )
        high = squares.astype(jnp.bfloat16)
        low = (squares - high.astype(jnp.float32)).astype(jnp.bfloat16)
        sums = contract(ones, jnp.concatenate([high, low], axis=1), ((1,), (1,)))[:1]
        inv_ref[l : l + 1, h * chunk : (h + 1) * chunk] = (
            lax.rsqrt(sums / features + epsilon) * features ** (-0.5)
        )


def result_columns(cand_count, capacity, slot_ref, probes):
    probe_count, query_count = probes.shape
    total_lists = slot_ref.shape[0]
    position = jnp.zeros(probes.shape, jnp.float32)
    for t in range(total_lists):
        position = jnp.where(probes == t, slot_ref[t].astype(jnp.float32), position)
    lists = lax.broadcasted_iota(jnp.int32, (total_lists, query_count), 0)
    named = [lists == probes[p : p + 1] for p in range(probe_count)]
    counts = functools.reduce(jnp.add, [n.astype(jnp.float32) for n in named])
    square = (query_count, query_count)
    before = lax.broadcasted_iota(jnp.int32, square, 0) < lax.broadcasted_iota(
        jnp.int32, square, 1
    )
    earlier = contract(
        counts.astype(jnp.bfloat16), before.astype(jnp.float32).astype(jnp.bfloat16), ((1,), (0,))
    )
    rank = jnp.concatenate(
        [jnp.sum(jnp.where(n, earlier, 0.0), axis=0, keepdims=True) for n in named], axis=0
    )
    rows = query_count * probe_count * cand_count
    row = lax.broadcasted_iota(jnp.int32, (rows, probe_count), 0)
    lane = lax.broadcasted_iota(jnp.int32, (rows, probe_count), 1)
    spread = (row // cand_count) % probe_count == lane
    spread = spread.astype(jnp.float32).astype(jnp.bfloat16)
    row = lax.broadcasted_iota(jnp.int32, (rows, query_count), 0)
    lane = lax.broadcasted_iota(jnp.int32, (rows, query_count), 1)
    own = row // (probe_count * cand_count) == lane
    value = contract(spread, position.astype(jnp.bfloat16), ((1,), (0,))) * (
        cand_count * capacity
    ) + contract(spread, rank.astype(jnp.bfloat16), ((1,), (0,)))
    column = jnp.sum(jnp.where(own, value, 0.0), axis=1, keepdims=True)
    shift = (lax.broadcasted_iota(jnp.int32, (rows, 1), 0) % cand_count) * capacity
    return column.astype(jnp.int32) + shift


def stage_corpus(list_slot, probes, corpus, cand_count, capacity):
    local_lists, list_length, features = corpus.shape
    chunk = min(list_length, 256)
    query_count, probe_count = probes.shape
    whole = pl.BlockSpec(memory_space=pltpu.VMEM)
    return pl.pallas_call(
        functools.partial(stage_kernel, (cand_count, capacity, chunk)),
        out_shape=(
            pltpu.VMEM(corpus.shape, corpus.dtype),
            jax.ShapeDtypeStruct((local_lists, list_length), jnp.float32),
            jax.ShapeDtypeStruct((query_count * probe_count * cand_count, 1), jnp.int32),
        ),
        in_specs=[
            pl.BlockSpec(memory_space=pltpu.SMEM),
            whole,
            pl.BlockSpec(memory_space=pltpu.HBM),
        ],
        out_specs=(whole, whole, whole),
        scratch_shapes=[
            pltpu.SemaphoreType.DMA((local_lists * (list_length // chunk),)),
        ],
        compiler_params=pltpu.CompilerParams(vmem_limit_bytes=24 * MIB),
        cost_estimate=pl.CostEstimate(
            flops=2 * corpus.size, bytes_accessed=2 * corpus.size, transcendentals=0
        ),
    )(list_slot, in_hbm(probes.T), in_hbm(corpus))


def score_kernel(sizes, me_ref, slot_ref, corpus_ref, inv_ref, *refs):
    owners, query_count, probe_count, cand_count, capacity, chunk = sizes
    message_refs, out_refs = refs[: len(refs) // 2], refs[len(refs) // 2 :]
    local_lists, list_length, features = corpus_ref.shape
    total = owners * query_count
    per_list = list_length // chunk
    message = jnp.concatenate([r[...].reshape(-1, r.shape[-1]) for r in message_refs], axis=0)

    width = probe_count * (1 + cand_count)
    padded = -(-width // 16) * 16
    eye = lax.broadcasted_iota(jnp.int32, (padded, LANES), 0) == lax.broadcasted_iota(
        jnp.int32, (padded, LANES), 1
    )
    turned = contract(
        eye.astype(jnp.float32).astype(jnp.bfloat16), message[:, features:], ((1,), (1,))
    )
    probes = turned[:probe_count]
    cands = [
        turned[probe_count * (1 + c) : probe_count * (2 + c)] for c in range(cand_count)
    ]

    slots = slot_ref[...]
    names = lax.broadcasted_iota(jnp.int32, slots.shape, 1).astype(jnp.float32)
    first = me_ref[0] * local_lists
    hits, wanted = [], []
    for l in range(local_lists):
        name = jnp.sum(jnp.where(slots == first + l, names, 0.0), axis=1, keepdims=True)
        named = probes == name
        hits.append(jnp.sum(named.astype(jnp.float32), axis=0, keepdims=True))
        wanted.append(
            [jnp.sum(jnp.where(named, c, 0.0), axis=0, keepdims=True) for c in cands]
        )
    hit = jnp.concatenate(hits, axis=0)

    span = min(total, LANES)
    earlier = lax.broadcasted_iota(jnp.int32, (span, span), 0)
    later = lax.broadcasted_iota(jnp.int32, (span, span), 1)
    before = (earlier < later) & (earlier // query_count == later // query_count)
    before = before.astype(jnp.float32).astype(jnp.bfloat16)
    hit_low = hit.astype(jnp.bfloat16)
    rank = jnp.concatenate(
        [
            contract(hit_low[:, j : j + span], before, ((1,), (0,)))
            for j in range(0, total, span)
        ],
        axis=1,
    )
    source = (lax.broadcasted_iota(jnp.int32, (1, total), 1) // query_count) * capacity
    target = jnp.where(hit > 0.5, rank.astype(jnp.int32) + source, -1)

    room = owners * capacity
    step = capacity * cand_count
    places = lax.broadcasted_iota(jnp.int32, (room, total), 0)
    queries = message[:, :features]
    for l in range(local_lists):
        pick = (places == target[l : l + 1]).astype(jnp.float32)
        blocks = [jnp.sum(pick * w, axis=1, keepdims=True) for w in wanted[l]]
        rows = contract(pick.astype(jnp.bfloat16), queries, ((1,), (0,)))
        inv_query = lax.rsqrt(jnp.sum(rows * rows, axis=1, keepdims=True) / features + epsilon)
        rows = rows.astype(jnp.bfloat16)
        chosen = [jnp.zeros((room, BLOCK), jnp.float32) for _ in range(cand_count)]
        for h in range(per_list):
            span_rows = slice(h * chunk, (h + 1) * chunk)
            products = contract(rows, corpus_ref[l, span_rows, :], ((1,), (1,)))
            scaled = products * inv_query * inv_ref[l : l + 1, span_rows]
            for j in range(chunk // BLOCK):
                number = (h * chunk + j * BLOCK) // BLOCK
                piece = scaled[:, j * BLOCK : (j + 1) * BLOCK]
                chosen = [
                    jnp.where(block == number, piece, old)
                    for block, old in zip(blocks, chosen)
                ]
        chosen = jnp.concatenate(
            [c.reshape(owners, capacity, BLOCK) for c in chosen], axis=1
        ).astype(jnp.bfloat16)
        each = owners // len(out_refs)
        for k, out_ref in enumerate(out_refs):
            out_ref[:, l * step : (l + 1) * step, :] = chosen[k * each : (k + 1) * each]


def block_scores(sizes, me, list_slot, corpus, inv_rows, messages):
    owners, query_count, probe_count, cand_count, capacity, chunk = sizes
    local_lists = corpus.shape[0]
    shape = (owners // len(messages), local_lists * cand_count * capacity, BLOCK)
    whole = pl.BlockSpec(memory_space=pltpu.VMEM)
    return pl.pallas_call(
        functools.partial(score_kernel, sizes),
        out_shape=[jax.ShapeDtypeStruct(shape, jnp.bfloat16) for _ in messages],
        in_specs=[pl.BlockSpec(memory_space=pltpu.SMEM)] + [whole] * (3 + len(messages)),
        out_specs=[whole] * len(messages),
        compiler_params=pltpu.CompilerParams(vmem_limit_bytes=40 * MIB),
        cost_estimate=pl.CostEstimate(
            flops=2 * owners * capacity * corpus.size,
            bytes_accessed=2 * corpus.size,
            transcendentals=0,
        ),
    )(me, list_slot, corpus, inv_rows, *messages)


def place_kernel(column_ref, *refs):
    pieces, out_ref = refs[:-1], refs[-1]
    returned = jnp.concatenate([r[...].reshape(-1, r.shape[-1]) for r in pieces], axis=0)
    lanes = lax.broadcasted_iota(jnp.int32, (out_ref.shape[0], returned.shape[0]), 1)
    pick = (lanes == column_ref[...]).astype(jnp.float32).astype(jnp.bfloat16)
    out_ref[...] = contract(pick, returned, ((1,), (0,))).astype(jnp.bfloat16)


def place(column, pieces):
    whole = pl.BlockSpec(memory_space=pltpu.VMEM)
    return pl.pallas_call(
        place_kernel,
        out_shape=jax.ShapeDtypeStruct((column.shape[0], BLOCK), jnp.bfloat16),
        in_specs=[whole] * (1 + len(pieces)),
        out_specs=whole,
        compiler_params=pltpu.CompilerParams(vmem_limit_bytes=24 * MIB),
    )(column, *pieces)


def message_kernel(queries_ref, probes_ref, cand_ref, out_ref):
    owners, query_count, width = out_ref.shape
    features = queries_ref.shape[1]
    cand_count = cand_ref.shape[1]
    rows = jnp.concatenate(
        [probes_ref[...]] + [cand_ref[:, c, :] for c in range(cand_count)], axis=0
    ).astype(jnp.float32)
    eye = lax.broadcasted_iota(jnp.int32, (rows.shape[0], LANES), 0) == lax.broadcasted_iota(
        jnp.int32, (rows.shape[0], LANES), 1
    )
    indices = contract(
        rows.astype(jnp.bfloat16),
        eye.astype(jnp.float32).astype(jnp.bfloat16),
        ((0,), (0,)),
    ).astype(jnp.bfloat16)
    for k in range(owners):
        out_ref[k, :, :features] = queries_ref[...]
        out_ref[k, :, features:] = indices


def make_message(queries, probes, cand, owners):
    query_count, features = queries.shape
    whole = pl.BlockSpec(memory_space=pltpu.VMEM)
    return pl.pallas_call(
        message_kernel,
        out_shape=jax.ShapeDtypeStruct((owners, query_count, features + LANES), queries.dtype),
        in_specs=[whole] * 3,
        out_specs=whole,
        compiler_params=pltpu.CompilerParams(vmem_limit_bytes=24 * MIB),
    )(in_hbm(queries), in_hbm(probes.T), in_hbm(cand.transpose(1, 2, 0)))


def on_device(queries, corpus, list_slot, probes, cand):
    owners = lax.axis_size("lists")
    query_count, features = queries.shape
    probe_count = probes.shape[1]
    cand_count = cand.shape[2]
    local_lists, list_length, _ = corpus.shape
    total_lists = list_slot.shape[0]
    pair_count = query_count * probe_count
    capacity = min(query_count, max(2, (2 * pair_count + total_lists - 1) // total_lists))
    sizes = (owners, query_count, probe_count, cand_count, capacity, min(list_length, 512))
    me = lax.axis_index("lists").astype(jnp.int32)

    message = make_message(queries, probes, cand, owners)
    messages = lax.all_to_all(message, "lists", split_axis=0, concat_axis=0, tiled=True)
    held, inv_rows, column = stage_corpus(list_slot, probes, corpus, cand_count, capacity)
    scores = block_scores(sizes, me.reshape(1), list_slot[None, :], held, inv_rows, [messages])
    pieces = lax.all_to_all(scores[0], "lists", split_axis=0, concat_axis=0, tiled=True)

    chosen = place(column, [pieces])
    return chosen.reshape(query_count, probe_count, cand_count, BLOCK)


def solution(mesh):
    placed = (
        P(("groups", "lists", "rep"), None),
        P(("groups", "lists"), None, None),
        P("groups"),
        P(("groups", "lists", "rep"), None),
        P(("groups", "lists", "rep"), None, None),
    )
    return jax.shard_map(
        on_device,
        mesh=mesh,
        in_specs=placed,
        out_specs=P(("groups", "lists", "rep"), None, None, None),
        check_vma=False,
    )
```

```python
import functools

import jax
import jax.numpy as jnp
from jax import lax
from jax.experimental import pallas as pl
from jax.experimental.pallas import tpu as pltpu
from jax.sharding import PartitionSpec as P

BLOCK = 128
LANES = 128
MIB = 2**20

epsilon = 1e-06


def contract(a, b, dims, precision=None):
    return lax.dot_general(
        a, b, (dims, ((), ())), precision=precision, preferred_element_type=jnp.float32
    )


def in_hbm(value):
    return pltpu.with_memory_space_constraint(value, pltpu.HBM)


def norm_kernel(sizes, slot_ref, probes_ref, corpus_ref, inv_ref, column_ref, held_ref, sems):
    cand_count, capacity, chunk = sizes
    local_lists, list_length, features = held_ref.shape
    per_list = list_length // chunk

    def copy(i):
        l, h = divmod(i, per_list)
        rows = pl.ds(h * chunk, chunk)
        return pltpu.make_async_copy(corpus_ref.at[l, rows], held_ref.at[l, rows], sems.at[i])

    for i in range(local_lists * per_list):
        copy(i).start()
    column_ref[...] = result_columns(cand_count, capacity, slot_ref, probes_ref[...])
    ones = jnp.ones((8, 2 * LANES), jnp.bfloat16)
    for i in range(local_lists * per_list):
        l, h = divmod(i, per_list)
        copy(i).wait()
        wide = held_ref[l, h * chunk : (h + 1) * chunk, :].astype(jnp.float32)
        squares = functools.reduce(
            jnp.add, [wide[:, j : j + LANES] ** 2 for j in range(0, features, LANES)]
        )
        high = squares.astype(jnp.bfloat16)
        low = (squares - high.astype(jnp.float32)).astype(jnp.bfloat16)
        sums = contract(ones, jnp.concatenate([high, low], axis=1), ((1,), (1,)))[:1]
        inv_ref[l : l + 1, h * chunk : (h + 1) * chunk] = (
            lax.rsqrt(sums / features + epsilon) * features ** (-0.5)
        )


def result_columns(cand_count, capacity, slot_ref, probes):
    probe_count, query_count = probes.shape
    total_lists = slot_ref.shape[0]
    position = jnp.zeros(probes.shape, jnp.float32)
    for t in range(total_lists):
        position = jnp.where(probes == t, slot_ref[t].astype(jnp.float32), position)
    lists = lax.broadcasted_iota(jnp.int32, (total_lists, query_count), 0)
    named = [lists == probes[p : p + 1] for p in range(probe_count)]
    counts = functools.reduce(jnp.add, [n.astype(jnp.float32) for n in named])
    square = (query_count, query_count)
    before = lax.broadcasted_iota(jnp.int32, square, 0) < lax.broadcasted_iota(
        jnp.int32, square, 1
    )
    earlier = contract(
        counts.astype(jnp.bfloat16), before.astype(jnp.float32).astype(jnp.bfloat16), ((1,), (0,))
    )
    rank = jnp.concatenate(
        [jnp.sum(jnp.where(n, earlier, 0.0), axis=0, keepdims=True) for n in named], axis=0
    )
    rows = query_count * probe_count * cand_count
    row = lax.broadcasted_iota(jnp.int32, (rows, probe_count), 0)
    lane = lax.broadcasted_iota(jnp.int32, (rows, probe_count), 1)
    spread = (row // cand_count) % probe_count == lane
    spread = spread.astype(jnp.float32).astype(jnp.bfloat16)
    row = lax.broadcasted_iota(jnp.int32, (rows, query_count), 0)
    lane = lax.broadcasted_iota(jnp.int32, (rows, query_count), 1)
    own = row // (probe_count * cand_count) == lane
    value = contract(spread, position.astype(jnp.bfloat16), ((1,), (0,))) * (
        cand_count * capacity
    ) + contract(spread, rank.astype(jnp.bfloat16), ((1,), (0,)))
    column = jnp.sum(jnp.where(own, value, 0.0), axis=1, keepdims=True)
    shift = (lax.broadcasted_iota(jnp.int32, (rows, 1), 0) % cand_count) * capacity
    return column.astype(jnp.int32) + shift


def row_norms(list_slot, probes, corpus, cand_count, capacity):
    local_lists, list_length, features = corpus.shape
    chunk = min(list_length, 256)
    query_count, probe_count = probes.shape
    whole = pl.BlockSpec(memory_space=pltpu.VMEM)
    return pl.pallas_call(
        functools.partial(norm_kernel, (cand_count, capacity, chunk)),
        out_shape=(
            jax.ShapeDtypeStruct((local_lists, list_length), jnp.float32),
            jax.ShapeDtypeStruct((query_count * probe_count * cand_count, 1), jnp.int32),
        ),
        in_specs=[
            pl.BlockSpec(memory_space=pltpu.SMEM),
            whole,
            pl.BlockSpec(memory_space=pltpu.HBM),
        ],
        out_specs=(whole, whole),
        scratch_shapes=[
            pltpu.VMEM(corpus.shape, corpus.dtype),
            pltpu.SemaphoreType.DMA((local_lists * (list_length // chunk),)),
        ],
        compiler_params=pltpu.CompilerParams(vmem_limit_bytes=24 * MIB),
        cost_estimate=pl.CostEstimate(
            flops=2 * corpus.size, bytes_accessed=2 * corpus.size, transcendentals=0
        ),
    )(list_slot, in_hbm(probes.T), in_hbm(corpus))


def score_kernel(sizes, me_ref, slot_ref, corpus_ref, inv_ref, message_ref, out_ref, held, sems):
    owners, query_count, probe_count, cand_count, capacity, chunk = sizes
    local_lists, list_length, features = held.shape
    total = owners * query_count
    per_list = list_length // chunk

    def copy(i):
        l, h = divmod(i, per_list)
        rows = pl.ds(h * chunk, chunk)
        return pltpu.make_async_copy(corpus_ref.at[l, rows], held.at[l, rows], sems.at[i])

    for i in range(local_lists * per_list):
        copy(i).start()
    message = message_ref[...].reshape(total, -1)

    width = probe_count * (1 + cand_count)
    padded = -(-width // 16) * 16
    eye = lax.broadcasted_iota(jnp.int32, (padded, LANES), 0) == lax.broadcasted_iota(
        jnp.int32, (padded, LANES), 1
    )
    turned = contract(
        eye.astype(jnp.float32).astype(jnp.bfloat16), message[:, features:], ((1,), (1,))
    )
    probes = turned[:probe_count]
    cands = [
        turned[probe_count * (1 + c) : probe_count * (2 + c)] for c in range(cand_count)
    ]

    slots = slot_ref[...]
    names = lax.broadcasted_iota(jnp.int32, slots.shape, 1).astype(jnp.float32)
    first = me_ref[0] * local_lists
    hits, wanted = [], []
    for l in range(local_lists):
        name = jnp.sum(jnp.where(slots == first + l, names, 0.0), axis=1, keepdims=True)
        named = probes == name
        hits.append(jnp.sum(named.astype(jnp.float32), axis=0, keepdims=True))
        wanted.append(
            [jnp.sum(jnp.where(named, c, 0.0), axis=0, keepdims=True) for c in cands]
        )
    hit = jnp.concatenate(hits, axis=0)

    span = min(total, LANES)
    earlier = lax.broadcasted_iota(jnp.int32, (span, span), 0)
    later = lax.broadcasted_iota(jnp.int32, (span, span), 1)
    before = (earlier < later) & (earlier // query_count == later // query_count)
    before = before.astype(jnp.float32).astype(jnp.bfloat16)
    hit_low = hit.astype(jnp.bfloat16)
    rank = jnp.concatenate(
        [
            contract(hit_low[:, j : j + span], before, ((1,), (0,)))
            for j in range(0, total, span)
        ],
        axis=1,
    )
    source = (lax.broadcasted_iota(jnp.int32, (1, total), 1) // query_count) * capacity
    target = jnp.where(hit > 0.5, rank.astype(jnp.int32) + source, -1)

    room = owners * capacity
    step = capacity * cand_count
    places = lax.broadcasted_iota(jnp.int32, (room, total), 0)
    queries = message[:, :features]
    for l in range(local_lists):
        pick = (places == target[l : l + 1]).astype(jnp.float32)
        blocks = [jnp.sum(pick * w, axis=1, keepdims=True) for w in wanted[l]]
        rows = contract(pick.astype(jnp.bfloat16), queries, ((1,), (0,)))
        inv_query = lax.rsqrt(jnp.sum(rows * rows, axis=1, keepdims=True) / features + epsilon)
        rows = rows.astype(jnp.bfloat16)
        chosen = [jnp.zeros((room, BLOCK), jnp.float32) for _ in range(cand_count)]
        for h in range(per_list):
            span_rows = slice(h * chunk, (h + 1) * chunk)
            copy(l * per_list + h).wait()
            products = contract(rows, held[l, span_rows, :], ((1,), (1,)))
            scaled = products * inv_query * inv_ref[l : l + 1, span_rows]
            for j in range(chunk // BLOCK):
                number = (h * chunk + j * BLOCK) // BLOCK
                piece = scaled[:, j * BLOCK : (j + 1) * BLOCK]
                chosen = [
                    jnp.where(block == number, piece, old)
                    for block, old in zip(blocks, chosen)
                ]
        chosen = jnp.concatenate(
            [c.reshape(owners, capacity, BLOCK) for c in chosen], axis=1
        ).astype(jnp.bfloat16)
        out_ref[:, l * step : (l + 1) * step, :] = chosen


def block_scores(sizes, me, list_slot, corpus, inv_rows, messages):
    owners, query_count, probe_count, cand_count, capacity, chunk = sizes
    local_lists, list_length, _ = corpus.shape
    whole = pl.BlockSpec(memory_space=pltpu.VMEM)
    return pl.pallas_call(
        functools.partial(score_kernel, sizes),
        out_shape=jax.ShapeDtypeStruct(
            (owners, local_lists * cand_count * capacity, BLOCK), jnp.bfloat16
        ),
        in_specs=[
            pl.BlockSpec(memory_space=pltpu.SMEM),
            whole,
            pl.BlockSpec(memory_space=pltpu.HBM),
            whole,
            whole,
        ],
        out_specs=whole,
        scratch_shapes=[
            pltpu.VMEM(corpus.shape, corpus.dtype),
            pltpu.SemaphoreType.DMA((local_lists * (list_length // chunk),)),
        ],
        compiler_params=pltpu.CompilerParams(vmem_limit_bytes=40 * MIB),
        cost_estimate=pl.CostEstimate(
            flops=2 * owners * capacity * corpus.size,
            bytes_accessed=2 * corpus.size,
            transcendentals=0,
        ),
    )(me, list_slot, in_hbm(corpus), inv_rows, messages)


def place_kernel(column_ref, returned_ref, out_ref):
    returned = returned_ref[...].reshape(-1, returned_ref.shape[-1])
    lanes = lax.broadcasted_iota(jnp.int32, (out_ref.shape[0], returned.shape[0]), 1)
    pick = (lanes == column_ref[...]).astype(jnp.float32).astype(jnp.bfloat16)
    out_ref[...] = contract(pick, returned, ((1,), (0,))).astype(jnp.bfloat16)


def place(column, returned):
    whole = pl.BlockSpec(memory_space=pltpu.VMEM)
    return pl.pallas_call(
        place_kernel,
        out_shape=jax.ShapeDtypeStruct((column.shape[0], BLOCK), jnp.bfloat16),
        in_specs=[whole] * 2,
        out_specs=whole,
        compiler_params=pltpu.CompilerParams(vmem_limit_bytes=24 * MIB),
    )(column, returned)


def message_kernel(queries_ref, probes_ref, cand_ref, out_ref):
    owners, query_count, width = out_ref.shape
    features = queries_ref.shape[1]
    cand_count = cand_ref.shape[1]
    rows = jnp.concatenate(
        [probes_ref[...]] + [cand_ref[:, c, :] for c in range(cand_count)], axis=0
    ).astype(jnp.float32)
    eye = lax.broadcasted_iota(jnp.int32, (rows.shape[0], LANES), 0) == lax.broadcasted_iota(
        jnp.int32, (rows.shape[0], LANES), 1
    )
    indices = contract(
        rows.astype(jnp.bfloat16),
        eye.astype(jnp.float32).astype(jnp.bfloat16),
        ((0,), (0,)),
    ).astype(jnp.bfloat16)
    for k in range(owners):
        out_ref[k, :, :features] = queries_ref[...]
        out_ref[k, :, features:] = indices


def make_message(queries, probes, cand, owners):
    query_count, features = queries.shape
    whole = pl.BlockSpec(memory_space=pltpu.VMEM)
    return pl.pallas_call(
        message_kernel,
        out_shape=jax.ShapeDtypeStruct((owners, query_count, features + LANES), queries.dtype),
        in_specs=[whole] * 3,
        out_specs=whole,
        compiler_params=pltpu.CompilerParams(vmem_limit_bytes=24 * MIB),
    )(in_hbm(queries), in_hbm(probes.T), in_hbm(cand.transpose(1, 2, 0)))


def on_device(queries, corpus, list_slot, probes, cand):
    owners = lax.axis_size("lists")
    query_count, features = queries.shape
    probe_count = probes.shape[1]
    cand_count = cand.shape[2]
    local_lists, list_length, _ = corpus.shape
    total_lists = list_slot.shape[0]
    pair_count = query_count * probe_count
    capacity = min(query_count, max(2, (2 * pair_count + total_lists - 1) // total_lists))
    sizes = (owners, query_count, probe_count, cand_count, capacity, min(list_length, 512))
    me = lax.axis_index("lists").astype(jnp.int32)

    message = make_message(queries, probes, cand, owners)
    messages = lax.all_to_all(message, "lists", split_axis=0, concat_axis=0, tiled=True)
    inv_rows, column = row_norms(list_slot, probes, corpus, cand_count, capacity)
    scores = block_scores(sizes, me.reshape(1), list_slot[None, :], corpus, inv_rows, messages)
    returned = lax.all_to_all(scores, "lists", split_axis=0, concat_axis=0, tiled=True)
    chosen = place(column, returned)
    return chosen.reshape(query_count, probe_count, cand_count, BLOCK)


def solution(mesh):
    placed = (
        P(("groups", "lists", "rep"), None),
        P(("groups", "lists"), None, None),
        P("groups"),
        P(("groups", "lists", "rep"), None),
        P(("groups", "lists", "rep"), None, None),
    )
    return jax.shard_map(
        on_device,
        mesh=mesh,
        in_specs=placed,
        out_specs=P(("groups", "lists", "rep"), None, None, None),
        check_vma=False,
    )
```

```python
import functools

import jax
import jax.numpy as jnp
from jax import lax
from jax.experimental import pallas as pl
from jax.experimental.pallas import tpu as pltpu
from jax.sharding import PartitionSpec as P

BLOCK = 128
LANES = 128
MIB = 2**20

epsilon = 1e-06


def contract(a, b, dims, precision=None):
    return lax.dot_general(
        a, b, (dims, ((), ())), precision=precision, preferred_element_type=jnp.float32
    )


def in_hbm(value):
    return pltpu.with_memory_space_constraint(value, pltpu.HBM)


def exchange_order(owners):
    if owners > 16:
        return list(range(owners))
    return sorted(range(owners), key=lambda i: (abs(2 * i + 1 - owners) // 4, i))


def exchange(value):
    order = exchange_order(lax.axis_size("lists"))
    return lax.all_to_all(
        value, "lists", split_axis=0, concat_axis=0, axis_index_groups=[order], tiled=True
    )


def norm_kernel(sizes, slot_ref, probes_ref, corpus_ref, inv_ref, column_ref, held_ref, sems):
    cand_count, capacity, chunk = sizes
    local_lists, list_length, features = held_ref.shape
    per_list = list_length // chunk

    def copy(i):
        l, h = divmod(i, per_list)
        rows = pl.ds(h * chunk, chunk)
        return pltpu.make_async_copy(corpus_ref.at[l, rows], held_ref.at[l, rows], sems.at[i])

    for i in range(local_lists * per_list):
        copy(i).start()
    column_ref[...] = result_columns(
        cand_count, capacity, local_lists, slot_ref, probes_ref[...]
    )
    ones = jnp.ones((8, 2 * LANES), jnp.bfloat16)
    for i in range(local_lists * per_list):
        l, h = divmod(i, per_list)
        copy(i).wait()
        wide = held_ref[l, h * chunk : (h + 1) * chunk, :].astype(jnp.float32)
        squares = functools.reduce(
            jnp.add, [wide[:, j : j + LANES] ** 2 for j in range(0, features, LANES)]
        )
        high = squares.astype(jnp.bfloat16)
        low = (squares - high.astype(jnp.float32)).astype(jnp.bfloat16)
        sums = contract(ones, jnp.concatenate([high, low], axis=1), ((1,), (1,)))[:1]
        inv_ref[l : l + 1, h * chunk : (h + 1) * chunk] = (
            lax.rsqrt(sums / features + epsilon) * features ** (-0.5)
        )


def result_columns(cand_count, capacity, local_lists, slot_ref, probes):
    probe_count, query_count = probes.shape
    total_lists = slot_ref.shape[0]
    order = exchange_order(total_lists // local_lists)
    position = jnp.zeros(probes.shape, jnp.float32)
    for t in range(total_lists):
        owner = slot_ref[t] // local_lists
        place = owner
        for j, i in enumerate(order):
            if i != j:
                place = jnp.where(owner == i, j, place)
        spot = place * local_lists + slot_ref[t] % local_lists
        position = jnp.where(probes == t, spot.astype(jnp.float32), position)
    lists = lax.broadcasted_iota(jnp.int32, (total_lists, query_count), 0)
    named = [lists == probes[p : p + 1] for p in range(probe_count)]
    counts = functools.reduce(jnp.add, [n.astype(jnp.float32) for n in named])
    square = (query_count, query_count)
    before = lax.broadcasted_iota(jnp.int32, square, 0) < lax.broadcasted_iota(
        jnp.int32, square, 1
    )
    earlier = contract(
        counts.astype(jnp.bfloat16), before.astype(jnp.float32).astype(jnp.bfloat16), ((1,), (0,))
    )
    rank = jnp.concatenate(
        [jnp.sum(jnp.where(n, earlier, 0.0), axis=0, keepdims=True) for n in named], axis=0
    )
    rows = query_count * probe_count * cand_count
    row = lax.broadcasted_iota(jnp.int32, (rows, probe_count), 0)
    lane = lax.broadcasted_iota(jnp.int32, (rows, probe_count), 1)
    spread = (row // cand_count) % probe_count == lane
    spread = spread.astype(jnp.float32).astype(jnp.bfloat16)
    row = lax.broadcasted_iota(jnp.int32, (rows, query_count), 0)
    lane = lax.broadcasted_iota(jnp.int32, (rows, query_count), 1)
    own = row // (probe_count * cand_count) == lane
    value = contract(spread, position.astype(jnp.bfloat16), ((1,), (0,))) * (
        cand_count * capacity
    ) + contract(spread, rank.astype(jnp.bfloat16), ((1,), (0,)))
    column = jnp.sum(jnp.where(own, value, 0.0), axis=1, keepdims=True)
    shift = (lax.broadcasted_iota(jnp.int32, (rows, 1), 0) % cand_count) * capacity
    return column.astype(jnp.int32) + shift


def row_norms(list_slot, probes, corpus, cand_count, capacity):
    local_lists, list_length, features = corpus.shape
    chunk = min(list_length, 256)
    query_count, probe_count = probes.shape
    whole = pl.BlockSpec(memory_space=pltpu.VMEM)
    return pl.pallas_call(
        functools.partial(norm_kernel, (cand_count, capacity, chunk)),
        out_shape=(
            jax.ShapeDtypeStruct((local_lists, list_length), jnp.float32),
            jax.ShapeDtypeStruct((query_count * probe_count * cand_count, 1), jnp.int32),
        ),
        in_specs=[
            pl.BlockSpec(memory_space=pltpu.SMEM),
            whole,
            pl.BlockSpec(memory_space=pltpu.HBM),
        ],
        out_specs=(whole, whole),
        scratch_shapes=[
            pltpu.VMEM(corpus.shape, corpus.dtype),
            pltpu.SemaphoreType.DMA((local_lists * (list_length // chunk),)),
        ],
        compiler_params=pltpu.CompilerParams(vmem_limit_bytes=24 * MIB),
        cost_estimate=pl.CostEstimate(
            flops=2 * corpus.size, bytes_accessed=2 * corpus.size, transcendentals=0
        ),
    )(list_slot, in_hbm(probes.T), in_hbm(corpus))


def score_kernel(sizes, me_ref, slot_ref, corpus_ref, inv_ref, message_ref, out_ref, held, sems):
    owners, query_count, probe_count, cand_count, capacity, chunk = sizes
    local_lists, list_length, features = held.shape
    total = owners * query_count
    per_list = list_length // chunk

    def copy(i):
        l, h = divmod(i, per_list)
        rows = pl.ds(h * chunk, chunk)
        return pltpu.make_async_copy(corpus_ref.at[l, rows], held.at[l, rows], sems.at[i])

    for i in range(local_lists * per_list):
        copy(i).start()
    message = message_ref[...].reshape(total, -1)

    width = probe_count * (1 + cand_count)
    padded = -(-width // 16) * 16
    eye = lax.broadcasted_iota(jnp.int32, (padded, LANES), 0) == lax.broadcasted_iota(
        jnp.int32, (padded, LANES), 1
    )
    turned = contract(
        eye.astype(jnp.float32).astype(jnp.bfloat16), message[:, features:], ((1,), (1,))
    )
    probes = turned[:probe_count]
    cands = [
        turned[probe_count * (1 + c) : probe_count * (2 + c)] for c in range(cand_count)
    ]

    slots = slot_ref[...]
    names = lax.broadcasted_iota(jnp.int32, slots.shape, 1).astype(jnp.float32)
    first = me_ref[0] * local_lists
    hits, wanted = [], []
    for l in range(local_lists):
        name = jnp.sum(jnp.where(slots == first + l, names, 0.0), axis=1, keepdims=True)
        named = probes == name
        hits.append(jnp.sum(named.astype(jnp.float32), axis=0, keepdims=True))
        wanted.append(
            [jnp.sum(jnp.where(named, c, 0.0), axis=0, keepdims=True) for c in cands]
        )
    hit = jnp.concatenate(hits, axis=0)

    span = min(total, LANES)
    earlier = lax.broadcasted_iota(jnp.int32, (span, span), 0)
    later = lax.broadcasted_iota(jnp.int32, (span, span), 1)
    before = (earlier < later) & (earlier // query_count == later // query_count)
    before = before.astype(jnp.float32).astype(jnp.bfloat16)
    hit_low = hit.astype(jnp.bfloat16)
    rank = jnp.concatenate(
        [
            contract(hit_low[:, j : j + span], before, ((1,), (0,)))
            for j in range(0, total, span)
        ],
        axis=1,
    )
    source = (lax.broadcasted_iota(jnp.int32, (1, total), 1) // query_count) * capacity
    target = jnp.where(hit > 0.5, rank.astype(jnp.int32) + source, -1)

    room = owners * capacity
    step = capacity * cand_count
    places = lax.broadcasted_iota(jnp.int32, (room, total), 0)
    queries = message[:, :features]
    for l in range(local_lists):
        pick = (places == target[l : l + 1]).astype(jnp.float32)
        blocks = [jnp.sum(pick * w, axis=1, keepdims=True) for w in wanted[l]]
        rows = contract(pick.astype(jnp.bfloat16), queries, ((1,), (0,)))
        inv_query = lax.rsqrt(jnp.sum(rows * rows, axis=1, keepdims=True) / features + epsilon)
        rows = rows.astype(jnp.bfloat16)
        chosen = [jnp.zeros((room, BLOCK), jnp.float32) for _ in range(cand_count)]
        for h in range(per_list):
            span_rows = slice(h * chunk, (h + 1) * chunk)
            copy(l * per_list + h).wait()
            products = contract(rows, held[l, span_rows, :], ((1,), (1,)))
            scaled = products * inv_query * inv_ref[l : l + 1, span_rows]
            for j in range(chunk // BLOCK):
                number = (h * chunk + j * BLOCK) // BLOCK
                piece = scaled[:, j * BLOCK : (j + 1) * BLOCK]
                chosen = [
                    jnp.where(block == number, piece, old)
                    for block, old in zip(blocks, chosen)
                ]
        chosen = jnp.concatenate(
            [c.reshape(owners, capacity, BLOCK) for c in chosen], axis=1
        ).astype(jnp.bfloat16)
        out_ref[:, l * step : (l + 1) * step, :] = chosen


def block_scores(sizes, me, list_slot, corpus, inv_rows, messages):
    owners, query_count, probe_count, cand_count, capacity, chunk = sizes
    local_lists, list_length, _ = corpus.shape
    whole = pl.BlockSpec(memory_space=pltpu.VMEM)
    return pl.pallas_call(
        functools.partial(score_kernel, sizes),
        out_shape=jax.ShapeDtypeStruct(
            (owners, local_lists * cand_count * capacity, BLOCK), jnp.bfloat16
        ),
        in_specs=[
            pl.BlockSpec(memory_space=pltpu.SMEM),
            whole,
            pl.BlockSpec(memory_space=pltpu.HBM),
            whole,
            whole,
        ],
        out_specs=whole,
        scratch_shapes=[
            pltpu.VMEM(corpus.shape, corpus.dtype),
            pltpu.SemaphoreType.DMA((local_lists * (list_length // chunk),)),
        ],
        compiler_params=pltpu.CompilerParams(vmem_limit_bytes=40 * MIB),
        cost_estimate=pl.CostEstimate(
            flops=2 * owners * capacity * corpus.size,
            bytes_accessed=2 * corpus.size,
            transcendentals=0,
        ),
    )(me, list_slot, in_hbm(corpus), inv_rows, messages)


def place_kernel(column_ref, returned_ref, out_ref):
    returned = returned_ref[...].reshape(-1, returned_ref.shape[-1])
    lanes = lax.broadcasted_iota(jnp.int32, (out_ref.shape[0], returned.shape[0]), 1)
    pick = (lanes == column_ref[...]).astype(jnp.float32).astype(jnp.bfloat16)
    out_ref[...] = contract(pick, returned, ((1,), (0,))).astype(jnp.bfloat16)


def place(column, returned):
    whole = pl.BlockSpec(memory_space=pltpu.VMEM)
    return pl.pallas_call(
        place_kernel,
        out_shape=jax.ShapeDtypeStruct((column.shape[0], BLOCK), jnp.bfloat16),
        in_specs=[whole] * 2,
        out_specs=whole,
        compiler_params=pltpu.CompilerParams(vmem_limit_bytes=24 * MIB),
    )(column, returned)


def message_kernel(queries_ref, probes_ref, cand_ref, out_ref):
    owners, query_count, width = out_ref.shape
    features = queries_ref.shape[1]
    cand_count = cand_ref.shape[1]
    rows = jnp.concatenate(
        [probes_ref[...]] + [cand_ref[:, c, :] for c in range(cand_count)], axis=0
    ).astype(jnp.float32)
    eye = lax.broadcasted_iota(jnp.int32, (rows.shape[0], LANES), 0) == lax.broadcasted_iota(
        jnp.int32, (rows.shape[0], LANES), 1
    )
    indices = contract(
        rows.astype(jnp.bfloat16),
        eye.astype(jnp.float32).astype(jnp.bfloat16),
        ((0,), (0,)),
    ).astype(jnp.bfloat16)
    for k in range(owners):
        out_ref[k, :, :features] = queries_ref[...]
        out_ref[k, :, features:] = indices


def make_message(queries, probes, cand, owners):
    query_count, features = queries.shape
    whole = pl.BlockSpec(memory_space=pltpu.VMEM)
    return pl.pallas_call(
        message_kernel,
        out_shape=jax.ShapeDtypeStruct((owners, query_count, features + LANES), queries.dtype),
        in_specs=[whole] * 3,
        out_specs=whole,
        compiler_params=pltpu.CompilerParams(vmem_limit_bytes=24 * MIB),
    )(in_hbm(queries), in_hbm(probes.T), in_hbm(cand.transpose(1, 2, 0)))


def on_device(queries, corpus, list_slot, probes, cand):
    owners = lax.axis_size("lists")
    query_count, features = queries.shape
    probe_count = probes.shape[1]
    cand_count = cand.shape[2]
    local_lists, list_length, _ = corpus.shape
    total_lists = list_slot.shape[0]
    pair_count = query_count * probe_count
    capacity = min(query_count, max(2, (2 * pair_count + total_lists - 1) // total_lists))
    sizes = (owners, query_count, probe_count, cand_count, capacity, min(list_length, 512))
    me = lax.axis_index("lists").astype(jnp.int32)

    message = make_message(queries, probes, cand, owners)
    messages = exchange(message)
    inv_rows, column = row_norms(list_slot, probes, corpus, cand_count, capacity)
    scores = block_scores(sizes, me.reshape(1), list_slot[None, :], corpus, inv_rows, messages)
    returned = exchange(scores)
    chosen = place(column, returned)
    return chosen.reshape(query_count, probe_count, cand_count, BLOCK)


def solution(mesh):
    placed = (
        P(("groups", "lists", "rep"), None),
        P(("groups", "lists"), None, None),
        P("groups"),
        P(("groups", "lists", "rep"), None),
        P(("groups", "lists", "rep"), None, None),
    )
    return jax.shard_map(
        on_device,
        mesh=mesh,
        in_specs=placed,
        out_specs=P(("groups", "lists", "rep"), None, None, None),
        check_vma=False,
    )
```

```python
import functools

import jax
import jax.numpy as jnp
from jax import lax
from jax.experimental import pallas as pl
from jax.experimental.pallas import tpu as pltpu
from jax.sharding import PartitionSpec as P

BLOCK = 128
LANES = 128
MIB = 2**20

epsilon = 1e-06


def contract(a, b, dims, precision=None):
    return lax.dot_general(
        a, b, (dims, ((), ())), precision=precision, preferred_element_type=jnp.float32
    )


def in_hbm(value):
    return pltpu.with_memory_space_constraint(value, pltpu.HBM)


def exchange(value):
    order = list(reversed(range(lax.axis_size("lists"))))
    return lax.all_to_all(
        value, "lists", split_axis=0, concat_axis=0, axis_index_groups=[order], tiled=True
    )


def norm_kernel(
    sizes, slot_ref, probes_ref, corpus_ref, inv_ref, column_ref, held, parts, slots, sems, slot_sem
):
    cand_count, capacity, chunk = sizes
    local_lists, list_length, features = held.shape
    per_list = list_length // chunk

    def copy(i):
        l, h = divmod(i, per_list)
        rows = pl.ds(h * chunk, chunk)
        return pltpu.make_async_copy(corpus_ref.at[l, rows], held.at[l, rows], sems.at[i])

    slot_copy = pltpu.make_async_copy(slot_ref, slots, slot_sem)
    slot_copy.start()
    for i in range(local_lists * per_list):
        copy(i).start()
    slot_copy.wait()
    column_ref[...] = result_columns(cand_count, capacity, local_lists, slots, probes_ref[...])
    ones = jnp.ones((8, 2 * LANES), jnp.bfloat16)
    for l in range(local_lists):
        for h in range(per_list):
            copy(l * per_list + h).wait()
            rows = slice(h * chunk, (h + 1) * chunk)
            wide = held[l, rows, :].astype(jnp.float32)
            squares = functools.reduce(
                jnp.add, [wide[:, j : j + LANES] ** 2 for j in range(0, features, LANES)]
            )
            high = squares.astype(jnp.bfloat16)
            parts[l, rows, :LANES] = high
            parts[l, rows, LANES:] = (squares - high.astype(jnp.float32)).astype(jnp.bfloat16)
        sums = contract(ones, parts[l], ((1,), (1,)))[:1]
        inv_ref[l : l + 1, :] = lax.rsqrt(sums / features + epsilon) * features ** (-0.5)


def result_columns(cand_count, capacity, local_lists, slot_ref, probes):
    probe_count, query_count = probes.shape
    total_lists = slot_ref.shape[0]
    owners = total_lists // local_lists
    position = jnp.zeros(probes.shape, jnp.float32)
    for t in range(total_lists):
        owner = slot_ref[t] // local_lists
        spot = (owners - 1 - owner) * local_lists + slot_ref[t] % local_lists
        position = jnp.where(probes == t, spot.astype(jnp.float32), position)
    lists = lax.broadcasted_iota(jnp.int32, (total_lists, query_count), 0)
    named = [lists == probes[p : p + 1] for p in range(probe_count)]
    counts = functools.reduce(jnp.add, [n.astype(jnp.float32) for n in named])
    square = (query_count, query_count)
    before = lax.broadcasted_iota(jnp.int32, square, 0) < lax.broadcasted_iota(
        jnp.int32, square, 1
    )
    earlier = contract(
        counts.astype(jnp.bfloat16), before.astype(jnp.float32).astype(jnp.bfloat16), ((1,), (0,))
    )
    rank = jnp.concatenate(
        [jnp.sum(jnp.where(n, earlier, 0.0), axis=0, keepdims=True) for n in named], axis=0
    )
    rows = query_count * probe_count * cand_count
    row = lax.broadcasted_iota(jnp.int32, (rows, probe_count), 0)
    lane = lax.broadcasted_iota(jnp.int32, (rows, probe_count), 1)
    spread = (row // cand_count) % probe_count == lane
    spread = spread.astype(jnp.float32).astype(jnp.bfloat16)
    row = lax.broadcasted_iota(jnp.int32, (rows, query_count), 0)
    lane = lax.broadcasted_iota(jnp.int32, (rows, query_count), 1)
    own = row // (probe_count * cand_count) == lane
    value = contract(spread, position.astype(jnp.bfloat16), ((1,), (0,))) * (
        cand_count * capacity
    ) + contract(spread, rank.astype(jnp.bfloat16), ((1,), (0,)))
    column = jnp.sum(jnp.where(own, value, 0.0), axis=1, keepdims=True)
    shift = (lax.broadcasted_iota(jnp.int32, (rows, 1), 0) % cand_count) * capacity
    return column.astype(jnp.int32) + shift


def row_norms(list_slot, probes, corpus, cand_count, capacity):
    local_lists, list_length, features = corpus.shape
    chunk = min(list_length, 256)
    query_count, probe_count = probes.shape
    whole = pl.BlockSpec(memory_space=pltpu.VMEM)
    return pl.pallas_call(
        functools.partial(norm_kernel, (cand_count, capacity, chunk)),
        out_shape=(
            jax.ShapeDtypeStruct((local_lists, list_length), jnp.float32),
            jax.ShapeDtypeStruct((query_count * probe_count * cand_count, 1), jnp.int32),
        ),
        in_specs=[
            pl.BlockSpec(memory_space=pltpu.HBM),
            whole,
            pl.BlockSpec(memory_space=pltpu.HBM),
        ],
        out_specs=(whole, whole),
        scratch_shapes=[
            pltpu.VMEM(corpus.shape, corpus.dtype),
            pltpu.VMEM((local_lists, list_length, 2 * LANES), jnp.bfloat16),
            pltpu.SMEM(list_slot.shape, list_slot.dtype),
            pltpu.SemaphoreType.DMA((local_lists * (list_length // chunk),)),
            pltpu.SemaphoreType.DMA,
        ],
        compiler_params=pltpu.CompilerParams(vmem_limit_bytes=24 * MIB),
        cost_estimate=pl.CostEstimate(
            flops=2 * corpus.size, bytes_accessed=2 * corpus.size, transcendentals=0
        ),
    )(in_hbm(list_slot), in_hbm(probes.T), in_hbm(corpus))


def score_kernel(sizes, me_ref, slot_ref, corpus_ref, inv_ref, message_ref, out_ref, held, sems):
    owners, query_count, probe_count, cand_count, capacity, chunk = sizes
    local_lists, list_length, features = held.shape
    total = owners * query_count
    per_list = list_length // chunk

    def copy(i):
        l, h = divmod(i, per_list)
        rows = pl.ds(h * chunk, chunk)
        return pltpu.make_async_copy(corpus_ref.at[l, rows], held.at[l, rows], sems.at[i])

    for i in range(local_lists * per_list):
        copy(i).start()
    message = message_ref[...].reshape(total, -1)

    width = probe_count * (1 + cand_count)
    padded = -(-width // 16) * 16
    eye = lax.broadcasted_iota(jnp.int32, (padded, LANES), 0) == lax.broadcasted_iota(
        jnp.int32, (padded, LANES), 1
    )
    turned = contract(
        eye.astype(jnp.float32).astype(jnp.bfloat16), message[:, features:], ((1,), (1,))
    )
    probes = turned[:probe_count]
    cands = [
        turned[probe_count * (1 + c) : probe_count * (2 + c)] for c in range(cand_count)
    ]

    slots = slot_ref[...]
    names = lax.broadcasted_iota(jnp.int32, slots.shape, 1).astype(jnp.float32)
    first = me_ref[0] * local_lists
    hits, wanted = [], []
    for l in range(local_lists):
        name = jnp.sum(jnp.where(slots == first + l, names, 0.0), axis=1, keepdims=True)
        named = probes == name
        hits.append(jnp.sum(named.astype(jnp.float32), axis=0, keepdims=True))
        wanted.append(
            [jnp.sum(jnp.where(named, c, 0.0), axis=0, keepdims=True) for c in cands]
        )
    hit = jnp.concatenate(hits, axis=0)

    span = min(total, LANES)
    earlier = lax.broadcasted_iota(jnp.int32, (span, span), 0)
    later = lax.broadcasted_iota(jnp.int32, (span, span), 1)
    before = (earlier < later) & (earlier // query_count == later // query_count)
    before = before.astype(jnp.float32).astype(jnp.bfloat16)
    hit_low = hit.astype(jnp.bfloat16)
    rank = jnp.concatenate(
        [
            contract(hit_low[:, j : j + span], before, ((1,), (0,)))
            for j in range(0, total, span)
        ],
        axis=1,
    )
    source = (lax.broadcasted_iota(jnp.int32, (1, total), 1) // query_count) * capacity
    target = jnp.where(hit > 0.5, rank.astype(jnp.int32) + source, -1)

    room = owners * capacity
    step = capacity * cand_count
    places = lax.broadcasted_iota(jnp.int32, (room, total), 0)
    queries = message[:, :features]
    for l in range(local_lists):
        pick = (places == target[l : l + 1]).astype(jnp.float32)
        blocks = [jnp.sum(pick * w, axis=1, keepdims=True) for w in wanted[l]]
        rows = contract(pick.astype(jnp.bfloat16), queries, ((1,), (0,)))
        inv_query = lax.rsqrt(jnp.sum(rows * rows, axis=1, keepdims=True) / features + epsilon)
        rows = rows.astype(jnp.bfloat16)
        chosen = [jnp.zeros((room, BLOCK), jnp.float32) for _ in range(cand_count)]
        for h in range(per_list):
            span_rows = slice(h * chunk, (h + 1) * chunk)
            copy(l * per_list + h).wait()
            products = contract(rows, held[l, span_rows, :], ((1,), (1,)))
            scaled = products * inv_query * inv_ref[l : l + 1, span_rows]
            for j in range(chunk // BLOCK):
                number = (h * chunk + j * BLOCK) // BLOCK
                piece = scaled[:, j * BLOCK : (j + 1) * BLOCK]
                chosen = [
                    jnp.where(block == number, piece, old)
                    for block, old in zip(blocks, chosen)
                ]
        chosen = jnp.concatenate(
            [c.reshape(owners, capacity, BLOCK) for c in chosen], axis=1
        ).astype(jnp.bfloat16)
        out_ref[:, l * step : (l + 1) * step, :] = chosen


def block_scores(sizes, me, list_slot, corpus, inv_rows, messages):
    owners, query_count, probe_count, cand_count, capacity, chunk = sizes
    local_lists, list_length, _ = corpus.shape
    whole = pl.BlockSpec(memory_space=pltpu.VMEM)
    return pl.pallas_call(
        functools.partial(score_kernel, sizes),
        out_shape=jax.ShapeDtypeStruct(
            (owners, local_lists * cand_count * capacity, BLOCK), jnp.bfloat16
        ),
        in_specs=[
            pl.BlockSpec(memory_space=pltpu.SMEM),
            whole,
            pl.BlockSpec(memory_space=pltpu.HBM),
            whole,
            whole,
        ],
        out_specs=whole,
        scratch_shapes=[
            pltpu.VMEM(corpus.shape, corpus.dtype),
            pltpu.SemaphoreType.DMA((local_lists * (list_length // chunk),)),
        ],
        compiler_params=pltpu.CompilerParams(vmem_limit_bytes=40 * MIB),
        cost_estimate=pl.CostEstimate(
            flops=2 * owners * capacity * corpus.size,
            bytes_accessed=2 * corpus.size,
            transcendentals=0,
        ),
    )(me, list_slot, in_hbm(corpus), inv_rows, messages)


def place_kernel(column_ref, returned_ref, out_ref):
    returned = returned_ref[...].reshape(-1, returned_ref.shape[-1])
    lanes = lax.broadcasted_iota(jnp.int32, (out_ref.shape[0], returned.shape[0]), 1)
    pick = (lanes == column_ref[...]).astype(jnp.float32).astype(jnp.bfloat16)
    out_ref[...] = contract(pick, returned, ((1,), (0,))).astype(jnp.bfloat16)


def place(column, returned):
    whole = pl.BlockSpec(memory_space=pltpu.VMEM)
    return pl.pallas_call(
        place_kernel,
        out_shape=jax.ShapeDtypeStruct((column.shape[0], BLOCK), jnp.bfloat16),
        in_specs=[whole] * 2,
        out_specs=whole,
        compiler_params=pltpu.CompilerParams(vmem_limit_bytes=24 * MIB),
    )(column, returned)


def message_kernel(queries_ref, probes_ref, cand_ref, out_ref):
    owners, query_count, width = out_ref.shape
    features = queries_ref.shape[1]
    cand_count = cand_ref.shape[1]
    rows = jnp.concatenate(
        [probes_ref[...]] + [cand_ref[:, c, :] for c in range(cand_count)], axis=0
    ).astype(jnp.float32)
    eye = lax.broadcasted_iota(jnp.int32, (rows.shape[0], LANES), 0) == lax.broadcasted_iota(
        jnp.int32, (rows.shape[0], LANES), 1
    )
    indices = contract(
        rows.astype(jnp.bfloat16),
        eye.astype(jnp.float32).astype(jnp.bfloat16),
        ((0,), (0,)),
    ).astype(jnp.bfloat16)
    for k in range(owners):
        out_ref[k, :, :features] = queries_ref[...]
        out_ref[k, :, features:] = indices


def make_message(queries, probes, cand, owners):
    query_count, features = queries.shape
    whole = pl.BlockSpec(memory_space=pltpu.VMEM)
    return pl.pallas_call(
        message_kernel,
        out_shape=jax.ShapeDtypeStruct((owners, query_count, features + LANES), queries.dtype),
        in_specs=[whole] * 3,
        out_specs=whole,
        compiler_params=pltpu.CompilerParams(vmem_limit_bytes=24 * MIB),
    )(in_hbm(queries), in_hbm(probes.T), in_hbm(cand.transpose(1, 2, 0)))


def on_device(queries, corpus, list_slot, probes, cand):
    owners = lax.axis_size("lists")
    query_count, features = queries.shape
    probe_count = probes.shape[1]
    cand_count = cand.shape[2]
    local_lists, list_length, _ = corpus.shape
    total_lists = list_slot.shape[0]
    pair_count = query_count * probe_count
    capacity = min(query_count, max(2, (2 * pair_count + total_lists - 1) // total_lists))
    sizes = (owners, query_count, probe_count, cand_count, capacity, min(list_length, 512))
    me = lax.axis_index("lists").astype(jnp.int32)

    message = make_message(queries, probes, cand, owners)
    messages = exchange(message)
    inv_rows, column = row_norms(list_slot, probes, corpus, cand_count, capacity)
    scores = block_scores(sizes, me.reshape(1), list_slot[None, :], corpus, inv_rows, messages)
    returned = exchange(scores)
    chosen = place(column, returned)
    return chosen.reshape(query_count, probe_count, cand_count, BLOCK)


def solution(mesh):
    placed = (
        P(("groups", "lists", "rep"), None),
        P(("groups", "lists"), None, None),
        P("groups"),
        P(("groups", "lists", "rep"), None),
        P(("groups", "lists", "rep"), None, None),
    )
    return jax.shard_map(
        on_device,
        mesh=mesh,
        in_specs=placed,
        out_specs=P(("groups", "lists", "rep"), None, None, None),
        check_vma=False,
    )
```

```python
import functools

import jax
import jax.numpy as jnp
from jax import lax
from jax.experimental import pallas as pl
from jax.experimental.pallas import tpu as pltpu
from jax.sharding import PartitionSpec as P

BLOCK = 128
LANES = 128
MIB = 2**20

epsilon = 1e-06


def contract(a, b, dims, precision=None):
    return lax.dot_general(
        a, b, (dims, ((), ())), precision=precision, preferred_element_type=jnp.float32
    )


def in_hbm(value):
    return pltpu.with_memory_space_constraint(value, pltpu.HBM)


def exchange_order(owners):
    if owners > 16:
        return list(range(owners))
    return sorted(range(owners), key=lambda i: (abs(2 * i + 1 - owners) // 4, i))


def exchange(value):
    order = exchange_order(lax.axis_size("lists"))
    return lax.all_to_all(
        value, "lists", split_axis=0, concat_axis=0, axis_index_groups=[order], tiled=True
    )


def norm_kernel(
    sizes, slot_ref, probes_ref, corpus_ref, inv_ref, column_ref, held, parts, slots, sems, slot_sem
):
    cand_count, capacity, chunk = sizes
    local_lists, list_length, features = held.shape
    per_list = list_length // chunk

    def copy(i):
        l, h = divmod(i, per_list)
        rows = pl.ds(h * chunk, chunk)
        return pltpu.make_async_copy(corpus_ref.at[l, rows], held.at[l, rows], sems.at[i])

    slot_copy = pltpu.make_async_copy(slot_ref, slots, slot_sem)
    slot_copy.start()
    for i in range(local_lists * per_list):
        copy(i).start()
    slot_copy.wait()
    column_ref[...] = result_columns(cand_count, capacity, local_lists, slots, probes_ref[...])
    ones = jnp.ones((8, 2 * LANES), jnp.bfloat16)
    for l in range(local_lists):
        for h in range(per_list):
            copy(l * per_list + h).wait()
            rows = slice(h * chunk, (h + 1) * chunk)
            wide = held[l, rows, :].astype(jnp.float32)
            squares = functools.reduce(
                jnp.add, [wide[:, j : j + LANES] ** 2 for j in range(0, features, LANES)]
            )
            high = squares.astype(jnp.bfloat16)
            parts[l, rows, :LANES] = high
            parts[l, rows, LANES:] = (squares - high.astype(jnp.float32)).astype(jnp.bfloat16)
        sums = contract(ones, parts[l], ((1,), (1,)))[:1]
        inv_ref[l : l + 1, :] = lax.rsqrt(sums / features + epsilon) * features ** (-0.5)


def row_sums(parts):
    high = parts.astype(jnp.bfloat16)
    low = (parts - high.astype(jnp.float32)).astype(jnp.bfloat16)
    terms = jnp.concatenate([high, low], axis=1)
    ones = jnp.ones((8, terms.shape[1]), jnp.bfloat16)
    return contract(ones, terms, ((1,), (1,)))[:1]


def result_columns(cand_count, capacity, local_lists, slot_ref, probes):
    probe_count, query_count = probes.shape
    total_lists = slot_ref.shape[0]
    order = exchange_order(total_lists // local_lists)
    position = jnp.zeros(probes.shape, jnp.float32)
    for t in range(total_lists):
        owner = slot_ref[t] // local_lists
        place = owner
        for j, i in enumerate(order):
            if i != j:
                place = jnp.where(owner == i, j, place)
        spot = place * local_lists + slot_ref[t] % local_lists
        position = jnp.where(probes == t, spot.astype(jnp.float32), position)
    lists = lax.broadcasted_iota(jnp.int32, (total_lists, query_count), 0)
    named = [lists == probes[p : p + 1] for p in range(probe_count)]
    counts = functools.reduce(jnp.add, [n.astype(jnp.float32) for n in named])
    square = (query_count, query_count)
    before = lax.broadcasted_iota(jnp.int32, square, 0) < lax.broadcasted_iota(
        jnp.int32, square, 1
    )
    earlier = contract(
        counts.astype(jnp.bfloat16), before.astype(jnp.float32).astype(jnp.bfloat16), ((1,), (0,))
    )
    rank = jnp.concatenate(
        [jnp.sum(jnp.where(n, earlier, 0.0), axis=0, keepdims=True) for n in named], axis=0
    )
    rows = query_count * probe_count * cand_count
    row = lax.broadcasted_iota(jnp.int32, (rows, probe_count), 0)
    lane = lax.broadcasted_iota(jnp.int32, (rows, probe_count), 1)
    spread = (row // cand_count) % probe_count == lane
    spread = spread.astype(jnp.float32).astype(jnp.bfloat16)
    row = lax.broadcasted_iota(jnp.int32, (rows, query_count), 0)
    lane = lax.broadcasted_iota(jnp.int32, (rows, query_count), 1)
    own = row // (probe_count * cand_count) == lane
    value = contract(spread, position.astype(jnp.bfloat16), ((1,), (0,))) * (
        cand_count * capacity
    ) + contract(spread, rank.astype(jnp.bfloat16), ((1,), (0,)))
    column = jnp.sum(jnp.where(own, value, 0.0), axis=1, keepdims=True)
    shift = (lax.broadcasted_iota(jnp.int32, (rows, 1), 0) % cand_count) * capacity
    return column.astype(jnp.int32) + shift


def row_norms(list_slot, probes, corpus, cand_count, capacity):
    local_lists, list_length, features = corpus.shape
    chunk = min(list_length, 256)
    query_count, probe_count = probes.shape
    whole = pl.BlockSpec(memory_space=pltpu.VMEM)
    return pl.pallas_call(
        functools.partial(norm_kernel, (cand_count, capacity, chunk)),
        out_shape=(
            jax.ShapeDtypeStruct((local_lists, list_length), jnp.float32),
            jax.ShapeDtypeStruct((query_count * probe_count * cand_count, 1), jnp.int32),
        ),
        in_specs=[
            pl.BlockSpec(memory_space=pltpu.HBM),
            whole,
            pl.BlockSpec(memory_space=pltpu.HBM),
        ],
        out_specs=(whole, whole),
        scratch_shapes=[
            pltpu.VMEM(corpus.shape, corpus.dtype),
            pltpu.VMEM((local_lists, list_length, 2 * LANES), jnp.bfloat16),
            pltpu.SMEM(list_slot.shape, list_slot.dtype),
            pltpu.SemaphoreType.DMA((local_lists * (list_length // chunk),)),
            pltpu.SemaphoreType.DMA,
        ],
        compiler_params=pltpu.CompilerParams(vmem_limit_bytes=24 * MIB),
        cost_estimate=pl.CostEstimate(
            flops=2 * corpus.size, bytes_accessed=2 * corpus.size, transcendentals=0
        ),
    )(in_hbm(list_slot), in_hbm(probes.T), in_hbm(corpus))


def score_kernel(
    sizes, me_ref, slot_ref, corpus_ref, inv_ref, message_ref, out_ref, held, picked, sems
):
    owners, query_count, probe_count, cand_count, capacity, chunk, flight = sizes
    local_lists, list_length, features = held.shape
    total = owners * query_count
    room = owners * capacity
    step = capacity * cand_count
    per_list = list_length // chunk
    chunks = local_lists * per_list

    def copy(i):
        l, h = divmod(i, per_list)
        rows = pl.ds(h * chunk, chunk)
        return pltpu.make_async_copy(corpus_ref.at[l, rows], held.at[l, rows], sems.at[i])

    for i in range(min(flight, chunks)):
        copy(i).start()
    message = message_ref[...].reshape(total, -1)

    width = probe_count * (1 + cand_count)
    padded = -(-width // 16) * 16
    eye = lax.broadcasted_iota(jnp.int32, (padded, LANES), 0) == lax.broadcasted_iota(
        jnp.int32, (padded, LANES), 1
    )
    turned = contract(
        eye.astype(jnp.float32).astype(jnp.bfloat16), message[:, features:], ((1,), (1,))
    )
    probes = turned[:probe_count]
    cands = [
        turned[probe_count * (1 + c) : probe_count * (2 + c)] for c in range(cand_count)
    ]
    queries = message[:, :features]
    wide = queries.astype(jnp.float32)
    squares = functools.reduce(
        jnp.add, [wide[:, j : j + LANES] ** 2 for j in range(0, features, LANES)]
    )
    inv_query = lax.rsqrt(row_sums(squares) / features + epsilon)

    slots = slot_ref[...]
    names = lax.broadcasted_iota(jnp.int32, slots.shape, 1).astype(jnp.float32)
    first = me_ref[0] * local_lists
    hits, wanted = [], []
    for l in range(local_lists):
        name = jnp.sum(jnp.where(slots == first + l, names, 0.0), axis=1, keepdims=True)
        named = probes == name
        hits.append(jnp.sum(named.astype(jnp.float32), axis=0, keepdims=True))
        wanted.append(
            [jnp.sum(jnp.where(named, c, 0.0), axis=0, keepdims=True) for c in cands]
        )
    hit = jnp.concatenate(hits, axis=0)

    span = min(total, LANES)
    earlier = lax.broadcasted_iota(jnp.int32, (span, span), 0)
    later = lax.broadcasted_iota(jnp.int32, (span, span), 1)
    before = (earlier < later) & (earlier // query_count == later // query_count)
    before = before.astype(jnp.float32).astype(jnp.bfloat16)
    hit_low = hit.astype(jnp.bfloat16)
    rank = jnp.concatenate(
        [
            contract(hit_low[:, j : j + span], before, ((1,), (0,)))
            for j in range(0, total, span)
        ],
        axis=1,
    )
    source = (lax.broadcasted_iota(jnp.int32, (1, total), 1) // query_count) * capacity
    target = jnp.where(hit > 0.5, rank.astype(jnp.int32) + source, -1)

    places = lax.broadcasted_iota(jnp.int32, (room, total), 0)
    picks = [(places == target[l : l + 1]).astype(jnp.float32) for l in range(local_lists)]
    pick = jnp.concatenate(picks, axis=0).astype(jnp.bfloat16)
    picked[...] = contract(pick, queries, ((1,), (0,))).astype(jnp.bfloat16)
    scales = [jnp.sum(p * inv_query, axis=1, keepdims=True) for p in picks]
    blocks = [
        [jnp.sum(p * w, axis=1, keepdims=True) for w in wanted[l]] for l, p in enumerate(picks)
    ]

    for l in range(local_lists):
        rows = picked[l * room : (l + 1) * room, :]
        chosen = [jnp.zeros((room, BLOCK), jnp.float32) for _ in range(cand_count)]
        for h in range(per_list):
            i = l * per_list + h
            copy(i).wait()
            if i + flight < chunks:
                copy(i + flight).start()
            part = slice(h * chunk, (h + 1) * chunk)
            products = contract(rows, held[l, part, :], ((1,), (1,)))
            scaled = products * scales[l] * inv_ref[l : l + 1, part]
            for j in range(chunk // BLOCK):
                number = (h * chunk + j * BLOCK) // BLOCK
                piece = scaled[:, j * BLOCK : (j + 1) * BLOCK]
                chosen = [
                    jnp.where(block == number, piece, old)
                    for block, old in zip(blocks[l], chosen)
                ]
        out_ref[:, l * step : (l + 1) * step, :] = jnp.concatenate(
            [c.reshape(owners, capacity, BLOCK) for c in chosen], axis=1
        ).astype(jnp.bfloat16)


def block_scores(sizes, me, list_slot, corpus, inv_rows, messages):
    owners, query_count, probe_count, cand_count, capacity, chunk, flight = sizes
    local_lists, list_length, features = corpus.shape
    whole = pl.BlockSpec(memory_space=pltpu.VMEM)
    return pl.pallas_call(
        functools.partial(score_kernel, sizes),
        out_shape=jax.ShapeDtypeStruct(
            (owners, local_lists * cand_count * capacity, BLOCK), jnp.bfloat16
        ),
        in_specs=[
            pl.BlockSpec(memory_space=pltpu.SMEM),
            whole,
            pl.BlockSpec(memory_space=pltpu.HBM),
            whole,
            whole,
        ],
        out_specs=whole,
        scratch_shapes=[
            pltpu.VMEM(corpus.shape, corpus.dtype),
            pltpu.VMEM((local_lists * owners * capacity, features), corpus.dtype),
            pltpu.SemaphoreType.DMA((local_lists * (list_length // chunk),)),
        ],
        compiler_params=pltpu.CompilerParams(vmem_limit_bytes=40 * MIB),
        cost_estimate=pl.CostEstimate(
            flops=2 * owners * capacity * corpus.size,
            bytes_accessed=2 * corpus.size,
            transcendentals=0,
        ),
    )(me, list_slot, in_hbm(corpus), inv_rows, messages)


def place_kernel(column_ref, returned_ref, out_ref):
    returned = returned_ref[...].reshape(-1, returned_ref.shape[-1])
    lanes = lax.broadcasted_iota(jnp.int32, (out_ref.shape[0], returned.shape[0]), 1)
    pick = (lanes == column_ref[...]).astype(jnp.float32).astype(jnp.bfloat16)
    out_ref[...] = contract(pick, returned, ((1,), (0,))).astype(jnp.bfloat16)


def place(column, returned):
    whole = pl.BlockSpec(memory_space=pltpu.VMEM)
    return pl.pallas_call(
        place_kernel,
        out_shape=jax.ShapeDtypeStruct((column.shape[0], BLOCK), jnp.bfloat16),
        in_specs=[whole] * 2,
        out_specs=whole,
        compiler_params=pltpu.CompilerParams(vmem_limit_bytes=24 * MIB),
    )(column, returned)


def message_kernel(queries_ref, probes_ref, cand_ref, out_ref, sems):
    owners, query_count, width = out_ref.shape
    features = queries_ref.shape[1]
    cand_count = cand_ref.shape[1]
    copies = [
        pltpu.make_async_copy(queries_ref, out_ref.at[k, :, pl.ds(0, features)], sems.at[k])
        for k in range(owners)
    ]
    for c in copies:
        c.start()
    rows = jnp.concatenate(
        [probes_ref[...]] + [cand_ref[:, c, :] for c in range(cand_count)], axis=0
    ).astype(jnp.float32)
    eye = lax.broadcasted_iota(jnp.int32, (rows.shape[0], LANES), 0) == lax.broadcasted_iota(
        jnp.int32, (rows.shape[0], LANES), 1
    )
    indices = contract(
        rows.astype(jnp.bfloat16),
        eye.astype(jnp.float32).astype(jnp.bfloat16),
        ((0,), (0,)),
    ).astype(jnp.bfloat16)
    for k in range(owners):
        out_ref[k, :, features:] = indices
    for c in copies:
        c.wait()


def make_message(queries, probes, cand, owners):
    query_count, features = queries.shape
    whole = pl.BlockSpec(memory_space=pltpu.VMEM)
    return pl.pallas_call(
        message_kernel,
        out_shape=pltpu.VMEM((owners, query_count, features + LANES), queries.dtype),
        in_specs=[pl.BlockSpec(memory_space=pltpu.HBM), whole, whole],
        out_specs=whole,
        scratch_shapes=[pltpu.SemaphoreType.DMA((owners,))],
        compiler_params=pltpu.CompilerParams(vmem_limit_bytes=24 * MIB),
    )(in_hbm(queries), in_hbm(probes.T), in_hbm(cand.transpose(1, 2, 0)))


def on_device(queries, corpus, list_slot, probes, cand):
    owners = lax.axis_size("lists")
    query_count, features = queries.shape
    probe_count = probes.shape[1]
    cand_count = cand.shape[2]
    local_lists, list_length, _ = corpus.shape
    total_lists = list_slot.shape[0]
    pair_count = query_count * probe_count
    capacity = min(query_count, max(2, (2 * pair_count + total_lists - 1) // total_lists))
    sizes = (owners, query_count, probe_count, cand_count, capacity, min(list_length, 256), 6)
    me = lax.axis_index("lists").astype(jnp.int32)

    message = make_message(queries, probes, cand, owners)
    messages = exchange(message)
    inv_rows, column = row_norms(list_slot, probes, corpus, cand_count, capacity)
    scores = block_scores(sizes, me.reshape(1), list_slot[None, :], corpus, inv_rows, messages)
    returned = exchange(scores)
    chosen = place(column, returned)
    return chosen.reshape(query_count, probe_count, cand_count, BLOCK)


def solution(mesh):
    placed = (
        P(("groups", "lists", "rep"), None),
        P(("groups", "lists"), None, None),
        P("groups"),
        P(("groups", "lists", "rep"), None),
        P(("groups", "lists", "rep"), None, None),
    )
    return jax.shard_map(
        on_device,
        mesh=mesh,
        in_specs=placed,
        out_specs=P(("groups", "lists", "rep"), None, None, None),
        check_vma=False,
    )
```

```python
import functools

import jax
import jax.numpy as jnp
from jax import lax
from jax.experimental import pallas as pl
from jax.experimental.pallas import tpu as pltpu
from jax.sharding import PartitionSpec as P

BLOCK = 128
LANES = 128
MIB = 2**20

epsilon = 1e-06


def contract(a, b, dims, precision=None):
    return lax.dot_general(
        a, b, (dims, ((), ())), precision=precision, preferred_element_type=jnp.float32
    )


def in_hbm(value):
    return pltpu.with_memory_space_constraint(value, pltpu.HBM)


def in_vmem(value):
    return pltpu.with_memory_space_constraint(value, pltpu.VMEM)


def exchange_order(owners):
    if owners > 16:
        return list(range(owners))
    return sorted(range(owners), key=lambda i: (abs(2 * i + 1 - owners) // 4, i))


def exchange(value):
    order = exchange_order(lax.axis_size("lists"))
    return lax.all_to_all(
        value, "lists", split_axis=0, concat_axis=0, axis_index_groups=[order], tiled=True
    )


def norm_kernel(
    sizes,
    slot_ref,
    probes_ref,
    corpus_ref,
    staged_ref,
    inv_ref,
    column_ref,
    held,
    parts,
    slots,
    sems,
    slot_sem,
):
    cand_count, capacity, chunk = sizes
    local_lists, list_length, features = corpus_ref.shape
    per_list = list_length // chunk

    def place(l):
        return staged_ref.at[0] if l == 0 else held.at[l - 1]

    def copy(i):
        l, h = divmod(i, per_list)
        rows = pl.ds(h * chunk, chunk)
        return pltpu.make_async_copy(corpus_ref.at[l, rows], place(l).at[rows], sems.at[i])

    slot_copy = pltpu.make_async_copy(slot_ref, slots, slot_sem)
    slot_copy.start()
    for i in range(local_lists * per_list):
        copy(i).start()
    slot_copy.wait()
    column_ref[...] = result_columns(cand_count, capacity, local_lists, slots, probes_ref[...])
    ones = jnp.ones((8, 2 * LANES), jnp.bfloat16)
    for l in range(local_lists):
        for h in range(per_list):
            copy(l * per_list + h).wait()
            rows = slice(h * chunk, (h + 1) * chunk)
            wide = place(l)[rows, :].astype(jnp.float32)
            squares = functools.reduce(
                jnp.add, [wide[:, j : j + LANES] ** 2 for j in range(0, features, LANES)]
            )
            high = squares.astype(jnp.bfloat16)
            parts[l, rows, :LANES] = high
            parts[l, rows, LANES:] = (squares - high.astype(jnp.float32)).astype(jnp.bfloat16)
        sums = contract(ones, parts[l], ((1,), (1,)))[:1]
        inv_ref[l : l + 1, :] = lax.rsqrt(sums / features + epsilon) * features ** (-0.5)


def row_sums(parts):
    high = parts.astype(jnp.bfloat16)
    low = (parts - high.astype(jnp.float32)).astype(jnp.bfloat16)
    terms = jnp.concatenate([high, low], axis=1)
    ones = jnp.ones((8, terms.shape[1]), jnp.bfloat16)
    return contract(ones, terms, ((1,), (1,)))[:1]


def result_columns(cand_count, capacity, local_lists, slot_ref, probes):
    probe_count, query_count = probes.shape
    total_lists = slot_ref.shape[0]
    order = exchange_order(total_lists // local_lists)
    position = jnp.zeros(probes.shape, jnp.float32)
    for t in range(total_lists):
        owner = slot_ref[t] // local_lists
        place = owner
        for j, i in enumerate(order):
            if i != j:
                place = jnp.where(owner == i, j, place)
        spot = place * local_lists + slot_ref[t] % local_lists
        position = jnp.where(probes == t, spot.astype(jnp.float32), position)
    lists = lax.broadcasted_iota(jnp.int32, (total_lists, query_count), 0)
    named = [lists == probes[p : p + 1] for p in range(probe_count)]
    counts = functools.reduce(jnp.add, [n.astype(jnp.float32) for n in named])
    square = (query_count, query_count)
    before = lax.broadcasted_iota(jnp.int32, square, 0) < lax.broadcasted_iota(
        jnp.int32, square, 1
    )
    earlier = contract(
        counts.astype(jnp.bfloat16), before.astype(jnp.float32).astype(jnp.bfloat16), ((1,), (0,))
    )
    rank = jnp.concatenate(
        [jnp.sum(jnp.where(n, earlier, 0.0), axis=0, keepdims=True) for n in named], axis=0
    )
    rows = query_count * probe_count * cand_count
    row = lax.broadcasted_iota(jnp.int32, (rows, probe_count), 0)
    lane = lax.broadcasted_iota(jnp.int32, (rows, probe_count), 1)
    spread = (row // cand_count) % probe_count == lane
    spread = spread.astype(jnp.float32).astype(jnp.bfloat16)
    row = lax.broadcasted_iota(jnp.int32, (rows, query_count), 0)
    lane = lax.broadcasted_iota(jnp.int32, (rows, query_count), 1)
    own = row // (probe_count * cand_count) == lane
    value = contract(spread, position.astype(jnp.bfloat16), ((1,), (0,))) * (
        cand_count * capacity
    ) + contract(spread, rank.astype(jnp.bfloat16), ((1,), (0,)))
    column = jnp.sum(jnp.where(own, value, 0.0), axis=1, keepdims=True)
    shift = (lax.broadcasted_iota(jnp.int32, (rows, 1), 0) % cand_count) * capacity
    return column.astype(jnp.int32) + shift


def row_norms(list_slot, probes, corpus, cand_count, capacity):
    local_lists, list_length, features = corpus.shape
    chunk = min(list_length, 256)
    query_count, probe_count = probes.shape
    whole = pl.BlockSpec(memory_space=pltpu.VMEM)
    return pl.pallas_call(
        functools.partial(norm_kernel, (cand_count, capacity, chunk)),
        out_shape=(
            pltpu.VMEM((1, list_length, features), corpus.dtype),
            jax.ShapeDtypeStruct((local_lists, list_length), jnp.float32),
            jax.ShapeDtypeStruct((query_count * probe_count * cand_count, 1), jnp.int32),
        ),
        in_specs=[
            pl.BlockSpec(memory_space=pltpu.HBM),
            whole,
            pl.BlockSpec(memory_space=pltpu.HBM),
        ],
        out_specs=(whole, whole, whole),
        scratch_shapes=[
            pltpu.VMEM((max(local_lists - 1, 1), list_length, features), corpus.dtype),
            pltpu.VMEM((local_lists, list_length, 2 * LANES), jnp.bfloat16),
            pltpu.SMEM(list_slot.shape, list_slot.dtype),
            pltpu.SemaphoreType.DMA((local_lists * (list_length // chunk),)),
            pltpu.SemaphoreType.DMA,
        ],
        compiler_params=pltpu.CompilerParams(vmem_limit_bytes=24 * MIB),
        cost_estimate=pl.CostEstimate(
            flops=2 * corpus.size, bytes_accessed=2 * corpus.size, transcendentals=0
        ),
    )(in_hbm(list_slot), in_hbm(probes.T), in_hbm(corpus))


def score_kernel(
    sizes, me_ref, slot_ref, corpus_ref, staged_ref, inv_ref, message_ref, out_ref, held, picked, sems
):
    owners, query_count, probe_count, cand_count, capacity = sizes
    local_lists, list_length, features = corpus_ref.shape
    total = owners * query_count
    room = owners * capacity
    step = capacity * cand_count

    def copy(l):
        return pltpu.make_async_copy(corpus_ref.at[l], held.at[l - 1], sems.at[l - 1])

    for l in range(1, local_lists):
        copy(l).start()
    message = message_ref[...].reshape(total, -1)

    chunk = min(list_length, 512)

    width = probe_count * (1 + cand_count)
    padded = -(-width // 16) * 16
    eye = lax.broadcasted_iota(jnp.int32, (padded, LANES), 0) == lax.broadcasted_iota(
        jnp.int32, (padded, LANES), 1
    )
    turned = contract(
        eye.astype(jnp.float32).astype(jnp.bfloat16), message[:, features:], ((1,), (1,))
    )
    probes = turned[:probe_count]
    cands = [
        turned[probe_count * (1 + c) : probe_count * (2 + c)] for c in range(cand_count)
    ]
    queries = message[:, :features]
    wide = queries.astype(jnp.float32)
    squares = functools.reduce(
        jnp.add, [wide[:, j : j + LANES] ** 2 for j in range(0, features, LANES)]
    )
    inv_query = lax.rsqrt(row_sums(squares) / features + epsilon)

    slots = slot_ref[...]
    names = lax.broadcasted_iota(jnp.int32, slots.shape, 1).astype(jnp.float32)
    first = me_ref[0] * local_lists
    hits, wanted = [], []
    for l in range(local_lists):
        name = jnp.sum(jnp.where(slots == first + l, names, 0.0), axis=1, keepdims=True)
        named = probes == name
        hits.append(jnp.sum(named.astype(jnp.float32), axis=0, keepdims=True))
        wanted.append(
            [jnp.sum(jnp.where(named, c, 0.0), axis=0, keepdims=True) for c in cands]
        )
    hit = jnp.concatenate(hits, axis=0)

    span = min(total, LANES)
    earlier = lax.broadcasted_iota(jnp.int32, (span, span), 0)
    later = lax.broadcasted_iota(jnp.int32, (span, span), 1)
    before = (earlier < later) & (earlier // query_count == later // query_count)
    before = before.astype(jnp.float32).astype(jnp.bfloat16)
    hit_low = hit.astype(jnp.bfloat16)
    rank = jnp.concatenate(
        [
            contract(hit_low[:, j : j + span], before, ((1,), (0,)))
            for j in range(0, total, span)
        ],
        axis=1,
    )
    source = (lax.broadcasted_iota(jnp.int32, (1, total), 1) // query_count) * capacity
    target = jnp.where(hit > 0.5, rank.astype(jnp.int32) + source, -1)

    places = lax.broadcasted_iota(jnp.int32, (room, total), 0)
    picks = [(places == target[l : l + 1]).astype(jnp.float32) for l in range(local_lists)]
    pick = jnp.concatenate(picks, axis=0).astype(jnp.bfloat16)
    picked[...] = contract(pick, queries, ((1,), (0,))).astype(jnp.bfloat16)
    scales = [jnp.sum(p * inv_query, axis=1, keepdims=True) for p in picks]
    blocks = [
        [jnp.sum(p * w, axis=1, keepdims=True) for w in wanted[l]] for l, p in enumerate(picks)
    ]

    for l in range(local_lists):
        rows = picked[l * room : (l + 1) * room, :]
        if l > 0:
            copy(l).wait()
        source = staged_ref.at[0] if l == 0 else held.at[l - 1]
        chosen = [jnp.zeros((room, BLOCK), jnp.float32) for _ in range(cand_count)]
        for h in range(0, list_length, chunk):
            part = slice(h, h + chunk)
            products = contract(rows, source[part, :], ((1,), (1,)))
            scaled = products * scales[l] * inv_ref[l : l + 1, part]
            for j in range(0, chunk, BLOCK):
                piece = scaled[:, j : j + BLOCK]
                chosen = [
                    jnp.where(block == (h + j) // BLOCK, piece, old)
                    for block, old in zip(blocks[l], chosen)
                ]
        out_ref[:, l * step : (l + 1) * step, :] = jnp.concatenate(
            [c.reshape(owners, capacity, BLOCK) for c in chosen], axis=1
        ).astype(jnp.bfloat16)


def block_scores(sizes, me, list_slot, corpus, staged, inv_rows, messages):
    owners, query_count, probe_count, cand_count, capacity = sizes
    local_lists, list_length, features = corpus.shape
    streamed = max(local_lists - 1, 1)
    whole = pl.BlockSpec(memory_space=pltpu.VMEM)
    return pl.pallas_call(
        functools.partial(score_kernel, sizes),
        out_shape=jax.ShapeDtypeStruct(
            (owners, local_lists * cand_count * capacity, BLOCK), jnp.bfloat16
        ),
        in_specs=[
            pl.BlockSpec(memory_space=pltpu.SMEM),
            whole,
            pl.BlockSpec(memory_space=pltpu.HBM),
            whole,
            whole,
            whole,
        ],
        out_specs=whole,
        scratch_shapes=[
            pltpu.VMEM((streamed, list_length, features), corpus.dtype),
            pltpu.VMEM((local_lists * owners * capacity, features), corpus.dtype),
            pltpu.SemaphoreType.DMA((streamed,)),
        ],
        compiler_params=pltpu.CompilerParams(vmem_limit_bytes=40 * MIB),
        cost_estimate=pl.CostEstimate(
            flops=2 * owners * capacity * corpus.size,
            bytes_accessed=2 * corpus.size,
            transcendentals=0,
        ),
    )(me, list_slot, in_hbm(corpus), in_vmem(staged), inv_rows, messages)


def place_kernel(column_ref, returned_ref, out_ref):
    returned = returned_ref[...].reshape(-1, returned_ref.shape[-1])
    lanes = lax.broadcasted_iota(jnp.int32, (out_ref.shape[0], returned.shape[0]), 1)
    pick = (lanes == column_ref[...]).astype(jnp.float32).astype(jnp.bfloat16)
    out_ref[...] = contract(pick, returned, ((1,), (0,))).astype(jnp.bfloat16)


def place(column, returned):
    whole = pl.BlockSpec(memory_space=pltpu.VMEM)
    return pl.pallas_call(
        place_kernel,
        out_shape=jax.ShapeDtypeStruct((column.shape[0], BLOCK), jnp.bfloat16),
        in_specs=[whole] * 2,
        out_specs=whole,
        compiler_params=pltpu.CompilerParams(vmem_limit_bytes=24 * MIB),
    )(column, returned)


def message_kernel(queries_ref, probes_ref, cand_ref, out_ref):
    owners, query_count, width = out_ref.shape
    features = queries_ref.shape[1]
    cand_count = cand_ref.shape[1]
    rows = jnp.concatenate(
        [probes_ref[...]] + [cand_ref[:, c, :] for c in range(cand_count)], axis=0
    ).astype(jnp.float32)
    eye = lax.broadcasted_iota(jnp.int32, (rows.shape[0], LANES), 0) == lax.broadcasted_iota(
        jnp.int32, (rows.shape[0], LANES), 1
    )
    indices = contract(
        rows.astype(jnp.bfloat16),
        eye.astype(jnp.float32).astype(jnp.bfloat16),
        ((0,), (0,)),
    ).astype(jnp.bfloat16)
    for k in range(owners):
        out_ref[k, :, :features] = queries_ref[...]
        out_ref[k, :, features:] = indices


def make_message(queries, probes, cand, owners):
    query_count, features = queries.shape
    whole = pl.BlockSpec(memory_space=pltpu.VMEM)
    return pl.pallas_call(
        message_kernel,
        out_shape=pltpu.VMEM((owners, query_count, features + LANES), queries.dtype),
        in_specs=[whole] * 3,
        out_specs=whole,
        compiler_params=pltpu.CompilerParams(vmem_limit_bytes=24 * MIB),
    )(in_hbm(queries), in_hbm(probes.T), in_hbm(cand.transpose(1, 2, 0)))


def on_device(queries, corpus, list_slot, probes, cand):
    owners = lax.axis_size("lists")
    query_count, features = queries.shape
    probe_count = probes.shape[1]
    cand_count = cand.shape[2]
    local_lists, list_length, _ = corpus.shape
    total_lists = list_slot.shape[0]
    pair_count = query_count * probe_count
    capacity = min(query_count, max(2, (2 * pair_count + total_lists - 1) // total_lists))
    sizes = (owners, query_count, probe_count, cand_count, capacity)
    me = lax.axis_index("lists").astype(jnp.int32)

    message = make_message(queries, probes, cand, owners)
    messages = exchange(message)
    staged, inv_rows, column = row_norms(list_slot, probes, corpus, cand_count, capacity)
    scores = block_scores(sizes, me.reshape(1), list_slot[None, :], corpus, staged, inv_rows, messages)
    returned = exchange(scores)
    chosen = place(column, returned)
    return chosen.reshape(query_count, probe_count, cand_count, BLOCK)


def solution(mesh):
    placed = (
        P(("groups", "lists", "rep"), None),
        P(("groups", "lists"), None, None),
        P("groups"),
        P(("groups", "lists", "rep"), None),
        P(("groups", "lists", "rep"), None, None),
    )
    return jax.shard_map(
        on_device,
        mesh=mesh,
        in_specs=placed,
        out_specs=P(("groups", "lists", "rep"), None, None, None),
        check_vma=False,
    )
```

```python
import functools

import jax
import jax.numpy as jnp
from jax import lax
from jax.experimental import pallas as pl
from jax.experimental.pallas import tpu as pltpu
from jax.sharding import PartitionSpec as P

BLOCK = 128
LANES = 128
MIB = 2**20

epsilon = 1e-06


def contract(a, b, dims, precision=None):
    return lax.dot_general(
        a, b, (dims, ((), ())), precision=precision, preferred_element_type=jnp.float32
    )


def in_hbm(value):
    return pltpu.with_memory_space_constraint(value, pltpu.HBM)


def in_vmem(value):
    return pltpu.with_memory_space_constraint(value, pltpu.VMEM)


def exchange_order(owners):
    if owners > 16:
        return list(range(owners))
    return sorted(range(owners), key=lambda i: (abs(i - owners // 2 - 0.25), i))


def exchange(value):
    order = exchange_order(lax.axis_size("lists"))
    return lax.all_to_all(
        value, "lists", split_axis=0, concat_axis=0, axis_index_groups=[order], tiled=True
    )


def staged_rows(local_lists, list_length):
    return min(local_lists * list_length, list_length + list_length // 4)


def norm_kernel(
    sizes,
    slot_ref,
    probes_ref,
    corpus_ref,
    staged_ref,
    inv_ref,
    column_ref,
    held,
    parts,
    slots,
    sems,
    slot_sem,
):
    cand_count, capacity, chunk = sizes
    total_rows, features = corpus_ref.shape
    local_lists, list_length = inv_ref.shape
    staged = staged_ref.shape[0]

    def place(row):
        return staged_ref.at[row : row + chunk] if row < staged else held.at[
            row - staged : row - staged + chunk
        ]

    def copy(row):
        return pltpu.make_async_copy(
            corpus_ref.at[row : row + chunk], place(row), sems.at[row // chunk]
        )

    slot_copy = pltpu.make_async_copy(slot_ref, slots, slot_sem)
    slot_copy.start()
    for row in range(0, total_rows, chunk):
        copy(row).start()
    slot_copy.wait()
    column_ref[...] = result_columns(cand_count, capacity, local_lists, slots, probes_ref[...])
    ones = jnp.ones((8, 2 * LANES), jnp.bfloat16)
    for l in range(local_lists):
        for row in range(l * list_length, (l + 1) * list_length, chunk):
            copy(row).wait()
            wide = place(row)[...].astype(jnp.float32)
            squares = functools.reduce(
                jnp.add, [wide[:, j : j + LANES] ** 2 for j in range(0, features, LANES)]
            )
            high = squares.astype(jnp.bfloat16)
            parts[row : row + chunk, :LANES] = high
            parts[row : row + chunk, LANES:] = (squares - high.astype(jnp.float32)).astype(
                jnp.bfloat16
            )
        whole = parts[l * list_length : (l + 1) * list_length, :]
        sums = contract(ones, whole, ((1,), (1,)))[:1]
        inv_ref[l : l + 1, :] = lax.rsqrt(sums / features + epsilon) * features ** (-0.5)


def row_sums(parts):
    high = parts.astype(jnp.bfloat16)
    low = (parts - high.astype(jnp.float32)).astype(jnp.bfloat16)
    terms = jnp.concatenate([high, low], axis=1)
    ones = jnp.ones((8, terms.shape[1]), jnp.bfloat16)
    return contract(ones, terms, ((1,), (1,)))[:1]


def result_columns(cand_count, capacity, local_lists, slot_ref, probes):
    probe_count, query_count = probes.shape
    total_lists = slot_ref.shape[0]
    order = exchange_order(total_lists // local_lists)
    position = jnp.zeros(probes.shape, jnp.float32)
    for t in range(total_lists):
        owner = slot_ref[t] // local_lists
        place = owner
        for j, i in enumerate(order):
            if i != j:
                place = jnp.where(owner == i, j, place)
        spot = place * local_lists + slot_ref[t] % local_lists
        position = jnp.where(probes == t, spot.astype(jnp.float32), position)
    lists = lax.broadcasted_iota(jnp.int32, (total_lists, query_count), 0)
    named = [lists == probes[p : p + 1] for p in range(probe_count)]
    counts = functools.reduce(jnp.add, [n.astype(jnp.float32) for n in named])
    square = (query_count, query_count)
    before = lax.broadcasted_iota(jnp.int32, square, 0) < lax.broadcasted_iota(
        jnp.int32, square, 1
    )
    earlier = contract(
        counts.astype(jnp.bfloat16), before.astype(jnp.float32).astype(jnp.bfloat16), ((1,), (0,))
    )
    rank = jnp.concatenate(
        [jnp.sum(jnp.where(n, earlier, 0.0), axis=0, keepdims=True) for n in named], axis=0
    )
    rows = query_count * probe_count * cand_count
    row = lax.broadcasted_iota(jnp.int32, (rows, probe_count), 0)
    lane = lax.broadcasted_iota(jnp.int32, (rows, probe_count), 1)
    spread = (row // cand_count) % probe_count == lane
    spread = spread.astype(jnp.float32).astype(jnp.bfloat16)
    row = lax.broadcasted_iota(jnp.int32, (rows, query_count), 0)
    lane = lax.broadcasted_iota(jnp.int32, (rows, query_count), 1)
    own = row // (probe_count * cand_count) == lane
    value = contract(spread, position.astype(jnp.bfloat16), ((1,), (0,))) * (
        cand_count * capacity
    ) + contract(spread, rank.astype(jnp.bfloat16), ((1,), (0,)))
    column = jnp.sum(jnp.where(own, value, 0.0), axis=1, keepdims=True)
    shift = (lax.broadcasted_iota(jnp.int32, (rows, 1), 0) % cand_count) * capacity
    return column.astype(jnp.int32) + shift


def row_norms(list_slot, probes, corpus, local_lists, cand_count, capacity):
    total_rows, features = corpus.shape
    list_length = total_rows // local_lists
    chunk = min(list_length, 256)
    staged = staged_rows(local_lists, list_length)
    query_count, probe_count = probes.shape
    whole = pl.BlockSpec(memory_space=pltpu.VMEM)
    return pl.pallas_call(
        functools.partial(norm_kernel, (cand_count, capacity, chunk)),
        out_shape=(
            pltpu.VMEM((staged, features), corpus.dtype),
            jax.ShapeDtypeStruct((local_lists, list_length), jnp.float32),
            jax.ShapeDtypeStruct((query_count * probe_count * cand_count, 1), jnp.int32),
        ),
        in_specs=[
            pl.BlockSpec(memory_space=pltpu.HBM),
            whole,
            pl.BlockSpec(memory_space=pltpu.HBM),
        ],
        out_specs=(whole, whole, whole),
        scratch_shapes=[
            pltpu.VMEM((max(total_rows - staged, 16), features), corpus.dtype),
            pltpu.VMEM((total_rows, 2 * LANES), jnp.bfloat16),
            pltpu.SMEM(list_slot.shape, list_slot.dtype),
            pltpu.SemaphoreType.DMA((total_rows // chunk,)),
            pltpu.SemaphoreType.DMA,
        ],
        compiler_params=pltpu.CompilerParams(vmem_limit_bytes=24 * MIB),
        cost_estimate=pl.CostEstimate(
            flops=2 * corpus.size, bytes_accessed=2 * corpus.size, transcendentals=0
        ),
    )(in_hbm(list_slot), in_hbm(probes.T), in_hbm(corpus))


def score_kernel(
    sizes, me_ref, slot_ref, corpus_ref, staged_ref, inv_ref, message_ref, out_ref, held, picked, sems
):
    owners, query_count, probe_count, cand_count, capacity, streams = sizes
    total_rows, features = corpus_ref.shape
    local_lists, list_length = inv_ref.shape
    staged = staged_ref.shape[0]
    total = owners * query_count
    room = owners * capacity
    step = capacity * cand_count

    def copy(i):
        begin, end = streams[i]
        return pltpu.make_async_copy(
            corpus_ref.at[begin:end], held.at[begin - staged : end - staged], sems.at[i]
        )

    for i in range(len(streams)):
        copy(i).start()
    message = message_ref[...].reshape(total, -1)


    width = probe_count * (1 + cand_count)
    padded = -(-width // 16) * 16
    eye = lax.broadcasted_iota(jnp.int32, (padded, LANES), 0) == lax.broadcasted_iota(
        jnp.int32, (padded, LANES), 1
    )
    turned = contract(
        eye.astype(jnp.float32).astype(jnp.bfloat16), message[:, features:], ((1,), (1,))
    )
    probes = turned[:probe_count]
    cands = [
        turned[probe_count * (1 + c) : probe_count * (2 + c)] for c in range(cand_count)
    ]
    queries = message[:, :features]
    wide = queries.astype(jnp.float32)
    squares = functools.reduce(
        jnp.add, [wide[:, j : j + LANES] ** 2 for j in range(0, features, LANES)]
    )
    inv_query = lax.rsqrt(row_sums(squares) / features + epsilon)

    slots = slot_ref[...]
    names = lax.broadcasted_iota(jnp.int32, slots.shape, 1).astype(jnp.float32)
    first = me_ref[0] * local_lists
    hits, wanted = [], []
    for l in range(local_lists):
        name = jnp.sum(jnp.where(slots == first + l, names, 0.0), axis=1, keepdims=True)
        named = probes == name
        hits.append(jnp.sum(named.astype(jnp.float32), axis=0, keepdims=True))
        wanted.append(
            [jnp.sum(jnp.where(named, c, 0.0), axis=0, keepdims=True) for c in cands]
        )
    hit = jnp.concatenate(hits, axis=0)

    span = min(total, LANES)
    earlier = lax.broadcasted_iota(jnp.int32, (span, span), 0)
    later = lax.broadcasted_iota(jnp.int32, (span, span), 1)
    before = (earlier < later) & (earlier // query_count == later // query_count)
    before = before.astype(jnp.float32).astype(jnp.bfloat16)
    hit_low = hit.astype(jnp.bfloat16)
    rank = jnp.concatenate(
        [
            contract(hit_low[:, j : j + span], before, ((1,), (0,)))
            for j in range(0, total, span)
        ],
        axis=1,
    )
    source = (lax.broadcasted_iota(jnp.int32, (1, total), 1) // query_count) * capacity
    target = jnp.where(hit > 0.5, rank.astype(jnp.int32) + source, -1)

    places = lax.broadcasted_iota(jnp.int32, (room, total), 0)
    picks = [(places == target[l : l + 1]).astype(jnp.float32) for l in range(local_lists)]
    pick = jnp.concatenate(picks, axis=0).astype(jnp.bfloat16)
    picked[...] = contract(pick, queries, ((1,), (0,))).astype(jnp.bfloat16)
    scales = [jnp.sum(p * inv_query, axis=1, keepdims=True) for p in picks]
    blocks = [
        [jnp.sum(p * w, axis=1, keepdims=True) for w in wanted[l]] for l, p in enumerate(picks)
    ]

    for l in range(local_lists):
        rows = picked[l * room : (l + 1) * room, :]
        chosen = [jnp.zeros((room, BLOCK), jnp.float32) for _ in range(cand_count)]
        row = l * list_length
        while row < (l + 1) * list_length:
            if row < staged:
                end = min(row + 512, staged, (l + 1) * list_length)
                values = staged_ref[row:end, :]
            else:
                number = [begin for begin, _ in streams].index(row)
                end = streams[number][1]
                copy(number).wait()
                values = held[row - staged : end - staged, :]
            products = contract(rows, values, ((1,), (1,)))
            first = row - l * list_length
            scaled = products * scales[l] * inv_ref[l : l + 1, first : first + end - row]
            for j in range(0, end - row, BLOCK):
                piece = scaled[:, j : j + BLOCK]
                chosen = [
                    jnp.where(block == (first + j) // BLOCK, piece, old)
                    for block, old in zip(blocks[l], chosen)
                ]
            row = end
        out_ref[:, l * step : (l + 1) * step, :] = jnp.concatenate(
            [c.reshape(owners, capacity, BLOCK) for c in chosen], axis=1
        ).astype(jnp.bfloat16)


def stream_ranges(local_lists, list_length):
    row, end = staged_rows(local_lists, list_length), local_lists * list_length
    ranges = []
    while row < end:
        to = (row // list_length + 1) * list_length
        if to == end and to - row > list_length // 2:
            to = end - list_length // 2
        ranges.append((row, to))
        row = to
    return tuple(ranges)


def block_scores(sizes, me, list_slot, corpus, staged, inv_rows, messages):
    owners, query_count, probe_count, cand_count, capacity = sizes
    local_lists, list_length = inv_rows.shape
    total_rows, features = corpus.shape
    streams = stream_ranges(local_lists, list_length)
    whole = pl.BlockSpec(memory_space=pltpu.VMEM)
    return pl.pallas_call(
        functools.partial(score_kernel, sizes + (streams,)),
        out_shape=jax.ShapeDtypeStruct(
            (owners, local_lists * cand_count * capacity, BLOCK), jnp.bfloat16
        ),
        in_specs=[
            pl.BlockSpec(memory_space=pltpu.SMEM),
            whole,
            pl.BlockSpec(memory_space=pltpu.HBM),
            whole,
            whole,
            whole,
        ],
        out_specs=whole,
        scratch_shapes=[
            pltpu.VMEM((max(total_rows - staged.shape[0], 16), features), corpus.dtype),
            pltpu.VMEM((local_lists * owners * capacity, features), corpus.dtype),
            pltpu.SemaphoreType.DMA((max(len(streams), 1),)),
        ],
        compiler_params=pltpu.CompilerParams(vmem_limit_bytes=40 * MIB),
        cost_estimate=pl.CostEstimate(
            flops=2 * owners * capacity * corpus.size,
            bytes_accessed=2 * corpus.size,
            transcendentals=0,
        ),
    )(me, list_slot, in_hbm(corpus), in_vmem(staged), inv_rows, messages)


def place_kernel(column_ref, returned_ref, out_ref):
    returned = returned_ref[...].reshape(-1, returned_ref.shape[-1])
    lanes = lax.broadcasted_iota(jnp.int32, (out_ref.shape[0], returned.shape[0]), 1)
    pick = (lanes == column_ref[...]).astype(jnp.float32).astype(jnp.bfloat16)
    out_ref[...] = contract(pick, returned, ((1,), (0,))).astype(jnp.bfloat16)


def place(column, returned):
    whole = pl.BlockSpec(memory_space=pltpu.VMEM)
    return pl.pallas_call(
        place_kernel,
        out_shape=jax.ShapeDtypeStruct((column.shape[0], BLOCK), jnp.bfloat16),
        in_specs=[whole] * 2,
        out_specs=whole,
        compiler_params=pltpu.CompilerParams(vmem_limit_bytes=24 * MIB),
    )(column, returned)


def message_kernel(queries_ref, probes_ref, cand_ref, out_ref):
    owners, query_count, width = out_ref.shape
    features = queries_ref.shape[1]
    cand_count = cand_ref.shape[1]
    rows = jnp.concatenate(
        [probes_ref[...]] + [cand_ref[:, c, :] for c in range(cand_count)], axis=0
    ).astype(jnp.float32)
    eye = lax.broadcasted_iota(jnp.int32, (rows.shape[0], LANES), 0) == lax.broadcasted_iota(
        jnp.int32, (rows.shape[0], LANES), 1
    )
    indices = contract(
        rows.astype(jnp.bfloat16),
        eye.astype(jnp.float32).astype(jnp.bfloat16),
        ((0,), (0,)),
    ).astype(jnp.bfloat16)
    for k in range(owners):
        out_ref[k, :, :features] = queries_ref[...]
        out_ref[k, :, features:] = indices


def make_message(queries, probes, cand, owners):
    query_count, features = queries.shape
    whole = pl.BlockSpec(memory_space=pltpu.VMEM)
    return pl.pallas_call(
        message_kernel,
        out_shape=jax.ShapeDtypeStruct((owners, query_count, features + LANES), queries.dtype),
        in_specs=[whole] * 3,
        out_specs=whole,
        compiler_params=pltpu.CompilerParams(vmem_limit_bytes=24 * MIB),
    )(in_hbm(queries), in_hbm(probes.T), in_hbm(cand.transpose(1, 2, 0)))


def on_device(queries, corpus, list_slot, probes, cand):
    owners = lax.axis_size("lists")
    query_count, features = queries.shape
    probe_count = probes.shape[1]
    cand_count = cand.shape[2]
    local_lists = corpus.shape[0]
    corpus = corpus.reshape(-1, features)
    total_lists = list_slot.shape[0]
    pair_count = query_count * probe_count
    capacity = min(query_count, max(2, (2 * pair_count + total_lists - 1) // total_lists))
    sizes = (owners, query_count, probe_count, cand_count, capacity)
    me = lax.axis_index("lists").astype(jnp.int32)

    message = make_message(queries, probes, cand, owners)
    messages = exchange(message)
    staged, inv_rows, column = row_norms(
        list_slot, probes, corpus, local_lists, cand_count, capacity
    )
    scores = block_scores(sizes, me.reshape(1), list_slot[None, :], corpus, staged, inv_rows, messages)
    returned = exchange(scores)
    chosen = place(column, returned)
    return chosen.reshape(query_count, probe_count, cand_count, BLOCK)


def solution(mesh):
    placed = (
        P(("groups", "lists", "rep"), None),
        P(("groups", "lists"), None, None),
        P("groups"),
        P(("groups", "lists", "rep"), None),
        P(("groups", "lists", "rep"), None, None),
    )
    return jax.shard_map(
        on_device,
        mesh=mesh,
        in_specs=placed,
        out_specs=P(("groups", "lists", "rep"), None, None, None),
        check_vma=False,
    )
```

```python
import functools

import jax
import jax.numpy as jnp
from jax import lax
from jax.experimental import pallas as pl
from jax.experimental.pallas import tpu as pltpu
from jax.sharding import PartitionSpec as P

BLOCK = 128
LANES = 128
MIB = 2**20

epsilon = 1e-06


def contract(a, b, dims, precision=None):
    return lax.dot_general(
        a, b, (dims, ((), ())), precision=precision, preferred_element_type=jnp.float32
    )


def in_hbm(value):
    return pltpu.with_memory_space_constraint(value, pltpu.HBM)


def in_vmem(value):
    return pltpu.with_memory_space_constraint(value, pltpu.VMEM)


def exchange_order(owners):
    if owners > 16:
        return list(range(owners))
    return sorted(range(owners), key=lambda i: (abs(i // 2 - owners // 4 - 0.25), -i))


def exchange(value):
    order = exchange_order(lax.axis_size("lists"))
    return lax.all_to_all(
        value, "lists", split_axis=0, concat_axis=0, axis_index_groups=[order], tiled=True
    )


def staged_rows(local_lists, list_length):
    return min(local_lists * list_length, list_length + list_length // 2)


def norm_kernel(
    sizes,
    slot_ref,
    probes_ref,
    corpus_ref,
    staged_ref,
    inv_ref,
    column_ref,
    held,
    parts,
    slots,
    sems,
    slot_sem,
):
    cand_count, capacity, chunk = sizes
    total_rows, features = corpus_ref.shape
    local_lists, list_length = inv_ref.shape
    staged = staged_ref.shape[0]

    def place(row):
        return staged_ref.at[row : row + chunk] if row < staged else held.at[
            row - staged : row - staged + chunk
        ]

    def copy(row):
        return pltpu.make_async_copy(
            corpus_ref.at[row : row + chunk], place(row), sems.at[row // chunk]
        )

    slot_copy = pltpu.make_async_copy(slot_ref, slots, slot_sem)
    slot_copy.start()
    for row in range(0, total_rows, chunk):
        copy(row).start()
    slot_copy.wait()
    column_ref[...] = result_columns(cand_count, capacity, local_lists, slots, probes_ref[...])
    ones = jnp.ones((8, 2 * LANES), jnp.bfloat16)
    for l in range(local_lists):
        for row in range(l * list_length, (l + 1) * list_length, chunk):
            copy(row).wait()
            wide = place(row)[...].astype(jnp.float32)
            squares = functools.reduce(
                jnp.add, [wide[:, j : j + LANES] ** 2 for j in range(0, features, LANES)]
            )
            high = squares.astype(jnp.bfloat16)
            parts[row : row + chunk, :LANES] = high
            parts[row : row + chunk, LANES:] = (squares - high.astype(jnp.float32)).astype(
                jnp.bfloat16
            )
        whole = parts[l * list_length : (l + 1) * list_length, :]
        sums = contract(ones, whole, ((1,), (1,)))[:1]
        inv_ref[l : l + 1, :] = lax.rsqrt(sums / features + epsilon) * features ** (-0.5)


def row_sums(parts):
    high = parts.astype(jnp.bfloat16)
    low = (parts - high.astype(jnp.float32)).astype(jnp.bfloat16)
    terms = jnp.concatenate([high, low], axis=1)
    ones = jnp.ones((8, terms.shape[1]), jnp.bfloat16)
    return contract(ones, terms, ((1,), (1,)))[:1]


def result_columns(cand_count, capacity, local_lists, slot_ref, probes):
    probe_count, query_count = probes.shape
    total_lists = slot_ref.shape[0]
    order = exchange_order(total_lists // local_lists)
    position = jnp.zeros(probes.shape, jnp.float32)
    for t in range(total_lists):
        owner = slot_ref[t] // local_lists
        place = owner
        for j, i in enumerate(order):
            if i != j:
                place = jnp.where(owner == i, j, place)
        spot = place * local_lists + slot_ref[t] % local_lists
        position = jnp.where(probes == t, spot.astype(jnp.float32), position)
    lists = lax.broadcasted_iota(jnp.int32, (total_lists, query_count), 0)
    named = [lists == probes[p : p + 1] for p in range(probe_count)]
    counts = functools.reduce(jnp.add, [n.astype(jnp.float32) for n in named])
    square = (query_count, query_count)
    before = lax.broadcasted_iota(jnp.int32, square, 0) < lax.broadcasted_iota(
        jnp.int32, square, 1
    )
    earlier = contract(
        counts.astype(jnp.bfloat16), before.astype(jnp.float32).astype(jnp.bfloat16), ((1,), (0,))
    )
    rank = jnp.concatenate(
        [jnp.sum(jnp.where(n, earlier, 0.0), axis=0, keepdims=True) for n in named], axis=0
    )
    rows = query_count * probe_count * cand_count
    row = lax.broadcasted_iota(jnp.int32, (rows, probe_count), 0)
    lane = lax.broadcasted_iota(jnp.int32, (rows, probe_count), 1)
    spread = (row // cand_count) % probe_count == lane
    spread = spread.astype(jnp.float32).astype(jnp.bfloat16)
    row = lax.broadcasted_iota(jnp.int32, (rows, query_count), 0)
    lane = lax.broadcasted_iota(jnp.int32, (rows, query_count), 1)
    own = row // (probe_count * cand_count) == lane
    value = contract(spread, position.astype(jnp.bfloat16), ((1,), (0,))) * (
        cand_count * capacity
    ) + contract(spread, rank.astype(jnp.bfloat16), ((1,), (0,)))
    column = jnp.sum(jnp.where(own, value, 0.0), axis=1, keepdims=True)
    shift = (lax.broadcasted_iota(jnp.int32, (rows, 1), 0) % cand_count) * capacity
    return column.astype(jnp.int32) + shift


def row_norms(list_slot, probes, corpus, local_lists, cand_count, capacity):
    total_rows, features = corpus.shape
    list_length = total_rows // local_lists
    chunk = min(list_length, 256)
    staged = staged_rows(local_lists, list_length)
    query_count, probe_count = probes.shape
    whole = pl.BlockSpec(memory_space=pltpu.VMEM)
    return pl.pallas_call(
        functools.partial(norm_kernel, (cand_count, capacity, chunk)),
        out_shape=(
            pltpu.VMEM((staged, features), corpus.dtype),
            jax.ShapeDtypeStruct((local_lists, list_length), jnp.float32),
            jax.ShapeDtypeStruct((query_count * probe_count * cand_count, 1), jnp.int32),
        ),
        in_specs=[
            pl.BlockSpec(memory_space=pltpu.HBM),
            whole,
            pl.BlockSpec(memory_space=pltpu.HBM),
        ],
        out_specs=(whole, whole, whole),
        scratch_shapes=[
            pltpu.VMEM((max(total_rows - staged, 16), features), corpus.dtype),
            pltpu.VMEM((total_rows, 2 * LANES), jnp.bfloat16),
            pltpu.SMEM(list_slot.shape, list_slot.dtype),
            pltpu.SemaphoreType.DMA((total_rows // chunk,)),
            pltpu.SemaphoreType.DMA,
        ],
        compiler_params=pltpu.CompilerParams(vmem_limit_bytes=24 * MIB),
        cost_estimate=pl.CostEstimate(
            flops=2 * corpus.size, bytes_accessed=2 * corpus.size, transcendentals=0
        ),
    )(in_hbm(list_slot), in_hbm(probes.T), in_hbm(corpus))


def score_kernel(
    sizes, me_ref, slot_ref, corpus_ref, staged_ref, inv_ref, message_ref, out_ref, held, picked, sems
):
    owners, query_count, probe_count, cand_count, capacity, streams = sizes
    total_rows, features = corpus_ref.shape
    local_lists, list_length = inv_ref.shape
    staged = staged_ref.shape[0]
    total = owners * query_count
    room = owners * capacity
    step = capacity * cand_count

    def copy(i):
        begin, end = streams[i]
        return pltpu.make_async_copy(
            corpus_ref.at[begin:end], held.at[begin - staged : end - staged], sems.at[i]
        )

    for i in range(len(streams)):
        copy(i).start()
    columns = [
        jnp.concatenate(
            [message_ref[s, j : j + query_count, :] for s in range(owners)], axis=0
        )
        for j in range(0, query_count * (features // LANES), query_count)
    ]
    queries = jnp.concatenate(columns, axis=1)
    squares = functools.reduce(jnp.add, [c.astype(jnp.float32) ** 2 for c in columns])
    height = message_ref.shape[1]
    tiles = [
        message_ref[s, height - probe_count :, :].astype(jnp.float32) for s in range(owners)
    ]
    probes, *cands = [
        jnp.concatenate([t[:, i : i + query_count] for t in tiles], axis=1)
        for i in range(0, query_count * (1 + cand_count), query_count)
    ]
    inv_query = lax.rsqrt(row_sums(squares) / features + epsilon)

    slots = slot_ref[...]
    names = lax.broadcasted_iota(jnp.int32, slots.shape, 1).astype(jnp.float32)
    first = me_ref[0] * local_lists
    hits, wanted = [], []
    for l in range(local_lists):
        name = jnp.sum(jnp.where(slots == first + l, names, 0.0), axis=1, keepdims=True)
        named = probes == name
        hits.append(jnp.sum(named.astype(jnp.float32), axis=0, keepdims=True))
        wanted.append(
            [jnp.sum(jnp.where(named, c, 0.0), axis=0, keepdims=True) for c in cands]
        )
    hit = jnp.concatenate(hits, axis=0)

    span = min(total, LANES)
    earlier = lax.broadcasted_iota(jnp.int32, (span, span), 0)
    later = lax.broadcasted_iota(jnp.int32, (span, span), 1)
    before = (earlier < later) & (earlier // query_count == later // query_count)
    before = before.astype(jnp.float32).astype(jnp.bfloat16)
    hit_low = hit.astype(jnp.bfloat16)
    rank = jnp.concatenate(
        [
            contract(hit_low[:, j : j + span], before, ((1,), (0,)))
            for j in range(0, total, span)
        ],
        axis=1,
    )
    source = (lax.broadcasted_iota(jnp.int32, (1, total), 1) // query_count) * capacity
    target = jnp.where(hit > 0.5, rank.astype(jnp.int32) + source, -1)

    places = lax.broadcasted_iota(jnp.int32, (room, total), 0)
    picks = [(places == target[l : l + 1]).astype(jnp.float32) for l in range(local_lists)]
    pick = jnp.concatenate(picks, axis=0).astype(jnp.bfloat16)
    picked[...] = contract(pick, queries, ((1,), (0,))).astype(jnp.bfloat16)
    scales = [jnp.sum(p * inv_query, axis=1, keepdims=True) for p in picks]
    blocks = [
        [jnp.sum(p * w, axis=1, keepdims=True) for w in wanted[l]] for l, p in enumerate(picks)
    ]

    for l in range(local_lists):
        rows = picked[l * room : (l + 1) * room, :]
        chosen = [jnp.zeros((room, BLOCK), jnp.float32) for _ in range(cand_count)]
        row = l * list_length
        while row < (l + 1) * list_length:
            if row < staged:
                end = min(row + 512, staged, (l + 1) * list_length)
                values = staged_ref[row:end, :]
            else:
                number = [begin for begin, _ in streams].index(row)
                end = streams[number][1]
                copy(number).wait()
                values = held[row - staged : end - staged, :]
            products = contract(rows, values, ((1,), (1,)))
            first = row - l * list_length
            scaled = products * scales[l] * inv_ref[l : l + 1, first : first + end - row]
            for j in range(0, end - row, BLOCK):
                piece = scaled[:, j : j + BLOCK]
                chosen = [
                    jnp.where(block == (first + j) // BLOCK, piece, old)
                    for block, old in zip(blocks[l], chosen)
                ]
            row = end
        out_ref[:, l * step : (l + 1) * step, :] = jnp.concatenate(
            [c.reshape(owners, capacity, BLOCK) for c in chosen], axis=1
        ).astype(jnp.bfloat16)


def stream_ranges(local_lists, list_length):
    row, end = staged_rows(local_lists, list_length), local_lists * list_length
    ranges = []
    while row < end:
        to = (row // list_length + 1) * list_length
        if to == end and to - row > list_length // 2:
            to = end - list_length // 2
        ranges.append((row, to))
        row = to
    return tuple(ranges)


def block_scores(sizes, me, list_slot, corpus, staged, inv_rows, messages):
    owners, query_count, probe_count, cand_count, capacity = sizes
    local_lists, list_length = inv_rows.shape
    total_rows, features = corpus.shape
    streams = stream_ranges(local_lists, list_length)
    whole = pl.BlockSpec(memory_space=pltpu.VMEM)
    return pl.pallas_call(
        functools.partial(score_kernel, sizes + (streams,)),
        out_shape=jax.ShapeDtypeStruct(
            (owners, local_lists * cand_count * capacity, BLOCK), jnp.bfloat16
        ),
        in_specs=[
            pl.BlockSpec(memory_space=pltpu.SMEM),
            whole,
            pl.BlockSpec(memory_space=pltpu.HBM),
            whole,
            whole,
            whole,
        ],
        out_specs=whole,
        scratch_shapes=[
            pltpu.VMEM((max(total_rows - staged.shape[0], 16), features), corpus.dtype),
            pltpu.VMEM((local_lists * owners * capacity, features), corpus.dtype),
            pltpu.SemaphoreType.DMA((max(len(streams), 1),)),
        ],
        compiler_params=pltpu.CompilerParams(vmem_limit_bytes=40 * MIB),
        cost_estimate=pl.CostEstimate(
            flops=2 * owners * capacity * corpus.size,
            bytes_accessed=2 * corpus.size,
            transcendentals=0,
        ),
    )(me, list_slot, in_hbm(corpus), in_vmem(staged), inv_rows, messages)


def place_kernel(column_ref, returned_ref, out_ref):
    returned = returned_ref[...].reshape(-1, returned_ref.shape[-1])
    lanes = lax.broadcasted_iota(jnp.int32, (out_ref.shape[0], returned.shape[0]), 1)
    pick = (lanes == column_ref[...]).astype(jnp.float32).astype(jnp.bfloat16)
    out_ref[...] = contract(pick, returned, ((1,), (0,))).astype(jnp.bfloat16)


def place(column, returned):
    whole = pl.BlockSpec(memory_space=pltpu.VMEM)
    return pl.pallas_call(
        place_kernel,
        out_shape=jax.ShapeDtypeStruct((column.shape[0], BLOCK), jnp.bfloat16),
        in_specs=[whole] * 2,
        out_specs=whole,
        compiler_params=pltpu.CompilerParams(vmem_limit_bytes=24 * MIB),
    )(column, returned)


def message_kernel(queries_ref, probes_ref, cand_ref, out_ref):
    owners, height, lanes = out_ref.shape
    query_count, features = queries_ref.shape
    probe_count, cand_count, _ = cand_ref.shape
    pieces = [probes_ref[...]] + [cand_ref[:, c, :] for c in range(cand_count)]
    spare = lanes - len(pieces) * query_count
    pieces.append(jnp.zeros((probe_count, spare), jnp.int32))
    indices = jnp.concatenate(pieces, axis=1).astype(jnp.float32).astype(jnp.bfloat16)
    for k in range(owners):
        for j in range(features // lanes):
            out_ref[k, j * query_count : (j + 1) * query_count, :] = queries_ref[
                :, j * lanes : (j + 1) * lanes
            ]
        out_ref[k, height - probe_count :, :] = indices


def make_message(queries, probes, cand, owners):
    query_count, features = queries.shape
    probe_count = probes.shape[1]
    height = query_count * (features // LANES) + probe_count
    whole = pl.BlockSpec(memory_space=pltpu.VMEM)
    return pl.pallas_call(
        message_kernel,
        out_shape=jax.ShapeDtypeStruct((owners, height, LANES), queries.dtype),
        in_specs=[whole] * 3,
        out_specs=whole,
        compiler_params=pltpu.CompilerParams(vmem_limit_bytes=24 * MIB),
    )(in_hbm(queries), in_hbm(probes.T), in_hbm(cand.transpose(1, 2, 0)))


def on_device(queries, corpus, list_slot, probes, cand):
    owners = lax.axis_size("lists")
    query_count, features = queries.shape
    probe_count = probes.shape[1]
    cand_count = cand.shape[2]
    local_lists = corpus.shape[0]
    corpus = corpus.reshape(-1, features)
    total_lists = list_slot.shape[0]
    pair_count = query_count * probe_count
    capacity = min(query_count, max(2, (2 * pair_count + total_lists - 1) // total_lists))
    sizes = (owners, query_count, probe_count, cand_count, capacity)
    me = lax.axis_index("lists").astype(jnp.int32)

    message = make_message(queries, probes, cand, owners)
    messages = exchange(message)
    staged, inv_rows, column = row_norms(
        list_slot, probes, corpus, local_lists, cand_count, capacity
    )
    scores = block_scores(sizes, me.reshape(1), list_slot[None, :], corpus, staged, inv_rows, messages)
    returned = exchange(scores)
    chosen = place(column, returned)
    return chosen.reshape(query_count, probe_count, cand_count, BLOCK)


def solution(mesh):
    placed = (
        P(("groups", "lists", "rep"), None),
        P(("groups", "lists"), None, None),
        P("groups"),
        P(("groups", "lists", "rep"), None),
        P(("groups", "lists", "rep"), None, None),
    )
    return jax.shard_map(
        on_device,
        mesh=mesh,
        in_specs=placed,
        out_specs=P(("groups", "lists", "rep"), None, None, None),
        check_vma=False,
    )
```

```python
import functools

import jax
import jax.numpy as jnp
from jax import lax
from jax.experimental import pallas as pl
from jax.experimental.pallas import tpu as pltpu
from jax.sharding import PartitionSpec as P

BLOCK = 128
LANES = 128
MIB = 2**20

epsilon = 1e-06


def contract(a, b, dims, precision=None):
    return lax.dot_general(
        a, b, (dims, ((), ())), precision=precision, preferred_element_type=jnp.float32
    )


def in_hbm(value):
    return pltpu.with_memory_space_constraint(value, pltpu.HBM)


def in_vmem(value):
    return pltpu.with_memory_space_constraint(value, pltpu.VMEM)


def exchange_order(owners):
    if owners > 16:
        return list(range(owners))
    return sorted(range(owners), key=lambda i: (abs(i - owners // 2 - 0.25), i))


def exchange(value):
    order = exchange_order(lax.axis_size("lists"))
    return lax.all_to_all(
        value, "lists", split_axis=0, concat_axis=0, axis_index_groups=[order], tiled=True
    )


def staged_rows(local_lists, list_length):
    return min(local_lists * list_length, list_length + 3 * list_length // 8)


def norm_kernel(
    sizes,
    slot_ref,
    probes_ref,
    corpus_ref,
    staged_ref,
    inv_ref,
    column_ref,
    held,
    parts,
    slots,
    sems,
    slot_sem,
):
    cand_count, capacity, chunk = sizes
    total_rows, features = corpus_ref.shape
    local_lists, list_length = inv_ref.shape
    staged = staged_ref.shape[0]

    cuts = sorted(set(range(0, total_rows + 1, chunk)) | {staged})
    ranges = list(zip(cuts[:-1], cuts[1:]))

    def place(row, end):
        if row < staged:
            return staged_ref.at[row:end]
        return held.at[row - staged : end - staged]

    def copy(row, end):
        return pltpu.make_async_copy(
            corpus_ref.at[row:end], place(row, end), sems.at[cuts.index(row)]
        )

    slot_copy = pltpu.make_async_copy(slot_ref, slots, slot_sem)
    slot_copy.start()
    for row, end in ranges:
        copy(row, end).start()
    slot_copy.wait()
    column_ref[...] = result_columns(cand_count, capacity, local_lists, slots, probes_ref[...])
    ones = jnp.ones((8, 2 * LANES), jnp.bfloat16)
    for l in range(local_lists):
        for row, end in ranges:
            if row // list_length != l:
                continue
            copy(row, end).wait()
            wide = place(row, end)[...].astype(jnp.float32)
            squares = functools.reduce(
                jnp.add, [wide[:, j : j + LANES] ** 2 for j in range(0, features, LANES)]
            )
            high = squares.astype(jnp.bfloat16)
            parts[row:end, :LANES] = high
            parts[row:end, LANES:] = (squares - high.astype(jnp.float32)).astype(
                jnp.bfloat16
            )
        whole = parts[l * list_length : (l + 1) * list_length, :]
        sums = contract(ones, whole, ((1,), (1,)))[:1]
        inv_ref[l : l + 1, :] = lax.rsqrt(sums / features + epsilon) * features ** (-0.5)


def row_sums(parts):
    high = parts.astype(jnp.bfloat16)
    low = (parts - high.astype(jnp.float32)).astype(jnp.bfloat16)
    terms = jnp.concatenate([high, low], axis=1)
    ones = jnp.ones((8, terms.shape[1]), jnp.bfloat16)
    return contract(ones, terms, ((1,), (1,)))[:1]


def result_columns(cand_count, capacity, local_lists, slot_ref, probes):
    probe_count, query_count = probes.shape
    total_lists = slot_ref.shape[0]
    order = exchange_order(total_lists // local_lists)
    position = jnp.zeros(probes.shape, jnp.float32)
    for t in range(total_lists):
        owner = slot_ref[t] // local_lists
        place = owner
        for j, i in enumerate(order):
            if i != j:
                place = jnp.where(owner == i, j, place)
        spot = place * local_lists + slot_ref[t] % local_lists
        position = jnp.where(probes == t, spot.astype(jnp.float32), position)
    lists = lax.broadcasted_iota(jnp.int32, (total_lists, query_count), 0)
    named = [lists == probes[p : p + 1] for p in range(probe_count)]
    counts = functools.reduce(jnp.add, [n.astype(jnp.float32) for n in named])
    square = (query_count, query_count)
    before = lax.broadcasted_iota(jnp.int32, square, 0) < lax.broadcasted_iota(
        jnp.int32, square, 1
    )
    earlier = contract(
        counts.astype(jnp.bfloat16), before.astype(jnp.float32).astype(jnp.bfloat16), ((1,), (0,))
    )
    rank = jnp.concatenate(
        [jnp.sum(jnp.where(n, earlier, 0.0), axis=0, keepdims=True) for n in named], axis=0
    )
    rows = query_count * probe_count * cand_count
    row = lax.broadcasted_iota(jnp.int32, (rows, probe_count), 0)
    lane = lax.broadcasted_iota(jnp.int32, (rows, probe_count), 1)
    spread = (row // cand_count) % probe_count == lane
    spread = spread.astype(jnp.float32).astype(jnp.bfloat16)
    row = lax.broadcasted_iota(jnp.int32, (rows, query_count), 0)
    lane = lax.broadcasted_iota(jnp.int32, (rows, query_count), 1)
    own = row // (probe_count * cand_count) == lane
    value = contract(spread, position.astype(jnp.bfloat16), ((1,), (0,))) * (
        cand_count * capacity
    ) + contract(spread, rank.astype(jnp.bfloat16), ((1,), (0,)))
    column = jnp.sum(jnp.where(own, value, 0.0), axis=1, keepdims=True)
    shift = (lax.broadcasted_iota(jnp.int32, (rows, 1), 0) % cand_count) * capacity
    return column.astype(jnp.int32) + shift


def row_norms(list_slot, probes, corpus, local_lists, cand_count, capacity):
    total_rows, features = corpus.shape
    list_length = total_rows // local_lists
    chunk = min(list_length, 256)
    staged = staged_rows(local_lists, list_length)
    query_count, probe_count = probes.shape
    whole = pl.BlockSpec(memory_space=pltpu.VMEM)
    return pl.pallas_call(
        functools.partial(norm_kernel, (cand_count, capacity, chunk)),
        out_shape=(
            pltpu.VMEM((staged, features), corpus.dtype),
            jax.ShapeDtypeStruct((local_lists, list_length), jnp.float32),
            jax.ShapeDtypeStruct((query_count * probe_count * cand_count, 1), jnp.int32),
        ),
        in_specs=[
            pl.BlockSpec(memory_space=pltpu.HBM),
            whole,
            pl.BlockSpec(memory_space=pltpu.HBM),
        ],
        out_specs=(whole, whole, whole),
        scratch_shapes=[
            pltpu.VMEM((max(total_rows - staged, 16), features), corpus.dtype),
            pltpu.VMEM((total_rows, 2 * LANES), jnp.bfloat16),
            pltpu.SMEM(list_slot.shape, list_slot.dtype),
            pltpu.SemaphoreType.DMA((total_rows // chunk + 1,)),
            pltpu.SemaphoreType.DMA,
        ],
        compiler_params=pltpu.CompilerParams(vmem_limit_bytes=24 * MIB),
        cost_estimate=pl.CostEstimate(
            flops=2 * corpus.size, bytes_accessed=2 * corpus.size, transcendentals=0
        ),
    )(in_hbm(list_slot), in_hbm(probes.T), in_hbm(corpus))


def score_kernel(
    sizes, me_ref, slot_ref, corpus_ref, staged_ref, inv_ref, message_ref, out_ref, held, picked, sems
):
    owners, query_count, probe_count, cand_count, capacity, streams = sizes
    total_rows, features = corpus_ref.shape
    local_lists, list_length = inv_ref.shape
    staged = staged_ref.shape[0]
    total = owners * query_count
    room = owners * capacity
    step = capacity * cand_count

    def copies(begin, end):
        cuts = list(range(begin, end, min(256, list_length))) + [end]
        return [
            pltpu.make_async_copy(
                corpus_ref.at[a:b],
                held.at[a - staged : b - staged],
                sems.at[(a - staged) // LANES],
            )
            for a, b in zip(cuts[:-1], cuts[1:])
        ]

    for begin, end in streams:
        for c in copies(begin, end):
            c.start()
    columns = [
        jnp.concatenate(
            [message_ref[s, j : j + query_count, :] for s in range(owners)], axis=0
        )
        for j in range(0, query_count * (features // LANES), query_count)
    ]
    queries = jnp.concatenate(columns, axis=1)
    squares = functools.reduce(jnp.add, [c.astype(jnp.float32) ** 2 for c in columns])
    height = message_ref.shape[1]
    tiles = [
        message_ref[s, height - probe_count :, :].astype(jnp.float32) for s in range(owners)
    ]
    probes, *cands = [
        jnp.concatenate([t[:, i : i + query_count] for t in tiles], axis=1)
        for i in range(0, query_count * (1 + cand_count), query_count)
    ]
    inv_query = lax.rsqrt(row_sums(squares) / features + epsilon)

    slots = slot_ref[...]
    names = lax.broadcasted_iota(jnp.int32, slots.shape, 1).astype(jnp.float32)
    first = me_ref[0] * local_lists
    hits, wanted = [], []
    for l in range(local_lists):
        name = jnp.sum(jnp.where(slots == first + l, names, 0.0), axis=1, keepdims=True)
        named = probes == name
        hits.append(jnp.sum(named.astype(jnp.float32), axis=0, keepdims=True))
        wanted.append(
            [jnp.sum(jnp.where(named, c, 0.0), axis=0, keepdims=True) for c in cands]
        )
    hit = jnp.concatenate(hits, axis=0)

    span = min(total, LANES)
    earlier = lax.broadcasted_iota(jnp.int32, (span, span), 0)
    later = lax.broadcasted_iota(jnp.int32, (span, span), 1)
    before = (earlier < later) & (earlier // query_count == later // query_count)
    before = before.astype(jnp.float32).astype(jnp.bfloat16)
    hit_low = hit.astype(jnp.bfloat16)
    rank = jnp.concatenate(
        [
            contract(hit_low[:, j : j + span], before, ((1,), (0,)))
            for j in range(0, total, span)
        ],
        axis=1,
    )
    source = (lax.broadcasted_iota(jnp.int32, (1, total), 1) // query_count) * capacity
    target = jnp.where(hit > 0.5, rank.astype(jnp.int32) + source, -1)

    places = lax.broadcasted_iota(jnp.int32, (room, total), 0)
    picks = [(places == target[l : l + 1]).astype(jnp.float32) for l in range(local_lists)]
    pick = jnp.concatenate(picks, axis=0).astype(jnp.bfloat16)
    picked[...] = contract(pick, queries, ((1,), (0,))).astype(jnp.bfloat16)
    scales = [jnp.sum(p * inv_query, axis=1, keepdims=True) for p in picks]
    blocks = [
        [jnp.sum(p * w, axis=1, keepdims=True) for w in wanted[l]] for l, p in enumerate(picks)
    ]

    for l in range(local_lists):
        rows = picked[l * room : (l + 1) * room, :]
        chosen = [jnp.zeros((room, BLOCK), jnp.float32) for _ in range(cand_count)]
        row = l * list_length
        while row < (l + 1) * list_length:
            if row < staged:
                end = min(row + 512, staged, (l + 1) * list_length)
                values = staged_ref[row:end, :]
            else:
                end = dict(streams)[row]
                for c in copies(row, end):
                    c.wait()
                values = held[row - staged : end - staged, :]
            products = contract(rows, values, ((1,), (1,)))
            first = row - l * list_length
            scaled = products * scales[l] * inv_ref[l : l + 1, first : first + end - row]
            for j in range(0, end - row, BLOCK):
                piece = scaled[:, j : j + BLOCK]
                chosen = [
                    jnp.where(block == (first + j) // BLOCK, piece, old)
                    for block, old in zip(blocks[l], chosen)
                ]
            row = end
        out_ref[:, l * step : (l + 1) * step, :] = jnp.concatenate(
            [c.reshape(owners, capacity, BLOCK) for c in chosen], axis=1
        ).astype(jnp.bfloat16)


def stream_ranges(local_lists, list_length):
    row, end = staged_rows(local_lists, list_length), local_lists * list_length
    ranges = []
    while row < end:
        to = (row // list_length + 1) * list_length
        if to == end and to - row > list_length // 2:
            to = end - list_length // 2
        ranges.append((row, to))
        row = to
    return tuple(ranges)


def block_scores(sizes, me, list_slot, corpus, staged, inv_rows, messages):
    owners, query_count, probe_count, cand_count, capacity = sizes
    local_lists, list_length = inv_rows.shape
    total_rows, features = corpus.shape
    streams = stream_ranges(local_lists, list_length)
    whole = pl.BlockSpec(memory_space=pltpu.VMEM)
    return pl.pallas_call(
        functools.partial(score_kernel, sizes + (streams,)),
        out_shape=jax.ShapeDtypeStruct(
            (owners, local_lists * cand_count * capacity, BLOCK), jnp.bfloat16
        ),
        in_specs=[
            pl.BlockSpec(memory_space=pltpu.SMEM),
            whole,
            pl.BlockSpec(memory_space=pltpu.HBM),
            whole,
            whole,
            whole,
        ],
        out_specs=whole,
        scratch_shapes=[
            pltpu.VMEM((max(total_rows - staged.shape[0], 16), features), corpus.dtype),
            pltpu.VMEM((local_lists * owners * capacity, features), corpus.dtype),
            pltpu.SemaphoreType.DMA((max((total_rows - staged.shape[0]) // LANES, 1),)),
        ],
        compiler_params=pltpu.CompilerParams(vmem_limit_bytes=40 * MIB),
        cost_estimate=pl.CostEstimate(
            flops=2 * owners * capacity * corpus.size,
            bytes_accessed=2 * corpus.size,
            transcendentals=0,
        ),
    )(me, list_slot, in_hbm(corpus), in_vmem(staged), inv_rows, messages)


def place_kernel(column_ref, returned_ref, out_ref):
    returned = returned_ref[...].reshape(-1, returned_ref.shape[-1])
    lanes = lax.broadcasted_iota(jnp.int32, (out_ref.shape[0], returned.shape[0]), 1)
    pick = (lanes == column_ref[...]).astype(jnp.float32).astype(jnp.bfloat16)
    out_ref[...] = contract(pick, returned, ((1,), (0,))).astype(jnp.bfloat16)


def place(column, returned):
    whole = pl.BlockSpec(memory_space=pltpu.VMEM)
    return pl.pallas_call(
        place_kernel,
        out_shape=jax.ShapeDtypeStruct((column.shape[0], BLOCK), jnp.bfloat16),
        in_specs=[whole] * 2,
        out_specs=whole,
        compiler_params=pltpu.CompilerParams(vmem_limit_bytes=24 * MIB),
    )(column, returned)


def message_kernel(queries_ref, probes_ref, cand_ref, out_ref):
    owners, height, lanes = out_ref.shape
    query_count, features = queries_ref.shape
    probe_count, cand_count, _ = cand_ref.shape
    pieces = [probes_ref[...]] + [cand_ref[:, c, :] for c in range(cand_count)]
    spare = lanes - len(pieces) * query_count
    pieces.append(jnp.zeros((probe_count, spare), jnp.int32))
    indices = jnp.concatenate(pieces, axis=1).astype(jnp.float32).astype(jnp.bfloat16)
    for k in range(owners):
        for j in range(features // lanes):
            out_ref[k, j * query_count : (j + 1) * query_count, :] = queries_ref[
                :, j * lanes : (j + 1) * lanes
            ]
        out_ref[k, height - probe_count :, :] = indices


def make_message(queries, probes, cand, owners):
    query_count, features = queries.shape
    probe_count = probes.shape[1]
    height = query_count * (features // LANES) + probe_count
    whole = pl.BlockSpec(memory_space=pltpu.VMEM)
    return pl.pallas_call(
        message_kernel,
        out_shape=jax.ShapeDtypeStruct((owners, height, LANES), queries.dtype),
        in_specs=[whole] * 3,
        out_specs=whole,
        compiler_params=pltpu.CompilerParams(vmem_limit_bytes=24 * MIB),
    )(in_hbm(queries), in_hbm(probes.T), in_hbm(cand.transpose(1, 2, 0)))


def on_device(queries, corpus, list_slot, probes, cand):
    owners = lax.axis_size("lists")
    query_count, features = queries.shape
    probe_count = probes.shape[1]
    cand_count = cand.shape[2]
    local_lists = corpus.shape[0]
    corpus = corpus.reshape(-1, features)
    total_lists = list_slot.shape[0]
    pair_count = query_count * probe_count
    capacity = min(query_count, max(2, (2 * pair_count + total_lists - 1) // total_lists))
    sizes = (owners, query_count, probe_count, cand_count, capacity)
    me = lax.axis_index("lists").astype(jnp.int32)

    message = make_message(queries, probes, cand, owners)
    messages = exchange(message)
    staged, inv_rows, column = row_norms(
        list_slot, probes, corpus, local_lists, cand_count, capacity
    )
    scores = block_scores(sizes, me.reshape(1), list_slot[None, :], corpus, staged, inv_rows, messages)
    returned = exchange(scores)
    chosen = place(column, returned)
    return chosen.reshape(query_count, probe_count, cand_count, BLOCK)


def solution(mesh):
    placed = (
        P(("groups", "lists", "rep"), None),
        P(("groups", "lists"), None, None),
        P("groups"),
        P(("groups", "lists", "rep"), None),
        P(("groups", "lists", "rep"), None, None),
    )
    return jax.shard_map(
        on_device,
        mesh=mesh,
        in_specs=placed,
        out_specs=P(("groups", "lists", "rep"), None, None, None),
        check_vma=False,
    )
```

```python
import functools

import jax
import jax.numpy as jnp
from jax import lax
from jax.experimental import pallas as pl
from jax.experimental.pallas import tpu as pltpu
from jax.sharding import PartitionSpec as P

BLOCK = 128
LANES = 128
MIB = 2**20

epsilon = 1e-06


def contract(a, b, dims, precision=None):
    return lax.dot_general(
        a, b, (dims, ((), ())), precision=precision, preferred_element_type=jnp.float32
    )


def in_hbm(value):
    return pltpu.with_memory_space_constraint(value, pltpu.HBM)


def in_vmem(value):
    return pltpu.with_memory_space_constraint(value, pltpu.VMEM)


def exchange_order(owners):
    if owners > 16:
        return list(range(owners))
    return sorted(range(owners), key=lambda i: (abs(i - owners // 2 - 0.25), i))


def exchange(value):
    order = exchange_order(lax.axis_size("lists"))
    return lax.all_to_all(
        value, "lists", split_axis=0, concat_axis=0, axis_index_groups=[order], tiled=True
    )


def staged_rows(local_lists, list_length):
    return min(local_lists * list_length, list_length + list_length // 4)


def norm_kernel(
    sizes,
    slot_ref,
    probes_ref,
    corpus_ref,
    staged_ref,
    inv_ref,
    column_ref,
    held,
    parts,
    slots,
    sems,
    slot_sem,
):
    cand_count, capacity, chunk = sizes
    total_rows, features = corpus_ref.shape
    local_lists, list_length = inv_ref.shape
    staged = staged_ref.shape[0]

    cuts = sorted(set(range(0, total_rows + 1, list_length)) | {staged})
    ranges = list(zip(cuts[:-1], cuts[1:]))

    def place(row, end):
        if row < staged:
            return staged_ref.at[row:end]
        return held.at[row - staged : end - staged]

    def copy(row, end):
        return pltpu.make_async_copy(
            corpus_ref.at[row:end], place(row, end), sems.at[cuts.index(row)]
        )

    slot_copy = pltpu.make_async_copy(slot_ref, slots, slot_sem)
    slot_copy.start()
    for row, end in ranges:
        copy(row, end).start()
    slot_copy.wait()
    column_ref[...] = result_columns(cand_count, capacity, local_lists, slots, probes_ref[...])
    ones = jnp.ones((8, 2 * LANES), jnp.bfloat16)
    for l in range(local_lists):
        for begin, to in ranges:
            if begin // list_length != l:
                continue
            copy(begin, to).wait()
            for row in range(begin, to, chunk):
                end = min(row + chunk, to)
                wide = place(row, end)[...].astype(jnp.float32)
                squares = functools.reduce(
                    jnp.add, [wide[:, j : j + LANES] ** 2 for j in range(0, features, LANES)]
                )
                high = squares.astype(jnp.bfloat16)
                low = (squares - high.astype(jnp.float32)).astype(jnp.bfloat16)
                parts[row:end, :LANES] = high
                parts[row:end, LANES:] = low
        whole = parts[l * list_length : (l + 1) * list_length, :]
        sums = contract(ones, whole, ((1,), (1,)))[:1]
        inv_ref[l : l + 1, :] = lax.rsqrt(sums / features + epsilon) * features ** (-0.5)


def row_sums(parts):
    high = parts.astype(jnp.bfloat16)
    low = (parts - high.astype(jnp.float32)).astype(jnp.bfloat16)
    terms = jnp.concatenate([high, low], axis=1)
    ones = jnp.ones((8, terms.shape[1]), jnp.bfloat16)
    return contract(ones, terms, ((1,), (1,)))[:1]


def result_columns(cand_count, capacity, local_lists, slot_ref, probes):
    probe_count, query_count = probes.shape
    total_lists = slot_ref.shape[0]
    order = exchange_order(total_lists // local_lists)
    position = jnp.zeros(probes.shape, jnp.float32)
    for t in range(total_lists):
        owner = slot_ref[t] // local_lists
        place = owner
        for j, i in enumerate(order):
            if i != j:
                place = jnp.where(owner == i, j, place)
        spot = place * local_lists + slot_ref[t] % local_lists
        position = jnp.where(probes == t, spot.astype(jnp.float32), position)
    lists = lax.broadcasted_iota(jnp.int32, (total_lists, query_count), 0)
    named = [lists == probes[p : p + 1] for p in range(probe_count)]
    counts = functools.reduce(jnp.add, [n.astype(jnp.float32) for n in named])
    square = (query_count, query_count)
    before = lax.broadcasted_iota(jnp.int32, square, 0) < lax.broadcasted_iota(
        jnp.int32, square, 1
    )
    earlier = contract(
        counts.astype(jnp.bfloat16), before.astype(jnp.float32).astype(jnp.bfloat16), ((1,), (0,))
    )
    rank = jnp.concatenate(
        [jnp.sum(jnp.where(n, earlier, 0.0), axis=0, keepdims=True) for n in named], axis=0
    )
    rows = query_count * probe_count * cand_count
    row = lax.broadcasted_iota(jnp.int32, (rows, probe_count), 0)
    lane = lax.broadcasted_iota(jnp.int32, (rows, probe_count), 1)
    spread = (row // cand_count) % probe_count == lane
    spread = spread.astype(jnp.float32).astype(jnp.bfloat16)
    row = lax.broadcasted_iota(jnp.int32, (rows, query_count), 0)
    lane = lax.broadcasted_iota(jnp.int32, (rows, query_count), 1)
    own = row // (probe_count * cand_count) == lane
    value = contract(spread, position.astype(jnp.bfloat16), ((1,), (0,))) * (
        cand_count * capacity
    ) + contract(spread, rank.astype(jnp.bfloat16), ((1,), (0,)))
    column = jnp.sum(jnp.where(own, value, 0.0), axis=1, keepdims=True)
    shift = (lax.broadcasted_iota(jnp.int32, (rows, 1), 0) % cand_count) * capacity
    return column.astype(jnp.int32) + shift


def row_norms(list_slot, probes, corpus, local_lists, cand_count, capacity):
    total_rows, features = corpus.shape
    list_length = total_rows // local_lists
    chunk = min(list_length, 256)
    staged = staged_rows(local_lists, list_length)
    query_count, probe_count = probes.shape
    whole = pl.BlockSpec(memory_space=pltpu.VMEM)
    return pl.pallas_call(
        functools.partial(norm_kernel, (cand_count, capacity, chunk)),
        out_shape=(
            pltpu.VMEM((staged, features), corpus.dtype),
            jax.ShapeDtypeStruct((local_lists, list_length), jnp.float32),
            jax.ShapeDtypeStruct((query_count * probe_count * cand_count, 1), jnp.int32),
        ),
        in_specs=[
            pl.BlockSpec(memory_space=pltpu.HBM),
            whole,
            pl.BlockSpec(memory_space=pltpu.HBM),
        ],
        out_specs=(whole, whole, whole),
        scratch_shapes=[
            pltpu.VMEM((max(total_rows - staged, 16), features), corpus.dtype),
            pltpu.VMEM((total_rows, 2 * LANES), jnp.bfloat16),
            pltpu.SMEM(list_slot.shape, list_slot.dtype),
            pltpu.SemaphoreType.DMA((local_lists + 1,)),
            pltpu.SemaphoreType.DMA,
        ],
        compiler_params=pltpu.CompilerParams(vmem_limit_bytes=24 * MIB),
        cost_estimate=pl.CostEstimate(
            flops=2 * corpus.size, bytes_accessed=2 * corpus.size, transcendentals=0
        ),
    )(in_hbm(list_slot), in_hbm(probes.T), in_hbm(corpus))


def score_kernel(
    sizes, me_ref, slot_ref, corpus_ref, staged_ref, inv_ref, message_ref, out_ref, held, picked, sems
):
    owners, query_count, probe_count, cand_count, capacity, streams = sizes
    total_rows, features = corpus_ref.shape
    local_lists, list_length = inv_ref.shape
    staged = staged_ref.shape[0]
    total = owners * query_count
    room = owners * capacity
    step = capacity * cand_count

    def copy(begin, end):
        return pltpu.make_async_copy(
            corpus_ref.at[begin:end],
            held.at[begin - staged : end - staged],
            sems.at[streams.index((begin, end))],
        )

    for begin, end in streams:
        copy(begin, end).start()

    columns = [
        jnp.concatenate(
            [message_ref[s, j : j + query_count, :] for s in range(owners)], axis=0
        )
        for j in range(0, query_count * (features // LANES), query_count)
    ]
    queries = jnp.concatenate(columns, axis=1)
    squares = functools.reduce(jnp.add, [c.astype(jnp.float32) ** 2 for c in columns])
    height = message_ref.shape[1]
    tiles = [
        message_ref[s, height - probe_count :, :].astype(jnp.float32) for s in range(owners)
    ]
    probes, *cands = [
        jnp.concatenate([t[:, i : i + query_count] for t in tiles], axis=1)
        for i in range(0, query_count * (1 + cand_count), query_count)
    ]
    inv_query = lax.rsqrt(row_sums(squares) / features + epsilon)

    slots = slot_ref[...]
    names = lax.broadcasted_iota(jnp.int32, slots.shape, 1).astype(jnp.float32)
    first = me_ref[0] * local_lists
    hits, wanted = [], []
    for l in range(local_lists):
        name = jnp.sum(jnp.where(slots == first + l, names, 0.0), axis=1, keepdims=True)
        named = probes == name
        hits.append(jnp.sum(named.astype(jnp.float32), axis=0, keepdims=True))
        wanted.append(
            [jnp.sum(jnp.where(named, c, 0.0), axis=0, keepdims=True) for c in cands]
        )
    hit = jnp.concatenate(hits, axis=0)

    span = min(total, LANES)
    earlier = lax.broadcasted_iota(jnp.int32, (span, span), 0)
    later = lax.broadcasted_iota(jnp.int32, (span, span), 1)
    before = (earlier < later) & (earlier // query_count == later // query_count)
    before = before.astype(jnp.float32).astype(jnp.bfloat16)
    hit_low = hit.astype(jnp.bfloat16)
    rank = jnp.concatenate(
        [
            contract(hit_low[:, j : j + span], before, ((1,), (0,)))
            for j in range(0, total, span)
        ],
        axis=1,
    )
    source = (lax.broadcasted_iota(jnp.int32, (1, total), 1) // query_count) * capacity
    target = jnp.where(hit > 0.5, rank.astype(jnp.int32) + source, -1)

    places = lax.broadcasted_iota(jnp.int32, (room, total), 0)
    picks = [(places == target[l : l + 1]).astype(jnp.float32) for l in range(local_lists)]
    pick = jnp.concatenate(picks, axis=0).astype(jnp.bfloat16)
    picked[...] = contract(pick, queries, ((1,), (0,))).astype(jnp.bfloat16)
    scales = [jnp.sum(p * inv_query, axis=1, keepdims=True) for p in picks]
    blocks = [
        [jnp.sum(p * w, axis=1, keepdims=True) for w in wanted[l]] for l, p in enumerate(picks)
    ]

    for l in range(local_lists):
        rows = picked[l * room : (l + 1) * room, :]
        chosen = [jnp.zeros((room, BLOCK), jnp.float32) for _ in range(cand_count)]
        row = l * list_length
        while row < (l + 1) * list_length:
            if row < staged:
                end = min(row + 512, staged, (l + 1) * list_length)
                values = staged_ref[row:end, :]
            else:
                end = dict(streams)[row]
                copy(row, end).wait()
                values = held[row - staged : end - staged, :]
            products = contract(rows, values, ((1,), (1,)))
            first = row - l * list_length
            scaled = products * scales[l] * inv_ref[l : l + 1, first : first + end - row]
            for j in range(0, end - row, BLOCK):
                piece = scaled[:, j : j + BLOCK]
                chosen = [
                    jnp.where(block == (first + j) // BLOCK, piece, old)
                    for block, old in zip(blocks[l], chosen)
                ]
            row = end
        out_ref[:, l * step : (l + 1) * step, :] = jnp.concatenate(
            [c.reshape(owners, capacity, BLOCK) for c in chosen], axis=1
        ).astype(jnp.bfloat16)


def stream_ranges(local_lists, list_length):
    row, end = staged_rows(local_lists, list_length), local_lists * list_length
    ranges = []
    while row < end:
        to = (row // list_length + 1) * list_length
        if to == end and to - row > list_length // 2:
            to = end - list_length // 2
        ranges.append((row, to))
        row = to
    return tuple(ranges)


def block_scores(sizes, me, list_slot, corpus, staged, inv_rows, messages):
    owners, query_count, probe_count, cand_count, capacity = sizes
    local_lists, list_length = inv_rows.shape
    total_rows, features = corpus.shape
    streams = stream_ranges(local_lists, list_length)
    whole = pl.BlockSpec(memory_space=pltpu.VMEM)
    return pl.pallas_call(
        functools.partial(score_kernel, sizes + (streams,)),
        out_shape=jax.ShapeDtypeStruct(
            (owners, local_lists * cand_count * capacity, BLOCK), jnp.bfloat16
        ),
        in_specs=[
            pl.BlockSpec(memory_space=pltpu.SMEM),
            whole,
            pl.BlockSpec(memory_space=pltpu.HBM),
            whole,
            whole,
            whole,
        ],
        out_specs=whole,
        scratch_shapes=[
            pltpu.VMEM((max(total_rows - staged.shape[0], 16), features), corpus.dtype),
            pltpu.VMEM((local_lists * owners * capacity, features), corpus.dtype),
            pltpu.SemaphoreType.DMA((max(len(streams), 1),)),
        ],
        compiler_params=pltpu.CompilerParams(vmem_limit_bytes=40 * MIB),
        cost_estimate=pl.CostEstimate(
            flops=2 * owners * capacity * corpus.size,
            bytes_accessed=2 * corpus.size,
            transcendentals=0,
        ),
    )(me, list_slot, in_hbm(corpus), in_vmem(staged), inv_rows, messages)


def place_kernel(column_ref, returned_ref, out_ref):
    returned = returned_ref[...].reshape(-1, returned_ref.shape[-1])
    lanes = lax.broadcasted_iota(jnp.int32, (out_ref.shape[0], returned.shape[0]), 1)
    pick = (lanes == column_ref[...]).astype(jnp.float32).astype(jnp.bfloat16)
    out_ref[...] = contract(pick, returned, ((1,), (0,))).astype(jnp.bfloat16)


def place(column, returned):
    whole = pl.BlockSpec(memory_space=pltpu.VMEM)
    return pl.pallas_call(
        place_kernel,
        out_shape=jax.ShapeDtypeStruct((column.shape[0], BLOCK), jnp.bfloat16),
        in_specs=[whole] * 2,
        out_specs=whole,
        compiler_params=pltpu.CompilerParams(vmem_limit_bytes=24 * MIB),
    )(column, returned)


def message_kernel(queries_ref, probes_ref, cand_ref, out_ref):
    owners, height, lanes = out_ref.shape
    query_count, features = queries_ref.shape
    probe_count, cand_count, _ = cand_ref.shape
    pieces = [probes_ref[...]] + [cand_ref[:, c, :] for c in range(cand_count)]
    spare = lanes - len(pieces) * query_count
    pieces.append(jnp.zeros((probe_count, spare), jnp.int32))
    indices = jnp.concatenate(pieces, axis=1).astype(jnp.float32).astype(jnp.bfloat16)
    for k in range(owners):
        for j in range(features // lanes):
            out_ref[k, j * query_count : (j + 1) * query_count, :] = queries_ref[
                :, j * lanes : (j + 1) * lanes
            ]
        out_ref[k, height - probe_count :, :] = indices


def make_message(queries, probes, cand, owners):
    query_count, features = queries.shape
    probe_count = probes.shape[1]
    height = query_count * (features // LANES) + probe_count
    whole = pl.BlockSpec(memory_space=pltpu.VMEM)
    return pl.pallas_call(
        message_kernel,
        out_shape=pltpu.VMEM((owners, height, LANES), queries.dtype),
        in_specs=[whole] * 3,
        out_specs=whole,
        compiler_params=pltpu.CompilerParams(vmem_limit_bytes=24 * MIB),
    )(in_hbm(queries), in_hbm(probes.T), in_hbm(cand.transpose(1, 2, 0)))


def on_device(queries, corpus, list_slot, probes, cand):
    owners = lax.axis_size("lists")
    query_count, features = queries.shape
    probe_count = probes.shape[1]
    cand_count = cand.shape[2]
    local_lists = corpus.shape[0]
    corpus = corpus.reshape(-1, features)
    total_lists = list_slot.shape[0]
    pair_count = query_count * probe_count
    capacity = min(query_count, max(2, (2 * pair_count + total_lists - 1) // total_lists))
    sizes = (owners, query_count, probe_count, cand_count, capacity)
    me = lax.axis_index("lists").astype(jnp.int32)

    message = make_message(queries, probes, cand, owners)
    messages = exchange(message)
    staged, inv_rows, column = row_norms(
        list_slot, probes, corpus, local_lists, cand_count, capacity
    )
    scores = block_scores(sizes, me.reshape(1), list_slot[None, :], corpus, staged, inv_rows, messages)
    returned = exchange(scores)
    chosen = place(column, returned)
    return chosen.reshape(query_count, probe_count, cand_count, BLOCK)


def solution(mesh):
    placed = (
        P(("groups", "lists", "rep"), None),
        P(("groups", "lists"), None, None),
        P("groups"),
        P(("groups", "lists", "rep"), None),
        P(("groups", "lists", "rep"), None, None),
    )
    return jax.shard_map(
        on_device,
        mesh=mesh,
        in_specs=placed,
        out_specs=P(("groups", "lists", "rep"), None, None, None),
        check_vma=False,
    )
```

```python
import functools

import jax
import jax.numpy as jnp
from jax import lax
from jax.experimental import pallas as pl
from jax.experimental.pallas import tpu as pltpu
from jax.sharding import PartitionSpec as P

BLOCK = 128
LANES = 128
MIB = 2**20

epsilon = 1e-06


def contract(a, b, dims, precision=None):
    return lax.dot_general(
        a, b, (dims, ((), ())), precision=precision, preferred_element_type=jnp.float32
    )


def in_hbm(value):
    return pltpu.with_memory_space_constraint(value, pltpu.HBM)


def in_vmem(value):
    return pltpu.with_memory_space_constraint(value, pltpu.VMEM)


def exchange_order(owners):
    if owners > 16:
        return list(range(owners))
    leader = owners // 2
    ends = owners // 4
    return sorted(
        range(owners), key=lambda i: (i != leader, ends <= i < owners - ends, i % 2, i)
    )


def exchange(value):
    order = exchange_order(lax.axis_size("lists"))
    return lax.all_to_all(
        value, "lists", split_axis=0, concat_axis=0, axis_index_groups=[order], tiled=True
    )


def staged_rows(local_lists, list_length):
    return min(local_lists * list_length, list_length + list_length // 4)


def norm_kernel(
    sizes,
    slot_ref,
    probes_ref,
    corpus_ref,
    staged_ref,
    inv_ref,
    column_ref,
    held,
    parts,
    slots,
    sems,
    slot_sem,
):
    cand_count, capacity, chunk = sizes
    total_rows, features = corpus_ref.shape
    local_lists, list_length = inv_ref.shape
    staged = staged_ref.shape[0]

    cuts = sorted(set(range(0, total_rows + 1, list_length)) | {staged})
    ranges = list(zip(cuts[:-1], cuts[1:]))

    def place(row, end):
        if row < staged:
            return staged_ref.at[row:end]
        return held.at[row - staged : end - staged]

    def copy(row, end):
        return pltpu.make_async_copy(
            corpus_ref.at[row:end], place(row, end), sems.at[cuts.index(row)]
        )

    slot_copy = pltpu.make_async_copy(slot_ref, slots, slot_sem)
    slot_copy.start()
    for row, end in ranges:
        copy(row, end).start()
    slot_copy.wait()
    column_ref[...] = result_columns(cand_count, capacity, local_lists, slots, probes_ref[...])
    ones = jnp.ones((8, 2 * LANES), jnp.bfloat16)
    for l in range(local_lists):
        for begin, to in ranges:
            if begin // list_length != l:
                continue
            copy(begin, to).wait()
            for row in range(begin, to, chunk):
                end = min(row + chunk, to)
                wide = place(row, end)[...].astype(jnp.float32)
                squares = functools.reduce(
                    jnp.add, [wide[:, j : j + LANES] ** 2 for j in range(0, features, LANES)]
                )
                high = squares.astype(jnp.bfloat16)
                low = (squares - high.astype(jnp.float32)).astype(jnp.bfloat16)
                parts[row:end, :LANES] = high
                parts[row:end, LANES:] = low
        whole = parts[l * list_length : (l + 1) * list_length, :]
        sums = contract(ones, whole, ((1,), (1,)))[:1]
        inv_ref[l : l + 1, :] = lax.rsqrt(sums / features + epsilon) * features ** (-0.5)


def row_sums(parts):
    high = parts.astype(jnp.bfloat16)
    low = (parts - high.astype(jnp.float32)).astype(jnp.bfloat16)
    terms = jnp.concatenate([high, low], axis=1)
    ones = jnp.ones((8, terms.shape[1]), jnp.bfloat16)
    return contract(ones, terms, ((1,), (1,)))[:1]


def result_columns(cand_count, capacity, local_lists, slot_ref, probes):
    probe_count, query_count = probes.shape
    total_lists = slot_ref.shape[0]
    order = exchange_order(total_lists // local_lists)
    position = jnp.zeros(probes.shape, jnp.float32)
    for t in range(total_lists):
        owner = slot_ref[t] // local_lists
        place = owner
        for j, i in enumerate(order):
            if i != j:
                place = jnp.where(owner == i, j, place)
        spot = place * local_lists + slot_ref[t] % local_lists
        position = jnp.where(probes == t, spot.astype(jnp.float32), position)
    lists = lax.broadcasted_iota(jnp.int32, (total_lists, query_count), 0)
    named = [lists == probes[p : p + 1] for p in range(probe_count)]
    counts = functools.reduce(jnp.add, [n.astype(jnp.float32) for n in named])
    square = (query_count, query_count)
    before = lax.broadcasted_iota(jnp.int32, square, 0) < lax.broadcasted_iota(
        jnp.int32, square, 1
    )
    earlier = contract(
        counts.astype(jnp.bfloat16), before.astype(jnp.float32).astype(jnp.bfloat16), ((1,), (0,))
    )
    rank = jnp.concatenate(
        [jnp.sum(jnp.where(n, earlier, 0.0), axis=0, keepdims=True) for n in named], axis=0
    )
    rows = query_count * probe_count * cand_count
    row = lax.broadcasted_iota(jnp.int32, (rows, probe_count), 0)
    lane = lax.broadcasted_iota(jnp.int32, (rows, probe_count), 1)
    spread = (row // cand_count) % probe_count == lane
    spread = spread.astype(jnp.float32).astype(jnp.bfloat16)
    row = lax.broadcasted_iota(jnp.int32, (rows, query_count), 0)
    lane = lax.broadcasted_iota(jnp.int32, (rows, query_count), 1)
    own = row // (probe_count * cand_count) == lane
    value = contract(spread, position.astype(jnp.bfloat16), ((1,), (0,))) * (
        cand_count * capacity
    ) + contract(spread, rank.astype(jnp.bfloat16), ((1,), (0,)))
    column = jnp.sum(jnp.where(own, value, 0.0), axis=1, keepdims=True)
    shift = (lax.broadcasted_iota(jnp.int32, (rows, 1), 0) % cand_count) * capacity
    return column.astype(jnp.int32) + shift


def row_norms(list_slot, probes, corpus, local_lists, cand_count, capacity):
    total_rows, features = corpus.shape
    list_length = total_rows // local_lists
    chunk = min(list_length, 256)
    staged = staged_rows(local_lists, list_length)
    query_count, probe_count = probes.shape
    whole = pl.BlockSpec(memory_space=pltpu.VMEM)
    return pl.pallas_call(
        functools.partial(norm_kernel, (cand_count, capacity, chunk)),
        out_shape=(
            pltpu.VMEM((staged, features), corpus.dtype),
            jax.ShapeDtypeStruct((local_lists, list_length), jnp.float32),
            jax.ShapeDtypeStruct((query_count * probe_count * cand_count, 1), jnp.int32),
        ),
        in_specs=[
            pl.BlockSpec(memory_space=pltpu.HBM),
            whole,
            pl.BlockSpec(memory_space=pltpu.HBM),
        ],
        out_specs=(whole, whole, whole),
        scratch_shapes=[
            pltpu.VMEM((max(total_rows - staged, 16), features), corpus.dtype),
            pltpu.VMEM((total_rows, 2 * LANES), jnp.bfloat16),
            pltpu.SMEM(list_slot.shape, list_slot.dtype),
            pltpu.SemaphoreType.DMA((local_lists + 1,)),
            pltpu.SemaphoreType.DMA,
        ],
        compiler_params=pltpu.CompilerParams(vmem_limit_bytes=24 * MIB),
        cost_estimate=pl.CostEstimate(
            flops=2 * corpus.size, bytes_accessed=2 * corpus.size, transcendentals=0
        ),
    )(in_hbm(list_slot), in_hbm(probes.T), in_hbm(corpus))


def score_kernel(
    sizes, me_ref, slot_ref, corpus_ref, staged_ref, inv_ref, message_ref, out_ref, held, picked, sems
):
    owners, query_count, probe_count, cand_count, capacity, streams = sizes
    total_rows, features = corpus_ref.shape
    local_lists, list_length = inv_ref.shape
    staged = staged_ref.shape[0]
    total = owners * query_count
    room = owners * capacity
    step = capacity * cand_count

    def copy(begin, end):
        return pltpu.make_async_copy(
            corpus_ref.at[begin:end],
            held.at[begin - staged : end - staged],
            sems.at[streams.index((begin, end))],
        )

    for begin, end in streams:
        copy(begin, end).start()

    columns = [
        jnp.concatenate(
            [message_ref[s, j : j + query_count, :] for s in range(owners)], axis=0
        )
        for j in range(0, query_count * (features // LANES), query_count)
    ]
    queries = jnp.concatenate(columns, axis=1)
    squares = functools.reduce(jnp.add, [c.astype(jnp.float32) ** 2 for c in columns])
    height = message_ref.shape[1]
    tiles = [
        message_ref[s, height - probe_count :, :].astype(jnp.float32) for s in range(owners)
    ]
    probes, *cands = [
        jnp.concatenate([t[:, i : i + query_count] for t in tiles], axis=1)
        for i in range(0, query_count * (1 + cand_count), query_count)
    ]
    inv_query = lax.rsqrt(row_sums(squares) / features + epsilon)

    slots = slot_ref[...]
    names = lax.broadcasted_iota(jnp.int32, slots.shape, 1).astype(jnp.float32)
    first = me_ref[0] * local_lists
    hits, wanted = [], []
    for l in range(local_lists):
        name = jnp.sum(jnp.where(slots == first + l, names, 0.0), axis=1, keepdims=True)
        named = probes == name
        hits.append(jnp.sum(named.astype(jnp.float32), axis=0, keepdims=True))
        wanted.append(
            [jnp.sum(jnp.where(named, c, 0.0), axis=0, keepdims=True) for c in cands]
        )
    hit = jnp.concatenate(hits, axis=0)

    span = min(total, LANES)
    earlier = lax.broadcasted_iota(jnp.int32, (span, span), 0)
    later = lax.broadcasted_iota(jnp.int32, (span, span), 1)
    before = (earlier < later) & (earlier // query_count == later // query_count)
    before = before.astype(jnp.float32).astype(jnp.bfloat16)
    hit_low = hit.astype(jnp.bfloat16)
    rank = jnp.concatenate(
        [
            contract(hit_low[:, j : j + span], before, ((1,), (0,)))
            for j in range(0, total, span)
        ],
        axis=1,
    )
    source = (lax.broadcasted_iota(jnp.int32, (1, total), 1) // query_count) * capacity
    target = jnp.where(hit > 0.5, rank.astype(jnp.int32) + source, -1)

    places = lax.broadcasted_iota(jnp.int32, (room, total), 0)
    picks = [(places == target[l : l + 1]).astype(jnp.float32) for l in range(local_lists)]
    pick = jnp.concatenate(picks, axis=0).astype(jnp.bfloat16)
    picked[...] = contract(pick, queries, ((1,), (0,))).astype(jnp.bfloat16)
    scales = [jnp.sum(p * inv_query, axis=1, keepdims=True) for p in picks]
    blocks = [
        [jnp.sum(p * w, axis=1, keepdims=True) for w in wanted[l]] for l, p in enumerate(picks)
    ]

    for l in range(local_lists):
        rows = picked[l * room : (l + 1) * room, :]
        chosen = [jnp.zeros((room, BLOCK), jnp.float32) for _ in range(cand_count)]
        row = l * list_length
        while row < (l + 1) * list_length:
            if row < staged:
                end = min(row + 512, staged, (l + 1) * list_length)
                values = staged_ref[row:end, :]
            else:
                end = dict(streams)[row]
                copy(row, end).wait()
                values = held[row - staged : end - staged, :]
            products = contract(rows, values, ((1,), (1,)))
            first = row - l * list_length
            scaled = products * scales[l] * inv_ref[l : l + 1, first : first + end - row]
            for j in range(0, end - row, BLOCK):
                piece = scaled[:, j : j + BLOCK]
                chosen = [
                    jnp.where(block == (first + j) // BLOCK, piece, old)
                    for block, old in zip(blocks[l], chosen)
                ]
            row = end
        out_ref[:, l * step : (l + 1) * step, :] = jnp.concatenate(
            [c.reshape(owners, capacity, BLOCK) for c in chosen], axis=1
        ).astype(jnp.bfloat16)


def stream_ranges(local_lists, list_length):
    row, end = staged_rows(local_lists, list_length), local_lists * list_length
    ranges = []
    while row < end:
        to = (row // list_length + 1) * list_length
        if to == end and to - row > list_length // 2:
            to = end - list_length // 2
        ranges.append((row, to))
        row = to
    return tuple(ranges)


def block_scores(sizes, me, list_slot, corpus, staged, inv_rows, messages):
    owners, query_count, probe_count, cand_count, capacity = sizes
    local_lists, list_length = inv_rows.shape
    total_rows, features = corpus.shape
    streams = stream_ranges(local_lists, list_length)
    whole = pl.BlockSpec(memory_space=pltpu.VMEM)
    return pl.pallas_call(
        functools.partial(score_kernel, sizes + (streams,)),
        out_shape=jax.ShapeDtypeStruct(
            (owners, local_lists * cand_count * capacity, BLOCK), jnp.bfloat16
        ),
        in_specs=[
            pl.BlockSpec(memory_space=pltpu.SMEM),
            whole,
            pl.BlockSpec(memory_space=pltpu.HBM),
            whole,
            whole,
            whole,
        ],
        out_specs=whole,
        scratch_shapes=[
            pltpu.VMEM((max(total_rows - staged.shape[0], 16), features), corpus.dtype),
            pltpu.VMEM((local_lists * owners * capacity, features), corpus.dtype),
            pltpu.SemaphoreType.DMA((max(len(streams), 1),)),
        ],
        compiler_params=pltpu.CompilerParams(vmem_limit_bytes=40 * MIB),
        cost_estimate=pl.CostEstimate(
            flops=2 * owners * capacity * corpus.size,
            bytes_accessed=2 * corpus.size,
            transcendentals=0,
        ),
    )(me, list_slot, in_hbm(corpus), in_vmem(staged), inv_rows, messages)


def place_kernel(column_ref, returned_ref, out_ref):
    returned = returned_ref[...].reshape(-1, returned_ref.shape[-1])
    lanes = lax.broadcasted_iota(jnp.int32, (out_ref.shape[0], returned.shape[0]), 1)
    pick = (lanes == column_ref[...]).astype(jnp.float32).astype(jnp.bfloat16)
    out_ref[...] = contract(pick, returned, ((1,), (0,))).astype(jnp.bfloat16)


def place(column, returned):
    whole = pl.BlockSpec(memory_space=pltpu.VMEM)
    return pl.pallas_call(
        place_kernel,
        out_shape=jax.ShapeDtypeStruct((column.shape[0], BLOCK), jnp.bfloat16),
        in_specs=[whole] * 2,
        out_specs=whole,
        compiler_params=pltpu.CompilerParams(vmem_limit_bytes=24 * MIB),
    )(column, returned)


def message_kernel(
    queries_ref, probes_ref, cand_ref, out_ref, queries_vmem, probes_vmem, cand_vmem, sems
):
    owners, height, lanes = out_ref.shape
    query_count, features = queries_ref.shape
    probe_count, cand_count, _ = cand_ref.shape
    pairs = (
        (probes_ref, probes_vmem),
        (cand_ref, cand_vmem),
        (queries_ref, queries_vmem),
    )
    copies = [
        pltpu.make_async_copy(source, target, sems.at[i])
        for i, (source, target) in enumerate(pairs)
    ]
    for c in copies:
        c.start()
    copies[0].wait()
    copies[1].wait()
    pieces = [probes_vmem[...]] + [cand_vmem[:, c, :] for c in range(cand_count)]
    spare = lanes - len(pieces) * query_count
    pieces.append(jnp.zeros((probe_count, spare), jnp.int32))
    indices = jnp.concatenate(pieces, axis=1).astype(jnp.float32).astype(jnp.bfloat16)
    for k in range(owners):
        out_ref[k, height - probe_count :, :] = indices
    copies[2].wait()
    for j in range(features // lanes):
        column = queries_vmem[:, j * lanes : (j + 1) * lanes]
        for k in range(owners):
            out_ref[k, j * query_count : (j + 1) * query_count, :] = column


def make_message(queries, probes, cand, owners):
    query_count, features = queries.shape
    probe_count = probes.shape[1]
    height = query_count * (features // LANES) + probe_count
    whole = pl.BlockSpec(memory_space=pltpu.VMEM)
    return pl.pallas_call(
        message_kernel,
        out_shape=pltpu.VMEM((owners, height, LANES), queries.dtype),
        in_specs=[pl.BlockSpec(memory_space=pltpu.HBM)] * 3,
        out_specs=whole,
        scratch_shapes=[
            pltpu.VMEM(queries.shape, queries.dtype),
            pltpu.VMEM(probes.shape[::-1], probes.dtype),
            pltpu.VMEM(cand.transpose(1, 2, 0).shape, cand.dtype),
            pltpu.SemaphoreType.DMA((3,)),
        ],
        compiler_params=pltpu.CompilerParams(vmem_limit_bytes=24 * MIB),
    )(in_hbm(queries), in_hbm(probes.T), in_hbm(cand.transpose(1, 2, 0)))


def on_device(queries, corpus, list_slot, probes, cand):
    owners = lax.axis_size("lists")
    query_count, features = queries.shape
    probe_count = probes.shape[1]
    cand_count = cand.shape[2]
    local_lists = corpus.shape[0]
    corpus = corpus.reshape(-1, features)
    total_lists = list_slot.shape[0]
    pair_count = query_count * probe_count
    capacity = min(query_count, max(2, (2 * pair_count + total_lists - 1) // total_lists))
    sizes = (owners, query_count, probe_count, cand_count, capacity)
    me = lax.axis_index("lists").astype(jnp.int32)

    message = make_message(queries, probes, cand, owners)
    messages = exchange(message)
    staged, inv_rows, column = row_norms(
        list_slot, probes, corpus, local_lists, cand_count, capacity
    )
    scores = block_scores(sizes, me.reshape(1), list_slot[None, :], corpus, staged, inv_rows, messages)
    returned = exchange(scores)
    chosen = place(column, returned)
    return chosen.reshape(query_count, probe_count, cand_count, BLOCK)


def solution(mesh):
    placed = (
        P(("groups", "lists", "rep"), None),
        P(("groups", "lists"), None, None),
        P("groups"),
        P(("groups", "lists", "rep"), None),
        P(("groups", "lists", "rep"), None, None),
    )
    return jax.shard_map(
        on_device,
        mesh=mesh,
        in_specs=placed,
        out_specs=P(("groups", "lists", "rep"), None, None, None),
        check_vma=False,
    )
```

```python
import functools

import jax
import jax.numpy as jnp
from jax import lax
from jax.experimental import pallas as pl
from jax.experimental.pallas import tpu as pltpu
from jax.sharding import PartitionSpec as P

BLOCK = 128
LANES = 128
MIB = 2**20

epsilon = 1e-06


def contract(a, b, dims, precision=None):
    return lax.dot_general(
        a, b, (dims, ((), ())), precision=precision, preferred_element_type=jnp.float32
    )


def in_hbm(value):
    return pltpu.with_memory_space_constraint(value, pltpu.HBM)


def in_vmem(value):
    return pltpu.with_memory_space_constraint(value, pltpu.VMEM)


def exchange_order(owners):
    if owners > 16:
        return list(range(owners))
    leader = owners // 2
    ends = owners // 4
    return sorted(
        range(owners), key=lambda i: (i != leader, ends <= i < owners - ends, i % 2, i)
    )


def exchange(value):
    order = exchange_order(lax.axis_size("lists"))
    return lax.all_to_all(
        value, "lists", split_axis=0, concat_axis=0, axis_index_groups=[order], tiled=True
    )


def staged_rows(local_lists, list_length):
    return min(local_lists * list_length, list_length + 3 * list_length // 8)


def norm_kernel(
    sizes,
    slot_ref,
    probes_ref,
    corpus_ref,
    staged_ref,
    inv_ref,
    column_ref,
    held,
    parts,
    slots,
    sems,
    slot_sem,
):
    cand_count, capacity, chunk = sizes
    total_rows, features = corpus_ref.shape
    local_lists, list_length = inv_ref.shape
    staged = staged_ref.shape[0]

    cuts = sorted(set(range(0, total_rows + 1, list_length)) | {staged})
    ranges = list(zip(cuts[:-1], cuts[1:]))

    def place(row, end):
        if row < staged:
            return staged_ref.at[row:end]
        return held.at[row - staged : end - staged]

    def copy(row, end):
        return pltpu.make_async_copy(
            corpus_ref.at[row:end], place(row, end), sems.at[cuts.index(row)]
        )

    slot_copy = pltpu.make_async_copy(slot_ref, slots, slot_sem)
    slot_copy.start()
    for row, end in ranges:
        copy(row, end).start()
    slot_copy.wait()
    column_ref[...] = result_columns(cand_count, capacity, local_lists, slots, probes_ref[...])
    ones = jnp.ones((8, 2 * LANES), jnp.bfloat16)
    for l in range(local_lists):
        for begin, to in ranges:
            if begin // list_length != l:
                continue
            copy(begin, to).wait()
            for row in range(begin, to, chunk):
                end = min(row + chunk, to)
                wide = place(row, end)[...].astype(jnp.float32)
                squares = functools.reduce(
                    jnp.add, [wide[:, j : j + LANES] ** 2 for j in range(0, features, LANES)]
                )
                high = squares.astype(jnp.bfloat16)
                low = (squares - high.astype(jnp.float32)).astype(jnp.bfloat16)
                parts[row:end, :LANES] = high
                parts[row:end, LANES:] = low
        whole = parts[l * list_length : (l + 1) * list_length, :]
        sums = contract(ones, whole, ((1,), (1,)))[:1]
        inv_ref[l : l + 1, :] = lax.rsqrt(sums / features + epsilon) * features ** (-0.5)


def row_sums(parts):
    high = parts.astype(jnp.bfloat16)
    low = (parts - high.astype(jnp.float32)).astype(jnp.bfloat16)
    terms = jnp.concatenate([high, low], axis=1)
    ones = jnp.ones((8, terms.shape[1]), jnp.bfloat16)
    return contract(ones, terms, ((1,), (1,)))[:1]


def result_columns(cand_count, capacity, local_lists, slot_ref, probes):
    probe_count, query_count = probes.shape
    total_lists = slot_ref.shape[0]
    order = exchange_order(total_lists // local_lists)
    position = jnp.zeros(probes.shape, jnp.float32)
    for t in range(total_lists):
        owner = slot_ref[t] // local_lists
        place = owner
        for j, i in enumerate(order):
            if i != j:
                place = jnp.where(owner == i, j, place)
        spot = place * local_lists + slot_ref[t] % local_lists
        position = jnp.where(probes == t, spot.astype(jnp.float32), position)
    lists = lax.broadcasted_iota(jnp.int32, (total_lists, query_count), 0)
    named = [lists == probes[p : p + 1] for p in range(probe_count)]
    counts = functools.reduce(jnp.add, [n.astype(jnp.float32) for n in named])
    square = (query_count, query_count)
    before = lax.broadcasted_iota(jnp.int32, square, 0) < lax.broadcasted_iota(
        jnp.int32, square, 1
    )
    earlier = contract(
        counts.astype(jnp.bfloat16), before.astype(jnp.float32).astype(jnp.bfloat16), ((1,), (0,))
    )
    rank = jnp.concatenate(
        [jnp.sum(jnp.where(n, earlier, 0.0), axis=0, keepdims=True) for n in named], axis=0
    )
    rows = query_count * probe_count * cand_count
    row = lax.broadcasted_iota(jnp.int32, (rows, probe_count), 0)
    lane = lax.broadcasted_iota(jnp.int32, (rows, probe_count), 1)
    spread = (row // cand_count) % probe_count == lane
    spread = spread.astype(jnp.float32).astype(jnp.bfloat16)
    row = lax.broadcasted_iota(jnp.int32, (rows, query_count), 0)
    lane = lax.broadcasted_iota(jnp.int32, (rows, query_count), 1)
    own = row // (probe_count * cand_count) == lane
    value = contract(spread, position.astype(jnp.bfloat16), ((1,), (0,))) * (
        cand_count * capacity
    ) + contract(spread, rank.astype(jnp.bfloat16), ((1,), (0,)))
    column = jnp.sum(jnp.where(own, value, 0.0), axis=1, keepdims=True)
    shift = (lax.broadcasted_iota(jnp.int32, (rows, 1), 0) % cand_count) * capacity
    return column.astype(jnp.int32) + shift


def row_norms(list_slot, probes, corpus, local_lists, cand_count, capacity):
    total_rows, features = corpus.shape
    list_length = total_rows // local_lists
    chunk = min(list_length, 256)
    staged = staged_rows(local_lists, list_length)
    query_count, probe_count = probes.shape
    whole = pl.BlockSpec(memory_space=pltpu.VMEM)
    return pl.pallas_call(
        functools.partial(norm_kernel, (cand_count, capacity, chunk)),
        out_shape=(
            pltpu.VMEM((staged, features), corpus.dtype),
            jax.ShapeDtypeStruct((local_lists, list_length), jnp.float32),
            jax.ShapeDtypeStruct((query_count * probe_count * cand_count, 1), jnp.int32),
        ),
        in_specs=[
            pl.BlockSpec(memory_space=pltpu.HBM),
            whole,
            pl.BlockSpec(memory_space=pltpu.HBM),
        ],
        out_specs=(whole, whole, whole),
        scratch_shapes=[
            pltpu.VMEM((max(total_rows - staged, 16), features), corpus.dtype),
            pltpu.VMEM((total_rows, 2 * LANES), jnp.bfloat16),
            pltpu.SMEM(list_slot.shape, list_slot.dtype),
            pltpu.SemaphoreType.DMA((local_lists + 1,)),
            pltpu.SemaphoreType.DMA,
        ],
        compiler_params=pltpu.CompilerParams(vmem_limit_bytes=24 * MIB),
        cost_estimate=pl.CostEstimate(
            flops=2 * corpus.size, bytes_accessed=2 * corpus.size, transcendentals=0
        ),
    )(in_hbm(list_slot), in_hbm(probes.T), in_hbm(corpus))


def score_kernel(
    sizes, me_ref, slot_ref, corpus_ref, staged_ref, inv_ref, message_ref, out_ref, held, picked, sems
):
    owners, query_count, probe_count, cand_count, capacity, streams = sizes
    total_rows, features = corpus_ref.shape
    local_lists, list_length = inv_ref.shape
    staged = staged_ref.shape[0]
    total = owners * query_count
    room = owners * capacity
    step = capacity * cand_count

    def copy(begin, end):
        return pltpu.make_async_copy(
            corpus_ref.at[begin:end],
            held.at[begin - staged : end - staged],
            sems.at[streams.index((begin, end))],
        )

    for begin, end in streams:
        copy(begin, end).start()

    columns = [
        jnp.concatenate(
            [message_ref[s, j : j + query_count, :] for s in range(owners)], axis=0
        )
        for j in range(0, query_count * (features // LANES), query_count)
    ]
    queries = jnp.concatenate(columns, axis=1)
    squares = functools.reduce(jnp.add, [c.astype(jnp.float32) ** 2 for c in columns])
    height = message_ref.shape[1]
    tiles = [
        message_ref[s, height - probe_count :, :].astype(jnp.float32) for s in range(owners)
    ]
    probes, *cands = [
        jnp.concatenate([t[:, i : i + query_count] for t in tiles], axis=1)
        for i in range(0, query_count * (1 + cand_count), query_count)
    ]
    inv_query = lax.rsqrt(row_sums(squares) / features + epsilon)

    slots = slot_ref[...]
    names = lax.broadcasted_iota(jnp.int32, slots.shape, 1).astype(jnp.float32)
    first = me_ref[0] * local_lists
    hits, wanted = [], []
    for l in range(local_lists):
        name = jnp.sum(jnp.where(slots == first + l, names, 0.0), axis=1, keepdims=True)
        named = probes == name
        hits.append(jnp.sum(named.astype(jnp.float32), axis=0, keepdims=True))
        wanted.append(
            [jnp.sum(jnp.where(named, c, 0.0), axis=0, keepdims=True) for c in cands]
        )
    hit = jnp.concatenate(hits, axis=0)

    span = min(total, LANES)
    earlier = lax.broadcasted_iota(jnp.int32, (span, span), 0)
    later = lax.broadcasted_iota(jnp.int32, (span, span), 1)
    before = (earlier < later) & (earlier // query_count == later // query_count)
    before = before.astype(jnp.float32).astype(jnp.bfloat16)
    hit_low = hit.astype(jnp.bfloat16)
    rank = jnp.concatenate(
        [
            contract(hit_low[:, j : j + span], before, ((1,), (0,)))
            for j in range(0, total, span)
        ],
        axis=1,
    )
    source = (lax.broadcasted_iota(jnp.int32, (1, total), 1) // query_count) * capacity
    target = jnp.where(hit > 0.5, rank.astype(jnp.int32) + source, -1)

    places = lax.broadcasted_iota(jnp.int32, (room, total), 0)
    picks = [(places == target[l : l + 1]).astype(jnp.float32) for l in range(local_lists)]
    pick = jnp.concatenate(picks, axis=0).astype(jnp.bfloat16)
    picked[...] = contract(pick, queries, ((1,), (0,))).astype(jnp.bfloat16)
    scales = [jnp.sum(p * inv_query, axis=1, keepdims=True) for p in picks]
    blocks = [
        [jnp.sum(p * w, axis=1, keepdims=True) for w in wanted[l]] for l, p in enumerate(picks)
    ]

    for l in range(local_lists):
        rows = picked[l * room : (l + 1) * room, :]
        chosen = [jnp.zeros((room, BLOCK), jnp.float32) for _ in range(cand_count)]
        row = l * list_length
        while row < (l + 1) * list_length:
            if row < staged:
                end = min(row + 512, staged, (l + 1) * list_length)
                values = staged_ref[row:end, :]
            else:
                end = dict(streams)[row]
                copy(row, end).wait()
                values = held[row - staged : end - staged, :]
            products = contract(rows, values, ((1,), (1,)))
            first = row - l * list_length
            scaled = products * scales[l] * inv_ref[l : l + 1, first : first + end - row]
            for j in range(0, end - row, BLOCK):
                piece = scaled[:, j : j + BLOCK]
                chosen = [
                    jnp.where(block == (first + j) // BLOCK, piece, old)
                    for block, old in zip(blocks[l], chosen)
                ]
            row = end
        out_ref[:, l * step : (l + 1) * step, :] = jnp.concatenate(
            [c.reshape(owners, capacity, BLOCK) for c in chosen], axis=1
        ).astype(jnp.bfloat16)


def stream_ranges(local_lists, list_length):
    row, end = staged_rows(local_lists, list_length), local_lists * list_length
    ranges = []
    while row < end:
        to = (row // list_length + 1) * list_length
        if to == end and to - row > list_length // 4:
            to = end - list_length // 4
        ranges.append((row, to))
        row = to
    return tuple(ranges)


def block_scores(sizes, me, list_slot, corpus, staged, inv_rows, messages):
    owners, query_count, probe_count, cand_count, capacity = sizes
    local_lists, list_length = inv_rows.shape
    total_rows, features = corpus.shape
    streams = stream_ranges(local_lists, list_length)
    whole = pl.BlockSpec(memory_space=pltpu.VMEM)
    return pl.pallas_call(
        functools.partial(score_kernel, sizes + (streams,)),
        out_shape=jax.ShapeDtypeStruct(
            (owners, local_lists * cand_count * capacity, BLOCK), jnp.bfloat16
        ),
        in_specs=[
            pl.BlockSpec(memory_space=pltpu.SMEM),
            whole,
            pl.BlockSpec(memory_space=pltpu.HBM),
            whole,
            whole,
            whole,
        ],
        out_specs=whole,
        scratch_shapes=[
            pltpu.VMEM((max(total_rows - staged.shape[0], 16), features), corpus.dtype),
            pltpu.VMEM((local_lists * owners * capacity, features), corpus.dtype),
            pltpu.SemaphoreType.DMA((max(len(streams), 1),)),
        ],
        compiler_params=pltpu.CompilerParams(vmem_limit_bytes=40 * MIB),
        cost_estimate=pl.CostEstimate(
            flops=2 * owners * capacity * corpus.size,
            bytes_accessed=2 * corpus.size,
            transcendentals=0,
        ),
    )(me, list_slot, in_hbm(corpus), in_vmem(staged), inv_rows, messages)


def place_kernel(column_ref, returned_ref, out_ref, half_ref, sems):
    returned = returned_ref[...].reshape(-1, returned_ref.shape[-1])
    rows = out_ref.shape[0] // half_ref.shape[0]
    copies = []
    for h in range(half_ref.shape[0]):
        part = slice(h * rows, (h + 1) * rows)
        lanes = lax.broadcasted_iota(jnp.int32, (rows, returned.shape[0]), 1)
        pick = (lanes == column_ref[part, :]).astype(jnp.float32).astype(jnp.bfloat16)
        half_ref[h] = contract(pick, returned, ((1,), (0,))).astype(jnp.bfloat16)
        copies.append(pltpu.make_async_copy(half_ref.at[h], out_ref.at[part], sems.at[h]))
        copies[-1].start()
    for c in copies:
        c.wait()


def place(column, returned):
    whole = pl.BlockSpec(memory_space=pltpu.VMEM)
    rows, halves = column.shape[0], 2
    return pl.pallas_call(
        place_kernel,
        out_shape=jax.ShapeDtypeStruct((rows, BLOCK), jnp.bfloat16),
        in_specs=[whole] * 2,
        out_specs=pl.BlockSpec(memory_space=pltpu.HBM),
        scratch_shapes=[
            pltpu.VMEM((halves, rows // halves, BLOCK), jnp.bfloat16),
            pltpu.SemaphoreType.DMA((halves,)),
        ],
        compiler_params=pltpu.CompilerParams(vmem_limit_bytes=24 * MIB),
    )(column, returned)


def message_kernel(
    queries_ref, probes_ref, cand_ref, out_ref, queries_vmem, probes_vmem, cand_vmem, sems
):
    owners, height, lanes = out_ref.shape
    query_count, features = queries_ref.shape
    probe_count, cand_count, _ = cand_ref.shape
    pairs = (
        (probes_ref, probes_vmem),
        (cand_ref, cand_vmem),
        (queries_ref, queries_vmem),
    )
    copies = [
        pltpu.make_async_copy(source, target, sems.at[i])
        for i, (source, target) in enumerate(pairs)
    ]
    for c in copies:
        c.start()
    copies[0].wait()
    copies[1].wait()
    pieces = [probes_vmem[...]] + [cand_vmem[:, c, :] for c in range(cand_count)]
    spare = lanes - len(pieces) * query_count
    pieces.append(jnp.zeros((probe_count, spare), jnp.int32))
    indices = jnp.concatenate(pieces, axis=1).astype(jnp.float32).astype(jnp.bfloat16)
    for k in range(owners):
        out_ref[k, height - probe_count :, :] = indices
    copies[2].wait()
    for j in range(features // lanes):
        column = queries_vmem[:, j * lanes : (j + 1) * lanes]
        for k in range(owners):
            out_ref[k, j * query_count : (j + 1) * query_count, :] = column


def make_message(queries, probes, cand, owners):
    query_count, features = queries.shape
    probe_count = probes.shape[1]
    height = query_count * (features // LANES) + probe_count
    whole = pl.BlockSpec(memory_space=pltpu.VMEM)
    return pl.pallas_call(
        message_kernel,
        out_shape=jax.ShapeDtypeStruct((owners, height, LANES), queries.dtype),
        in_specs=[pl.BlockSpec(memory_space=pltpu.HBM)] * 3,
        out_specs=whole,
        scratch_shapes=[
            pltpu.VMEM(queries.shape, queries.dtype),
            pltpu.VMEM(probes.shape[::-1], probes.dtype),
            pltpu.VMEM(cand.transpose(1, 2, 0).shape, cand.dtype),
            pltpu.SemaphoreType.DMA((3,)),
        ],
        compiler_params=pltpu.CompilerParams(vmem_limit_bytes=24 * MIB),
    )(in_hbm(queries), in_hbm(probes.T), in_hbm(cand.transpose(1, 2, 0)))


def on_device(queries, corpus, list_slot, probes, cand):
    owners = lax.axis_size("lists")
    query_count, features = queries.shape
    probe_count = probes.shape[1]
    cand_count = cand.shape[2]
    local_lists = corpus.shape[0]
    corpus = corpus.reshape(-1, features)
    total_lists = list_slot.shape[0]
    pair_count = query_count * probe_count
    capacity = min(query_count, max(2, (2 * pair_count + total_lists - 1) // total_lists))
    sizes = (owners, query_count, probe_count, cand_count, capacity)
    me = lax.axis_index("lists").astype(jnp.int32)

    message = make_message(queries, probes, cand, owners)
    messages = exchange(message)
    staged, inv_rows, column = row_norms(
        list_slot, probes, corpus, local_lists, cand_count, capacity
    )
    scores = block_scores(sizes, me.reshape(1), list_slot[None, :], corpus, staged, inv_rows, messages)
    returned = exchange(scores)
    chosen = place(column, returned)
    return chosen.reshape(query_count, probe_count, cand_count, BLOCK)


def solution(mesh):
    placed = (
        P(("groups", "lists", "rep"), None),
        P(("groups", "lists"), None, None),
        P("groups"),
        P(("groups", "lists", "rep"), None),
        P(("groups", "lists", "rep"), None, None),
    )
    return jax.shard_map(
        on_device,
        mesh=mesh,
        in_specs=placed,
        out_specs=P(("groups", "lists", "rep"), None, None, None),
        check_vma=False,
    )
```

```python
import functools

import jax
import jax.numpy as jnp
from jax import lax
from jax.experimental import pallas as pl
from jax.experimental.pallas import tpu as pltpu
from jax.sharding import PartitionSpec as P

BLOCK = 128
LANES = 128
MIB = 2**20

epsilon = 1e-06


def contract(a, b, dims, precision=None):
    return lax.dot_general(
        a, b, (dims, ((), ())), precision=precision, preferred_element_type=jnp.float32
    )


def in_hbm(value):
    return pltpu.with_memory_space_constraint(value, pltpu.HBM)


def in_vmem(value):
    return pltpu.with_memory_space_constraint(value, pltpu.VMEM)


def exchange_order(owners):
    if owners > 16:
        return list(range(owners))
    leader = owners // 2
    ends = owners // 4
    return sorted(
        range(owners), key=lambda i: (i != leader, ends <= i < owners - ends, i % 2, i)
    )


def exchange(value):
    order = exchange_order(lax.axis_size("lists"))
    return lax.all_to_all(
        value, "lists", split_axis=0, concat_axis=0, axis_index_groups=[order], tiled=True
    )


def staged_rows(local_lists, list_length):
    return min(local_lists * list_length, list_length + 3 * list_length // 8)


def norm_kernel(
    sizes,
    slot_ref,
    probes_ref,
    corpus_ref,
    staged_ref,
    inv_ref,
    column_ref,
    held,
    parts,
    slots,
    sems,
    slot_sem,
):
    cand_count, capacity, chunk = sizes
    total_rows, features = corpus_ref.shape
    local_lists, list_length = inv_ref.shape
    staged = staged_ref.shape[0]

    cuts = sorted(set(range(0, total_rows + 1, list_length)) | {staged})
    ranges = list(zip(cuts[:-1], cuts[1:]))

    def place(row, end):
        if row < staged:
            return staged_ref.at[row:end]
        return held.at[row - staged : end - staged]

    def copy(row, end):
        return pltpu.make_async_copy(
            corpus_ref.at[row:end], place(row, end), sems.at[cuts.index(row)]
        )

    slot_copy = pltpu.make_async_copy(slot_ref, slots, slot_sem)
    slot_copy.start()
    for row, end in ranges:
        copy(row, end).start()
    slot_copy.wait()
    column_ref[...] = result_columns(cand_count, capacity, local_lists, slots, probes_ref[...])
    ones = jnp.ones((8, 2 * LANES), jnp.bfloat16)
    for l in range(local_lists):
        for begin, to in ranges:
            if begin // list_length != l:
                continue
            copy(begin, to).wait()
            for row in range(begin, to, chunk):
                end = min(row + chunk, to)
                wide = place(row, end)[...].astype(jnp.float32)
                squares = functools.reduce(
                    jnp.add, [wide[:, j : j + LANES] ** 2 for j in range(0, features, LANES)]
                )
                high = squares.astype(jnp.bfloat16)
                low = (squares - high.astype(jnp.float32)).astype(jnp.bfloat16)
                parts[row:end, :LANES] = high
                parts[row:end, LANES:] = low
        whole = parts[l * list_length : (l + 1) * list_length, :]
        sums = contract(ones, whole, ((1,), (1,)))[:1]
        inv_ref[l : l + 1, :] = lax.rsqrt(sums / features + epsilon) * features ** (-0.5)


def row_sums(parts):
    high = parts.astype(jnp.bfloat16)
    low = (parts - high.astype(jnp.float32)).astype(jnp.bfloat16)
    terms = jnp.concatenate([high, low], axis=1)
    ones = jnp.ones((8, terms.shape[1]), jnp.bfloat16)
    return contract(ones, terms, ((1,), (1,)))[:1]


def result_columns(cand_count, capacity, local_lists, slot_ref, probes):
    probe_count, query_count = probes.shape
    total_lists = slot_ref.shape[0]
    order = exchange_order(total_lists // local_lists)
    position = jnp.zeros(probes.shape, jnp.float32)
    for t in range(total_lists):
        owner = slot_ref[t] // local_lists
        place = owner
        for j, i in enumerate(order):
            if i != j:
                place = jnp.where(owner == i, j, place)
        spot = place * local_lists + slot_ref[t] % local_lists
        position = jnp.where(probes == t, spot.astype(jnp.float32), position)
    lists = lax.broadcasted_iota(jnp.int32, (total_lists, query_count), 0)
    named = [lists == probes[p : p + 1] for p in range(probe_count)]
    counts = functools.reduce(jnp.add, [n.astype(jnp.float32) for n in named])
    square = (query_count, query_count)
    before = lax.broadcasted_iota(jnp.int32, square, 0) < lax.broadcasted_iota(
        jnp.int32, square, 1
    )
    earlier = contract(
        counts.astype(jnp.bfloat16), before.astype(jnp.float32).astype(jnp.bfloat16), ((1,), (0,))
    )
    rank = jnp.concatenate(
        [jnp.sum(jnp.where(n, earlier, 0.0), axis=0, keepdims=True) for n in named], axis=0
    )
    rows = query_count * probe_count * cand_count
    row = lax.broadcasted_iota(jnp.int32, (rows, probe_count), 0)
    lane = lax.broadcasted_iota(jnp.int32, (rows, probe_count), 1)
    spread = (row // cand_count) % probe_count == lane
    spread = spread.astype(jnp.float32).astype(jnp.bfloat16)
    row = lax.broadcasted_iota(jnp.int32, (rows, query_count), 0)
    lane = lax.broadcasted_iota(jnp.int32, (rows, query_count), 1)
    own = row // (probe_count * cand_count) == lane
    value = contract(spread, position.astype(jnp.bfloat16), ((1,), (0,))) * (
        cand_count * capacity
    ) + contract(spread, rank.astype(jnp.bfloat16), ((1,), (0,)))
    column = jnp.sum(jnp.where(own, value, 0.0), axis=1, keepdims=True)
    shift = (lax.broadcasted_iota(jnp.int32, (rows, 1), 0) % cand_count) * capacity
    return column.astype(jnp.int32) + shift


def row_norms(list_slot, probes, corpus, local_lists, cand_count, capacity):
    total_rows, features = corpus.shape
    list_length = total_rows // local_lists
    chunk = min(list_length, 256)
    staged = staged_rows(local_lists, list_length)
    query_count, probe_count = probes.shape
    whole = pl.BlockSpec(memory_space=pltpu.VMEM)
    return pl.pallas_call(
        functools.partial(norm_kernel, (cand_count, capacity, chunk)),
        out_shape=(
            pltpu.VMEM((staged, features), corpus.dtype),
            jax.ShapeDtypeStruct((local_lists, list_length), jnp.float32),
            jax.ShapeDtypeStruct((query_count * probe_count * cand_count, 1), jnp.int32),
        ),
        in_specs=[
            pl.BlockSpec(memory_space=pltpu.HBM),
            whole,
            pl.BlockSpec(memory_space=pltpu.HBM),
        ],
        out_specs=(whole, whole, whole),
        scratch_shapes=[
            pltpu.VMEM((max(total_rows - staged, 16), features), corpus.dtype),
            pltpu.VMEM((total_rows, 2 * LANES), jnp.bfloat16),
            pltpu.SMEM(list_slot.shape, list_slot.dtype),
            pltpu.SemaphoreType.DMA((local_lists + 1,)),
            pltpu.SemaphoreType.DMA,
        ],
        compiler_params=pltpu.CompilerParams(vmem_limit_bytes=24 * MIB),
        cost_estimate=pl.CostEstimate(
            flops=2 * corpus.size, bytes_accessed=2 * corpus.size, transcendentals=0
        ),
    )(in_hbm(list_slot), in_hbm(probes.T), in_hbm(corpus))


def score_kernel(
    sizes, me_ref, slot_ref, corpus_ref, staged_ref, inv_ref, message_ref, out_ref, held, picked, sems
):
    owners, query_count, probe_count, cand_count, capacity, streams = sizes
    total_rows, features = corpus_ref.shape
    local_lists, list_length = inv_ref.shape
    staged = staged_ref.shape[0]
    total = owners * query_count
    room = owners * capacity
    step = capacity * cand_count

    def copy(begin, end):
        return pltpu.make_async_copy(
            corpus_ref.at[begin:end],
            held.at[begin - staged : end - staged],
            sems.at[streams.index((begin, end))],
        )

    for begin, end in streams:
        copy(begin, end).start()

    columns = [
        jnp.concatenate(
            [message_ref[s, j : j + query_count, :] for s in range(owners)], axis=0
        )
        for j in range(0, query_count * (features // LANES), query_count)
    ]
    queries = jnp.concatenate(columns, axis=1)
    squares = functools.reduce(jnp.add, [c.astype(jnp.float32) ** 2 for c in columns])
    height = message_ref.shape[1]
    tiles = [
        message_ref[s, height - probe_count :, :].astype(jnp.float32) for s in range(owners)
    ]
    probes, *cands = [
        jnp.concatenate([t[:, i : i + query_count] for t in tiles], axis=1)
        for i in range(0, query_count * (1 + cand_count), query_count)
    ]
    inv_query = lax.rsqrt(row_sums(squares) / features + epsilon)

    slots = slot_ref[...]
    names = lax.broadcasted_iota(jnp.int32, slots.shape, 1).astype(jnp.float32)
    first = me_ref[0] * local_lists
    hits, wanted = [], []
    for l in range(local_lists):
        name = jnp.sum(jnp.where(slots == first + l, names, 0.0), axis=1, keepdims=True)
        named = probes == name
        hits.append(jnp.sum(named.astype(jnp.float32), axis=0, keepdims=True))
        wanted.append(
            [jnp.sum(jnp.where(named, c, 0.0), axis=0, keepdims=True) for c in cands]
        )
    hit = jnp.concatenate(hits, axis=0)

    span = min(total, LANES)
    earlier = lax.broadcasted_iota(jnp.int32, (span, span), 0)
    later = lax.broadcasted_iota(jnp.int32, (span, span), 1)
    before = (earlier < later) & (earlier // query_count == later // query_count)
    before = before.astype(jnp.float32).astype(jnp.bfloat16)
    hit_low = hit.astype(jnp.bfloat16)
    rank = jnp.concatenate(
        [
            contract(hit_low[:, j : j + span], before, ((1,), (0,)))
            for j in range(0, total, span)
        ],
        axis=1,
    )
    source = (lax.broadcasted_iota(jnp.int32, (1, total), 1) // query_count) * capacity
    target = jnp.where(hit > 0.5, rank.astype(jnp.int32) + source, -1)

    places = lax.broadcasted_iota(jnp.int32, (room, total), 0)
    picks = [(places == target[l : l + 1]).astype(jnp.float32) for l in range(local_lists)]
    pick = jnp.concatenate(picks, axis=0).astype(jnp.bfloat16)
    picked[...] = contract(pick, queries, ((1,), (0,))).astype(jnp.bfloat16)
    scales = [jnp.sum(p * inv_query, axis=1, keepdims=True) for p in picks]
    blocks = [
        [jnp.sum(p * w, axis=1, keepdims=True) for w in wanted[l]] for l, p in enumerate(picks)
    ]
    lane = lax.broadcasted_iota(jnp.int32, (1, cand_count * room), 1)
    block_lanes = []
    for l in range(local_lists):
        twice = jnp.concatenate([picks[l]] * cand_count, axis=0).astype(jnp.bfloat16)
        spare = jnp.zeros((8 - cand_count, total), jnp.float32)
        lines = jnp.concatenate(wanted[l] + [spare], axis=0).astype(jnp.bfloat16)
        lines = contract(lines, twice, ((1,), (1,)))
        block = lines[:1]
        for c in range(1, cand_count):
            block = jnp.where(lane >= c * room, lines[c : c + 1], block)
        block_lanes.append(block)

    for l in range(local_lists):
        rows = picked[l * room : (l + 1) * room, :]
        rows = jnp.concatenate([rows] * cand_count, axis=0)
        chosen = jnp.zeros((BLOCK, cand_count * room), jnp.float32)
        for row in range(l * list_length, (l + 1) * list_length, BLOCK):
            if row >= staged and row in dict(streams):
                copy(row, dict(streams)[row]).wait()
            values = (
                staged_ref[row : row + BLOCK, :]
                if row < staged
                else held[row - staged : row - staged + BLOCK, :]
            )
            products = contract(values, rows, ((1,), (1,)))
            number = (row - l * list_length) // BLOCK
            chosen = jnp.where(block_lanes[l] == number, products, chosen)
        chosen = chosen.T
        parts = []
        for c in range(cand_count):
            inv_row = jnp.zeros((room, BLOCK), jnp.float32)
            for j in range(0, list_length, BLOCK):
                inv_row = jnp.where(
                    blocks[l][c] == j // BLOCK, inv_ref[l : l + 1, j : j + BLOCK], inv_row
                )
            scaled = chosen[c * room : (c + 1) * room, :] * scales[l] * inv_row
            parts.append(scaled.reshape(owners, capacity, BLOCK))
        out_ref[:, l * step : (l + 1) * step, :] = jnp.concatenate(parts, axis=1).astype(
            jnp.bfloat16
        )


def stream_ranges(local_lists, list_length):
    row, end = staged_rows(local_lists, list_length), local_lists * list_length
    ranges = []
    while row < end:
        to = (row // list_length + 1) * list_length
        if to == end and to - row > list_length // 2:
            to = end - list_length // 2
        ranges.append((row, to))
        row = to
    return tuple(ranges)


def block_scores(sizes, me, list_slot, corpus, staged, inv_rows, messages):
    owners, query_count, probe_count, cand_count, capacity = sizes
    local_lists, list_length = inv_rows.shape
    total_rows, features = corpus.shape
    streams = stream_ranges(local_lists, list_length)
    whole = pl.BlockSpec(memory_space=pltpu.VMEM)
    return pl.pallas_call(
        functools.partial(score_kernel, sizes + (streams,)),
        out_shape=jax.ShapeDtypeStruct(
            (owners, local_lists * cand_count * capacity, BLOCK), jnp.bfloat16
        ),
        in_specs=[
            pl.BlockSpec(memory_space=pltpu.SMEM),
            whole,
            pl.BlockSpec(memory_space=pltpu.HBM),
            whole,
            whole,
            whole,
        ],
        out_specs=whole,
        scratch_shapes=[
            pltpu.VMEM((max(total_rows - staged.shape[0], 16), features), corpus.dtype),
            pltpu.VMEM((local_lists * owners * capacity, features), corpus.dtype),
            pltpu.SemaphoreType.DMA((max(len(streams), 1),)),
        ],
        compiler_params=pltpu.CompilerParams(vmem_limit_bytes=40 * MIB),
        cost_estimate=pl.CostEstimate(
            flops=2 * owners * capacity * corpus.size,
            bytes_accessed=2 * corpus.size,
            transcendentals=0,
        ),
    )(me, list_slot, in_hbm(corpus), in_vmem(staged), inv_rows, messages)


def place_kernel(column_ref, returned_ref, out_ref, half_ref, sems):
    returned = returned_ref[...].reshape(-1, returned_ref.shape[-1])
    rows = out_ref.shape[0] // half_ref.shape[0]
    copies = []
    for h in range(half_ref.shape[0]):
        part = slice(h * rows, (h + 1) * rows)
        lanes = lax.broadcasted_iota(jnp.int32, (rows, returned.shape[0]), 1)
        pick = (lanes == column_ref[part, :]).astype(jnp.float32).astype(jnp.bfloat16)
        half_ref[h] = contract(pick, returned, ((1,), (0,))).astype(jnp.bfloat16)
        copies.append(pltpu.make_async_copy(half_ref.at[h], out_ref.at[part], sems.at[h]))
        copies[-1].start()
    for c in copies:
        c.wait()


def place(column, returned):
    whole = pl.BlockSpec(memory_space=pltpu.VMEM)
    rows, halves = column.shape[0], 2
    return pl.pallas_call(
        place_kernel,
        out_shape=jax.ShapeDtypeStruct((rows, BLOCK), jnp.bfloat16),
        in_specs=[whole] * 2,
        out_specs=pl.BlockSpec(memory_space=pltpu.HBM),
        scratch_shapes=[
            pltpu.VMEM((halves, rows // halves, BLOCK), jnp.bfloat16),
            pltpu.SemaphoreType.DMA((halves,)),
        ],
        compiler_params=pltpu.CompilerParams(vmem_limit_bytes=24 * MIB),
    )(column, returned)


def message_kernel(
    queries_ref, probes_ref, cand_ref, out_ref, queries_vmem, probes_vmem, cand_vmem, sems
):
    owners, height, lanes = out_ref.shape
    query_count, features = queries_ref.shape
    probe_count, cand_count, _ = cand_ref.shape
    pairs = (
        (probes_ref, probes_vmem),
        (cand_ref, cand_vmem),
        (queries_ref, queries_vmem),
    )
    copies = [
        pltpu.make_async_copy(source, target, sems.at[i])
        for i, (source, target) in enumerate(pairs)
    ]
    for c in copies:
        c.start()
    copies[0].wait()
    copies[1].wait()
    pieces = [probes_vmem[...]] + [cand_vmem[:, c, :] for c in range(cand_count)]
    spare = lanes - len(pieces) * query_count
    pieces.append(jnp.zeros((probe_count, spare), jnp.int32))
    indices = jnp.concatenate(pieces, axis=1).astype(jnp.float32).astype(jnp.bfloat16)
    for k in range(owners):
        out_ref[k, height - probe_count :, :] = indices
    copies[2].wait()
    for j in range(features // lanes):
        column = queries_vmem[:, j * lanes : (j + 1) * lanes]
        for k in range(owners):
            out_ref[k, j * query_count : (j + 1) * query_count, :] = column


def make_message(queries, probes, cand, owners):
    query_count, features = queries.shape
    probe_count = probes.shape[1]
    height = query_count * (features // LANES) + probe_count
    whole = pl.BlockSpec(memory_space=pltpu.VMEM)
    return pl.pallas_call(
        message_kernel,
        out_shape=jax.ShapeDtypeStruct((owners, height, LANES), queries.dtype),
        in_specs=[pl.BlockSpec(memory_space=pltpu.HBM)] * 3,
        out_specs=whole,
        scratch_shapes=[
            pltpu.VMEM(queries.shape, queries.dtype),
            pltpu.VMEM(probes.shape[::-1], probes.dtype),
            pltpu.VMEM(cand.transpose(1, 2, 0).shape, cand.dtype),
            pltpu.SemaphoreType.DMA((3,)),
        ],
        compiler_params=pltpu.CompilerParams(vmem_limit_bytes=24 * MIB),
    )(in_hbm(queries), in_hbm(probes.T), in_hbm(cand.transpose(1, 2, 0)))


def on_device(queries, corpus, list_slot, probes, cand):
    owners = lax.axis_size("lists")
    query_count, features = queries.shape
    probe_count = probes.shape[1]
    cand_count = cand.shape[2]
    local_lists = corpus.shape[0]
    corpus = corpus.reshape(-1, features)
    total_lists = list_slot.shape[0]
    pair_count = query_count * probe_count
    capacity = min(query_count, max(2, (2 * pair_count + total_lists - 1) // total_lists))
    sizes = (owners, query_count, probe_count, cand_count, capacity)
    me = lax.axis_index("lists").astype(jnp.int32)

    message = make_message(queries, probes, cand, owners)
    messages = exchange(message)
    staged, inv_rows, column = row_norms(
        list_slot, probes, corpus, local_lists, cand_count, capacity
    )
    scores = block_scores(sizes, me.reshape(1), list_slot[None, :], corpus, staged, inv_rows, messages)
    returned = exchange(scores)
    chosen = place(column, returned)
    return chosen.reshape(query_count, probe_count, cand_count, BLOCK)


def solution(mesh):
    placed = (
        P(("groups", "lists", "rep"), None),
        P(("groups", "lists"), None, None),
        P("groups"),
        P(("groups", "lists", "rep"), None),
        P(("groups", "lists", "rep"), None, None),
    )
    return jax.shard_map(
        on_device,
        mesh=mesh,
        in_specs=placed,
        out_specs=P(("groups", "lists", "rep"), None, None, None),
        check_vma=False,
    )
```

```python
import functools

import jax
import jax.numpy as jnp
from jax import lax
from jax.experimental import pallas as pl
from jax.experimental.pallas import tpu as pltpu
from jax.sharding import PartitionSpec as P

BLOCK = 128
LANES = 128
MIB = 2**20

epsilon = 1e-06


def contract(a, b, dims, precision=None):
    return lax.dot_general(
        a, b, (dims, ((), ())), precision=precision, preferred_element_type=jnp.float32
    )


def in_hbm(value):
    return pltpu.with_memory_space_constraint(value, pltpu.HBM)


def in_vmem(value):
    return pltpu.with_memory_space_constraint(value, pltpu.VMEM)


def exchange_order(owners):
    if owners > 16:
        return list(range(owners))
    leader = owners // 2
    ends = owners // 4
    return sorted(
        range(owners), key=lambda i: (i != leader, ends <= i < owners - ends, i % 2, i)
    )


def exchange(value):
    order = exchange_order(lax.axis_size("lists"))
    return lax.all_to_all(
        value, "lists", split_axis=0, concat_axis=0, axis_index_groups=[order], tiled=True
    )


def staged_rows(local_lists, list_length):
    return min(local_lists * list_length, list_length + list_length // 2)


def norm_kernel(
    sizes,
    slot_ref,
    probes_ref,
    corpus_ref,
    staged_ref,
    inv_ref,
    column_ref,
    held,
    parts,
    slots,
    sems,
    slot_sem,
):
    cand_count, capacity, chunk = sizes
    total_rows, features = corpus_ref.shape
    local_lists, list_length = inv_ref.shape
    staged = staged_ref.shape[0]

    cuts = sorted(set(range(0, total_rows + 1, list_length)) | {staged})
    ranges = list(zip(cuts[:-1], cuts[1:]))

    def place(row, end):
        if row < staged:
            return staged_ref.at[row:end]
        return held.at[row - staged : end - staged]

    def copy(row, end):
        return pltpu.make_async_copy(
            corpus_ref.at[row:end], place(row, end), sems.at[cuts.index(row)]
        )

    slot_copy = pltpu.make_async_copy(slot_ref, slots, slot_sem)
    slot_copy.start()
    for row, end in ranges:
        copy(row, end).start()
    slot_copy.wait()
    column_ref[...] = result_columns(cand_count, capacity, local_lists, slots, probes_ref[...])
    ones = jnp.ones((8, 2 * LANES), jnp.bfloat16)
    for l in range(local_lists):
        for begin, to in ranges:
            if begin // list_length != l:
                continue
            copy(begin, to).wait()
            for row in range(begin, to, chunk):
                end = min(row + chunk, to)
                wide = place(row, end)[...].astype(jnp.float32)
                squares = functools.reduce(
                    jnp.add, [wide[:, j : j + LANES] ** 2 for j in range(0, features, LANES)]
                )
                high = squares.astype(jnp.bfloat16)
                low = (squares - high.astype(jnp.float32)).astype(jnp.bfloat16)
                parts[row:end, :LANES] = high
                parts[row:end, LANES:] = low
        whole = parts[l * list_length : (l + 1) * list_length, :]
        sums = contract(ones, whole, ((1,), (1,)))[:1]
        inv_ref[l : l + 1, :] = lax.rsqrt(sums / features + epsilon) * features ** (-0.5)


def row_sums(parts):
    high = parts.astype(jnp.bfloat16)
    low = (parts - high.astype(jnp.float32)).astype(jnp.bfloat16)
    terms = jnp.concatenate([high, low], axis=1)
    ones = jnp.ones((8, terms.shape[1]), jnp.bfloat16)
    return contract(ones, terms, ((1,), (1,)))[:1]


def result_columns(cand_count, capacity, local_lists, slot_ref, probes):
    probe_count, query_count = probes.shape
    total_lists = slot_ref.shape[0]
    order = exchange_order(total_lists // local_lists)
    position = jnp.zeros(probes.shape, jnp.float32)
    for t in range(total_lists):
        owner = slot_ref[t] // local_lists
        place = owner
        for j, i in enumerate(order):
            if i != j:
                place = jnp.where(owner == i, j, place)
        spot = place * local_lists + slot_ref[t] % local_lists
        position = jnp.where(probes == t, spot.astype(jnp.float32), position)
    lists = lax.broadcasted_iota(jnp.int32, (total_lists, query_count), 0)
    named = [lists == probes[p : p + 1] for p in range(probe_count)]
    counts = functools.reduce(jnp.add, [n.astype(jnp.float32) for n in named])
    square = (query_count, query_count)
    before = lax.broadcasted_iota(jnp.int32, square, 0) < lax.broadcasted_iota(
        jnp.int32, square, 1
    )
    earlier = contract(
        counts.astype(jnp.bfloat16), before.astype(jnp.float32).astype(jnp.bfloat16), ((1,), (0,))
    )
    rank = jnp.concatenate(
        [jnp.sum(jnp.where(n, earlier, 0.0), axis=0, keepdims=True) for n in named], axis=0
    )
    rows = probe_count * cand_count
    row = lax.broadcasted_iota(jnp.int32, (rows, probe_count), 0)
    lane = lax.broadcasted_iota(jnp.int32, (rows, probe_count), 1)
    spread = (row // cand_count == lane).astype(jnp.float32).astype(jnp.bfloat16)
    value = contract(spread, position.astype(jnp.bfloat16), ((1,), (0,))) * (
        cand_count * capacity
    ) + contract(spread, rank.astype(jnp.bfloat16), ((1,), (0,)))
    shift = (lax.broadcasted_iota(jnp.int32, value.shape, 0) % cand_count) * capacity
    return value.astype(jnp.int32) + shift


def row_norms(list_slot, probes, corpus, local_lists, cand_count, capacity):
    total_rows, features = corpus.shape
    list_length = total_rows // local_lists
    chunk = min(list_length, 256)
    staged = staged_rows(local_lists, list_length)
    query_count, probe_count = probes.shape
    whole = pl.BlockSpec(memory_space=pltpu.VMEM)
    return pl.pallas_call(
        functools.partial(norm_kernel, (cand_count, capacity, chunk)),
        out_shape=(
            pltpu.VMEM((staged, features), corpus.dtype),
            jax.ShapeDtypeStruct((local_lists, list_length), jnp.float32),
            jax.ShapeDtypeStruct((probe_count * cand_count, query_count), jnp.int32),
        ),
        in_specs=[
            pl.BlockSpec(memory_space=pltpu.HBM),
            whole,
            pl.BlockSpec(memory_space=pltpu.HBM),
        ],
        out_specs=(whole, whole, whole),
        scratch_shapes=[
            pltpu.VMEM((max(total_rows - staged, 16), features), corpus.dtype),
            pltpu.VMEM((total_rows, 2 * LANES), jnp.bfloat16),
            pltpu.SMEM(list_slot.shape, list_slot.dtype),
            pltpu.SemaphoreType.DMA((local_lists + 1,)),
            pltpu.SemaphoreType.DMA,
        ],
        compiler_params=pltpu.CompilerParams(vmem_limit_bytes=24 * MIB),
        cost_estimate=pl.CostEstimate(
            flops=2 * corpus.size, bytes_accessed=2 * corpus.size, transcendentals=0
        ),
    )(in_hbm(list_slot), in_hbm(probes.T), in_hbm(corpus))


def score_kernel(
    sizes, me_ref, slot_ref, corpus_ref, staged_ref, inv_ref, message_ref, out_ref, held, picked, sems
):
    owners, query_count, probe_count, cand_count, capacity, streams = sizes
    total_rows, features = corpus_ref.shape
    local_lists, list_length = inv_ref.shape
    staged = staged_ref.shape[0]
    total = owners * query_count
    room = owners * capacity
    step = capacity * cand_count

    def copy(begin, end):
        return pltpu.make_async_copy(
            corpus_ref.at[begin:end],
            held.at[begin - staged : end - staged],
            sems.at[streams.index((begin, end))],
        )

    for begin, end in streams:
        copy(begin, end).start()

    columns = [
        jnp.concatenate(
            [message_ref[s, j : j + query_count, :] for s in range(owners)], axis=0
        )
        for j in range(0, query_count * (features // LANES), query_count)
    ]
    queries = jnp.concatenate(columns, axis=1)
    squares = functools.reduce(jnp.add, [c.astype(jnp.float32) ** 2 for c in columns])
    height = message_ref.shape[1]
    tiles = [
        message_ref[s, height - probe_count :, :].astype(jnp.float32) for s in range(owners)
    ]
    probes, *cands = [
        jnp.concatenate([t[:, i : i + query_count] for t in tiles], axis=1)
        for i in range(0, query_count * (1 + cand_count), query_count)
    ]
    inv_query = lax.rsqrt(row_sums(squares) / features + epsilon)

    slots = slot_ref[...]
    names = lax.broadcasted_iota(jnp.int32, slots.shape, 1).astype(jnp.float32)
    first = me_ref[0] * local_lists
    hits, wanted = [], []
    for l in range(local_lists):
        name = jnp.sum(jnp.where(slots == first + l, names, 0.0), axis=1, keepdims=True)
        named = probes == name
        hits.append(jnp.sum(named.astype(jnp.float32), axis=0, keepdims=True))
        wanted.append(
            [jnp.sum(jnp.where(named, c, 0.0), axis=0, keepdims=True) for c in cands]
        )
    hit = jnp.concatenate(hits, axis=0)

    span = min(total, LANES)
    earlier = lax.broadcasted_iota(jnp.int32, (span, span), 0)
    later = lax.broadcasted_iota(jnp.int32, (span, span), 1)
    before = (earlier < later) & (earlier // query_count == later // query_count)
    before = before.astype(jnp.float32).astype(jnp.bfloat16)
    hit_low = hit.astype(jnp.bfloat16)
    rank = jnp.concatenate(
        [
            contract(hit_low[:, j : j + span], before, ((1,), (0,)))
            for j in range(0, total, span)
        ],
        axis=1,
    )
    source = (lax.broadcasted_iota(jnp.int32, (1, total), 1) // query_count) * capacity
    target = jnp.where(hit > 0.5, rank.astype(jnp.int32) + source, -1)

    places = lax.broadcasted_iota(jnp.int32, (room, total), 0)
    picks = [(places == target[l : l + 1]).astype(jnp.float32) for l in range(local_lists)]
    pick = jnp.concatenate(picks, axis=0).astype(jnp.bfloat16)
    picked[...] = contract(pick, queries, ((1,), (0,))).astype(jnp.bfloat16)
    scales = [jnp.sum(p * inv_query, axis=1, keepdims=True) for p in picks]
    blocks = [
        [jnp.sum(p * w, axis=1, keepdims=True) for w in wanted[l]] for l, p in enumerate(picks)
    ]

    for l in range(local_lists):
        rows = picked[l * room : (l + 1) * room, :]
        chosen = [jnp.zeros((room, BLOCK), jnp.float32) for _ in range(cand_count)]
        row = l * list_length
        while row < (l + 1) * list_length:
            if row < staged:
                end = min(row + 512, staged, (l + 1) * list_length)
                values = staged_ref[row:end, :]
            else:
                if row in dict(streams):
                    copy(row, dict(streams)[row]).wait()
                end = min(row + 512, (l + 1) * list_length)
                values = held[row - staged : end - staged, :]
            products = contract(rows, values, ((1,), (1,)))
            first = row - l * list_length
            scaled = products * scales[l] * inv_ref[l : l + 1, first : first + end - row]
            for j in range(0, end - row, BLOCK):
                piece = scaled[:, j : j + BLOCK]
                chosen = [
                    jnp.where(block == (first + j) // BLOCK, piece, old)
                    for block, old in zip(blocks[l], chosen)
                ]
            row = end
        out_ref[:, l * step : (l + 1) * step, :] = jnp.concatenate(
            [c.reshape(owners, capacity, BLOCK) for c in chosen], axis=1
        ).astype(jnp.bfloat16)


def stream_ranges(local_lists, list_length):
    row, end = staged_rows(local_lists, list_length), local_lists * list_length
    ranges = []
    while row < end:
        to = (row // list_length + 1) * list_length
        if to == end and to - row > list_length // 2:
            to = end - list_length // 2
        ranges.append((row, to))
        row = to
    return tuple(ranges)


def block_scores(sizes, me, list_slot, corpus, staged, inv_rows, messages):
    owners, query_count, probe_count, cand_count, capacity = sizes
    local_lists, list_length = inv_rows.shape
    total_rows, features = corpus.shape
    streams = stream_ranges(local_lists, list_length)
    whole = pl.BlockSpec(memory_space=pltpu.VMEM)
    return pl.pallas_call(
        functools.partial(score_kernel, sizes + (streams,)),
        out_shape=jax.ShapeDtypeStruct(
            (owners, local_lists * cand_count * capacity, BLOCK), jnp.bfloat16
        ),
        in_specs=[
            pl.BlockSpec(memory_space=pltpu.SMEM),
            whole,
            pl.BlockSpec(memory_space=pltpu.HBM),
            whole,
            whole,
            whole,
        ],
        out_specs=whole,
        scratch_shapes=[
            pltpu.VMEM((max(total_rows - staged.shape[0], 16), features), corpus.dtype),
            pltpu.VMEM((local_lists * owners * capacity, features), corpus.dtype),
            pltpu.SemaphoreType.DMA((max(len(streams), 1),)),
        ],
        compiler_params=pltpu.CompilerParams(vmem_limit_bytes=40 * MIB),
        cost_estimate=pl.CostEstimate(
            flops=2 * owners * capacity * corpus.size,
            bytes_accessed=2 * corpus.size,
            transcendentals=0,
        ),
    )(me, list_slot, in_hbm(corpus), in_vmem(staged), inv_rows, messages)


def place_kernel(column_ref, returned_ref, out_ref):
    returned = returned_ref[...].reshape(-1, returned_ref.shape[-1])
    each, query_count = column_ref.shape
    column = column_ref[...]
    lanes = lax.broadcasted_iota(jnp.int32, (each, returned.shape[0]), 1)
    pick = jnp.concatenate(
        [(lanes == column[:, i : i + 1]).astype(jnp.float32) for i in range(query_count)], axis=0
    ).astype(jnp.bfloat16)
    out_ref[...] = contract(pick, returned, ((1,), (0,))).astype(jnp.bfloat16)


def place(column, returned):
    whole = pl.BlockSpec(memory_space=pltpu.VMEM)
    return pl.pallas_call(
        place_kernel,
        out_shape=jax.ShapeDtypeStruct((column.size, BLOCK), jnp.bfloat16),
        in_specs=[whole] * 2,
        out_specs=whole,
        compiler_params=pltpu.CompilerParams(vmem_limit_bytes=24 * MIB),
    )(column, returned)


def message_kernel(
    queries_ref, probes_ref, cand_ref, out_ref, queries_vmem, probes_vmem, cand_vmem, sems
):
    owners, height, lanes = out_ref.shape
    query_count, features = queries_ref.shape
    probe_count, cand_count, _ = cand_ref.shape
    pairs = (
        (probes_ref, probes_vmem),
        (cand_ref, cand_vmem),
        (queries_ref, queries_vmem),
    )
    copies = [
        pltpu.make_async_copy(source, target, sems.at[i])
        for i, (source, target) in enumerate(pairs)
    ]
    for c in copies:
        c.start()
    copies[0].wait()
    copies[1].wait()
    pieces = [probes_vmem[...]] + [cand_vmem[:, c, :] for c in range(cand_count)]
    spare = lanes - len(pieces) * query_count
    pieces.append(jnp.zeros((probe_count, spare), jnp.int32))
    indices = jnp.concatenate(pieces, axis=1).astype(jnp.float32).astype(jnp.bfloat16)
    for k in range(owners):
        out_ref[k, height - probe_count :, :] = indices
    copies[2].wait()
    for j in range(features // lanes):
        column = queries_vmem[:, j * lanes : (j + 1) * lanes]
        for k in range(owners):
            out_ref[k, j * query_count : (j + 1) * query_count, :] = column


def make_message(queries, probes, cand, owners):
    query_count, features = queries.shape
    probe_count = probes.shape[1]
    height = query_count * (features // LANES) + probe_count
    whole = pl.BlockSpec(memory_space=pltpu.VMEM)
    return pl.pallas_call(
        message_kernel,
        out_shape=jax.ShapeDtypeStruct((owners, height, LANES), queries.dtype),
        in_specs=[pl.BlockSpec(memory_space=pltpu.HBM)] * 3,
        out_specs=whole,
        scratch_shapes=[
            pltpu.VMEM(queries.shape, queries.dtype),
            pltpu.VMEM(probes.shape[::-1], probes.dtype),
            pltpu.VMEM(cand.transpose(1, 2, 0).shape, cand.dtype),
            pltpu.SemaphoreType.DMA((3,)),
        ],
        compiler_params=pltpu.CompilerParams(vmem_limit_bytes=24 * MIB),
    )(in_hbm(queries), in_hbm(probes.T), in_hbm(cand.transpose(1, 2, 0)))


def on_device(queries, corpus, list_slot, probes, cand):
    owners = lax.axis_size("lists")
    query_count, features = queries.shape
    probe_count = probes.shape[1]
    cand_count = cand.shape[2]
    local_lists = corpus.shape[0]
    corpus = corpus.reshape(-1, features)
    total_lists = list_slot.shape[0]
    pair_count = query_count * probe_count
    capacity = min(query_count, max(2, (2 * pair_count + total_lists - 1) // total_lists))
    sizes = (owners, query_count, probe_count, cand_count, capacity)
    me = lax.axis_index("lists").astype(jnp.int32)

    message = make_message(queries, probes, cand, owners)
    messages = exchange(message)
    staged, inv_rows, column = row_norms(
        list_slot, probes, corpus, local_lists, cand_count, capacity
    )
    scores = block_scores(sizes, me.reshape(1), list_slot[None, :], corpus, staged, inv_rows, messages)
    returned = exchange(scores)
    chosen = place(column, returned)
    return chosen.reshape(query_count, probe_count, cand_count, BLOCK)


def solution(mesh):
    placed = (
        P(("groups", "lists", "rep"), None),
        P(("groups", "lists"), None, None),
        P("groups"),
        P(("groups", "lists", "rep"), None),
        P(("groups", "lists", "rep"), None, None),
    )
    return jax.shard_map(
        on_device,
        mesh=mesh,
        in_specs=placed,
        out_specs=P(("groups", "lists", "rep"), None, None, None),
        check_vma=False,
    )
```

```python
import functools

import jax
import jax.numpy as jnp
from jax import lax
from jax.experimental import pallas as pl
from jax.experimental.pallas import tpu as pltpu
from jax.sharding import PartitionSpec as P

BLOCK = 128
LANES = 128
MIB = 2**20

epsilon = 1e-06


def contract(a, b, dims, precision=None):
    return lax.dot_general(
        a, b, (dims, ((), ())), precision=precision, preferred_element_type=jnp.float32
    )


def in_hbm(value):
    return pltpu.with_memory_space_constraint(value, pltpu.HBM)


def in_vmem(value):
    return pltpu.with_memory_space_constraint(value, pltpu.VMEM)


def exchange_order(owners):
    if owners > 16:
        return list(range(owners))
    leader = owners // 2
    ends = owners // 4
    return sorted(
        range(owners), key=lambda i: (i != leader, ends <= i < owners - ends, i % 2, i)
    )


def exchange(value):
    order = exchange_order(lax.axis_size("lists"))
    return lax.all_to_all(
        value, "lists", split_axis=0, concat_axis=0, axis_index_groups=[order], tiled=True
    )


def staged_rows(local_lists, list_length):
    return min(local_lists * list_length, list_length + list_length // 2)


def norm_kernel(
    sizes,
    slot_ref,
    probes_ref,
    corpus_ref,
    staged_ref,
    inv_ref,
    column_ref,
    held,
    parts,
    slots,
    sems,
    slot_sem,
):
    cand_count, capacity, chunk = sizes
    total_rows, features = corpus_ref.shape
    local_lists, list_length = inv_ref.shape
    staged = staged_ref.shape[0]

    cuts = sorted(set(range(0, total_rows + 1, list_length)) | {staged})
    ranges = list(zip(cuts[:-1], cuts[1:]))

    def place(row, end):
        if row < staged:
            return staged_ref.at[row:end]
        return held.at[row - staged : end - staged]

    def copy(row, end):
        return pltpu.make_async_copy(
            corpus_ref.at[row:end], place(row, end), sems.at[cuts.index(row)]
        )

    slot_copy = pltpu.make_async_copy(slot_ref, slots, slot_sem)
    slot_copy.start()
    for row, end in ranges:
        copy(row, end).start()
    slot_copy.wait()
    column_ref[...] = result_columns(cand_count, capacity, local_lists, slots, probes_ref[...])
    ones = jnp.ones((8, 2 * LANES), jnp.bfloat16)
    for l in range(local_lists):
        for begin, to in ranges:
            if begin // list_length != l:
                continue
            copy(begin, to).wait()
            for row in range(begin, to, chunk):
                end = min(row + chunk, to)
                wide = place(row, end)[...].astype(jnp.float32)
                squares = functools.reduce(
                    jnp.add, [wide[:, j : j + LANES] ** 2 for j in range(0, features, LANES)]
                )
                high = squares.astype(jnp.bfloat16)
                low = (squares - high.astype(jnp.float32)).astype(jnp.bfloat16)
                parts[row:end, :LANES] = high
                parts[row:end, LANES:] = low
        whole = parts[l * list_length : (l + 1) * list_length, :]
        sums = contract(ones, whole, ((1,), (1,)))[:1]
        inv_ref[l : l + 1, :] = lax.rsqrt(sums / features + epsilon) * features ** (-0.5)


def row_sums(parts):
    high = parts.astype(jnp.bfloat16)
    low = (parts - high.astype(jnp.float32)).astype(jnp.bfloat16)
    terms = jnp.concatenate([high, low], axis=1)
    ones = jnp.ones((8, terms.shape[1]), jnp.bfloat16)
    return contract(ones, terms, ((1,), (1,)))[:1]


def result_columns(cand_count, capacity, local_lists, slot_ref, probes):
    probe_count, query_count = probes.shape
    total_lists = slot_ref.shape[0]
    order = exchange_order(total_lists // local_lists)
    position = jnp.zeros(probes.shape, jnp.float32)
    for t in range(total_lists):
        owner = slot_ref[t] // local_lists
        place = owner
        for j, i in enumerate(order):
            if i != j:
                place = jnp.where(owner == i, j, place)
        spot = place * local_lists + slot_ref[t] % local_lists
        position = jnp.where(probes == t, spot.astype(jnp.float32), position)
    lists = lax.broadcasted_iota(jnp.int32, (total_lists, query_count), 0)
    named = [lists == probes[p : p + 1] for p in range(probe_count)]
    counts = functools.reduce(jnp.add, [n.astype(jnp.float32) for n in named])
    square = (query_count, query_count)
    before = lax.broadcasted_iota(jnp.int32, square, 0) < lax.broadcasted_iota(
        jnp.int32, square, 1
    )
    earlier = contract(
        counts.astype(jnp.bfloat16), before.astype(jnp.float32).astype(jnp.bfloat16), ((1,), (0,))
    )
    rank = jnp.concatenate(
        [jnp.sum(jnp.where(n, earlier, 0.0), axis=0, keepdims=True) for n in named], axis=0
    )
    rows = probe_count * cand_count
    row = lax.broadcasted_iota(jnp.int32, (rows, probe_count), 0)
    lane = lax.broadcasted_iota(jnp.int32, (rows, probe_count), 1)
    spread = (row // cand_count == lane).astype(jnp.float32).astype(jnp.bfloat16)
    value = contract(spread, position.astype(jnp.bfloat16), ((1,), (0,))) * (
        cand_count * capacity
    ) + contract(spread, rank.astype(jnp.bfloat16), ((1,), (0,)))
    shift = (lax.broadcasted_iota(jnp.int32, value.shape, 0) % cand_count) * capacity
    return value.astype(jnp.int32) + shift


def row_norms(list_slot, probes, corpus, local_lists, cand_count, capacity):
    total_rows, features = corpus.shape
    list_length = total_rows // local_lists
    chunk = min(list_length, 256)
    staged = staged_rows(local_lists, list_length)
    query_count, probe_count = probes.shape
    whole = pl.BlockSpec(memory_space=pltpu.VMEM)
    return pl.pallas_call(
        functools.partial(norm_kernel, (cand_count, capacity, chunk)),
        out_shape=(
            pltpu.VMEM((staged, features), corpus.dtype),
            jax.ShapeDtypeStruct((local_lists, list_length), jnp.float32),
            jax.ShapeDtypeStruct((probe_count * cand_count, query_count), jnp.int32),
        ),
        in_specs=[
            pl.BlockSpec(memory_space=pltpu.HBM),
            whole,
            pl.BlockSpec(memory_space=pltpu.HBM),
        ],
        out_specs=(whole, whole, whole),
        scratch_shapes=[
            pltpu.VMEM((max(total_rows - staged, 16), features), corpus.dtype),
            pltpu.VMEM((total_rows, 2 * LANES), jnp.bfloat16),
            pltpu.SMEM(list_slot.shape, list_slot.dtype),
            pltpu.SemaphoreType.DMA((local_lists + 1,)),
            pltpu.SemaphoreType.DMA,
        ],
        compiler_params=pltpu.CompilerParams(vmem_limit_bytes=24 * MIB),
        cost_estimate=pl.CostEstimate(
            flops=2 * corpus.size, bytes_accessed=2 * corpus.size, transcendentals=0
        ),
    )(in_hbm(list_slot), in_hbm(probes.T), in_hbm(corpus))


def score_kernel(
    sizes,
    me_ref,
    slot_ref,
    corpus_ref,
    staged_ref,
    inv_ref,
    message_ref,
    out_ref,
    held,
    picked,
    sems,
    wide_ref=None,
):
    owners, query_count, probe_count, cand_count, capacity, streams = sizes
    total_rows, features = corpus_ref.shape
    local_lists, list_length = inv_ref.shape
    staged = staged_ref.shape[0]
    total = owners * query_count
    room = owners * capacity
    step = capacity * cand_count

    def copy(begin, end):
        return pltpu.make_async_copy(
            corpus_ref.at[begin:end],
            held.at[begin - staged : end - staged],
            sems.at[streams.index((begin, end))],
        )

    for begin, end in streams:
        copy(begin, end).start()

    columns = [
        jnp.concatenate(
            [message_ref[s, j : j + query_count, :] for s in range(owners)], axis=0
        )
        for j in range(0, query_count * (features // LANES), query_count)
    ]
    queries = jnp.concatenate(columns, axis=1)
    squares = functools.reduce(jnp.add, [c.astype(jnp.float32) ** 2 for c in columns])
    height = message_ref.shape[1]
    tiles = [
        message_ref[s, height - probe_count :, :].astype(jnp.float32) for s in range(owners)
    ]
    probes, *cands = [
        jnp.concatenate([t[:, i : i + query_count] for t in tiles], axis=1)
        for i in range(0, query_count * (1 + cand_count), query_count)
    ]
    inv_query = lax.rsqrt(row_sums(squares) / features + epsilon)

    slots = slot_ref[...]
    names = lax.broadcasted_iota(jnp.int32, slots.shape, 1).astype(jnp.float32)
    first = me_ref[0] * local_lists
    hits, wanted = [], []
    for l in range(local_lists):
        name = jnp.sum(jnp.where(slots == first + l, names, 0.0), axis=1, keepdims=True)
        named = probes == name
        hits.append(jnp.sum(named.astype(jnp.float32), axis=0, keepdims=True))
        wanted.append(
            [jnp.sum(jnp.where(named, c, 0.0), axis=0, keepdims=True) for c in cands]
        )
    hit = jnp.concatenate(hits, axis=0)

    span = min(total, LANES)
    earlier = lax.broadcasted_iota(jnp.int32, (span, span), 0)
    later = lax.broadcasted_iota(jnp.int32, (span, span), 1)
    before = (earlier < later) & (earlier // query_count == later // query_count)
    before = before.astype(jnp.float32).astype(jnp.bfloat16)
    hit_low = hit.astype(jnp.bfloat16)
    rank = jnp.concatenate(
        [
            contract(hit_low[:, j : j + span], before, ((1,), (0,)))
            for j in range(0, total, span)
        ],
        axis=1,
    )
    source = (lax.broadcasted_iota(jnp.int32, (1, total), 1) // query_count) * capacity
    target = jnp.where(hit > 0.5, rank.astype(jnp.int32) + source, -1)

    places = lax.broadcasted_iota(jnp.int32, (room, total), 0)
    picks = [(places == target[l : l + 1]).astype(jnp.float32) for l in range(local_lists)]
    pick = jnp.concatenate(picks, axis=0).astype(jnp.bfloat16)
    picked[...] = contract(pick, queries, ((1,), (0,))).astype(jnp.bfloat16)
    scales = [jnp.sum(p * inv_query, axis=1, keepdims=True) for p in picks]
    blocks = [
        [jnp.sum(p * w, axis=1, keepdims=True) for w in wanted[l]] for l, p in enumerate(picks)
    ]

    def store(l, parts):
        out_ref[:, l * step : (l + 1) * step, :] = jnp.concatenate(
            [p.reshape(owners, capacity, BLOCK) for p in parts], axis=1
        ).astype(jnp.bfloat16)

    for l in range(local_lists):
        if l == 0 and wide_ref is not None:
            inv_column = lax.rsqrt(jnp.sum(squares, axis=1, keepdims=True) / features + epsilon)
            for j in range(0, list_length, 2 * BLOCK):
                products = contract(queries, staged_ref[j : j + 2 * BLOCK, :], ((1,), (1,)))
                scaled = products * inv_column * inv_ref[:1, j : j + 2 * BLOCK]
                for i in range(2):
                    first = (j // BLOCK + i) * total
                    wide_ref[first : first + total, :] = scaled[
                        :, i * BLOCK : (i + 1) * BLOCK
                    ].astype(jnp.bfloat16)
            takes = [
                jnp.concatenate(
                    [
                        (places == jnp.where(w == j // BLOCK, target[:1], -1)).astype(jnp.float32)
                        for j in range(0, list_length, BLOCK)
                    ],
                    axis=1,
                )
                for w in wanted[0]
            ]
            take = jnp.concatenate(takes, axis=0).astype(jnp.bfloat16)
            taken = contract(take, wide_ref[...], ((1,), (0,)))
            store(0, [taken[c * room : (c + 1) * room, :] for c in range(cand_count)])
            continue
        rows = picked[l * room : (l + 1) * room, :]
        chosen = [jnp.zeros((room, BLOCK), jnp.float32) for _ in range(cand_count)]
        row = l * list_length
        while row < (l + 1) * list_length:
            if row < staged:
                end = min(row + 512, staged, (l + 1) * list_length)
                values = staged_ref[row:end, :]
            else:
                if row in dict(streams):
                    copy(row, dict(streams)[row]).wait()
                end = min(row + 512, (l + 1) * list_length)
                values = held[row - staged : end - staged, :]
            products = contract(rows, values, ((1,), (1,)))
            first = row - l * list_length
            scaled = products * scales[l] * inv_ref[l : l + 1, first : first + end - row]
            for j in range(0, end - row, BLOCK):
                piece = scaled[:, j : j + BLOCK]
                chosen = [
                    jnp.where(block == (first + j) // BLOCK, piece, old)
                    for block, old in zip(blocks[l], chosen)
                ]
            row = end
        store(l, chosen)


def stream_ranges(local_lists, list_length):
    row, end = staged_rows(local_lists, list_length), local_lists * list_length
    ranges = []
    while row < end:
        to = (row // list_length + 1) * list_length
        if to == end and to - row > list_length // 2:
            to = end - list_length // 2
        ranges.append((row, to))
        row = to
    return tuple(ranges)


def block_scores(sizes, me, list_slot, corpus, staged, inv_rows, messages):
    owners, query_count, probe_count, cand_count, capacity = sizes
    local_lists, list_length = inv_rows.shape
    total_rows, features = corpus.shape
    streams = stream_ranges(local_lists, list_length)
    wide = []
    if owners * query_count <= LANES:
        wide.append(
            pltpu.VMEM((list_length // BLOCK * owners * query_count, BLOCK), corpus.dtype)
        )
    whole = pl.BlockSpec(memory_space=pltpu.VMEM)
    return pl.pallas_call(
        functools.partial(score_kernel, sizes + (streams,)),
        out_shape=jax.ShapeDtypeStruct(
            (owners, local_lists * cand_count * capacity, BLOCK), jnp.bfloat16
        ),
        in_specs=[
            pl.BlockSpec(memory_space=pltpu.SMEM),
            whole,
            pl.BlockSpec(memory_space=pltpu.HBM),
            whole,
            whole,
            whole,
        ],
        out_specs=whole,
        scratch_shapes=[
            pltpu.VMEM((max(total_rows - staged.shape[0], 16), features), corpus.dtype),
            pltpu.VMEM((local_lists * owners * capacity, features), corpus.dtype),
            pltpu.SemaphoreType.DMA((max(len(streams), 1),)),
        ]
        + wide,
        compiler_params=pltpu.CompilerParams(vmem_limit_bytes=40 * MIB),
        cost_estimate=pl.CostEstimate(
            flops=2 * owners * capacity * corpus.size,
            bytes_accessed=2 * corpus.size,
            transcendentals=0,
        ),
    )(me, list_slot, in_hbm(corpus), in_vmem(staged), inv_rows, messages)


def place_kernel(column_ref, returned_ref, out_ref):
    returned = returned_ref[...].reshape(-1, returned_ref.shape[-1])
    each, query_count = column_ref.shape
    column = column_ref[...]
    lanes = lax.broadcasted_iota(jnp.int32, (each, returned.shape[0]), 1)
    pick = jnp.concatenate(
        [(lanes == column[:, i : i + 1]).astype(jnp.float32) for i in range(query_count)], axis=0
    ).astype(jnp.bfloat16)
    out_ref[...] = contract(pick, returned, ((1,), (0,))).astype(jnp.bfloat16)


def place(column, returned):
    whole = pl.BlockSpec(memory_space=pltpu.VMEM)
    return pl.pallas_call(
        place_kernel,
        out_shape=jax.ShapeDtypeStruct((column.size, BLOCK), jnp.bfloat16),
        in_specs=[whole] * 2,
        out_specs=whole,
        compiler_params=pltpu.CompilerParams(vmem_limit_bytes=24 * MIB),
    )(column, returned)


def message_kernel(
    queries_ref, probes_ref, cand_ref, out_ref, queries_vmem, probes_vmem, cand_vmem, sems
):
    owners, height, lanes = out_ref.shape
    query_count, features = queries_ref.shape
    probe_count, cand_count, _ = cand_ref.shape
    pairs = (
        (probes_ref, probes_vmem),
        (cand_ref, cand_vmem),
        (queries_ref, queries_vmem),
    )
    copies = [
        pltpu.make_async_copy(source, target, sems.at[i])
        for i, (source, target) in enumerate(pairs)
    ]
    for c in copies:
        c.start()
    copies[0].wait()
    copies[1].wait()
    pieces = [probes_vmem[...]] + [cand_vmem[:, c, :] for c in range(cand_count)]
    spare = lanes - len(pieces) * query_count
    pieces.append(jnp.zeros((probe_count, spare), jnp.int32))
    indices = jnp.concatenate(pieces, axis=1).astype(jnp.float32).astype(jnp.bfloat16)
    for k in range(owners):
        out_ref[k, height - probe_count :, :] = indices
    copies[2].wait()
    for j in range(features // lanes):
        column = queries_vmem[:, j * lanes : (j + 1) * lanes]
        for k in range(owners):
            out_ref[k, j * query_count : (j + 1) * query_count, :] = column


def make_message(queries, probes, cand, owners):
    query_count, features = queries.shape
    probe_count = probes.shape[1]
    height = query_count * (features // LANES) + probe_count
    whole = pl.BlockSpec(memory_space=pltpu.VMEM)
    return pl.pallas_call(
        message_kernel,
        out_shape=jax.ShapeDtypeStruct((owners, height, LANES), queries.dtype),
        in_specs=[pl.BlockSpec(memory_space=pltpu.HBM)] * 3,
        out_specs=whole,
        scratch_shapes=[
            pltpu.VMEM(queries.shape, queries.dtype),
            pltpu.VMEM(probes.shape[::-1], probes.dtype),
            pltpu.VMEM(cand.transpose(1, 2, 0).shape, cand.dtype),
            pltpu.SemaphoreType.DMA((3,)),
        ],
        compiler_params=pltpu.CompilerParams(vmem_limit_bytes=24 * MIB),
    )(in_hbm(queries), in_hbm(probes.T), in_hbm(cand.transpose(1, 2, 0)))


def on_device(queries, corpus, list_slot, probes, cand):
    owners = lax.axis_size("lists")
    query_count, features = queries.shape
    probe_count = probes.shape[1]
    cand_count = cand.shape[2]
    local_lists = corpus.shape[0]
    corpus = corpus.reshape(-1, features)
    total_lists = list_slot.shape[0]
    pair_count = query_count * probe_count
    capacity = min(query_count, max(2, (2 * pair_count + total_lists - 1) // total_lists))
    sizes = (owners, query_count, probe_count, cand_count, capacity)
    me = lax.axis_index("lists").astype(jnp.int32)

    message = make_message(queries, probes, cand, owners)
    messages = exchange(message)
    staged, inv_rows, column = row_norms(
        list_slot, probes, corpus, local_lists, cand_count, capacity
    )
    scores = block_scores(sizes, me.reshape(1), list_slot[None, :], corpus, staged, inv_rows, messages)
    returned = exchange(scores)
    chosen = place(column, returned)
    return chosen.reshape(query_count, probe_count, cand_count, BLOCK)


def solution(mesh):
    placed = (
        P(("groups", "lists", "rep"), None),
        P(("groups", "lists"), None, None),
        P("groups"),
        P(("groups", "lists", "rep"), None),
        P(("groups", "lists", "rep"), None, None),
    )
    return jax.shard_map(
        on_device,
        mesh=mesh,
        in_specs=placed,
        out_specs=P(("groups", "lists", "rep"), None, None, None),
        check_vma=False,
    )
```

```python
import functools

import jax
import jax.numpy as jnp
from jax import lax
from jax.experimental import pallas as pl
from jax.experimental.pallas import tpu as pltpu
from jax.sharding import PartitionSpec as P

BLOCK = 128
LANES = 128
MIB = 2**20

epsilon = 1e-06


def contract(a, b, dims, precision=None):
    return lax.dot_general(
        a, b, (dims, ((), ())), precision=precision, preferred_element_type=jnp.float32
    )


def in_hbm(value):
    return pltpu.with_memory_space_constraint(value, pltpu.HBM)


def in_vmem(value):
    return pltpu.with_memory_space_constraint(value, pltpu.VMEM)


def exchange_order(owners):
    if owners > 16:
        return list(range(owners))
    leader = owners // 2
    ends = owners // 4
    return sorted(
        range(owners), key=lambda i: (i != leader, ends <= i < owners - ends, i % 2, i)
    )


def exchange(value):
    order = exchange_order(lax.axis_size("lists"))
    return lax.all_to_all(
        value, "lists", split_axis=0, concat_axis=0, axis_index_groups=[order], tiled=True
    )


def staged_rows(local_lists, list_length):
    return min(local_lists * list_length, list_length + list_length // 2)


def fold_squares(value, target):
    wide = value.astype(jnp.float32)
    squares = functools.reduce(
        jnp.add, [wide[:, j : j + LANES] ** 2 for j in range(0, wide.shape[1], LANES)]
    )
    high = squares.astype(jnp.bfloat16)
    target[:, :LANES] = high
    target[:, LANES:] = (squares - high.astype(jnp.float32)).astype(jnp.bfloat16)


def inverse_rows(parts, features):
    ones = jnp.ones((8, 2 * LANES), jnp.bfloat16)
    sums = contract(ones, parts, ((1,), (1,)))[:1]
    return lax.rsqrt(sums / features + epsilon) * features ** (-0.5)


def norm_kernel(
    sizes,
    early_ref,
    slot_ref,
    probes_ref,
    first_ref,
    corpus_ref,
    staged_ref,
    inv_ref,
    column_ref,
    held,
    parts,
    slots,
    sems,
    slot_sem,
):
    cand_count, capacity, chunk = sizes
    total_rows, features = corpus_ref.shape
    local_lists, list_length = inv_ref.shape
    staged = staged_ref.shape[0]

    cuts = sorted(set(range(0, total_rows + 1, list_length)) | {staged})
    ranges = list(zip(cuts[:-1], cuts[1:]))

    def place(row, end):
        if row < staged:
            return staged_ref.at[row:end]
        return held.at[row - staged : end - staged]

    def copy(row, end):
        return pltpu.make_async_copy(
            corpus_ref.at[row:end], place(row, end), sems.at[cuts.index(row)]
        )

    slot_copy = pltpu.make_async_copy(slot_ref, slots, slot_sem)
    slot_copy.start()
    for row, end in ranges:
        copy(row, end).start()
    slot_copy.wait()
    column_ref[...] = result_columns(cand_count, capacity, local_lists, slots, probes_ref[...])

    def norms(l):
        for begin, to in ranges:
            if begin // list_length != l:
                continue
            for row in range(begin, to, chunk):
                end = min(row + chunk, to)
                fold_squares(place(row, end)[...], parts.at[row:end])
        whole = parts[l * list_length : (l + 1) * list_length, :]
        inv_ref[l : l + 1, :] = inverse_rows(whole, features)

    for l in range(local_lists):
        for begin, to in ranges:
            if begin // list_length == l:
                copy(begin, to).wait()
        if l == 0:

            @pl.when(early_ref[0] == 1)
            def _():
                inv_ref[:1, :] = first_ref[...]

            @pl.when(early_ref[0] == 0)
            def _():
                norms(0)

        else:
            norms(l)


def row_sums(parts):
    high = parts.astype(jnp.bfloat16)
    low = (parts - high.astype(jnp.float32)).astype(jnp.bfloat16)
    terms = jnp.concatenate([high, low], axis=1)
    ones = jnp.ones((8, terms.shape[1]), jnp.bfloat16)
    return contract(ones, terms, ((1,), (1,)))[:1]


def result_columns(cand_count, capacity, local_lists, slot_ref, probes):
    probe_count, query_count = probes.shape
    total_lists = slot_ref.shape[0]
    order = exchange_order(total_lists // local_lists)
    position = jnp.zeros(probes.shape, jnp.float32)
    for t in range(total_lists):
        owner = slot_ref[t] // local_lists
        place = owner
        for j, i in enumerate(order):
            if i != j:
                place = jnp.where(owner == i, j, place)
        spot = place * local_lists + slot_ref[t] % local_lists
        position = jnp.where(probes == t, spot.astype(jnp.float32), position)
    lists = lax.broadcasted_iota(jnp.int32, (total_lists, query_count), 0)
    named = [lists == probes[p : p + 1] for p in range(probe_count)]
    counts = functools.reduce(jnp.add, [n.astype(jnp.float32) for n in named])
    square = (query_count, query_count)
    before = lax.broadcasted_iota(jnp.int32, square, 0) < lax.broadcasted_iota(
        jnp.int32, square, 1
    )
    earlier = contract(
        counts.astype(jnp.bfloat16), before.astype(jnp.float32).astype(jnp.bfloat16), ((1,), (0,))
    )
    rank = jnp.concatenate(
        [jnp.sum(jnp.where(n, earlier, 0.0), axis=0, keepdims=True) for n in named], axis=0
    )
    rows = probe_count * cand_count
    row = lax.broadcasted_iota(jnp.int32, (rows, probe_count), 0)
    lane = lax.broadcasted_iota(jnp.int32, (rows, probe_count), 1)
    spread = (row // cand_count == lane).astype(jnp.float32).astype(jnp.bfloat16)
    value = contract(spread, position.astype(jnp.bfloat16), ((1,), (0,))) * (
        cand_count * capacity
    ) + contract(spread, rank.astype(jnp.bfloat16), ((1,), (0,)))
    shift = (lax.broadcasted_iota(jnp.int32, value.shape, 0) % cand_count) * capacity
    return value.astype(jnp.int32) + shift


def row_norms(early, list_slot, probes, first, corpus, local_lists, cand_count, capacity):
    total_rows, features = corpus.shape
    list_length = total_rows // local_lists
    chunk = min(list_length, 256)
    staged = staged_rows(local_lists, list_length)
    query_count, probe_count = probes.shape
    whole = pl.BlockSpec(memory_space=pltpu.VMEM)
    return pl.pallas_call(
        functools.partial(norm_kernel, (cand_count, capacity, chunk)),
        out_shape=(
            pltpu.VMEM((staged, features), corpus.dtype),
            jax.ShapeDtypeStruct((local_lists, list_length), jnp.float32),
            jax.ShapeDtypeStruct((probe_count * cand_count, query_count), jnp.int32),
        ),
        in_specs=[
            pl.BlockSpec(memory_space=pltpu.SMEM),
            pl.BlockSpec(memory_space=pltpu.HBM),
            whole,
            whole,
            pl.BlockSpec(memory_space=pltpu.HBM),
        ],
        out_specs=(whole, whole, whole),
        scratch_shapes=[
            pltpu.VMEM((max(total_rows - staged, 16), features), corpus.dtype),
            pltpu.VMEM((total_rows, 2 * LANES), jnp.bfloat16),
            pltpu.SMEM(list_slot.shape, list_slot.dtype),
            pltpu.SemaphoreType.DMA((local_lists + 1,)),
            pltpu.SemaphoreType.DMA,
        ],
        compiler_params=pltpu.CompilerParams(vmem_limit_bytes=24 * MIB),
        cost_estimate=pl.CostEstimate(
            flops=2 * corpus.size, bytes_accessed=2 * corpus.size, transcendentals=0
        ),
    )(early, in_hbm(list_slot), in_hbm(probes.T), in_hbm(first), in_hbm(corpus))


def score_kernel(
    sizes, me_ref, slot_ref, corpus_ref, staged_ref, inv_ref, message_ref, out_ref, held, picked, sems
):
    owners, query_count, probe_count, cand_count, capacity, streams = sizes
    total_rows, features = corpus_ref.shape
    local_lists, list_length = inv_ref.shape
    staged = staged_ref.shape[0]
    total = owners * query_count
    room = owners * capacity
    step = capacity * cand_count

    def copy(begin, end):
        return pltpu.make_async_copy(
            corpus_ref.at[begin:end],
            held.at[begin - staged : end - staged],
            sems.at[streams.index((begin, end))],
        )

    for begin, end in streams:
        copy(begin, end).start()

    columns = [
        jnp.concatenate(
            [message_ref[s, j : j + query_count, :] for s in range(owners)], axis=0
        )
        for j in range(0, query_count * (features // LANES), query_count)
    ]
    queries = jnp.concatenate(columns, axis=1)
    squares = functools.reduce(jnp.add, [c.astype(jnp.float32) ** 2 for c in columns])
    height = message_ref.shape[1]
    tiles = [
        message_ref[s, height - probe_count :, :].astype(jnp.float32) for s in range(owners)
    ]
    probes, *cands = [
        jnp.concatenate([t[:, i : i + query_count] for t in tiles], axis=1)
        for i in range(0, query_count * (1 + cand_count), query_count)
    ]
    inv_query = lax.rsqrt(row_sums(squares) / features + epsilon)

    slots = slot_ref[...]
    names = lax.broadcasted_iota(jnp.int32, slots.shape, 1).astype(jnp.float32)
    first = me_ref[0] * local_lists
    hits, wanted = [], []
    for l in range(local_lists):
        name = jnp.sum(jnp.where(slots == first + l, names, 0.0), axis=1, keepdims=True)
        named = probes == name
        hits.append(jnp.sum(named.astype(jnp.float32), axis=0, keepdims=True))
        wanted.append(
            [jnp.sum(jnp.where(named, c, 0.0), axis=0, keepdims=True) for c in cands]
        )
    hit = jnp.concatenate(hits, axis=0)

    span = min(total, LANES)
    earlier = lax.broadcasted_iota(jnp.int32, (span, span), 0)
    later = lax.broadcasted_iota(jnp.int32, (span, span), 1)
    before = (earlier < later) & (earlier // query_count == later // query_count)
    before = before.astype(jnp.float32).astype(jnp.bfloat16)
    hit_low = hit.astype(jnp.bfloat16)
    rank = jnp.concatenate(
        [
            contract(hit_low[:, j : j + span], before, ((1,), (0,)))
            for j in range(0, total, span)
        ],
        axis=1,
    )
    source = (lax.broadcasted_iota(jnp.int32, (1, total), 1) // query_count) * capacity
    target = jnp.where(hit > 0.5, rank.astype(jnp.int32) + source, -1)

    places = lax.broadcasted_iota(jnp.int32, (room, total), 0)
    picks = [(places == target[l : l + 1]).astype(jnp.float32) for l in range(local_lists)]
    pick = jnp.concatenate(picks, axis=0).astype(jnp.bfloat16)
    picked[...] = contract(pick, queries, ((1,), (0,))).astype(jnp.bfloat16)
    scales = [jnp.sum(p * inv_query, axis=1, keepdims=True) for p in picks]
    blocks = [
        [jnp.sum(p * w, axis=1, keepdims=True) for w in wanted[l]] for l, p in enumerate(picks)
    ]

    for l in range(local_lists):
        rows = picked[l * room : (l + 1) * room, :]
        chosen = [jnp.zeros((room, BLOCK), jnp.float32) for _ in range(cand_count)]
        row = l * list_length
        while row < (l + 1) * list_length:
            if row < staged:
                end = min(row + 512, staged, (l + 1) * list_length)
                values = staged_ref[row:end, :]
            else:
                if row in dict(streams):
                    copy(row, dict(streams)[row]).wait()
                end = min(row + 512, (l + 1) * list_length)
                values = held[row - staged : end - staged, :]
            products = contract(rows, values, ((1,), (1,)))
            first = row - l * list_length
            scaled = products * scales[l] * inv_ref[l : l + 1, first : first + end - row]
            for j in range(0, end - row, BLOCK):
                piece = scaled[:, j : j + BLOCK]
                chosen = [
                    jnp.where(block == (first + j) // BLOCK, piece, old)
                    for block, old in zip(blocks[l], chosen)
                ]
            row = end
        out_ref[:, l * step : (l + 1) * step, :] = jnp.concatenate(
            [c.reshape(owners, capacity, BLOCK) for c in chosen], axis=1
        ).astype(jnp.bfloat16)


def stream_ranges(local_lists, list_length):
    row, end = staged_rows(local_lists, list_length), local_lists * list_length
    ranges = []
    while row < end:
        to = (row // list_length + 1) * list_length
        if to == end and to - row > list_length // 2:
            to = end - list_length // 2
        ranges.append((row, to))
        row = to
    return tuple(ranges)


def block_scores(sizes, me, list_slot, corpus, staged, inv_rows, messages):
    owners, query_count, probe_count, cand_count, capacity = sizes
    local_lists, list_length = inv_rows.shape
    total_rows, features = corpus.shape
    streams = stream_ranges(local_lists, list_length)
    whole = pl.BlockSpec(memory_space=pltpu.VMEM)
    return pl.pallas_call(
        functools.partial(score_kernel, sizes + (streams,)),
        out_shape=jax.ShapeDtypeStruct(
            (owners, local_lists * cand_count * capacity, BLOCK), jnp.bfloat16
        ),
        in_specs=[
            pl.BlockSpec(memory_space=pltpu.SMEM),
            whole,
            pl.BlockSpec(memory_space=pltpu.HBM),
            whole,
            whole,
            whole,
        ],
        out_specs=whole,
        scratch_shapes=[
            pltpu.VMEM((max(total_rows - staged.shape[0], 16), features), corpus.dtype),
            pltpu.VMEM((local_lists * owners * capacity, features), corpus.dtype),
            pltpu.SemaphoreType.DMA((max(len(streams), 1),)),
        ],
        compiler_params=pltpu.CompilerParams(vmem_limit_bytes=40 * MIB),
        cost_estimate=pl.CostEstimate(
            flops=2 * owners * capacity * corpus.size,
            bytes_accessed=2 * corpus.size,
            transcendentals=0,
        ),
    )(me, list_slot, in_hbm(corpus), in_vmem(staged), inv_rows, messages)


def place_kernel(column_ref, returned_ref, out_ref):
    returned = returned_ref[...].reshape(-1, returned_ref.shape[-1])
    each, query_count = column_ref.shape
    column = column_ref[...]
    lanes = lax.broadcasted_iota(jnp.int32, (each, returned.shape[0]), 1)
    pick = jnp.concatenate(
        [(lanes == column[:, i : i + 1]).astype(jnp.float32) for i in range(query_count)], axis=0
    ).astype(jnp.bfloat16)
    out_ref[...] = contract(pick, returned, ((1,), (0,))).astype(jnp.bfloat16)


def place(column, returned):
    whole = pl.BlockSpec(memory_space=pltpu.VMEM)
    return pl.pallas_call(
        place_kernel,
        out_shape=jax.ShapeDtypeStruct((column.size, BLOCK), jnp.bfloat16),
        in_specs=[whole] * 2,
        out_specs=whole,
        compiler_params=pltpu.CompilerParams(vmem_limit_bytes=24 * MIB),
    )(column, returned)


def message_kernel(
    early_ref,
    queries_ref,
    probes_ref,
    cand_ref,
    corpus_ref,
    out_ref,
    first_ref,
    queries_vmem,
    probes_vmem,
    cand_vmem,
    held,
    parts,
    sems,
):
    owners, height, lanes = out_ref.shape
    query_count, features = queries_ref.shape
    probe_count, cand_count, _ = cand_ref.shape
    pairs = (
        (probes_ref, probes_vmem),
        (cand_ref, cand_vmem),
        (queries_ref, queries_vmem),
    )
    copies = [
        pltpu.make_async_copy(source, target, sems.at[i])
        for i, (source, target) in enumerate(pairs)
    ]
    list_copy = pltpu.make_async_copy(corpus_ref.at[: held.shape[0]], held, sems.at[3])

    @pl.when(early_ref[0] == 1)
    def _():
        list_copy.start()

    for c in copies:
        c.start()
    copies[0].wait()
    copies[1].wait()
    pieces = [probes_vmem[...]] + [cand_vmem[:, c, :] for c in range(cand_count)]
    spare = lanes - len(pieces) * query_count
    pieces.append(jnp.zeros((probe_count, spare), jnp.int32))
    indices = jnp.concatenate(pieces, axis=1).astype(jnp.float32).astype(jnp.bfloat16)
    for k in range(owners):
        out_ref[k, height - probe_count :, :] = indices
    copies[2].wait()
    for j in range(features // lanes):
        column = queries_vmem[:, j * lanes : (j + 1) * lanes]
        for k in range(owners):
            out_ref[k, j * query_count : (j + 1) * query_count, :] = column

    @pl.when(early_ref[0] == 1)
    def _():
        list_copy.wait()
        rows = min(held.shape[0], 256)
        for row in range(0, held.shape[0], rows):
            fold_squares(held[row : row + rows, :], parts.at[row : row + rows])
        first_ref[...] = inverse_rows(parts[...], features)

    @pl.when(early_ref[0] == 0)
    def _():
        first_ref[...] = jnp.zeros_like(first_ref)


def make_message(early, queries, probes, cand, corpus, owners, list_length):
    query_count, features = queries.shape
    probe_count = probes.shape[1]
    height = query_count * (features // LANES) + probe_count
    whole = pl.BlockSpec(memory_space=pltpu.VMEM)
    return pl.pallas_call(
        message_kernel,
        out_shape=(
            jax.ShapeDtypeStruct((owners, height, LANES), queries.dtype),
            pltpu.HBM((1, list_length), jnp.float32),
        ),
        in_specs=[pl.BlockSpec(memory_space=pltpu.SMEM)]
        + [pl.BlockSpec(memory_space=pltpu.HBM)] * 4,
        out_specs=(whole, whole),
        scratch_shapes=[
            pltpu.VMEM(queries.shape, queries.dtype),
            pltpu.VMEM(probes.shape[::-1], probes.dtype),
            pltpu.VMEM(cand.transpose(1, 2, 0).shape, cand.dtype),
            pltpu.VMEM((list_length, features), corpus.dtype),
            pltpu.VMEM((list_length, 2 * LANES), jnp.bfloat16),
            pltpu.SemaphoreType.DMA((4,)),
        ],
        compiler_params=pltpu.CompilerParams(vmem_limit_bytes=24 * MIB),
    )(early, in_hbm(queries), in_hbm(probes.T), in_hbm(cand.transpose(1, 2, 0)), in_hbm(corpus))


def on_device(queries, corpus, list_slot, probes, cand):
    owners = lax.axis_size("lists")
    query_count, features = queries.shape
    probe_count = probes.shape[1]
    cand_count = cand.shape[2]
    local_lists = corpus.shape[0]
    corpus = corpus.reshape(-1, features)
    total_lists = list_slot.shape[0]
    pair_count = query_count * probe_count
    capacity = min(query_count, max(2, (2 * pair_count + total_lists - 1) // total_lists))
    sizes = (owners, query_count, probe_count, cand_count, capacity)
    me = lax.axis_index("lists").astype(jnp.int32)

    reps = lax.axis_size("rep")
    early = (lax.axis_index("rep") == reps - 1).astype(jnp.int32).reshape(1) * int(reps > 1)
    list_length = corpus.shape[0] // local_lists
    message, first = make_message(early, queries, probes, cand, corpus, owners, list_length)
    messages = exchange(message)
    staged, inv_rows, column = row_norms(
        early, list_slot, probes, first, corpus, local_lists, cand_count, capacity
    )
    scores = block_scores(sizes, me.reshape(1), list_slot[None, :], corpus, staged, inv_rows, messages)
    returned = exchange(scores)
    chosen = place(column, returned)
    return chosen.reshape(query_count, probe_count, cand_count, BLOCK)


def solution(mesh):
    placed = (
        P(("groups", "lists", "rep"), None),
        P(("groups", "lists"), None, None),
        P("groups"),
        P(("groups", "lists", "rep"), None),
        P(("groups", "lists", "rep"), None, None),
    )
    return jax.shard_map(
        on_device,
        mesh=mesh,
        in_specs=placed,
        out_specs=P(("groups", "lists", "rep"), None, None, None),
        check_vma=False,
    )
```

```python
import functools

import jax
import jax.numpy as jnp
from jax import lax
from jax.experimental import pallas as pl
from jax.experimental.pallas import tpu as pltpu
from jax.sharding import PartitionSpec as P

BLOCK = 128
LANES = 128
MIB = 2**20

epsilon = 1e-06


def contract(a, b, dims, precision=None):
    return lax.dot_general(
        a, b, (dims, ((), ())), precision=precision, preferred_element_type=jnp.float32
    )


def in_hbm(value):
    return pltpu.with_memory_space_constraint(value, pltpu.HBM)


def in_vmem(value):
    return pltpu.with_memory_space_constraint(value, pltpu.VMEM)


def exchange_order(owners):
    return [(i + owners // 2) % owners for i in range(owners)]


def exchange(value):
    order = exchange_order(lax.axis_size("lists"))
    return lax.all_to_all(
        value, "lists", split_axis=0, concat_axis=0, axis_index_groups=[order], tiled=True
    )


def staged_rows(local_lists, list_length):
    return min(local_lists * list_length, list_length + list_length // 2)


def norm_kernel(
    sizes,
    slot_ref,
    probes_ref,
    corpus_ref,
    staged_ref,
    inv_ref,
    column_ref,
    held,
    parts,
    slots,
    sems,
    slot_sem,
):
    cand_count, capacity, chunk = sizes
    total_rows, features = corpus_ref.shape
    local_lists, list_length = inv_ref.shape
    staged = staged_ref.shape[0]

    cuts = sorted(set(range(0, total_rows + 1, list_length)) | {staged})
    ranges = list(zip(cuts[:-1], cuts[1:]))

    def place(row, end):
        if row < staged:
            return staged_ref.at[row:end]
        return held.at[row - staged : end - staged]

    def copy(row, end):
        return pltpu.make_async_copy(
            corpus_ref.at[row:end], place(row, end), sems.at[cuts.index(row)]
        )

    slot_copy = pltpu.make_async_copy(slot_ref, slots, slot_sem)
    slot_copy.start()
    for row, end in ranges:
        copy(row, end).start()
    slot_copy.wait()
    column_ref[...] = result_columns(cand_count, capacity, local_lists, slots, probes_ref[...])
    ones = jnp.ones((8, 2 * LANES), jnp.bfloat16)
    for l in range(local_lists):
        for begin, to in ranges:
            if begin // list_length != l:
                continue
            copy(begin, to).wait()
            for row in range(begin, to, chunk):
                end = min(row + chunk, to)
                wide = place(row, end)[...].astype(jnp.float32)
                squares = functools.reduce(
                    jnp.add, [wide[:, j : j + LANES] ** 2 for j in range(0, features, LANES)]
                )
                high = squares.astype(jnp.bfloat16)
                low = (squares - high.astype(jnp.float32)).astype(jnp.bfloat16)
                parts[row:end, :LANES] = high
                parts[row:end, LANES:] = low
        whole = parts[l * list_length : (l + 1) * list_length, :]
        sums = contract(ones, whole, ((1,), (1,)))[:1]
        inv_ref[l : l + 1, :] = lax.rsqrt(sums / features + epsilon) * features ** (-0.5)


def row_sums(parts):
    high = parts.astype(jnp.bfloat16)
    low = (parts - high.astype(jnp.float32)).astype(jnp.bfloat16)
    terms = jnp.concatenate([high, low], axis=1)
    ones = jnp.ones((8, terms.shape[1]), jnp.bfloat16)
    return contract(ones, terms, ((1,), (1,)))[:1]


def result_columns(cand_count, capacity, local_lists, slot_ref, probes):
    probe_count, query_count = probes.shape
    total_lists = slot_ref.shape[0]
    owners = total_lists // local_lists
    position = jnp.zeros(probes.shape, jnp.float32)
    for t in range(total_lists):
        owner = slot_ref[t] // local_lists
        place = (owner + owners // 2) % owners
        spot = place * local_lists + slot_ref[t] % local_lists
        position = jnp.where(probes == t, spot.astype(jnp.float32), position)
    lists = lax.broadcasted_iota(jnp.int32, (total_lists, query_count), 0)
    named = [lists == probes[p : p + 1] for p in range(probe_count)]
    counts = functools.reduce(jnp.add, [n.astype(jnp.float32) for n in named])
    square = (query_count, query_count)
    before = lax.broadcasted_iota(jnp.int32, square, 0) < lax.broadcasted_iota(
        jnp.int32, square, 1
    )
    earlier = contract(
        counts.astype(jnp.bfloat16), before.astype(jnp.float32).astype(jnp.bfloat16), ((1,), (0,))
    )
    rank = jnp.concatenate(
        [jnp.sum(jnp.where(n, earlier, 0.0), axis=0, keepdims=True) for n in named], axis=0
    )
    rows = probe_count * cand_count
    row = lax.broadcasted_iota(jnp.int32, (rows, probe_count), 0)
    lane = lax.broadcasted_iota(jnp.int32, (rows, probe_count), 1)
    spread = (row // cand_count == lane).astype(jnp.float32).astype(jnp.bfloat16)
    value = contract(spread, position.astype(jnp.bfloat16), ((1,), (0,))) * (
        cand_count * capacity
    ) + contract(spread, rank.astype(jnp.bfloat16), ((1,), (0,)))
    shift = (lax.broadcasted_iota(jnp.int32, value.shape, 0) % cand_count) * capacity
    return value.astype(jnp.int32) + shift


def row_norms(list_slot, probes, corpus, local_lists, cand_count, capacity):
    total_rows, features = corpus.shape
    list_length = total_rows // local_lists
    chunk = min(list_length, 256)
    staged = staged_rows(local_lists, list_length)
    query_count, probe_count = probes.shape
    whole = pl.BlockSpec(memory_space=pltpu.VMEM)
    return pl.pallas_call(
        functools.partial(norm_kernel, (cand_count, capacity, chunk)),
        out_shape=(
            pltpu.VMEM((staged, features), corpus.dtype),
            jax.ShapeDtypeStruct((local_lists, list_length), jnp.float32),
            jax.ShapeDtypeStruct((probe_count * cand_count, query_count), jnp.int32),
        ),
        in_specs=[
            pl.BlockSpec(memory_space=pltpu.HBM),
            whole,
            pl.BlockSpec(memory_space=pltpu.HBM),
        ],
        out_specs=(whole, whole, whole),
        scratch_shapes=[
            pltpu.VMEM((max(total_rows - staged, 16), features), corpus.dtype),
            pltpu.VMEM((total_rows, 2 * LANES), jnp.bfloat16),
            pltpu.SMEM(list_slot.shape, list_slot.dtype),
            pltpu.SemaphoreType.DMA((local_lists + 1,)),
            pltpu.SemaphoreType.DMA,
        ],
        compiler_params=pltpu.CompilerParams(vmem_limit_bytes=24 * MIB),
        cost_estimate=pl.CostEstimate(
            flops=2 * corpus.size, bytes_accessed=2 * corpus.size, transcendentals=0
        ),
    )(in_hbm(list_slot), in_hbm(probes.T), in_hbm(corpus))


def score_kernel(
    sizes, me_ref, slot_ref, corpus_ref, staged_ref, inv_ref, message_ref, out_ref, held, picked, sems
):
    owners, query_count, probe_count, cand_count, capacity, streams = sizes
    total_rows, features = corpus_ref.shape
    local_lists, list_length = inv_ref.shape
    staged = staged_ref.shape[0]
    total = owners * query_count
    room = owners * capacity
    step = capacity * cand_count

    def copy(begin, end):
        return pltpu.make_async_copy(
            corpus_ref.at[begin:end],
            held.at[begin - staged : end - staged],
            sems.at[streams.index((begin, end))],
        )

    for begin, end in streams:
        copy(begin, end).start()

    columns = [
        jnp.concatenate(
            [message_ref[s, j : j + query_count, :] for s in range(owners)], axis=0
        )
        for j in range(0, query_count * (features // LANES), query_count)
    ]
    queries = jnp.concatenate(columns, axis=1)
    squares = functools.reduce(jnp.add, [c.astype(jnp.float32) ** 2 for c in columns])
    height = message_ref.shape[1]
    tiles = [
        message_ref[s, height - probe_count :, :].astype(jnp.float32) for s in range(owners)
    ]
    probes, *cands = [
        jnp.concatenate([t[:, i : i + query_count] for t in tiles], axis=1)
        for i in range(0, query_count * (1 + cand_count), query_count)
    ]
    inv_query = lax.rsqrt(row_sums(squares) / features + epsilon)

    slots = slot_ref[...]
    names = lax.broadcasted_iota(jnp.int32, slots.shape, 1).astype(jnp.float32)
    first = me_ref[0] * local_lists
    hits, wanted = [], []
    for l in range(local_lists):
        name = jnp.sum(jnp.where(slots == first + l, names, 0.0), axis=1, keepdims=True)
        named = probes == name
        hits.append(jnp.sum(named.astype(jnp.float32), axis=0, keepdims=True))
        wanted.append(
            [jnp.sum(jnp.where(named, c, 0.0), axis=0, keepdims=True) for c in cands]
        )
    hit = jnp.concatenate(hits, axis=0)

    span = min(total, LANES)
    earlier = lax.broadcasted_iota(jnp.int32, (span, span), 0)
    later = lax.broadcasted_iota(jnp.int32, (span, span), 1)
    before = (earlier < later) & (earlier // query_count == later // query_count)
    before = before.astype(jnp.float32).astype(jnp.bfloat16)
    hit_low = hit.astype(jnp.bfloat16)
    rank = jnp.concatenate(
        [
            contract(hit_low[:, j : j + span], before, ((1,), (0,)))
            for j in range(0, total, span)
        ],
        axis=1,
    )
    source = (lax.broadcasted_iota(jnp.int32, (1, total), 1) // query_count) * capacity
    target = jnp.where(hit > 0.5, rank.astype(jnp.int32) + source, -1)

    places = lax.broadcasted_iota(jnp.int32, (room, total), 0)
    picks = [(places == target[l : l + 1]).astype(jnp.float32) for l in range(local_lists)]
    pick = jnp.concatenate(picks, axis=0).astype(jnp.bfloat16)
    picked[...] = contract(pick, queries, ((1,), (0,))).astype(jnp.bfloat16)
    scales = [jnp.sum(p * inv_query, axis=1, keepdims=True) for p in picks]
    blocks = [
        [jnp.sum(p * w, axis=1, keepdims=True) for w in wanted[l]] for l, p in enumerate(picks)
    ]

    for l in range(local_lists):
        rows = picked[l * room : (l + 1) * room, :]
        chosen = [jnp.zeros((room, BLOCK), jnp.float32) for _ in range(cand_count)]
        row = l * list_length
        while row < (l + 1) * list_length:
            if row < staged:
                end = min(row + 512, staged, (l + 1) * list_length)
                values = staged_ref[row:end, :]
            else:
                if row in dict(streams):
                    copy(row, dict(streams)[row]).wait()
                end = min(row + 512, (l + 1) * list_length)
                values = held[row - staged : end - staged, :]
            products = contract(rows, values, ((1,), (1,)))
            first = row - l * list_length
            scaled = products * scales[l] * inv_ref[l : l + 1, first : first + end - row]
            for j in range(0, end - row, BLOCK):
                piece = scaled[:, j : j + BLOCK]
                chosen = [
                    jnp.where(block == (first + j) // BLOCK, piece, old)
                    for block, old in zip(blocks[l], chosen)
                ]
            row = end
        out_ref[:, l * step : (l + 1) * step, :] = jnp.concatenate(
            [c.reshape(owners, capacity, BLOCK) for c in chosen], axis=1
        ).astype(jnp.bfloat16)


def stream_ranges(local_lists, list_length):
    row, end = staged_rows(local_lists, list_length), local_lists * list_length
    ranges = []
    while row < end:
        to = min(row + 512, (row // list_length + 1) * list_length)
        ranges.append((row, to))
        row = to
    return tuple(ranges)


def block_scores(sizes, me, list_slot, corpus, staged, inv_rows, messages):
    owners, query_count, probe_count, cand_count, capacity = sizes
    local_lists, list_length = inv_rows.shape
    total_rows, features = corpus.shape
    streams = stream_ranges(local_lists, list_length)
    whole = pl.BlockSpec(memory_space=pltpu.VMEM)
    return pl.pallas_call(
        functools.partial(score_kernel, sizes + (streams,)),
        out_shape=jax.ShapeDtypeStruct(
            (owners, local_lists * cand_count * capacity, BLOCK), jnp.bfloat16
        ),
        in_specs=[
            pl.BlockSpec(memory_space=pltpu.SMEM),
            whole,
            pl.BlockSpec(memory_space=pltpu.HBM),
            whole,
            whole,
            whole,
        ],
        out_specs=whole,
        scratch_shapes=[
            pltpu.VMEM((max(total_rows - staged.shape[0], 16), features), corpus.dtype),
            pltpu.VMEM((local_lists * owners * capacity, features), corpus.dtype),
            pltpu.SemaphoreType.DMA((max(len(streams), 1),)),
        ],
        compiler_params=pltpu.CompilerParams(vmem_limit_bytes=40 * MIB),
        cost_estimate=pl.CostEstimate(
            flops=2 * owners * capacity * corpus.size,
            bytes_accessed=2 * corpus.size,
            transcendentals=0,
        ),
    )(me, list_slot, in_hbm(corpus), in_vmem(staged), inv_rows, messages)


def place_kernel(column_ref, returned_ref, out_ref):
    returned = returned_ref[...].reshape(-1, returned_ref.shape[-1])
    each, query_count = column_ref.shape
    column = column_ref[...]
    lanes = lax.broadcasted_iota(jnp.int32, (each, returned.shape[0]), 1)
    pick = jnp.concatenate(
        [(lanes == column[:, i : i + 1]).astype(jnp.float32) for i in range(query_count)], axis=0
    ).astype(jnp.bfloat16)
    out_ref[...] = contract(pick, returned, ((1,), (0,))).astype(jnp.bfloat16)


def place(column, returned):
    whole = pl.BlockSpec(memory_space=pltpu.VMEM)
    return pl.pallas_call(
        place_kernel,
        out_shape=jax.ShapeDtypeStruct((column.size, BLOCK), jnp.bfloat16),
        in_specs=[whole] * 2,
        out_specs=whole,
        compiler_params=pltpu.CompilerParams(vmem_limit_bytes=24 * MIB),
    )(column, returned)


def message_kernel(
    queries_ref, probes_ref, cand_ref, out_ref, queries_vmem, probes_vmem, cand_vmem, sems
):
    owners, height, lanes = out_ref.shape
    query_count, features = queries_ref.shape
    probe_count, cand_count, _ = cand_ref.shape
    pairs = (
        (probes_ref, probes_vmem),
        (cand_ref, cand_vmem),
        (queries_ref, queries_vmem),
    )
    copies = [
        pltpu.make_async_copy(source, target, sems.at[i])
        for i, (source, target) in enumerate(pairs)
    ]
    for c in copies:
        c.start()
    copies[0].wait()
    copies[1].wait()
    pieces = [probes_vmem[...]] + [cand_vmem[:, c, :] for c in range(cand_count)]
    spare = lanes - len(pieces) * query_count
    pieces.append(jnp.zeros((probe_count, spare), jnp.int32))
    indices = jnp.concatenate(pieces, axis=1).astype(jnp.float32).astype(jnp.bfloat16)
    for k in range(owners):
        out_ref[k, height - probe_count :, :] = indices
    copies[2].wait()
    for j in range(features // lanes):
        column = queries_vmem[:, j * lanes : (j + 1) * lanes]
        for k in range(owners):
            out_ref[k, j * query_count : (j + 1) * query_count, :] = column


def make_message(queries, probes, cand, owners):
    query_count, features = queries.shape
    probe_count = probes.shape[1]
    height = query_count * (features // LANES) + probe_count
    whole = pl.BlockSpec(memory_space=pltpu.VMEM)
    return pl.pallas_call(
        message_kernel,
        out_shape=jax.ShapeDtypeStruct((owners, height, LANES), queries.dtype),
        in_specs=[pl.BlockSpec(memory_space=pltpu.HBM)] * 3,
        out_specs=whole,
        scratch_shapes=[
            pltpu.VMEM(queries.shape, queries.dtype),
            pltpu.VMEM(probes.shape[::-1], probes.dtype),
            pltpu.VMEM(cand.transpose(1, 2, 0).shape, cand.dtype),
            pltpu.SemaphoreType.DMA((3,)),
        ],
        compiler_params=pltpu.CompilerParams(vmem_limit_bytes=24 * MIB),
    )(in_hbm(queries), in_hbm(probes.T), in_hbm(cand.transpose(1, 2, 0)))


def on_device(queries, corpus, list_slot, probes, cand):
    owners = lax.axis_size("lists")
    query_count, features = queries.shape
    probe_count = probes.shape[1]
    cand_count = cand.shape[2]
    local_lists = corpus.shape[0]
    corpus = corpus.reshape(-1, features)
    total_lists = list_slot.shape[0]
    pair_count = query_count * probe_count
    capacity = min(query_count, max(2, (2 * pair_count + total_lists - 1) // total_lists))
    sizes = (owners, query_count, probe_count, cand_count, capacity)
    me = lax.axis_index("lists").astype(jnp.int32)

    message = make_message(queries, probes, cand, owners)
    messages = exchange(message)
    staged, inv_rows, column = row_norms(
        list_slot, probes, corpus, local_lists, cand_count, capacity
    )
    scores = block_scores(sizes, me.reshape(1), list_slot[None, :], corpus, staged, inv_rows, messages)
    returned = exchange(scores)
    chosen = place(column, returned)
    return chosen.reshape(query_count, probe_count, cand_count, BLOCK)


def solution(mesh):
    placed = (
        P(("groups", "lists", "rep"), None),
        P(("groups", "lists"), None, None),
        P("groups"),
        P(("groups", "lists", "rep"), None),
        P(("groups", "lists", "rep"), None, None),
    )
    return jax.shard_map(
        on_device,
        mesh=mesh,
        in_specs=placed,
        out_specs=P(("groups", "lists", "rep"), None, None, None),
        check_vma=False,
    )
```

```python
import functools

import jax
import jax.numpy as jnp
from jax import lax
from jax.experimental import pallas as pl
from jax.experimental.pallas import tpu as pltpu
from jax.sharding import PartitionSpec as P

BLOCK = 128
LANES = 128
MIB = 2**20

epsilon = 1e-06


def contract(a, b, dims, precision=None):
    return lax.dot_general(
        a, b, (dims, ((), ())), precision=precision, preferred_element_type=jnp.float32
    )


def in_hbm(value):
    return pltpu.with_memory_space_constraint(value, pltpu.HBM)


def in_vmem(value):
    return pltpu.with_memory_space_constraint(value, pltpu.VMEM)


def first_order(owners):
    return [(i + owners // 2) % owners for i in range(owners)]


def second_order(owners):
    if owners > 16:
        return first_order(owners)
    leader, ends = owners // 2, owners // 4
    return sorted(
        range(owners), key=lambda i: (i != leader, ends <= i < owners - ends, i % 2, i)
    )


def second_place(owner, owners):
    if owners > 16:
        return (owner + owners // 2) % owners
    place = owner
    for j, i in enumerate(second_order(owners)):
        place = jnp.where(owner == i, j, place)
    return place


def exchange(value, order):
    return lax.all_to_all(
        value, "lists", split_axis=0, concat_axis=0, axis_index_groups=[order], tiled=True
    )


def staged_rows(local_lists, list_length):
    return min(local_lists * list_length, list_length + list_length // 2)


def norm_kernel(
    sizes,
    slot_ref,
    probes_ref,
    corpus_ref,
    staged_ref,
    inv_ref,
    column_ref,
    held,
    parts,
    slots,
    sems,
    slot_sem,
):
    cand_count, capacity, chunk = sizes
    total_rows, features = corpus_ref.shape
    local_lists, list_length = inv_ref.shape
    staged = staged_ref.shape[0]

    cuts = sorted(set(range(0, total_rows + 1, list_length)) | {staged})
    ranges = list(zip(cuts[:-1], cuts[1:]))

    def place(row, end):
        if row < staged:
            return staged_ref.at[row:end]
        return held.at[row - staged : end - staged]

    def copy(row, end):
        return pltpu.make_async_copy(
            corpus_ref.at[row:end], place(row, end), sems.at[cuts.index(row)]
        )

    slot_copy = pltpu.make_async_copy(slot_ref, slots, slot_sem)
    slot_copy.start()
    for row, end in ranges:
        copy(row, end).start()
    slot_copy.wait()
    column_ref[...] = result_columns(cand_count, capacity, local_lists, slots, probes_ref[...])
    ones = jnp.ones((8, 2 * LANES), jnp.bfloat16)
    for l in range(local_lists):
        for begin, to in ranges:
            if begin // list_length != l:
                continue
            copy(begin, to).wait()
            for row in range(begin, to, chunk):
                end = min(row + chunk, to)
                wide = place(row, end)[...].astype(jnp.float32)
                squares = functools.reduce(
                    jnp.add, [wide[:, j : j + LANES] ** 2 for j in range(0, features, LANES)]
                )
                high = squares.astype(jnp.bfloat16)
                low = (squares - high.astype(jnp.float32)).astype(jnp.bfloat16)
                parts[row:end, :LANES] = high
                parts[row:end, LANES:] = low
        whole = parts[l * list_length : (l + 1) * list_length, :]
        sums = contract(ones, whole, ((1,), (1,)))[:1]
        inv_ref[l : l + 1, :] = lax.rsqrt(sums / features + epsilon) * features ** (-0.5)


def row_sums(parts):
    high = parts.astype(jnp.bfloat16)
    low = (parts - high.astype(jnp.float32)).astype(jnp.bfloat16)
    terms = jnp.concatenate([high, low], axis=1)
    ones = jnp.ones((8, terms.shape[1]), jnp.bfloat16)
    return contract(ones, terms, ((1,), (1,)))[:1]


def result_columns(cand_count, capacity, local_lists, slot_ref, probes):
    probe_count, query_count = probes.shape
    total_lists = slot_ref.shape[0]
    owners = total_lists // local_lists
    position = jnp.zeros(probes.shape, jnp.float32)
    for t in range(total_lists):
        owner = slot_ref[t] // local_lists
        place = second_place(owner, owners)
        spot = place * local_lists + slot_ref[t] % local_lists
        position = jnp.where(probes == t, spot.astype(jnp.float32), position)
    lists = lax.broadcasted_iota(jnp.int32, (total_lists, query_count), 0)
    named = [lists == probes[p : p + 1] for p in range(probe_count)]
    counts = functools.reduce(jnp.add, [n.astype(jnp.float32) for n in named])
    square = (query_count, query_count)
    before = lax.broadcasted_iota(jnp.int32, square, 0) < lax.broadcasted_iota(
        jnp.int32, square, 1
    )
    earlier = contract(
        counts.astype(jnp.bfloat16), before.astype(jnp.float32).astype(jnp.bfloat16), ((1,), (0,))
    )
    rank = jnp.concatenate(
        [jnp.sum(jnp.where(n, earlier, 0.0), axis=0, keepdims=True) for n in named], axis=0
    )
    rows = probe_count * cand_count
    row = lax.broadcasted_iota(jnp.int32, (rows, probe_count), 0)
    lane = lax.broadcasted_iota(jnp.int32, (rows, probe_count), 1)
    spread = (row // cand_count == lane).astype(jnp.float32).astype(jnp.bfloat16)
    value = contract(spread, position.astype(jnp.bfloat16), ((1,), (0,))) * (
        cand_count * capacity
    ) + contract(spread, rank.astype(jnp.bfloat16), ((1,), (0,)))
    shift = (lax.broadcasted_iota(jnp.int32, value.shape, 0) % cand_count) * capacity
    return value.astype(jnp.int32) + shift


def row_norms(list_slot, probes, corpus, local_lists, cand_count, capacity):
    total_rows, features = corpus.shape
    list_length = total_rows // local_lists
    chunk = min(list_length, 256)
    staged = staged_rows(local_lists, list_length)
    query_count, probe_count = probes.shape
    whole = pl.BlockSpec(memory_space=pltpu.VMEM)
    return pl.pallas_call(
        functools.partial(norm_kernel, (cand_count, capacity, chunk)),
        out_shape=(
            pltpu.VMEM((staged, features), corpus.dtype),
            jax.ShapeDtypeStruct((local_lists, list_length), jnp.float32),
            jax.ShapeDtypeStruct((probe_count * cand_count, query_count), jnp.int32),
        ),
        in_specs=[
            pl.BlockSpec(memory_space=pltpu.HBM),
            whole,
            pl.BlockSpec(memory_space=pltpu.HBM),
        ],
        out_specs=(whole, whole, whole),
        scratch_shapes=[
            pltpu.VMEM((max(total_rows - staged, 16), features), corpus.dtype),
            pltpu.VMEM((total_rows, 2 * LANES), jnp.bfloat16),
            pltpu.SMEM(list_slot.shape, list_slot.dtype),
            pltpu.SemaphoreType.DMA((local_lists + 1,)),
            pltpu.SemaphoreType.DMA,
        ],
        compiler_params=pltpu.CompilerParams(vmem_limit_bytes=24 * MIB),
        cost_estimate=pl.CostEstimate(
            flops=2 * corpus.size, bytes_accessed=2 * corpus.size, transcendentals=0
        ),
    )(in_hbm(list_slot), in_hbm(probes.T), in_hbm(corpus))


def score_kernel(
    sizes, me_ref, slot_ref, corpus_ref, staged_ref, inv_ref, message_ref, out_ref, held, picked, sems
):
    owners, query_count, probe_count, cand_count, capacity, streams = sizes
    total_rows, features = corpus_ref.shape
    local_lists, list_length = inv_ref.shape
    staged = staged_ref.shape[0]
    total = owners * query_count
    room = owners * capacity
    step = capacity * cand_count

    def copy(begin, end):
        return pltpu.make_async_copy(
            corpus_ref.at[begin:end],
            held.at[begin - staged : end - staged],
            sems.at[streams.index((begin, end))],
        )

    for begin, end in streams:
        copy(begin, end).start()

    columns = [
        jnp.concatenate(
            [message_ref[s, j : j + query_count, :] for s in range(owners)], axis=0
        )
        for j in range(0, query_count * (features // LANES), query_count)
    ]
    queries = jnp.concatenate(columns, axis=1)
    squares = functools.reduce(jnp.add, [c.astype(jnp.float32) ** 2 for c in columns])
    height = message_ref.shape[1]
    tiles = [
        message_ref[s, height - probe_count :, :].astype(jnp.float32) for s in range(owners)
    ]
    probes, *cands = [
        jnp.concatenate([t[:, i : i + query_count] for t in tiles], axis=1)
        for i in range(0, query_count * (1 + cand_count), query_count)
    ]
    inv_query = lax.rsqrt(row_sums(squares) / features + epsilon)

    slots = slot_ref[...]
    names = lax.broadcasted_iota(jnp.int32, slots.shape, 1).astype(jnp.float32)
    first = me_ref[0] * local_lists
    hits, wanted = [], []
    for l in range(local_lists):
        name = jnp.sum(jnp.where(slots == first + l, names, 0.0), axis=1, keepdims=True)
        named = probes == name
        hits.append(jnp.sum(named.astype(jnp.float32), axis=0, keepdims=True))
        wanted.append(
            [jnp.sum(jnp.where(named, c, 0.0), axis=0, keepdims=True) for c in cands]
        )
    hit = jnp.concatenate(hits, axis=0)

    span = min(total, LANES)
    earlier = lax.broadcasted_iota(jnp.int32, (span, span), 0)
    later = lax.broadcasted_iota(jnp.int32, (span, span), 1)
    before = (earlier < later) & (earlier // query_count == later // query_count)
    before = before.astype(jnp.float32).astype(jnp.bfloat16)
    hit_low = hit.astype(jnp.bfloat16)
    rank = jnp.concatenate(
        [
            contract(hit_low[:, j : j + span], before, ((1,), (0,)))
            for j in range(0, total, span)
        ],
        axis=1,
    )
    source = lax.broadcasted_iota(jnp.int32, (1, total), 1) // query_count
    source = second_place((source + owners // 2) % owners, owners) * capacity
    target = jnp.where(hit > 0.5, rank.astype(jnp.int32) + source, -1)

    places = lax.broadcasted_iota(jnp.int32, (room, total), 0)
    picks = [(places == target[l : l + 1]).astype(jnp.float32) for l in range(local_lists)]
    pick = jnp.concatenate(picks, axis=0).astype(jnp.bfloat16)
    picked[...] = contract(pick, queries, ((1,), (0,))).astype(jnp.bfloat16)
    scales = [jnp.sum(p * inv_query, axis=1, keepdims=True) for p in picks]
    blocks = [
        [jnp.sum(p * w, axis=1, keepdims=True) for w in wanted[l]] for l, p in enumerate(picks)
    ]

    for l in range(local_lists):
        rows = picked[l * room : (l + 1) * room, :]
        chosen = [jnp.zeros((room, BLOCK), jnp.float32) for _ in range(cand_count)]
        row = l * list_length
        while row < (l + 1) * list_length:
            if row < staged:
                end = min(row + 512, staged, (l + 1) * list_length)
                values = staged_ref[row:end, :]
            else:
                if row in dict(streams):
                    copy(row, dict(streams)[row]).wait()
                end = min(row + 512, (l + 1) * list_length)
                values = held[row - staged : end - staged, :]
            products = contract(rows, values, ((1,), (1,)))
            first = row - l * list_length
            scaled = products * scales[l] * inv_ref[l : l + 1, first : first + end - row]
            for j in range(0, end - row, BLOCK):
                piece = scaled[:, j : j + BLOCK]
                chosen = [
                    jnp.where(block == (first + j) // BLOCK, piece, old)
                    for block, old in zip(blocks[l], chosen)
                ]
            row = end
        out_ref[:, l * step : (l + 1) * step, :] = jnp.concatenate(
            [c.reshape(owners, capacity, BLOCK) for c in chosen], axis=1
        ).astype(jnp.bfloat16)


def stream_ranges(local_lists, list_length):
    row, end = staged_rows(local_lists, list_length), local_lists * list_length
    ranges = []
    while row < end:
        to = min(row + 512, (row // list_length + 1) * list_length)
        ranges.append((row, to))
        row = to
    return tuple(ranges)


def block_scores(sizes, me, list_slot, corpus, staged, inv_rows, messages):
    owners, query_count, probe_count, cand_count, capacity = sizes
    local_lists, list_length = inv_rows.shape
    total_rows, features = corpus.shape
    streams = stream_ranges(local_lists, list_length)
    whole = pl.BlockSpec(memory_space=pltpu.VMEM)
    return pl.pallas_call(
        functools.partial(score_kernel, sizes + (streams,)),
        out_shape=jax.ShapeDtypeStruct(
            (owners, local_lists * cand_count * capacity, BLOCK), jnp.bfloat16
        ),
        in_specs=[
            pl.BlockSpec(memory_space=pltpu.SMEM),
            whole,
            pl.BlockSpec(memory_space=pltpu.HBM),
            whole,
            whole,
            whole,
        ],
        out_specs=whole,
        scratch_shapes=[
            pltpu.VMEM((max(total_rows - staged.shape[0], 16), features), corpus.dtype),
            pltpu.VMEM((local_lists * owners * capacity, features), corpus.dtype),
            pltpu.SemaphoreType.DMA((max(len(streams), 1),)),
        ],
        compiler_params=pltpu.CompilerParams(vmem_limit_bytes=40 * MIB),
        cost_estimate=pl.CostEstimate(
            flops=2 * owners * capacity * corpus.size,
            bytes_accessed=2 * corpus.size,
            transcendentals=0,
        ),
    )(me, list_slot, in_hbm(corpus), in_vmem(staged), inv_rows, messages)


def place_kernel(column_ref, returned_ref, out_ref):
    returned = returned_ref[...].reshape(-1, returned_ref.shape[-1])
    each, query_count = column_ref.shape
    column = column_ref[...]
    lanes = lax.broadcasted_iota(jnp.int32, (each, returned.shape[0]), 1)
    pick = jnp.concatenate(
        [(lanes == column[:, i : i + 1]).astype(jnp.float32) for i in range(query_count)], axis=0
    ).astype(jnp.bfloat16)
    out_ref[...] = contract(pick, returned, ((1,), (0,))).astype(jnp.bfloat16)


def place(column, returned):
    whole = pl.BlockSpec(memory_space=pltpu.VMEM)
    return pl.pallas_call(
        place_kernel,
        out_shape=jax.ShapeDtypeStruct((column.size, BLOCK), jnp.bfloat16),
        in_specs=[whole] * 2,
        out_specs=whole,
        compiler_params=pltpu.CompilerParams(vmem_limit_bytes=24 * MIB),
    )(column, returned)


def message_kernel(
    queries_ref, probes_ref, cand_ref, out_ref, queries_vmem, probes_vmem, cand_vmem, sems
):
    owners, height, lanes = out_ref.shape
    query_count, features = queries_ref.shape
    probe_count, cand_count, _ = cand_ref.shape
    pairs = (
        (probes_ref, probes_vmem),
        (cand_ref, cand_vmem),
        (queries_ref, queries_vmem),
    )
    copies = [
        pltpu.make_async_copy(source, target, sems.at[i])
        for i, (source, target) in enumerate(pairs)
    ]
    for c in copies:
        c.start()
    copies[0].wait()
    copies[1].wait()
    pieces = [probes_vmem[...]] + [cand_vmem[:, c, :] for c in range(cand_count)]
    spare = lanes - len(pieces) * query_count
    pieces.append(jnp.zeros((probe_count, spare), jnp.int32))
    indices = jnp.concatenate(pieces, axis=1).astype(jnp.float32).astype(jnp.bfloat16)
    for k in range(owners):
        out_ref[k, height - probe_count :, :] = indices
    copies[2].wait()
    for j in range(features // lanes):
        column = queries_vmem[:, j * lanes : (j + 1) * lanes]
        for k in range(owners):
            out_ref[k, j * query_count : (j + 1) * query_count, :] = column


def make_message(queries, probes, cand, owners):
    query_count, features = queries.shape
    probe_count = probes.shape[1]
    height = query_count * (features // LANES) + probe_count
    whole = pl.BlockSpec(memory_space=pltpu.VMEM)
    return pl.pallas_call(
        message_kernel,
        out_shape=jax.ShapeDtypeStruct((owners, height, LANES), queries.dtype),
        in_specs=[pl.BlockSpec(memory_space=pltpu.HBM)] * 3,
        out_specs=whole,
        scratch_shapes=[
            pltpu.VMEM(queries.shape, queries.dtype),
            pltpu.VMEM(probes.shape[::-1], probes.dtype),
            pltpu.VMEM(cand.transpose(1, 2, 0).shape, cand.dtype),
            pltpu.SemaphoreType.DMA((3,)),
        ],
        compiler_params=pltpu.CompilerParams(vmem_limit_bytes=24 * MIB),
    )(in_hbm(queries), in_hbm(probes.T), in_hbm(cand.transpose(1, 2, 0)))


def on_device(queries, corpus, list_slot, probes, cand):
    owners = lax.axis_size("lists")
    query_count, features = queries.shape
    probe_count = probes.shape[1]
    cand_count = cand.shape[2]
    local_lists = corpus.shape[0]
    corpus = corpus.reshape(-1, features)
    total_lists = list_slot.shape[0]
    pair_count = query_count * probe_count
    capacity = min(query_count, max(2, (2 * pair_count + total_lists - 1) // total_lists))
    sizes = (owners, query_count, probe_count, cand_count, capacity)
    me = lax.axis_index("lists").astype(jnp.int32)

    message = make_message(queries, probes, cand, owners)
    messages = exchange(message, first_order(owners))
    staged, inv_rows, column = row_norms(
        list_slot, probes, corpus, local_lists, cand_count, capacity
    )
    scores = block_scores(sizes, me.reshape(1), list_slot[None, :], corpus, staged, inv_rows, messages)
    returned = exchange(scores, second_order(owners))
    chosen = place(column, returned)
    return chosen.reshape(query_count, probe_count, cand_count, BLOCK)


def solution(mesh):
    placed = (
        P(("groups", "lists", "rep"), None),
        P(("groups", "lists"), None, None),
        P("groups"),
        P(("groups", "lists", "rep"), None),
        P(("groups", "lists", "rep"), None, None),
    )
    return jax.shard_map(
        on_device,
        mesh=mesh,
        in_specs=placed,
        out_specs=P(("groups", "lists", "rep"), None, None, None),
        check_vma=False,
    )
```

```python
import functools

import jax
import jax.numpy as jnp
from jax import lax
from jax.experimental import pallas as pl
from jax.experimental.pallas import tpu as pltpu
from jax.sharding import PartitionSpec as P

BLOCK = 128
LANES = 128
MIB = 2**20

epsilon = 1e-06


def contract(a, b, dims, precision=None):
    return lax.dot_general(
        a, b, (dims, ((), ())), precision=precision, preferred_element_type=jnp.float32
    )


def in_hbm(value):
    return pltpu.with_memory_space_constraint(value, pltpu.HBM)


def in_vmem(value):
    return pltpu.with_memory_space_constraint(value, pltpu.VMEM)


def ring_order(owners):
    ring = list(range(0, owners, 2)) + list(reversed(range(1, owners, 2)))
    start = ring.index(owners // 2 - owners // 2 % 2)
    return ring[start:] + ring[:start]


def first_order(owners):
    return ring_order(owners) if owners <= 16 else list(range(owners))


def second_order(owners):
    return ring_order(owners) if owners <= 16 else list(range(owners))


def look_up(index, table):
    value = index
    for i, entry in enumerate(table):
        if i != entry:
            value = jnp.where(index == i, entry, value)
    return value


def exchange(value, order):
    return lax.all_to_all(
        value, "lists", split_axis=0, concat_axis=0, axis_index_groups=[order], tiled=True
    )


def staged_rows(local_lists, list_length):
    return min(local_lists * list_length, list_length + list_length // 2)


def norm_kernel(
    sizes,
    slot_ref,
    probes_ref,
    corpus_ref,
    staged_ref,
    inv_ref,
    column_ref,
    held,
    parts,
    slots,
    sems,
    slot_sem,
):
    cand_count, capacity, chunk = sizes
    total_rows, features = corpus_ref.shape
    local_lists, list_length = inv_ref.shape
    staged = staged_ref.shape[0]

    cuts = sorted(set(range(0, total_rows + 1, list_length)) | {staged})
    ranges = list(zip(cuts[:-1], cuts[1:]))

    def place(row, end):
        if row < staged:
            return staged_ref.at[row:end]
        return held.at[row - staged : end - staged]

    def copy(row, end):
        return pltpu.make_async_copy(
            corpus_ref.at[row:end], place(row, end), sems.at[cuts.index(row)]
        )

    slot_copy = pltpu.make_async_copy(slot_ref, slots, slot_sem)
    slot_copy.start()
    for row, end in ranges:
        copy(row, end).start()
    slot_copy.wait()
    column_ref[...] = result_columns(cand_count, capacity, local_lists, slots, probes_ref[...])
    ones = jnp.ones((8, 2 * LANES), jnp.bfloat16)
    for l in range(local_lists):
        for begin, to in ranges:
            if begin // list_length != l:
                continue
            copy(begin, to).wait()
            for row in range(begin, to, chunk):
                end = min(row + chunk, to)
                wide = place(row, end)[...].astype(jnp.float32)
                squares = functools.reduce(
                    jnp.add, [wide[:, j : j + LANES] ** 2 for j in range(0, features, LANES)]
                )
                high = squares.astype(jnp.bfloat16)
                low = (squares - high.astype(jnp.float32)).astype(jnp.bfloat16)
                parts[row:end, :LANES] = high
                parts[row:end, LANES:] = low
        whole = parts[l * list_length : (l + 1) * list_length, :]
        sums = contract(ones, whole, ((1,), (1,)))[:1]
        inv_ref[l : l + 1, :] = lax.rsqrt(sums / features + epsilon) * features ** (-0.5)


def row_sums(parts):
    high = parts.astype(jnp.bfloat16)
    low = (parts - high.astype(jnp.float32)).astype(jnp.bfloat16)
    terms = jnp.concatenate([high, low], axis=1)
    ones = jnp.ones((8, terms.shape[1]), jnp.bfloat16)
    return contract(ones, terms, ((1,), (1,)))[:1]


def result_columns(cand_count, capacity, local_lists, slot_ref, probes):
    probe_count, query_count = probes.shape
    total_lists = slot_ref.shape[0]
    order = second_order(total_lists // local_lists)
    places = [order.index(i) for i in range(len(order))]
    position = jnp.zeros(probes.shape, jnp.float32)
    for t in range(total_lists):
        owner = slot_ref[t] // local_lists
        place = look_up(owner, places)
        spot = place * local_lists + slot_ref[t] % local_lists
        position = jnp.where(probes == t, spot.astype(jnp.float32), position)
    lists = lax.broadcasted_iota(jnp.int32, (total_lists, query_count), 0)
    named = [lists == probes[p : p + 1] for p in range(probe_count)]
    counts = functools.reduce(jnp.add, [n.astype(jnp.float32) for n in named])
    square = (query_count, query_count)
    before = lax.broadcasted_iota(jnp.int32, square, 0) < lax.broadcasted_iota(
        jnp.int32, square, 1
    )
    earlier = contract(
        counts.astype(jnp.bfloat16), before.astype(jnp.float32).astype(jnp.bfloat16), ((1,), (0,))
    )
    rank = jnp.concatenate(
        [jnp.sum(jnp.where(n, earlier, 0.0), axis=0, keepdims=True) for n in named], axis=0
    )
    rows = probe_count * cand_count
    row = lax.broadcasted_iota(jnp.int32, (rows, probe_count), 0)
    lane = lax.broadcasted_iota(jnp.int32, (rows, probe_count), 1)
    spread = (row // cand_count == lane).astype(jnp.float32).astype(jnp.bfloat16)
    value = contract(spread, position.astype(jnp.bfloat16), ((1,), (0,))) * (
        cand_count * capacity
    ) + contract(spread, rank.astype(jnp.bfloat16), ((1,), (0,)))
    shift = (lax.broadcasted_iota(jnp.int32, value.shape, 0) % cand_count) * capacity
    return value.astype(jnp.int32) + shift


def row_norms(list_slot, probes, corpus, local_lists, cand_count, capacity):
    total_rows, features = corpus.shape
    list_length = total_rows // local_lists
    chunk = min(list_length, 256)
    staged = staged_rows(local_lists, list_length)
    query_count, probe_count = probes.shape
    whole = pl.BlockSpec(memory_space=pltpu.VMEM)
    return pl.pallas_call(
        functools.partial(norm_kernel, (cand_count, capacity, chunk)),
        out_shape=(
            pltpu.VMEM((staged, features), corpus.dtype),
            jax.ShapeDtypeStruct((local_lists, list_length), jnp.float32),
            jax.ShapeDtypeStruct((probe_count * cand_count, query_count), jnp.int32),
        ),
        in_specs=[
            pl.BlockSpec(memory_space=pltpu.HBM),
            whole,
            pl.BlockSpec(memory_space=pltpu.HBM),
        ],
        out_specs=(whole, whole, whole),
        scratch_shapes=[
            pltpu.VMEM((max(total_rows - staged, 16), features), corpus.dtype),
            pltpu.VMEM((total_rows, 2 * LANES), jnp.bfloat16),
            pltpu.SMEM(list_slot.shape, list_slot.dtype),
            pltpu.SemaphoreType.DMA((local_lists + 1,)),
            pltpu.SemaphoreType.DMA,
        ],
        compiler_params=pltpu.CompilerParams(vmem_limit_bytes=24 * MIB),
        cost_estimate=pl.CostEstimate(
            flops=2 * corpus.size, bytes_accessed=2 * corpus.size, transcendentals=0
        ),
    )(in_hbm(list_slot), in_hbm(probes.T), in_hbm(corpus))


def score_kernel(
    sizes, me_ref, slot_ref, corpus_ref, staged_ref, inv_ref, message_ref, out_ref, held, picked, sems
):
    owners, query_count, probe_count, cand_count, capacity, streams = sizes
    total_rows, features = corpus_ref.shape
    local_lists, list_length = inv_ref.shape
    staged = staged_ref.shape[0]
    total = owners * query_count
    room = owners * capacity
    step = capacity * cand_count

    def copy(begin, end):
        return pltpu.make_async_copy(
            corpus_ref.at[begin:end],
            held.at[begin - staged : end - staged],
            sems.at[streams.index((begin, end))],
        )

    for begin, end in streams:
        copy(begin, end).start()

    columns = [
        jnp.concatenate(
            [message_ref[s, j : j + query_count, :] for s in range(owners)], axis=0
        )
        for j in range(0, query_count * (features // LANES), query_count)
    ]
    queries = jnp.concatenate(columns, axis=1)
    squares = functools.reduce(jnp.add, [c.astype(jnp.float32) ** 2 for c in columns])
    height = message_ref.shape[1]
    tiles = [
        message_ref[s, height - probe_count :, :].astype(jnp.float32) for s in range(owners)
    ]
    probes, *cands = [
        jnp.concatenate([t[:, i : i + query_count] for t in tiles], axis=1)
        for i in range(0, query_count * (1 + cand_count), query_count)
    ]
    inv_query = lax.rsqrt(row_sums(squares) / features + epsilon)

    slots = slot_ref[...]
    names = lax.broadcasted_iota(jnp.int32, slots.shape, 1).astype(jnp.float32)
    first = me_ref[0] * local_lists
    hits, wanted = [], []
    for l in range(local_lists):
        name = jnp.sum(jnp.where(slots == first + l, names, 0.0), axis=1, keepdims=True)
        named = probes == name
        hits.append(jnp.sum(named.astype(jnp.float32), axis=0, keepdims=True))
        wanted.append(
            [jnp.sum(jnp.where(named, c, 0.0), axis=0, keepdims=True) for c in cands]
        )
    hit = jnp.concatenate(hits, axis=0)

    span = min(total, LANES)
    earlier = lax.broadcasted_iota(jnp.int32, (span, span), 0)
    later = lax.broadcasted_iota(jnp.int32, (span, span), 1)
    before = (earlier < later) & (earlier // query_count == later // query_count)
    before = before.astype(jnp.float32).astype(jnp.bfloat16)
    hit_low = hit.astype(jnp.bfloat16)
    rank = jnp.concatenate(
        [
            contract(hit_low[:, j : j + span], before, ((1,), (0,)))
            for j in range(0, total, span)
        ],
        axis=1,
    )
    source = lax.broadcasted_iota(jnp.int32, (1, total), 1) // query_count
    moved = [second_order(owners).index(i) for i in first_order(owners)]
    source = look_up(source, moved) * capacity
    target = jnp.where(hit > 0.5, rank.astype(jnp.int32) + source, -1)

    places = lax.broadcasted_iota(jnp.int32, (room, total), 0)
    picks = [(places == target[l : l + 1]).astype(jnp.float32) for l in range(local_lists)]
    pick = jnp.concatenate(picks, axis=0).astype(jnp.bfloat16)
    picked[...] = contract(pick, queries, ((1,), (0,))).astype(jnp.bfloat16)
    scales = [jnp.sum(p * inv_query, axis=1, keepdims=True) for p in picks]
    blocks = [
        [jnp.sum(p * w, axis=1, keepdims=True) for w in wanted[l]] for l, p in enumerate(picks)
    ]

    for l in range(local_lists):
        rows = picked[l * room : (l + 1) * room, :]
        chosen = [jnp.zeros((room, BLOCK), jnp.float32) for _ in range(cand_count)]
        row = l * list_length
        while row < (l + 1) * list_length:
            if row < staged:
                end = min(row + 512, staged, (l + 1) * list_length)
                values = staged_ref[row:end, :]
            else:
                if row in dict(streams):
                    copy(row, dict(streams)[row]).wait()
                end = min(row + 512, (l + 1) * list_length)
                values = held[row - staged : end - staged, :]
            products = contract(rows, values, ((1,), (1,)))
            first = row - l * list_length
            scaled = products * scales[l] * inv_ref[l : l + 1, first : first + end - row]
            for j in range(0, end - row, BLOCK):
                piece = scaled[:, j : j + BLOCK]
                chosen = [
                    jnp.where(block == (first + j) // BLOCK, piece, old)
                    for block, old in zip(blocks[l], chosen)
                ]
            row = end
        out_ref[:, l * step : (l + 1) * step, :] = jnp.concatenate(
            [c.reshape(owners, capacity, BLOCK) for c in chosen], axis=1
        ).astype(jnp.bfloat16)


def stream_ranges(local_lists, list_length):
    row, end = staged_rows(local_lists, list_length), local_lists * list_length
    ranges = []
    while row < end:
        to = min(row + 512, (row // list_length + 1) * list_length)
        ranges.append((row, to))
        row = to
    return tuple(ranges)


def block_scores(sizes, me, list_slot, corpus, staged, inv_rows, messages):
    owners, query_count, probe_count, cand_count, capacity = sizes
    local_lists, list_length = inv_rows.shape
    total_rows, features = corpus.shape
    streams = stream_ranges(local_lists, list_length)
    whole = pl.BlockSpec(memory_space=pltpu.VMEM)
    return pl.pallas_call(
        functools.partial(score_kernel, sizes + (streams,)),
        out_shape=jax.ShapeDtypeStruct(
            (owners, local_lists * cand_count * capacity, BLOCK), jnp.bfloat16
        ),
        in_specs=[
            pl.BlockSpec(memory_space=pltpu.SMEM),
            whole,
            pl.BlockSpec(memory_space=pltpu.HBM),
            whole,
            whole,
            whole,
        ],
        out_specs=whole,
        scratch_shapes=[
            pltpu.VMEM((max(total_rows - staged.shape[0], 16), features), corpus.dtype),
            pltpu.VMEM((local_lists * owners * capacity, features), corpus.dtype),
            pltpu.SemaphoreType.DMA((max(len(streams), 1),)),
        ],
        compiler_params=pltpu.CompilerParams(vmem_limit_bytes=40 * MIB),
        cost_estimate=pl.CostEstimate(
            flops=2 * owners * capacity * corpus.size,
            bytes_accessed=2 * corpus.size,
            transcendentals=0,
        ),
    )(me, list_slot, in_hbm(corpus), in_vmem(staged), inv_rows, messages)


def place_kernel(column_ref, returned_ref, out_ref):
    returned = returned_ref[...].reshape(-1, returned_ref.shape[-1])
    each, query_count = column_ref.shape
    column = column_ref[...]
    lanes = lax.broadcasted_iota(jnp.int32, (each, returned.shape[0]), 1)
    pick = jnp.concatenate(
        [(lanes == column[:, i : i + 1]).astype(jnp.float32) for i in range(query_count)], axis=0
    ).astype(jnp.bfloat16)
    out_ref[...] = contract(pick, returned, ((1,), (0,))).astype(jnp.bfloat16)


def place(column, returned):
    whole = pl.BlockSpec(memory_space=pltpu.VMEM)
    return pl.pallas_call(
        place_kernel,
        out_shape=jax.ShapeDtypeStruct((column.size, BLOCK), jnp.bfloat16),
        in_specs=[whole] * 2,
        out_specs=whole,
        compiler_params=pltpu.CompilerParams(vmem_limit_bytes=24 * MIB),
    )(column, returned)


def message_kernel(
    queries_ref, probes_ref, cand_ref, out_ref, queries_vmem, probes_vmem, cand_vmem, sems
):
    owners, height, lanes = out_ref.shape
    query_count, features = queries_ref.shape
    probe_count, cand_count, _ = cand_ref.shape
    pairs = (
        (probes_ref, probes_vmem),
        (cand_ref, cand_vmem),
        (queries_ref, queries_vmem),
    )
    copies = [
        pltpu.make_async_copy(source, target, sems.at[i])
        for i, (source, target) in enumerate(pairs)
    ]
    for c in copies:
        c.start()
    copies[0].wait()
    copies[1].wait()
    pieces = [probes_vmem[...]] + [cand_vmem[:, c, :] for c in range(cand_count)]
    spare = lanes - len(pieces) * query_count
    pieces.append(jnp.zeros((probe_count, spare), jnp.int32))
    indices = jnp.concatenate(pieces, axis=1).astype(jnp.float32).astype(jnp.bfloat16)
    for k in range(owners):
        out_ref[k, height - probe_count :, :] = indices
    copies[2].wait()
    for j in range(features // lanes):
        column = queries_vmem[:, j * lanes : (j + 1) * lanes]
        for k in range(owners):
            out_ref[k, j * query_count : (j + 1) * query_count, :] = column


def make_message(queries, probes, cand, owners):
    query_count, features = queries.shape
    probe_count = probes.shape[1]
    height = query_count * (features // LANES) + probe_count
    whole = pl.BlockSpec(memory_space=pltpu.VMEM)
    return pl.pallas_call(
        message_kernel,
        out_shape=jax.ShapeDtypeStruct((owners, height, LANES), queries.dtype),
        in_specs=[pl.BlockSpec(memory_space=pltpu.HBM)] * 3,
        out_specs=whole,
        scratch_shapes=[
            pltpu.VMEM(queries.shape, queries.dtype),
            pltpu.VMEM(probes.shape[::-1], probes.dtype),
            pltpu.VMEM(cand.transpose(1, 2, 0).shape, cand.dtype),
            pltpu.SemaphoreType.DMA((3,)),
        ],
        compiler_params=pltpu.CompilerParams(vmem_limit_bytes=24 * MIB),
    )(in_hbm(queries), in_hbm(probes.T), in_hbm(cand.transpose(1, 2, 0)))


def on_device(queries, corpus, list_slot, probes, cand):
    owners = lax.axis_size("lists")
    query_count, features = queries.shape
    probe_count = probes.shape[1]
    cand_count = cand.shape[2]
    local_lists = corpus.shape[0]
    corpus = corpus.reshape(-1, features)
    total_lists = list_slot.shape[0]
    pair_count = query_count * probe_count
    capacity = min(query_count, max(2, (2 * pair_count + total_lists - 1) // total_lists))
    sizes = (owners, query_count, probe_count, cand_count, capacity)
    me = lax.axis_index("lists").astype(jnp.int32)

    message = make_message(queries, probes, cand, owners)
    messages = exchange(message, first_order(owners))
    staged, inv_rows, column = row_norms(
        list_slot, probes, corpus, local_lists, cand_count, capacity
    )
    scores = block_scores(sizes, me.reshape(1), list_slot[None, :], corpus, staged, inv_rows, messages)
    returned = exchange(scores, second_order(owners))
    chosen = place(column, returned)
    return chosen.reshape(query_count, probe_count, cand_count, BLOCK)


def solution(mesh):
    placed = (
        P(("groups", "lists", "rep"), None),
        P(("groups", "lists"), None, None),
        P("groups"),
        P(("groups", "lists", "rep"), None),
        P(("groups", "lists", "rep"), None, None),
    )
    return jax.shard_map(
        on_device,
        mesh=mesh,
        in_specs=placed,
        out_specs=P(("groups", "lists", "rep"), None, None, None),
        check_vma=False,
    )
```

```python
import functools

import jax
import jax.numpy as jnp
from jax import lax
from jax.experimental import pallas as pl
from jax.experimental.pallas import tpu as pltpu
from jax.sharding import PartitionSpec as P

BLOCK = 128
LANES = 128
MIB = 2**20

epsilon = 1e-06


def contract(a, b, dims, precision=None):
    return lax.dot_general(
        a, b, (dims, ((), ())), precision=precision, preferred_element_type=jnp.float32
    )


def in_hbm(value):
    return pltpu.with_memory_space_constraint(value, pltpu.HBM)


def in_vmem(value):
    return pltpu.with_memory_space_constraint(value, pltpu.VMEM)


def first_order(owners):
    return [(i + owners // 2) % owners for i in range(owners)]


def second_order(owners):
    if owners > 16:
        return first_order(owners)
    leader, ends = owners // 2, owners // 4
    return sorted(
        range(owners), key=lambda i: (i != leader, ends <= i < owners - ends, i % 2, i)
    )


def second_place(owner, owners):
    if owners > 16:
        return (owner + owners // 2) % owners
    place = owner
    for j, i in enumerate(second_order(owners)):
        place = jnp.where(owner == i, j, place)
    return place


def exchange(value, order):
    return lax.all_to_all(
        value, "lists", split_axis=0, concat_axis=0, axis_index_groups=[order], tiled=True
    )


def staged_rows(local_lists, list_length):
    return min(local_lists * list_length, list_length + list_length // 2)


def norm_kernel(
    sizes,
    slot_ref,
    probes_ref,
    corpus_ref,
    staged_ref,
    inv_ref,
    column_ref,
    held,
    parts,
    slots,
    sems,
    slot_sem,
):
    cand_count, capacity, chunk = sizes
    total_rows, features = corpus_ref.shape
    local_lists, list_length = inv_ref.shape
    staged = staged_ref.shape[0]

    cuts = sorted(set(range(0, total_rows + 1, list_length)) | {staged})
    ranges = list(zip(cuts[:-1], cuts[1:]))

    def place(row, end):
        if row < staged:
            return staged_ref.at[row:end]
        return held.at[row - staged : end - staged]

    def copy(row, end):
        return pltpu.make_async_copy(
            corpus_ref.at[row:end], place(row, end), sems.at[cuts.index(row)]
        )

    slot_copy = pltpu.make_async_copy(slot_ref, slots, slot_sem)
    slot_copy.start()
    for i, (row, end) in enumerate(ranges):
        copy(row, end).start(priority=i % 2)
    slot_copy.wait()
    column_ref[...] = result_columns(cand_count, capacity, local_lists, slots, probes_ref[...])
    ones = jnp.ones((8, 2 * LANES), jnp.bfloat16)
    for l in range(local_lists):
        for begin, to in ranges:
            if begin // list_length != l:
                continue
            copy(begin, to).wait()
            for row in range(begin, to, chunk):
                end = min(row + chunk, to)
                wide = place(row, end)[...].astype(jnp.float32)
                squares = functools.reduce(
                    jnp.add, [wide[:, j : j + LANES] ** 2 for j in range(0, features, LANES)]
                )
                high = squares.astype(jnp.bfloat16)
                low = (squares - high.astype(jnp.float32)).astype(jnp.bfloat16)
                parts[row:end, :LANES] = high
                parts[row:end, LANES:] = low
        whole = parts[l * list_length : (l + 1) * list_length, :]
        sums = contract(ones, whole, ((1,), (1,)))[:1]
        inv_ref[l : l + 1, :] = lax.rsqrt(sums / features + epsilon) * features ** (-0.5)


def row_sums(parts):
    high = parts.astype(jnp.bfloat16)
    low = (parts - high.astype(jnp.float32)).astype(jnp.bfloat16)
    terms = jnp.concatenate([high, low], axis=1)
    ones = jnp.ones((8, terms.shape[1]), jnp.bfloat16)
    return contract(ones, terms, ((1,), (1,)))[:1]


def result_columns(cand_count, capacity, local_lists, slot_ref, probes):
    probe_count, query_count = probes.shape
    total_lists = slot_ref.shape[0]
    owners = total_lists // local_lists
    position = jnp.zeros(probes.shape, jnp.float32)
    for t in range(total_lists):
        owner = slot_ref[t] // local_lists
        place = second_place(owner, owners)
        spot = place * local_lists + slot_ref[t] % local_lists
        position = jnp.where(probes == t, spot.astype(jnp.float32), position)
    lists = lax.broadcasted_iota(jnp.int32, (total_lists, query_count), 0)
    named = [lists == probes[p : p + 1] for p in range(probe_count)]
    counts = functools.reduce(jnp.add, [n.astype(jnp.float32) for n in named])
    square = (query_count, query_count)
    before = lax.broadcasted_iota(jnp.int32, square, 0) < lax.broadcasted_iota(
        jnp.int32, square, 1
    )
    earlier = contract(
        counts.astype(jnp.bfloat16), before.astype(jnp.float32).astype(jnp.bfloat16), ((1,), (0,))
    )
    rank = jnp.concatenate(
        [jnp.sum(jnp.where(n, earlier, 0.0), axis=0, keepdims=True) for n in named], axis=0
    )
    rows = probe_count * cand_count
    row = lax.broadcasted_iota(jnp.int32, (rows, probe_count), 0)
    lane = lax.broadcasted_iota(jnp.int32, (rows, probe_count), 1)
    spread = (row // cand_count == lane).astype(jnp.float32).astype(jnp.bfloat16)
    value = contract(spread, position.astype(jnp.bfloat16), ((1,), (0,))) * (
        cand_count * capacity
    ) + contract(spread, rank.astype(jnp.bfloat16), ((1,), (0,)))
    shift = (lax.broadcasted_iota(jnp.int32, value.shape, 0) % cand_count) * capacity
    return value.astype(jnp.int32) + shift


def row_norms(list_slot, probes, corpus, local_lists, cand_count, capacity):
    total_rows, features = corpus.shape
    list_length = total_rows // local_lists
    chunk = min(list_length, 256)
    staged = staged_rows(local_lists, list_length)
    query_count, probe_count = probes.shape
    whole = pl.BlockSpec(memory_space=pltpu.VMEM)
    return pl.pallas_call(
        functools.partial(norm_kernel, (cand_count, capacity, chunk)),
        out_shape=(
            pltpu.VMEM((staged, features), corpus.dtype),
            jax.ShapeDtypeStruct((local_lists, list_length), jnp.float32),
            jax.ShapeDtypeStruct((probe_count * cand_count, query_count), jnp.int32),
        ),
        in_specs=[
            pl.BlockSpec(memory_space=pltpu.HBM),
            whole,
            pl.BlockSpec(memory_space=pltpu.HBM),
        ],
        out_specs=(whole, whole, whole),
        scratch_shapes=[
            pltpu.VMEM((max(total_rows - staged, 16), features), corpus.dtype),
            pltpu.VMEM((total_rows, 2 * LANES), jnp.bfloat16),
            pltpu.SMEM(list_slot.shape, list_slot.dtype),
            pltpu.SemaphoreType.DMA((local_lists + 1,)),
            pltpu.SemaphoreType.DMA,
        ],
        compiler_params=pltpu.CompilerParams(vmem_limit_bytes=24 * MIB),
        cost_estimate=pl.CostEstimate(
            flops=2 * corpus.size, bytes_accessed=2 * corpus.size, transcendentals=0
        ),
    )(in_hbm(list_slot), in_hbm(probes.T), in_hbm(corpus))


def score_kernel(
    sizes, me_ref, slot_ref, corpus_ref, staged_ref, inv_ref, message_ref, out_ref, held, picked, sems
):
    owners, query_count, probe_count, cand_count, capacity, streams = sizes
    total_rows, features = corpus_ref.shape
    local_lists, list_length = inv_ref.shape
    staged = staged_ref.shape[0]
    total = owners * query_count
    room = owners * capacity
    step = capacity * cand_count

    def copy(begin, end):
        return pltpu.make_async_copy(
            corpus_ref.at[begin:end],
            held.at[begin - staged : end - staged],
            sems.at[streams.index((begin, end))],
        )

    for i, (begin, end) in enumerate(streams):
        copy(begin, end).start(priority=i % 2)

    columns = [
        jnp.concatenate(
            [message_ref[s, j : j + query_count, :] for s in range(owners)], axis=0
        )
        for j in range(0, query_count * (features // LANES), query_count)
    ]
    queries = jnp.concatenate(columns, axis=1)
    squares = functools.reduce(jnp.add, [c.astype(jnp.float32) ** 2 for c in columns])
    height = message_ref.shape[1]
    tiles = [
        message_ref[s, height - probe_count :, :].astype(jnp.float32) for s in range(owners)
    ]
    probes, *cands = [
        jnp.concatenate([t[:, i : i + query_count] for t in tiles], axis=1)
        for i in range(0, query_count * (1 + cand_count), query_count)
    ]
    inv_query = lax.rsqrt(row_sums(squares) / features + epsilon)

    slots = slot_ref[...]
    names = lax.broadcasted_iota(jnp.int32, slots.shape, 1).astype(jnp.float32)
    first = me_ref[0] * local_lists
    hits, wanted = [], []
    for l in range(local_lists):
        name = jnp.sum(jnp.where(slots == first + l, names, 0.0), axis=1, keepdims=True)
        named = probes == name
        hits.append(jnp.sum(named.astype(jnp.float32), axis=0, keepdims=True))
        wanted.append(
            [jnp.sum(jnp.where(named, c, 0.0), axis=0, keepdims=True) for c in cands]
        )
    hit = jnp.concatenate(hits, axis=0)

    span = min(total, LANES)
    earlier = lax.broadcasted_iota(jnp.int32, (span, span), 0)
    later = lax.broadcasted_iota(jnp.int32, (span, span), 1)
    before = (earlier < later) & (earlier // query_count == later // query_count)
    before = before.astype(jnp.float32).astype(jnp.bfloat16)
    hit_low = hit.astype(jnp.bfloat16)
    rank = jnp.concatenate(
        [
            contract(hit_low[:, j : j + span], before, ((1,), (0,)))
            for j in range(0, total, span)
        ],
        axis=1,
    )
    source = lax.broadcasted_iota(jnp.int32, (1, total), 1) // query_count
    source = second_place((source + owners // 2) % owners, owners) * capacity
    target = jnp.where(hit > 0.5, rank.astype(jnp.int32) + source, -1)

    places = lax.broadcasted_iota(jnp.int32, (room, total), 0)
    picks = [(places == target[l : l + 1]).astype(jnp.float32) for l in range(local_lists)]
    pick = jnp.concatenate(picks, axis=0).astype(jnp.bfloat16)
    picked[...] = contract(pick, queries, ((1,), (0,))).astype(jnp.bfloat16)
    scales = [jnp.sum(p * inv_query, axis=1, keepdims=True) for p in picks]
    blocks = [
        [jnp.sum(p * w, axis=1, keepdims=True) for w in wanted[l]] for l, p in enumerate(picks)
    ]

    for l in range(local_lists):
        rows = picked[l * room : (l + 1) * room, :]
        chosen = [jnp.zeros((room, BLOCK), jnp.float32) for _ in range(cand_count)]
        row = l * list_length
        while row < (l + 1) * list_length:
            if row < staged:
                end = min(row + 512, staged, (l + 1) * list_length)
                values = staged_ref[row:end, :]
            else:
                if row in dict(streams):
                    copy(row, dict(streams)[row]).wait()
                end = min(row + 512, (l + 1) * list_length)
                values = held[row - staged : end - staged, :]
            products = contract(rows, values, ((1,), (1,)))
            first = row - l * list_length
            scaled = products * scales[l] * inv_ref[l : l + 1, first : first + end - row]
            for j in range(0, end - row, BLOCK):
                piece = scaled[:, j : j + BLOCK]
                chosen = [
                    jnp.where(block == (first + j) // BLOCK, piece, old)
                    for block, old in zip(blocks[l], chosen)
                ]
            row = end
        out_ref[:, l * step : (l + 1) * step, :] = jnp.concatenate(
            [c.reshape(owners, capacity, BLOCK) for c in chosen], axis=1
        ).astype(jnp.bfloat16)


def stream_ranges(local_lists, list_length):
    row, end = staged_rows(local_lists, list_length), local_lists * list_length
    ranges = []
    while row < end:
        to = min(row + 512, (row // list_length + 1) * list_length)
        ranges.append((row, to))
        row = to
    return tuple(ranges)


def block_scores(sizes, me, list_slot, corpus, staged, inv_rows, messages):
    owners, query_count, probe_count, cand_count, capacity = sizes
    local_lists, list_length = inv_rows.shape
    total_rows, features = corpus.shape
    streams = stream_ranges(local_lists, list_length)
    whole = pl.BlockSpec(memory_space=pltpu.VMEM)
    return pl.pallas_call(
        functools.partial(score_kernel, sizes + (streams,)),
        out_shape=jax.ShapeDtypeStruct(
            (owners, local_lists * cand_count * capacity, BLOCK), jnp.bfloat16
        ),
        in_specs=[
            pl.BlockSpec(memory_space=pltpu.SMEM),
            whole,
            pl.BlockSpec(memory_space=pltpu.HBM),
            whole,
            whole,
            whole,
        ],
        out_specs=whole,
        scratch_shapes=[
            pltpu.VMEM((max(total_rows - staged.shape[0], 16), features), corpus.dtype),
            pltpu.VMEM((local_lists * owners * capacity, features), corpus.dtype),
            pltpu.SemaphoreType.DMA((max(len(streams), 1),)),
        ],
        compiler_params=pltpu.CompilerParams(vmem_limit_bytes=40 * MIB),
        cost_estimate=pl.CostEstimate(
            flops=2 * owners * capacity * corpus.size,
            bytes_accessed=2 * corpus.size,
            transcendentals=0,
        ),
    )(me, list_slot, in_hbm(corpus), in_vmem(staged), inv_rows, messages)


def place_kernel(column_ref, returned_ref, out_ref):
    returned = returned_ref[...].reshape(-1, returned_ref.shape[-1])
    each, query_count = column_ref.shape
    column = column_ref[...]
    lanes = lax.broadcasted_iota(jnp.int32, (each, returned.shape[0]), 1)
    pick = jnp.concatenate(
        [(lanes == column[:, i : i + 1]).astype(jnp.float32) for i in range(query_count)], axis=0
    ).astype(jnp.bfloat16)
    out_ref[...] = contract(pick, returned, ((1,), (0,))).astype(jnp.bfloat16)


def place(column, returned):
    whole = pl.BlockSpec(memory_space=pltpu.VMEM)
    return pl.pallas_call(
        place_kernel,
        out_shape=jax.ShapeDtypeStruct((column.size, BLOCK), jnp.bfloat16),
        in_specs=[whole] * 2,
        out_specs=whole,
        compiler_params=pltpu.CompilerParams(vmem_limit_bytes=24 * MIB),
    )(column, returned)


def message_kernel(
    queries_ref, probes_ref, cand_ref, out_ref, queries_vmem, probes_vmem, cand_vmem, sems
):
    owners, height, lanes = out_ref.shape
    query_count, features = queries_ref.shape
    probe_count, cand_count, _ = cand_ref.shape
    pairs = (
        (probes_ref, probes_vmem),
        (cand_ref, cand_vmem),
        (queries_ref, queries_vmem),
    )
    copies = [
        pltpu.make_async_copy(source, target, sems.at[i])
        for i, (source, target) in enumerate(pairs)
    ]
    for c in copies:
        c.start()
    copies[0].wait()
    copies[1].wait()
    pieces = [probes_vmem[...]] + [cand_vmem[:, c, :] for c in range(cand_count)]
    spare = lanes - len(pieces) * query_count
    pieces.append(jnp.zeros((probe_count, spare), jnp.int32))
    indices = jnp.concatenate(pieces, axis=1).astype(jnp.float32).astype(jnp.bfloat16)
    for k in range(owners):
        out_ref[k, height - probe_count :, :] = indices
    copies[2].wait()
    for j in range(features // lanes):
        column = queries_vmem[:, j * lanes : (j + 1) * lanes]
        for k in range(owners):
            out_ref[k, j * query_count : (j + 1) * query_count, :] = column


def make_message(queries, probes, cand, owners):
    query_count, features = queries.shape
    probe_count = probes.shape[1]
    height = query_count * (features // LANES) + probe_count
    whole = pl.BlockSpec(memory_space=pltpu.VMEM)
    return pl.pallas_call(
        message_kernel,
        out_shape=jax.ShapeDtypeStruct((owners, height, LANES), queries.dtype),
        in_specs=[pl.BlockSpec(memory_space=pltpu.HBM)] * 3,
        out_specs=whole,
        scratch_shapes=[
            pltpu.VMEM(queries.shape, queries.dtype),
            pltpu.VMEM(probes.shape[::-1], probes.dtype),
            pltpu.VMEM(cand.transpose(1, 2, 0).shape, cand.dtype),
            pltpu.SemaphoreType.DMA((3,)),
        ],
        compiler_params=pltpu.CompilerParams(vmem_limit_bytes=24 * MIB),
    )(in_hbm(queries), in_hbm(probes.T), in_hbm(cand.transpose(1, 2, 0)))


def on_device(queries, corpus, list_slot, probes, cand):
    owners = lax.axis_size("lists")
    query_count, features = queries.shape
    probe_count = probes.shape[1]
    cand_count = cand.shape[2]
    local_lists = corpus.shape[0]
    corpus = corpus.reshape(-1, features)
    total_lists = list_slot.shape[0]
    pair_count = query_count * probe_count
    capacity = min(query_count, max(2, (2 * pair_count + total_lists - 1) // total_lists))
    sizes = (owners, query_count, probe_count, cand_count, capacity)
    me = lax.axis_index("lists").astype(jnp.int32)

    message = make_message(queries, probes, cand, owners)
    messages = exchange(message, first_order(owners))
    staged, inv_rows, column = row_norms(
        list_slot, probes, corpus, local_lists, cand_count, capacity
    )
    scores = block_scores(sizes, me.reshape(1), list_slot[None, :], corpus, staged, inv_rows, messages)
    returned = exchange(scores, second_order(owners))
    chosen = place(column, returned)
    return chosen.reshape(query_count, probe_count, cand_count, BLOCK)


def solution(mesh):
    placed = (
        P(("groups", "lists", "rep"), None),
        P(("groups", "lists"), None, None),
        P("groups"),
        P(("groups", "lists", "rep"), None),
        P(("groups", "lists", "rep"), None, None),
    )
    return jax.shard_map(
        on_device,
        mesh=mesh,
        in_specs=placed,
        out_specs=P(("groups", "lists", "rep"), None, None, None),
        check_vma=False,
    )
```

```python
import functools

import jax
import jax.numpy as jnp
from jax import lax
from jax.experimental import pallas as pl
from jax.experimental.pallas import tpu as pltpu
from jax.sharding import PartitionSpec as P

BLOCK = 128
LANES = 128
MIB = 2**20

epsilon = 1e-06


def contract(a, b, dims, precision=None):
    return lax.dot_general(
        a, b, (dims, ((), ())), precision=precision, preferred_element_type=jnp.float32
    )


def in_hbm(value):
    return pltpu.with_memory_space_constraint(value, pltpu.HBM)


def in_vmem(value):
    return pltpu.with_memory_space_constraint(value, pltpu.VMEM)


def exchange(value):
    owners, reps = lax.axis_size("lists"), lax.axis_size("rep")
    groups = [
        [(owners // 2 + direction(rep) * j) % owners * reps + rep for j in range(owners)]
        for rep in range(reps)
    ]
    return lax.all_to_all(
        value, ("lists", "rep"), split_axis=0, concat_axis=0, axis_index_groups=groups, tiled=True
    )


def direction(rep):
    return 1 - rep % 2 * 2


def staged_rows(local_lists, list_length):
    return min(local_lists * list_length, list_length + list_length // 2)


def norm_kernel(
    sizes,
    turn_ref,
    slot_ref,
    probes_ref,
    corpus_ref,
    staged_ref,
    inv_ref,
    column_ref,
    held,
    parts,
    slots,
    sems,
    slot_sem,
):
    cand_count, capacity, chunk = sizes
    total_rows, features = corpus_ref.shape
    local_lists, list_length = inv_ref.shape
    staged = staged_ref.shape[0]

    cuts = sorted(set(range(0, total_rows + 1, list_length)) | {staged})
    ranges = list(zip(cuts[:-1], cuts[1:]))

    def place(row, end):
        if row < staged:
            return staged_ref.at[row:end]
        return held.at[row - staged : end - staged]

    def copy(row, end):
        return pltpu.make_async_copy(
            corpus_ref.at[row:end], place(row, end), sems.at[cuts.index(row)]
        )

    slot_copy = pltpu.make_async_copy(slot_ref, slots, slot_sem)
    slot_copy.start()
    for row, end in ranges:
        copy(row, end).start()
    slot_copy.wait()
    column_ref[...] = result_columns(
        cand_count, capacity, local_lists, turn_ref[0], slots, probes_ref[...]
    )
    ones = jnp.ones((8, 2 * LANES), jnp.bfloat16)
    for l in range(local_lists):
        for begin, to in ranges:
            if begin // list_length != l:
                continue
            copy(begin, to).wait()
            for row in range(begin, to, chunk):
                end = min(row + chunk, to)
                wide = place(row, end)[...].astype(jnp.float32)
                squares = functools.reduce(
                    jnp.add, [wide[:, j : j + LANES] ** 2 for j in range(0, features, LANES)]
                )
                high = squares.astype(jnp.bfloat16)
                low = (squares - high.astype(jnp.float32)).astype(jnp.bfloat16)
                parts[row:end, :LANES] = high
                parts[row:end, LANES:] = low
        whole = parts[l * list_length : (l + 1) * list_length, :]
        sums = contract(ones, whole, ((1,), (1,)))[:1]
        inv_ref[l : l + 1, :] = lax.rsqrt(sums / features + epsilon) * features ** (-0.5)


def row_sums(parts):
    high = parts.astype(jnp.bfloat16)
    low = (parts - high.astype(jnp.float32)).astype(jnp.bfloat16)
    terms = jnp.concatenate([high, low], axis=1)
    ones = jnp.ones((8, terms.shape[1]), jnp.bfloat16)
    return contract(ones, terms, ((1,), (1,)))[:1]


def result_columns(cand_count, capacity, local_lists, turn, slot_ref, probes):
    probe_count, query_count = probes.shape
    total_lists = slot_ref.shape[0]
    owners = total_lists // local_lists
    position = jnp.zeros(probes.shape, jnp.float32)
    for t in range(total_lists):
        owner = slot_ref[t] // local_lists
        place = (turn * (owner - owners // 2) + owners) % owners
        spot = place * local_lists + slot_ref[t] % local_lists
        position = jnp.where(probes == t, spot.astype(jnp.float32), position)
    lists = lax.broadcasted_iota(jnp.int32, (total_lists, query_count), 0)
    named = [lists == probes[p : p + 1] for p in range(probe_count)]
    counts = functools.reduce(jnp.add, [n.astype(jnp.float32) for n in named])
    square = (query_count, query_count)
    before = lax.broadcasted_iota(jnp.int32, square, 0) < lax.broadcasted_iota(
        jnp.int32, square, 1
    )
    earlier = contract(
        counts.astype(jnp.bfloat16), before.astype(jnp.float32).astype(jnp.bfloat16), ((1,), (0,))
    )
    rank = jnp.concatenate(
        [jnp.sum(jnp.where(n, earlier, 0.0), axis=0, keepdims=True) for n in named], axis=0
    )
    rows = probe_count * cand_count
    row = lax.broadcasted_iota(jnp.int32, (rows, probe_count), 0)
    lane = lax.broadcasted_iota(jnp.int32, (rows, probe_count), 1)
    spread = (row // cand_count == lane).astype(jnp.float32).astype(jnp.bfloat16)
    value = contract(spread, position.astype(jnp.bfloat16), ((1,), (0,))) * (
        cand_count * capacity
    ) + contract(spread, rank.astype(jnp.bfloat16), ((1,), (0,)))
    shift = (lax.broadcasted_iota(jnp.int32, value.shape, 0) % cand_count) * capacity
    return value.astype(jnp.int32) + shift


def row_norms(turn, list_slot, probes, corpus, local_lists, cand_count, capacity):
    total_rows, features = corpus.shape
    list_length = total_rows // local_lists
    chunk = min(list_length, 256)
    staged = staged_rows(local_lists, list_length)
    query_count, probe_count = probes.shape
    whole = pl.BlockSpec(memory_space=pltpu.VMEM)
    return pl.pallas_call(
        functools.partial(norm_kernel, (cand_count, capacity, chunk)),
        out_shape=(
            pltpu.VMEM((staged, features), corpus.dtype),
            jax.ShapeDtypeStruct((local_lists, list_length), jnp.float32),
            jax.ShapeDtypeStruct((probe_count * cand_count, query_count), jnp.int32),
        ),
        in_specs=[
            pl.BlockSpec(memory_space=pltpu.SMEM),
            pl.BlockSpec(memory_space=pltpu.HBM),
            whole,
            pl.BlockSpec(memory_space=pltpu.HBM),
        ],
        out_specs=(whole, whole, whole),
        scratch_shapes=[
            pltpu.VMEM((max(total_rows - staged, 16), features), corpus.dtype),
            pltpu.VMEM((total_rows, 2 * LANES), jnp.bfloat16),
            pltpu.SMEM(list_slot.shape, list_slot.dtype),
            pltpu.SemaphoreType.DMA((local_lists + 1,)),
            pltpu.SemaphoreType.DMA,
        ],
        compiler_params=pltpu.CompilerParams(vmem_limit_bytes=24 * MIB),
        cost_estimate=pl.CostEstimate(
            flops=2 * corpus.size, bytes_accessed=2 * corpus.size, transcendentals=0
        ),
    )(turn, in_hbm(list_slot), in_hbm(probes.T), in_hbm(corpus))


def score_kernel(
    sizes, me_ref, slot_ref, corpus_ref, staged_ref, inv_ref, message_ref, out_ref, held, picked, sems
):
    owners, query_count, probe_count, cand_count, capacity, streams = sizes
    total_rows, features = corpus_ref.shape
    local_lists, list_length = inv_ref.shape
    staged = staged_ref.shape[0]
    total = owners * query_count
    room = owners * capacity
    step = capacity * cand_count

    def copy(begin, end):
        return pltpu.make_async_copy(
            corpus_ref.at[begin:end],
            held.at[begin - staged : end - staged],
            sems.at[streams.index((begin, end))],
        )

    for begin, end in streams:
        copy(begin, end).start()

    columns = [
        jnp.concatenate(
            [message_ref[s, j : j + query_count, :] for s in range(owners)], axis=0
        )
        for j in range(0, query_count * (features // LANES), query_count)
    ]
    queries = jnp.concatenate(columns, axis=1)
    squares = functools.reduce(jnp.add, [c.astype(jnp.float32) ** 2 for c in columns])
    height = message_ref.shape[1]
    tiles = [
        message_ref[s, height - probe_count :, :].astype(jnp.float32) for s in range(owners)
    ]
    probes, *cands = [
        jnp.concatenate([t[:, i : i + query_count] for t in tiles], axis=1)
        for i in range(0, query_count * (1 + cand_count), query_count)
    ]
    inv_query = lax.rsqrt(row_sums(squares) / features + epsilon)

    slots = slot_ref[...]
    names = lax.broadcasted_iota(jnp.int32, slots.shape, 1).astype(jnp.float32)
    first = me_ref[0] * local_lists
    hits, wanted = [], []
    for l in range(local_lists):
        name = jnp.sum(jnp.where(slots == first + l, names, 0.0), axis=1, keepdims=True)
        named = probes == name
        hits.append(jnp.sum(named.astype(jnp.float32), axis=0, keepdims=True))
        wanted.append(
            [jnp.sum(jnp.where(named, c, 0.0), axis=0, keepdims=True) for c in cands]
        )
    hit = jnp.concatenate(hits, axis=0)

    span = min(total, LANES)
    earlier = lax.broadcasted_iota(jnp.int32, (span, span), 0)
    later = lax.broadcasted_iota(jnp.int32, (span, span), 1)
    before = (earlier < later) & (earlier // query_count == later // query_count)
    before = before.astype(jnp.float32).astype(jnp.bfloat16)
    hit_low = hit.astype(jnp.bfloat16)
    rank = jnp.concatenate(
        [
            contract(hit_low[:, j : j + span], before, ((1,), (0,)))
            for j in range(0, total, span)
        ],
        axis=1,
    )
    source = (lax.broadcasted_iota(jnp.int32, (1, total), 1) // query_count) * capacity
    target = jnp.where(hit > 0.5, rank.astype(jnp.int32) + source, -1)

    places = lax.broadcasted_iota(jnp.int32, (room, total), 0)
    picks = [(places == target[l : l + 1]).astype(jnp.float32) for l in range(local_lists)]
    pick = jnp.concatenate(picks, axis=0).astype(jnp.bfloat16)
    picked[...] = contract(pick, queries, ((1,), (0,))).astype(jnp.bfloat16)
    scales = [jnp.sum(p * inv_query, axis=1, keepdims=True) for p in picks]
    blocks = [
        [jnp.sum(p * w, axis=1, keepdims=True) for w in wanted[l]] for l, p in enumerate(picks)
    ]

    for l in range(local_lists):
        rows = picked[l * room : (l + 1) * room, :]
        chosen = [jnp.zeros((room, BLOCK), jnp.float32) for _ in range(cand_count)]
        row = l * list_length
        while row < (l + 1) * list_length:
            if row < staged:
                end = min(row + 512, staged, (l + 1) * list_length)
                values = staged_ref[row:end, :]
            else:
                if row in dict(streams):
                    copy(row, dict(streams)[row]).wait()
                end = min(row + 512, (l + 1) * list_length)
                values = held[row - staged : end - staged, :]
            products = contract(rows, values, ((1,), (1,)))
            first = row - l * list_length
            scaled = products * scales[l] * inv_ref[l : l + 1, first : first + end - row]
            for j in range(0, end - row, BLOCK):
                piece = scaled[:, j : j + BLOCK]
                chosen = [
                    jnp.where(block == (first + j) // BLOCK, piece, old)
                    for block, old in zip(blocks[l], chosen)
                ]
            row = end
        out_ref[:, l * step : (l + 1) * step, :] = jnp.concatenate(
            [c.reshape(owners, capacity, BLOCK) for c in chosen], axis=1
        ).astype(jnp.bfloat16)


def stream_ranges(local_lists, list_length):
    row, end = staged_rows(local_lists, list_length), local_lists * list_length
    ranges = []
    while row < end:
        to = min(row + 512, (row // list_length + 1) * list_length)
        ranges.append((row, to))
        row = to
    return tuple(ranges)


def block_scores(sizes, me, list_slot, corpus, staged, inv_rows, messages):
    owners, query_count, probe_count, cand_count, capacity = sizes
    local_lists, list_length = inv_rows.shape
    total_rows, features = corpus.shape
    streams = stream_ranges(local_lists, list_length)
    whole = pl.BlockSpec(memory_space=pltpu.VMEM)
    return pl.pallas_call(
        functools.partial(score_kernel, sizes + (streams,)),
        out_shape=jax.ShapeDtypeStruct(
            (owners, local_lists * cand_count * capacity, BLOCK), jnp.bfloat16
        ),
        in_specs=[
            pl.BlockSpec(memory_space=pltpu.SMEM),
            whole,
            pl.BlockSpec(memory_space=pltpu.HBM),
            whole,
            whole,
            whole,
        ],
        out_specs=whole,
        scratch_shapes=[
            pltpu.VMEM((max(total_rows - staged.shape[0], 16), features), corpus.dtype),
            pltpu.VMEM((local_lists * owners * capacity, features), corpus.dtype),
            pltpu.SemaphoreType.DMA((max(len(streams), 1),)),
        ],
        compiler_params=pltpu.CompilerParams(vmem_limit_bytes=40 * MIB),
        cost_estimate=pl.CostEstimate(
            flops=2 * owners * capacity * corpus.size,
            bytes_accessed=2 * corpus.size,
            transcendentals=0,
        ),
    )(me, list_slot, in_hbm(corpus), in_vmem(staged), inv_rows, messages)


def place_kernel(column_ref, returned_ref, out_ref):
    returned = returned_ref[...].reshape(-1, returned_ref.shape[-1])
    each, query_count = column_ref.shape
    column = column_ref[...]
    lanes = lax.broadcasted_iota(jnp.int32, (each, returned.shape[0]), 1)
    pick = jnp.concatenate(
        [(lanes == column[:, i : i + 1]).astype(jnp.float32) for i in range(query_count)], axis=0
    ).astype(jnp.bfloat16)
    out_ref[...] = contract(pick, returned, ((1,), (0,))).astype(jnp.bfloat16)


def place(column, returned):
    whole = pl.BlockSpec(memory_space=pltpu.VMEM)
    return pl.pallas_call(
        place_kernel,
        out_shape=jax.ShapeDtypeStruct((column.size, BLOCK), jnp.bfloat16),
        in_specs=[whole] * 2,
        out_specs=whole,
        compiler_params=pltpu.CompilerParams(vmem_limit_bytes=24 * MIB),
    )(column, returned)


def message_kernel(
    queries_ref, probes_ref, cand_ref, out_ref, queries_vmem, probes_vmem, cand_vmem, sems
):
    owners, height, lanes = out_ref.shape
    query_count, features = queries_ref.shape
    probe_count, cand_count, _ = cand_ref.shape
    pairs = (
        (probes_ref, probes_vmem),
        (cand_ref, cand_vmem),
        (queries_ref, queries_vmem),
    )
    copies = [
        pltpu.make_async_copy(source, target, sems.at[i])
        for i, (source, target) in enumerate(pairs)
    ]
    for c in copies:
        c.start()
    copies[0].wait()
    copies[1].wait()
    pieces = [probes_vmem[...]] + [cand_vmem[:, c, :] for c in range(cand_count)]
    spare = lanes - len(pieces) * query_count
    pieces.append(jnp.zeros((probe_count, spare), jnp.int32))
    indices = jnp.concatenate(pieces, axis=1).astype(jnp.float32).astype(jnp.bfloat16)
    for k in range(owners):
        out_ref[k, height - probe_count :, :] = indices
    copies[2].wait()
    for j in range(features // lanes):
        column = queries_vmem[:, j * lanes : (j + 1) * lanes]
        for k in range(owners):
            out_ref[k, j * query_count : (j + 1) * query_count, :] = column


def make_message(queries, probes, cand, owners):
    query_count, features = queries.shape
    probe_count = probes.shape[1]
    height = query_count * (features // LANES) + probe_count
    whole = pl.BlockSpec(memory_space=pltpu.VMEM)
    return pl.pallas_call(
        message_kernel,
        out_shape=jax.ShapeDtypeStruct((owners, height, LANES), queries.dtype),
        in_specs=[pl.BlockSpec(memory_space=pltpu.HBM)] * 3,
        out_specs=whole,
        scratch_shapes=[
            pltpu.VMEM(queries.shape, queries.dtype),
            pltpu.VMEM(probes.shape[::-1], probes.dtype),
            pltpu.VMEM(cand.transpose(1, 2, 0).shape, cand.dtype),
            pltpu.SemaphoreType.DMA((3,)),
        ],
        compiler_params=pltpu.CompilerParams(vmem_limit_bytes=24 * MIB),
    )(in_hbm(queries), in_hbm(probes.T), in_hbm(cand.transpose(1, 2, 0)))


def on_device(queries, corpus, list_slot, probes, cand):
    owners = lax.axis_size("lists")
    query_count, features = queries.shape
    probe_count = probes.shape[1]
    cand_count = cand.shape[2]
    local_lists = corpus.shape[0]
    corpus = corpus.reshape(-1, features)
    total_lists = list_slot.shape[0]
    pair_count = query_count * probe_count
    capacity = min(query_count, max(2, (2 * pair_count + total_lists - 1) // total_lists))
    sizes = (owners, query_count, probe_count, cand_count, capacity)
    me = lax.axis_index("lists").astype(jnp.int32)

    turn = direction(lax.axis_index("rep").astype(jnp.int32)).reshape(1)
    message = make_message(queries, probes, cand, owners)
    messages = exchange(message)
    staged, inv_rows, column = row_norms(
        turn, list_slot, probes, corpus, local_lists, cand_count, capacity
    )
    scores = block_scores(sizes, me.reshape(1), list_slot[None, :], corpus, staged, inv_rows, messages)
    returned = exchange(scores)
    chosen = place(column, returned)
    return chosen.reshape(query_count, probe_count, cand_count, BLOCK)


def solution(mesh):
    placed = (
        P(("groups", "lists", "rep"), None),
        P(("groups", "lists"), None, None),
        P("groups"),
        P(("groups", "lists", "rep"), None),
        P(("groups", "lists", "rep"), None, None),
    )
    return jax.shard_map(
        on_device,
        mesh=mesh,
        in_specs=placed,
        out_specs=P(("groups", "lists", "rep"), None, None, None),
        check_vma=False,
    )
```

```python
import functools

import jax
import jax.numpy as jnp
from jax import lax
from jax.experimental import pallas as pl
from jax.experimental.pallas import tpu as pltpu
from jax.sharding import PartitionSpec as P

BLOCK = 128
LANES = 128
MIB = 2**20

epsilon = 1e-06


def contract(a, b, dims, precision=None):
    return lax.dot_general(
        a, b, (dims, ((), ())), precision=precision, preferred_element_type=jnp.float32
    )


def in_hbm(value):
    return pltpu.with_memory_space_constraint(value, pltpu.HBM)


def in_vmem(value):
    return pltpu.with_memory_space_constraint(value, pltpu.VMEM)


def first_order(owners):
    return [(i + owners // 2) % owners for i in range(owners)]


def second_order(owners):
    if owners > 16:
        return first_order(owners)
    leader, ends = owners // 2, owners // 4
    return sorted(
        range(owners), key=lambda i: (i != leader, ends <= i < owners - ends, i % 2, i)
    )


def second_place(owner, owners):
    if owners > 16:
        return (owner + owners // 2) % owners
    place = owner
    for j, i in enumerate(second_order(owners)):
        place = jnp.where(owner == i, j, place)
    return place


def exchange(value, order):
    return lax.all_to_all(
        value, "lists", split_axis=0, concat_axis=0, axis_index_groups=[order], tiled=True
    )


def staged_rows(local_lists, list_length):
    return min(local_lists * list_length, list_length + list_length // 2)


def norm_kernel(
    sizes,
    slot_ref,
    probes_ref,
    corpus_ref,
    staged_ref,
    inv_ref,
    column_ref,
    held,
    parts,
    slots,
    sems,
    slot_sem,
):
    cand_count, capacity, chunk = sizes
    total_rows, features = corpus_ref.shape
    local_lists, list_length = inv_ref.shape
    staged = staged_ref.shape[0]

    cuts = sorted(set(range(0, total_rows + 1, min(list_length, 512))) | {staged})
    ranges = list(zip(cuts[:-1], cuts[1:]))

    def place(row, end):
        if row < staged:
            return staged_ref.at[row:end]
        return held.at[row - staged : end - staged]

    def copy(row, end):
        return pltpu.make_async_copy(
            corpus_ref.at[row:end], place(row, end), sems.at[cuts.index(row)]
        )

    slot_copy = pltpu.make_async_copy(slot_ref, slots, slot_sem)
    slot_copy.start()
    for row, end in ranges:
        copy(row, end).start()
    slot_copy.wait()
    column_ref[...] = result_columns(cand_count, capacity, local_lists, slots, probes_ref[...])
    ones = jnp.ones((8, 2 * LANES), jnp.bfloat16)
    for l in range(local_lists):
        for begin, to in ranges:
            if begin // list_length != l:
                continue
            copy(begin, to).wait()
            for row in range(begin, to, chunk):
                end = min(row + chunk, to)
                wide = place(row, end)[...].astype(jnp.float32)
                squares = functools.reduce(
                    jnp.add, [wide[:, j : j + LANES] ** 2 for j in range(0, features, LANES)]
                )
                high = squares.astype(jnp.bfloat16)
                low = (squares - high.astype(jnp.float32)).astype(jnp.bfloat16)
                parts[row:end, :LANES] = high
                parts[row:end, LANES:] = low
        whole = parts[l * list_length : (l + 1) * list_length, :]
        sums = contract(ones, whole, ((1,), (1,)))[:1]
        inv_ref[l : l + 1, :] = lax.rsqrt(sums / features + epsilon) * features ** (-0.5)


def row_sums(parts):
    high = parts.astype(jnp.bfloat16)
    low = (parts - high.astype(jnp.float32)).astype(jnp.bfloat16)
    terms = jnp.concatenate([high, low], axis=1)
    ones = jnp.ones((8, terms.shape[1]), jnp.bfloat16)
    return contract(ones, terms, ((1,), (1,)))[:1]


def result_columns(cand_count, capacity, local_lists, slot_ref, probes):
    probe_count, query_count = probes.shape
    total_lists = slot_ref.shape[0]
    owners = total_lists // local_lists
    position = jnp.zeros(probes.shape, jnp.float32)
    for t in range(total_lists):
        owner = slot_ref[t] // local_lists
        place = second_place(owner, owners)
        spot = place * local_lists + slot_ref[t] % local_lists
        position = jnp.where(probes == t, spot.astype(jnp.float32), position)
    lists = lax.broadcasted_iota(jnp.int32, (total_lists, query_count), 0)
    named = [lists == probes[p : p + 1] for p in range(probe_count)]
    counts = functools.reduce(jnp.add, [n.astype(jnp.float32) for n in named])
    square = (query_count, query_count)
    before = lax.broadcasted_iota(jnp.int32, square, 0) < lax.broadcasted_iota(
        jnp.int32, square, 1
    )
    earlier = contract(
        counts.astype(jnp.bfloat16), before.astype(jnp.float32).astype(jnp.bfloat16), ((1,), (0,))
    )
    rank = jnp.concatenate(
        [jnp.sum(jnp.where(n, earlier, 0.0), axis=0, keepdims=True) for n in named], axis=0
    )
    rows = probe_count * cand_count
    row = lax.broadcasted_iota(jnp.int32, (rows, probe_count), 0)
    lane = lax.broadcasted_iota(jnp.int32, (rows, probe_count), 1)
    spread = (row // cand_count == lane).astype(jnp.float32).astype(jnp.bfloat16)
    value = contract(spread, position.astype(jnp.bfloat16), ((1,), (0,))) * (
        cand_count * capacity
    ) + contract(spread, rank.astype(jnp.bfloat16), ((1,), (0,)))
    shift = (lax.broadcasted_iota(jnp.int32, value.shape, 0) % cand_count) * capacity
    return value.astype(jnp.int32) + shift


def row_norms(list_slot, probes, corpus, local_lists, cand_count, capacity):
    total_rows, features = corpus.shape
    list_length = total_rows // local_lists
    chunk = min(list_length, 256)
    staged = staged_rows(local_lists, list_length)
    query_count, probe_count = probes.shape
    whole = pl.BlockSpec(memory_space=pltpu.VMEM)
    return pl.pallas_call(
        functools.partial(norm_kernel, (cand_count, capacity, chunk)),
        out_shape=(
            pltpu.VMEM((staged, features), corpus.dtype),
            jax.ShapeDtypeStruct((local_lists, list_length), jnp.float32),
            jax.ShapeDtypeStruct((probe_count * cand_count, query_count), jnp.int32),
        ),
        in_specs=[
            pl.BlockSpec(memory_space=pltpu.HBM),
            whole,
            pl.BlockSpec(memory_space=pltpu.HBM),
        ],
        out_specs=(whole, whole, whole),
        scratch_shapes=[
            pltpu.VMEM((max(total_rows - staged, 16), features), corpus.dtype),
            pltpu.VMEM((total_rows, 2 * LANES), jnp.bfloat16),
            pltpu.SMEM(list_slot.shape, list_slot.dtype),
            pltpu.SemaphoreType.DMA((total_rows // min(list_length, 512) + 1,)),
            pltpu.SemaphoreType.DMA,
        ],
        compiler_params=pltpu.CompilerParams(vmem_limit_bytes=24 * MIB),
        cost_estimate=pl.CostEstimate(
            flops=2 * corpus.size, bytes_accessed=2 * corpus.size, transcendentals=0
        ),
    )(in_hbm(list_slot), in_hbm(probes.T), in_hbm(corpus))


def score_kernel(
    sizes, me_ref, slot_ref, corpus_ref, staged_ref, inv_ref, message_ref, out_ref, held, picked, sems
):
    owners, query_count, probe_count, cand_count, capacity, streams = sizes
    total_rows, features = corpus_ref.shape
    local_lists, list_length = inv_ref.shape
    staged = staged_ref.shape[0]
    total = owners * query_count
    room = owners * capacity
    step = capacity * cand_count

    def copy(begin, end):
        return pltpu.make_async_copy(
            corpus_ref.at[begin:end],
            held.at[begin - staged : end - staged],
            sems.at[streams.index((begin, end))],
        )

    for begin, end in streams:
        copy(begin, end).start()

    columns = [
        jnp.concatenate(
            [message_ref[s, j : j + query_count, :] for s in range(owners)], axis=0
        )
        for j in range(0, query_count * (features // LANES), query_count)
    ]
    queries = jnp.concatenate(columns, axis=1)
    squares = functools.reduce(jnp.add, [c.astype(jnp.float32) ** 2 for c in columns])
    height = message_ref.shape[1]
    tiles = [
        message_ref[s, height - probe_count :, :].astype(jnp.float32) for s in range(owners)
    ]
    probes, *cands = [
        jnp.concatenate([t[:, i : i + query_count] for t in tiles], axis=1)
        for i in range(0, query_count * (1 + cand_count), query_count)
    ]
    inv_query = lax.rsqrt(row_sums(squares) / features + epsilon)

    slots = slot_ref[...]
    names = lax.broadcasted_iota(jnp.int32, slots.shape, 1).astype(jnp.float32)
    first = me_ref[0] * local_lists
    hits, wanted = [], []
    for l in range(local_lists):
        name = jnp.sum(jnp.where(slots == first + l, names, 0.0), axis=1, keepdims=True)
        named = probes == name
        hits.append(jnp.sum(named.astype(jnp.float32), axis=0, keepdims=True))
        wanted.append(
            [jnp.sum(jnp.where(named, c, 0.0), axis=0, keepdims=True) for c in cands]
        )
    hit = jnp.concatenate(hits, axis=0)

    span = min(total, LANES)
    earlier = lax.broadcasted_iota(jnp.int32, (span, span), 0)
    later = lax.broadcasted_iota(jnp.int32, (span, span), 1)
    before = (earlier < later) & (earlier // query_count == later // query_count)
    before = before.astype(jnp.float32).astype(jnp.bfloat16)
    hit_low = hit.astype(jnp.bfloat16)
    rank = jnp.concatenate(
        [
            contract(hit_low[:, j : j + span], before, ((1,), (0,)))
            for j in range(0, total, span)
        ],
        axis=1,
    )
    source = lax.broadcasted_iota(jnp.int32, (1, total), 1) // query_count
    source = second_place((source + owners // 2) % owners, owners) * capacity
    target = jnp.where(hit > 0.5, rank.astype(jnp.int32) + source, -1)

    places = lax.broadcasted_iota(jnp.int32, (room, total), 0)
    picks = [(places == target[l : l + 1]).astype(jnp.float32) for l in range(local_lists)]
    pick = jnp.concatenate(picks, axis=0).astype(jnp.bfloat16)
    picked[...] = contract(pick, queries, ((1,), (0,))).astype(jnp.bfloat16)
    scales = [jnp.sum(p * inv_query, axis=1, keepdims=True) for p in picks]
    blocks = [
        [jnp.sum(p * w, axis=1, keepdims=True) for w in wanted[l]] for l, p in enumerate(picks)
    ]

    for l in range(local_lists):
        rows = picked[l * room : (l + 1) * room, :]
        chosen = [jnp.zeros((room, BLOCK), jnp.float32) for _ in range(cand_count)]
        row = l * list_length
        while row < (l + 1) * list_length:
            if row < staged:
                end = min(row + 512, staged, (l + 1) * list_length)
                values = staged_ref[row:end, :]
            else:
                if row in dict(streams):
                    copy(row, dict(streams)[row]).wait()
                end = min(row + 512, (l + 1) * list_length)
                values = held[row - staged : end - staged, :]
            products = contract(rows, values, ((1,), (1,)))
            first = row - l * list_length
            scaled = products * scales[l] * inv_ref[l : l + 1, first : first + end - row]
            for j in range(0, end - row, BLOCK):
                piece = scaled[:, j : j + BLOCK]
                chosen = [
                    jnp.where(block == (first + j) // BLOCK, piece, old)
                    for block, old in zip(blocks[l], chosen)
                ]
            row = end
        out_ref[:, l * step : (l + 1) * step, :] = jnp.concatenate(
            [c.reshape(owners, capacity, BLOCK) for c in chosen], axis=1
        ).astype(jnp.bfloat16)


def stream_ranges(local_lists, list_length):
    row, end = staged_rows(local_lists, list_length), local_lists * list_length
    ranges = []
    while row < end:
        to = (row // list_length + 1) * list_length
        if to == end and to - row > list_length // 2:
            to = end - list_length // 2
        ranges.append((row, to))
        row = to
    return tuple(ranges)


def block_scores(sizes, me, list_slot, corpus, staged, inv_rows, messages):
    owners, query_count, probe_count, cand_count, capacity = sizes
    local_lists, list_length = inv_rows.shape
    total_rows, features = corpus.shape
    streams = stream_ranges(local_lists, list_length)
    whole = pl.BlockSpec(memory_space=pltpu.VMEM)
    return pl.pallas_call(
        functools.partial(score_kernel, sizes + (streams,)),
        out_shape=jax.ShapeDtypeStruct(
            (owners, local_lists * cand_count * capacity, BLOCK), jnp.bfloat16
        ),
        in_specs=[
            pl.BlockSpec(memory_space=pltpu.SMEM),
            whole,
            pl.BlockSpec(memory_space=pltpu.HBM),
            whole,
            whole,
            whole,
        ],
        out_specs=whole,
        scratch_shapes=[
            pltpu.VMEM((max(total_rows - staged.shape[0], 16), features), corpus.dtype),
            pltpu.VMEM((local_lists * owners * capacity, features), corpus.dtype),
            pltpu.SemaphoreType.DMA((max(len(streams), 1),)),
        ],
        compiler_params=pltpu.CompilerParams(vmem_limit_bytes=40 * MIB),
        cost_estimate=pl.CostEstimate(
            flops=2 * owners * capacity * corpus.size,
            bytes_accessed=2 * corpus.size,
            transcendentals=0,
        ),
    )(me, list_slot, in_hbm(corpus), in_vmem(staged), inv_rows, messages)


def place_kernel(column_ref, returned_ref, out_ref):
    returned = returned_ref[...].reshape(-1, returned_ref.shape[-1])
    each, query_count = column_ref.shape
    column = column_ref[...]
    lanes = lax.broadcasted_iota(jnp.int32, (each, returned.shape[0]), 1)
    pick = jnp.concatenate(
        [(lanes == column[:, i : i + 1]).astype(jnp.float32) for i in range(query_count)], axis=0
    ).astype(jnp.bfloat16)
    out_ref[...] = contract(pick, returned, ((1,), (0,))).astype(jnp.bfloat16)


def place(column, returned):
    whole = pl.BlockSpec(memory_space=pltpu.VMEM)
    return pl.pallas_call(
        place_kernel,
        out_shape=jax.ShapeDtypeStruct((column.size, BLOCK), jnp.bfloat16),
        in_specs=[whole] * 2,
        out_specs=whole,
        compiler_params=pltpu.CompilerParams(vmem_limit_bytes=24 * MIB),
    )(column, returned)


def message_kernel(
    queries_ref, probes_ref, cand_ref, out_ref, queries_vmem, probes_vmem, cand_vmem, sems
):
    owners, height, lanes = out_ref.shape
    query_count, features = queries_ref.shape
    probe_count, cand_count, _ = cand_ref.shape
    pairs = (
        (probes_ref, probes_vmem),
        (cand_ref, cand_vmem),
        (queries_ref, queries_vmem),
    )
    copies = [
        pltpu.make_async_copy(source, target, sems.at[i])
        for i, (source, target) in enumerate(pairs)
    ]
    for c in copies:
        c.start()
    copies[0].wait()
    copies[1].wait()
    pieces = [probes_vmem[...]] + [cand_vmem[:, c, :] for c in range(cand_count)]
    spare = lanes - len(pieces) * query_count
    pieces.append(jnp.zeros((probe_count, spare), jnp.int32))
    indices = jnp.concatenate(pieces, axis=1).astype(jnp.float32).astype(jnp.bfloat16)
    for k in range(owners):
        out_ref[k, height - probe_count :, :] = indices
    copies[2].wait()
    for j in range(features // lanes):
        column = queries_vmem[:, j * lanes : (j + 1) * lanes]
        for k in range(owners):
            out_ref[k, j * query_count : (j + 1) * query_count, :] = column


def make_message(queries, probes, cand, owners):
    query_count, features = queries.shape
    probe_count = probes.shape[1]
    height = query_count * (features // LANES) + probe_count
    whole = pl.BlockSpec(memory_space=pltpu.VMEM)
    return pl.pallas_call(
        message_kernel,
        out_shape=jax.ShapeDtypeStruct((owners, height, LANES), queries.dtype),
        in_specs=[pl.BlockSpec(memory_space=pltpu.HBM)] * 3,
        out_specs=whole,
        scratch_shapes=[
            pltpu.VMEM(queries.shape, queries.dtype),
            pltpu.VMEM(probes.shape[::-1], probes.dtype),
            pltpu.VMEM(cand.transpose(1, 2, 0).shape, cand.dtype),
            pltpu.SemaphoreType.DMA((3,)),
        ],
        compiler_params=pltpu.CompilerParams(vmem_limit_bytes=24 * MIB),
    )(in_hbm(queries), in_hbm(probes.T), in_hbm(cand.transpose(1, 2, 0)))


def on_device(queries, corpus, list_slot, probes, cand):
    owners = lax.axis_size("lists")
    query_count, features = queries.shape
    probe_count = probes.shape[1]
    cand_count = cand.shape[2]
    local_lists = corpus.shape[0]
    corpus = corpus.reshape(-1, features)
    total_lists = list_slot.shape[0]
    pair_count = query_count * probe_count
    capacity = min(query_count, max(2, (2 * pair_count + total_lists - 1) // total_lists))
    sizes = (owners, query_count, probe_count, cand_count, capacity)
    me = lax.axis_index("lists").astype(jnp.int32)

    message = make_message(queries, probes, cand, owners)
    messages = exchange(message, first_order(owners))
    staged, inv_rows, column = row_norms(
        list_slot, probes, corpus, local_lists, cand_count, capacity
    )
    scores = block_scores(sizes, me.reshape(1), list_slot[None, :], corpus, staged, inv_rows, messages)
    returned = exchange(scores, second_order(owners))
    chosen = place(column, returned)
    return chosen.reshape(query_count, probe_count, cand_count, BLOCK)


def solution(mesh):
    placed = (
        P(("groups", "lists", "rep"), None),
        P(("groups", "lists"), None, None),
        P("groups"),
        P(("groups", "lists", "rep"), None),
        P(("groups", "lists", "rep"), None, None),
    )
    return jax.shard_map(
        on_device,
        mesh=mesh,
        in_specs=placed,
        out_specs=P(("groups", "lists", "rep"), None, None, None),
        check_vma=False,
    )
```

```python
import functools

import jax
import jax.numpy as jnp
from jax import lax
from jax.experimental import pallas as pl
from jax.experimental.pallas import tpu as pltpu
from jax.sharding import PartitionSpec as P

BLOCK = 128
LANES = 128
MIB = 2**20

epsilon = 1e-06


def contract(a, b, dims, precision=None):
    return lax.dot_general(
        a, b, (dims, ((), ())), precision=precision, preferred_element_type=jnp.float32
    )


def in_hbm(value):
    return pltpu.with_memory_space_constraint(value, pltpu.HBM)


def in_vmem(value):
    return pltpu.with_memory_space_constraint(value, pltpu.VMEM)


def first_order(owners):
    return [(i + owners // 2) % owners for i in range(owners)]


def second_order(owners):
    return [(i + owners // 4) % owners for i in range(owners)]


def second_place(owner, owners):
    return (owner + owners - owners // 4) % owners


def exchange(value, order):
    return lax.all_to_all(
        value, "lists", split_axis=0, concat_axis=0, axis_index_groups=[order], tiled=True
    )


def staged_rows(local_lists, list_length):
    return min(local_lists * list_length, list_length + list_length // 2)


def norm_kernel(
    sizes,
    slot_ref,
    probes_ref,
    corpus_ref,
    staged_ref,
    inv_ref,
    column_ref,
    held,
    parts,
    slots,
    sems,
    slot_sem,
):
    cand_count, capacity, chunk = sizes
    total_rows, features = corpus_ref.shape
    local_lists, list_length = inv_ref.shape
    staged = staged_ref.shape[0]

    cuts = sorted(set(range(0, total_rows + 1, min(list_length, 512))) | {staged})
    ranges = list(zip(cuts[:-1], cuts[1:]))

    def place(row, end):
        if row < staged:
            return staged_ref.at[row:end]
        return held.at[row - staged : end - staged]

    def copy(row, end):
        return pltpu.make_async_copy(
            corpus_ref.at[row:end], place(row, end), sems.at[cuts.index(row)]
        )

    slot_copy = pltpu.make_async_copy(slot_ref, slots, slot_sem)
    slot_copy.start()
    for row, end in ranges:
        copy(row, end).start()
    slot_copy.wait()
    column_ref[...] = result_columns(cand_count, capacity, local_lists, slots, probes_ref[...])
    ones = jnp.ones((8, 2 * LANES), jnp.bfloat16)
    for l in range(local_lists):
        for begin, to in ranges:
            if begin // list_length != l:
                continue
            copy(begin, to).wait()
            for row in range(begin, to, chunk):
                end = min(row + chunk, to)
                wide = place(row, end)[...].astype(jnp.float32)
                squares = functools.reduce(
                    jnp.add, [wide[:, j : j + LANES] ** 2 for j in range(0, features, LANES)]
                )
                high = squares.astype(jnp.bfloat16)
                low = (squares - high.astype(jnp.float32)).astype(jnp.bfloat16)
                parts[row:end, :LANES] = high
                parts[row:end, LANES:] = low
        whole = parts[l * list_length : (l + 1) * list_length, :]
        sums = contract(ones, whole, ((1,), (1,)))[:1]
        inv_ref[l : l + 1, :] = lax.rsqrt(sums / features + epsilon) * features ** (-0.5)


def row_sums(parts):
    high = parts.astype(jnp.bfloat16)
    low = (parts - high.astype(jnp.float32)).astype(jnp.bfloat16)
    terms = jnp.concatenate([high, low], axis=1)
    ones = jnp.ones((8, terms.shape[1]), jnp.bfloat16)
    return contract(ones, terms, ((1,), (1,)))[:1]


def result_columns(cand_count, capacity, local_lists, slot_ref, probes):
    probe_count, query_count = probes.shape
    total_lists = slot_ref.shape[0]
    owners = total_lists // local_lists
    position = jnp.zeros(probes.shape, jnp.float32)
    for t in range(total_lists):
        owner = slot_ref[t] // local_lists
        place = second_place(owner, owners)
        spot = place * local_lists + slot_ref[t] % local_lists
        position = jnp.where(probes == t, spot.astype(jnp.float32), position)
    lists = lax.broadcasted_iota(jnp.int32, (total_lists, query_count), 0)
    named = [lists == probes[p : p + 1] for p in range(probe_count)]
    counts = functools.reduce(jnp.add, [n.astype(jnp.float32) for n in named])
    square = (query_count, query_count)
    before = lax.broadcasted_iota(jnp.int32, square, 0) < lax.broadcasted_iota(
        jnp.int32, square, 1
    )
    earlier = contract(
        counts.astype(jnp.bfloat16), before.astype(jnp.float32).astype(jnp.bfloat16), ((1,), (0,))
    )
    rank = jnp.concatenate(
        [jnp.sum(jnp.where(n, earlier, 0.0), axis=0, keepdims=True) for n in named], axis=0
    )
    rows = probe_count * cand_count
    row = lax.broadcasted_iota(jnp.int32, (rows, probe_count), 0)
    lane = lax.broadcasted_iota(jnp.int32, (rows, probe_count), 1)
    spread = (row // cand_count == lane).astype(jnp.float32).astype(jnp.bfloat16)
    value = contract(spread, position.astype(jnp.bfloat16), ((1,), (0,))) * (
        cand_count * capacity
    ) + contract(spread, rank.astype(jnp.bfloat16), ((1,), (0,)))
    shift = (lax.broadcasted_iota(jnp.int32, value.shape, 0) % cand_count) * capacity
    return value.astype(jnp.int32) + shift


def row_norms(list_slot, probes, corpus, local_lists, cand_count, capacity):
    total_rows, features = corpus.shape
    list_length = total_rows // local_lists
    chunk = min(list_length, 256)
    staged = staged_rows(local_lists, list_length)
    query_count, probe_count = probes.shape
    whole = pl.BlockSpec(memory_space=pltpu.VMEM)
    return pl.pallas_call(
        functools.partial(norm_kernel, (cand_count, capacity, chunk)),
        out_shape=(
            pltpu.VMEM((staged, features), corpus.dtype),
            jax.ShapeDtypeStruct((local_lists, list_length), jnp.float32),
            jax.ShapeDtypeStruct((probe_count * cand_count, query_count), jnp.int32),
        ),
        in_specs=[
            pl.BlockSpec(memory_space=pltpu.HBM),
            whole,
            pl.BlockSpec(memory_space=pltpu.HBM),
        ],
        out_specs=(whole, whole, whole),
        scratch_shapes=[
            pltpu.VMEM((max(total_rows - staged, 16), features), corpus.dtype),
            pltpu.VMEM((total_rows, 2 * LANES), jnp.bfloat16),
            pltpu.SMEM(list_slot.shape, list_slot.dtype),
            pltpu.SemaphoreType.DMA((total_rows // min(list_length, 512) + 1,)),
            pltpu.SemaphoreType.DMA,
        ],
        compiler_params=pltpu.CompilerParams(vmem_limit_bytes=24 * MIB),
        cost_estimate=pl.CostEstimate(
            flops=2 * corpus.size, bytes_accessed=2 * corpus.size, transcendentals=0
        ),
    )(in_hbm(list_slot), in_hbm(probes.T), in_hbm(corpus))


def score_kernel(
    sizes, me_ref, slot_ref, corpus_ref, staged_ref, inv_ref, message_ref, out_ref, held, picked, sems
):
    owners, query_count, probe_count, cand_count, capacity, streams = sizes
    total_rows, features = corpus_ref.shape
    local_lists, list_length = inv_ref.shape
    staged = staged_ref.shape[0]
    total = owners * query_count
    room = owners * capacity
    step = capacity * cand_count

    def copy(begin, end):
        return pltpu.make_async_copy(
            corpus_ref.at[begin:end],
            held.at[begin - staged : end - staged],
            sems.at[streams.index((begin, end))],
        )

    for begin, end in streams:
        copy(begin, end).start()

    columns = [
        jnp.concatenate(
            [message_ref[s, j : j + query_count, :] for s in range(owners)], axis=0
        )
        for j in range(0, query_count * (features // LANES), query_count)
    ]
    queries = jnp.concatenate(columns, axis=1)
    squares = functools.reduce(jnp.add, [c.astype(jnp.float32) ** 2 for c in columns])
    height = message_ref.shape[1]
    tiles = [
        message_ref[s, height - probe_count :, :].astype(jnp.float32) for s in range(owners)
    ]
    probes, *cands = [
        jnp.concatenate([t[:, i : i + query_count] for t in tiles], axis=1)
        for i in range(0, query_count * (1 + cand_count), query_count)
    ]
    inv_query = lax.rsqrt(row_sums(squares) / features + epsilon)

    slots = slot_ref[...]
    names = lax.broadcasted_iota(jnp.int32, slots.shape, 1).astype(jnp.float32)
    first = me_ref[0] * local_lists
    hits, wanted = [], []
    for l in range(local_lists):
        name = jnp.sum(jnp.where(slots == first + l, names, 0.0), axis=1, keepdims=True)
        named = probes == name
        hits.append(jnp.sum(named.astype(jnp.float32), axis=0, keepdims=True))
        wanted.append(
            [jnp.sum(jnp.where(named, c, 0.0), axis=0, keepdims=True) for c in cands]
        )
    hit = jnp.concatenate(hits, axis=0)

    span = min(total, LANES)
    earlier = lax.broadcasted_iota(jnp.int32, (span, span), 0)
    later = lax.broadcasted_iota(jnp.int32, (span, span), 1)
    before = (earlier < later) & (earlier // query_count == later // query_count)
    before = before.astype(jnp.float32).astype(jnp.bfloat16)
    hit_low = hit.astype(jnp.bfloat16)
    rank = jnp.concatenate(
        [
            contract(hit_low[:, j : j + span], before, ((1,), (0,)))
            for j in range(0, total, span)
        ],
        axis=1,
    )
    source = lax.broadcasted_iota(jnp.int32, (1, total), 1) // query_count
    source = second_place((source + owners // 2) % owners, owners) * capacity
    target = jnp.where(hit > 0.5, rank.astype(jnp.int32) + source, -1)

    places = lax.broadcasted_iota(jnp.int32, (room, total), 0)
    picks = [(places == target[l : l + 1]).astype(jnp.float32) for l in range(local_lists)]
    pick = jnp.concatenate(picks, axis=0).astype(jnp.bfloat16)
    picked[...] = contract(pick, queries, ((1,), (0,))).astype(jnp.bfloat16)
    scales = [jnp.sum(p * inv_query, axis=1, keepdims=True) for p in picks]
    blocks = [
        [jnp.sum(p * w, axis=1, keepdims=True) for w in wanted[l]] for l, p in enumerate(picks)
    ]

    for l in range(local_lists):
        rows = picked[l * room : (l + 1) * room, :]
        chosen = [jnp.zeros((room, BLOCK), jnp.float32) for _ in range(cand_count)]
        row = l * list_length
        while row < (l + 1) * list_length:
            if row < staged:
                end = min(row + 512, staged, (l + 1) * list_length)
                values = staged_ref[row:end, :]
            else:
                if row in dict(streams):
                    copy(row, dict(streams)[row]).wait()
                end = min(row + 512, (l + 1) * list_length)
                values = held[row - staged : end - staged, :]
            products = contract(rows, values, ((1,), (1,)))
            first = row - l * list_length
            scaled = products * scales[l] * inv_ref[l : l + 1, first : first + end - row]
            for j in range(0, end - row, BLOCK):
                piece = scaled[:, j : j + BLOCK]
                chosen = [
                    jnp.where(block == (first + j) // BLOCK, piece, old)
                    for block, old in zip(blocks[l], chosen)
                ]
            row = end
        out_ref[:, l * step : (l + 1) * step, :] = jnp.concatenate(
            [c.reshape(owners, capacity, BLOCK) for c in chosen], axis=1
        ).astype(jnp.bfloat16)


def stream_ranges(local_lists, list_length):
    row, end = staged_rows(local_lists, list_length), local_lists * list_length
    ranges = []
    while row < end:
        to = (row // list_length + 1) * list_length
        if to == end and to - row > list_length // 2:
            to = end - list_length // 2
        ranges.append((row, to))
        row = to
    return tuple(ranges)


def block_scores(sizes, me, list_slot, corpus, staged, inv_rows, messages):
    owners, query_count, probe_count, cand_count, capacity = sizes
    local_lists, list_length = inv_rows.shape
    total_rows, features = corpus.shape
    streams = stream_ranges(local_lists, list_length)
    whole = pl.BlockSpec(memory_space=pltpu.VMEM)
    return pl.pallas_call(
        functools.partial(score_kernel, sizes + (streams,)),
        out_shape=jax.ShapeDtypeStruct(
            (owners, local_lists * cand_count * capacity, BLOCK), jnp.bfloat16
        ),
        in_specs=[
            pl.BlockSpec(memory_space=pltpu.SMEM),
            whole,
            pl.BlockSpec(memory_space=pltpu.HBM),
            whole,
            whole,
            whole,
        ],
        out_specs=whole,
        scratch_shapes=[
            pltpu.VMEM((max(total_rows - staged.shape[0], 16), features), corpus.dtype),
            pltpu.VMEM((local_lists * owners * capacity, features), corpus.dtype),
            pltpu.SemaphoreType.DMA((max(len(streams), 1),)),
        ],
        compiler_params=pltpu.CompilerParams(vmem_limit_bytes=40 * MIB),
        cost_estimate=pl.CostEstimate(
            flops=2 * owners * capacity * corpus.size,
            bytes_accessed=2 * corpus.size,
            transcendentals=0,
        ),
    )(me, list_slot, in_hbm(corpus), in_vmem(staged), inv_rows, messages)


def place_kernel(column_ref, returned_ref, out_ref):
    returned = returned_ref[...].reshape(-1, returned_ref.shape[-1])
    each, query_count = column_ref.shape
    column = column_ref[...]
    lanes = lax.broadcasted_iota(jnp.int32, (each, returned.shape[0]), 1)
    pick = jnp.concatenate(
        [(lanes == column[:, i : i + 1]).astype(jnp.float32) for i in range(query_count)], axis=0
    ).astype(jnp.bfloat16)
    out_ref[...] = contract(pick, returned, ((1,), (0,))).astype(jnp.bfloat16)


def place(column, returned):
    whole = pl.BlockSpec(memory_space=pltpu.VMEM)
    return pl.pallas_call(
        place_kernel,
        out_shape=jax.ShapeDtypeStruct((column.size, BLOCK), jnp.bfloat16),
        in_specs=[whole] * 2,
        out_specs=whole,
        compiler_params=pltpu.CompilerParams(vmem_limit_bytes=24 * MIB),
    )(column, returned)


def message_kernel(
    queries_ref, probes_ref, cand_ref, out_ref, queries_vmem, probes_vmem, cand_vmem, sems
):
    owners, height, lanes = out_ref.shape
    query_count, features = queries_ref.shape
    probe_count, cand_count, _ = cand_ref.shape
    pairs = (
        (probes_ref, probes_vmem),
        (cand_ref, cand_vmem),
        (queries_ref, queries_vmem),
    )
    copies = [
        pltpu.make_async_copy(source, target, sems.at[i])
        for i, (source, target) in enumerate(pairs)
    ]
    for c in copies:
        c.start()
    copies[0].wait()
    copies[1].wait()
    pieces = [probes_vmem[...]] + [cand_vmem[:, c, :] for c in range(cand_count)]
    spare = lanes - len(pieces) * query_count
    pieces.append(jnp.zeros((probe_count, spare), jnp.int32))
    indices = jnp.concatenate(pieces, axis=1).astype(jnp.float32).astype(jnp.bfloat16)
    for k in range(owners):
        out_ref[k, height - probe_count :, :] = indices
    copies[2].wait()
    for j in range(features // lanes):
        column = queries_vmem[:, j * lanes : (j + 1) * lanes]
        for k in range(owners):
            out_ref[k, j * query_count : (j + 1) * query_count, :] = column


def make_message(queries, probes, cand, owners):
    query_count, features = queries.shape
    probe_count = probes.shape[1]
    height = query_count * (features // LANES) + probe_count
    whole = pl.BlockSpec(memory_space=pltpu.VMEM)
    return pl.pallas_call(
        message_kernel,
        out_shape=jax.ShapeDtypeStruct((owners, height, LANES), queries.dtype),
        in_specs=[pl.BlockSpec(memory_space=pltpu.HBM)] * 3,
        out_specs=whole,
        scratch_shapes=[
            pltpu.VMEM(queries.shape, queries.dtype),
            pltpu.VMEM(probes.shape[::-1], probes.dtype),
            pltpu.VMEM(cand.transpose(1, 2, 0).shape, cand.dtype),
            pltpu.SemaphoreType.DMA((3,)),
        ],
        compiler_params=pltpu.CompilerParams(vmem_limit_bytes=24 * MIB),
    )(in_hbm(queries), in_hbm(probes.T), in_hbm(cand.transpose(1, 2, 0)))


def on_device(queries, corpus, list_slot, probes, cand):
    owners = lax.axis_size("lists")
    query_count, features = queries.shape
    probe_count = probes.shape[1]
    cand_count = cand.shape[2]
    local_lists = corpus.shape[0]
    corpus = corpus.reshape(-1, features)
    total_lists = list_slot.shape[0]
    pair_count = query_count * probe_count
    capacity = min(query_count, max(2, (2 * pair_count + total_lists - 1) // total_lists))
    sizes = (owners, query_count, probe_count, cand_count, capacity)
    me = lax.axis_index("lists").astype(jnp.int32)

    message = make_message(queries, probes, cand, owners)
    messages = exchange(message, first_order(owners))
    staged, inv_rows, column = row_norms(
        list_slot, probes, corpus, local_lists, cand_count, capacity
    )
    scores = block_scores(sizes, me.reshape(1), list_slot[None, :], corpus, staged, inv_rows, messages)
    returned = exchange(scores, second_order(owners))
    chosen = place(column, returned)
    return chosen.reshape(query_count, probe_count, cand_count, BLOCK)


def solution(mesh):
    placed = (
        P(("groups", "lists", "rep"), None),
        P(("groups", "lists"), None, None),
        P("groups"),
        P(("groups", "lists", "rep"), None),
        P(("groups", "lists", "rep"), None, None),
    )
    return jax.shard_map(
        on_device,
        mesh=mesh,
        in_specs=placed,
        out_specs=P(("groups", "lists", "rep"), None, None, None),
        check_vma=False,
    )
```

```python
import functools

import jax
import jax.numpy as jnp
from jax import lax
from jax.experimental import pallas as pl
from jax.experimental.pallas import tpu as pltpu
from jax.sharding import PartitionSpec as P

BLOCK = 128
LANES = 128
MIB = 2**20

epsilon = 1e-06


def contract(a, b, dims, precision=None):
    return lax.dot_general(
        a, b, (dims, ((), ())), precision=precision, preferred_element_type=jnp.float32
    )


def in_hbm(value):
    return pltpu.with_memory_space_constraint(value, pltpu.HBM)


def in_vmem(value):
    return pltpu.with_memory_space_constraint(value, pltpu.VMEM)


def first_order(owners):
    return [(i + owners // 2) % owners for i in range(owners)]


def second_order(owners):
    return [(i + owners - owners // 4) % owners for i in range(owners)]


def second_place(owner, owners):
    return (owner + owners // 4) % owners


def exchange(value, order):
    return lax.all_to_all(
        value, "lists", split_axis=0, concat_axis=0, axis_index_groups=[order], tiled=True
    )


def staged_rows(local_lists, list_length):
    return min(local_lists * list_length, list_length + list_length // 2)


def norm_kernel(
    sizes,
    slot_ref,
    probes_ref,
    corpus_ref,
    staged_ref,
    inv_ref,
    column_ref,
    held,
    parts,
    slots,
    sems,
    slot_sem,
):
    cand_count, capacity, chunk = sizes
    total_rows, features = corpus_ref.shape
    local_lists, list_length = inv_ref.shape
    staged = staged_ref.shape[0]

    cuts = sorted(set(range(0, total_rows + 1, min(list_length, 512))) | {staged})
    ranges = list(zip(cuts[:-1], cuts[1:]))

    def place(row, end):
        if row < staged:
            return staged_ref.at[row:end]
        return held.at[row - staged : end - staged]

    def copy(row, end):
        return pltpu.make_async_copy(
            corpus_ref.at[row:end], place(row, end), sems.at[cuts.index(row)]
        )

    slot_copy = pltpu.make_async_copy(slot_ref, slots, slot_sem)
    slot_copy.start()
    for row, end in ranges:
        copy(row, end).start()
    slot_copy.wait()
    column_ref[...] = result_columns(cand_count, capacity, local_lists, slots, probes_ref[...])
    ones = jnp.ones((8, 2 * LANES), jnp.bfloat16)
    for l in range(local_lists):
        for begin, to in ranges:
            if begin // list_length != l:
                continue
            copy(begin, to).wait()
            for row in range(begin, to, chunk):
                end = min(row + chunk, to)
                wide = place(row, end)[...].astype(jnp.float32)
                squares = functools.reduce(
                    jnp.add, [wide[:, j : j + LANES] ** 2 for j in range(0, features, LANES)]
                )
                high = squares.astype(jnp.bfloat16)
                low = (squares - high.astype(jnp.float32)).astype(jnp.bfloat16)
                parts[row:end, :LANES] = high
                parts[row:end, LANES:] = low
        whole = parts[l * list_length : (l + 1) * list_length, :]
        sums = contract(ones, whole, ((1,), (1,)))[:1]
        inv_ref[l : l + 1, :] = lax.rsqrt(sums / features + epsilon) * features ** (-0.5)


def row_sums(parts):
    high = parts.astype(jnp.bfloat16)
    low = (parts - high.astype(jnp.float32)).astype(jnp.bfloat16)
    terms = jnp.concatenate([high, low], axis=1)
    ones = jnp.ones((8, terms.shape[1]), jnp.bfloat16)
    return contract(ones, terms, ((1,), (1,)))[:1]


def result_columns(cand_count, capacity, local_lists, slot_ref, probes):
    probe_count, query_count = probes.shape
    total_lists = slot_ref.shape[0]
    owners = total_lists // local_lists
    position = jnp.zeros(probes.shape, jnp.float32)
    for t in range(total_lists):
        owner = slot_ref[t] // local_lists
        place = second_place(owner, owners)
        spot = place * local_lists + slot_ref[t] % local_lists
        position = jnp.where(probes == t, spot.astype(jnp.float32), position)
    lists = lax.broadcasted_iota(jnp.int32, (total_lists, query_count), 0)
    named = [lists == probes[p : p + 1] for p in range(probe_count)]
    counts = functools.reduce(jnp.add, [n.astype(jnp.float32) for n in named])
    square = (query_count, query_count)
    before = lax.broadcasted_iota(jnp.int32, square, 0) < lax.broadcasted_iota(
        jnp.int32, square, 1
    )
    earlier = contract(
        counts.astype(jnp.bfloat16), before.astype(jnp.float32).astype(jnp.bfloat16), ((1,), (0,))
    )
    rank = jnp.concatenate(
        [jnp.sum(jnp.where(n, earlier, 0.0), axis=0, keepdims=True) for n in named], axis=0
    )
    rows = probe_count * cand_count
    row = lax.broadcasted_iota(jnp.int32, (rows, probe_count), 0)
    lane = lax.broadcasted_iota(jnp.int32, (rows, probe_count), 1)
    spread = (row // cand_count == lane).astype(jnp.float32).astype(jnp.bfloat16)
    value = contract(spread, position.astype(jnp.bfloat16), ((1,), (0,))) * (
        cand_count * capacity
    ) + contract(spread, rank.astype(jnp.bfloat16), ((1,), (0,)))
    shift = (lax.broadcasted_iota(jnp.int32, value.shape, 0) % cand_count) * capacity
    return value.astype(jnp.int32) + shift


def row_norms(list_slot, probes, corpus, local_lists, cand_count, capacity):
    total_rows, features = corpus.shape
    list_length = total_rows // local_lists
    chunk = min(list_length, 256)
    staged = staged_rows(local_lists, list_length)
    query_count, probe_count = probes.shape
    whole = pl.BlockSpec(memory_space=pltpu.VMEM)
    return pl.pallas_call(
        functools.partial(norm_kernel, (cand_count, capacity, chunk)),
        out_shape=(
            pltpu.VMEM((staged, features), corpus.dtype),
            jax.ShapeDtypeStruct((local_lists, list_length), jnp.float32),
            jax.ShapeDtypeStruct((probe_count * cand_count, query_count), jnp.int32),
        ),
        in_specs=[
            pl.BlockSpec(memory_space=pltpu.HBM),
            whole,
            pl.BlockSpec(memory_space=pltpu.HBM),
        ],
        out_specs=(whole, whole, whole),
        scratch_shapes=[
            pltpu.VMEM((max(total_rows - staged, 16), features), corpus.dtype),
            pltpu.VMEM((total_rows, 2 * LANES), jnp.bfloat16),
            pltpu.SMEM(list_slot.shape, list_slot.dtype),
            pltpu.SemaphoreType.DMA((total_rows // min(list_length, 512) + 1,)),
            pltpu.SemaphoreType.DMA,
        ],
        compiler_params=pltpu.CompilerParams(vmem_limit_bytes=24 * MIB),
        cost_estimate=pl.CostEstimate(
            flops=2 * corpus.size, bytes_accessed=2 * corpus.size, transcendentals=0
        ),
    )(in_hbm(list_slot), in_hbm(probes.T), in_hbm(corpus))


def score_kernel(
    sizes, me_ref, slot_ref, corpus_ref, staged_ref, inv_ref, message_ref, out_ref, held, picked, sems
):
    owners, query_count, probe_count, cand_count, capacity, streams = sizes
    total_rows, features = corpus_ref.shape
    local_lists, list_length = inv_ref.shape
    staged = staged_ref.shape[0]
    total = owners * query_count
    room = owners * capacity
    step = capacity * cand_count

    def copy(begin, end):
        return pltpu.make_async_copy(
            corpus_ref.at[begin:end],
            held.at[begin - staged : end - staged],
            sems.at[streams.index((begin, end))],
        )

    for begin, end in streams:
        copy(begin, end).start()

    columns = [
        jnp.concatenate(
            [message_ref[s, j : j + query_count, :] for s in range(owners)], axis=0
        )
        for j in range(0, query_count * (features // LANES), query_count)
    ]
    queries = jnp.concatenate(columns, axis=1)
    squares = functools.reduce(jnp.add, [c.astype(jnp.float32) ** 2 for c in columns])
    height = message_ref.shape[1]
    tiles = [
        message_ref[s, height - probe_count :, :].astype(jnp.float32) for s in range(owners)
    ]
    probes, *cands = [
        jnp.concatenate([t[:, i : i + query_count] for t in tiles], axis=1)
        for i in range(0, query_count * (1 + cand_count), query_count)
    ]
    inv_query = lax.rsqrt(row_sums(squares) / features + epsilon)

    slots = slot_ref[...]
    names = lax.broadcasted_iota(jnp.int32, slots.shape, 1).astype(jnp.float32)
    first = me_ref[0] * local_lists
    hits, wanted = [], []
    for l in range(local_lists):
        name = jnp.sum(jnp.where(slots == first + l, names, 0.0), axis=1, keepdims=True)
        named = probes == name
        hits.append(jnp.sum(named.astype(jnp.float32), axis=0, keepdims=True))
        wanted.append(
            [jnp.sum(jnp.where(named, c, 0.0), axis=0, keepdims=True) for c in cands]
        )
    hit = jnp.concatenate(hits, axis=0)

    span = min(total, LANES)
    earlier = lax.broadcasted_iota(jnp.int32, (span, span), 0)
    later = lax.broadcasted_iota(jnp.int32, (span, span), 1)
    before = (earlier < later) & (earlier // query_count == later // query_count)
    before = before.astype(jnp.float32).astype(jnp.bfloat16)
    hit_low = hit.astype(jnp.bfloat16)
    rank = jnp.concatenate(
        [
            contract(hit_low[:, j : j + span], before, ((1,), (0,)))
            for j in range(0, total, span)
        ],
        axis=1,
    )
    source = lax.broadcasted_iota(jnp.int32, (1, total), 1) // query_count
    source = second_place((source + owners // 2) % owners, owners) * capacity
    target = jnp.where(hit > 0.5, rank.astype(jnp.int32) + source, -1)

    places = lax.broadcasted_iota(jnp.int32, (room, total), 0)
    picks = [(places == target[l : l + 1]).astype(jnp.float32) for l in range(local_lists)]
    pick = jnp.concatenate(picks, axis=0).astype(jnp.bfloat16)
    picked[...] = contract(pick, queries, ((1,), (0,))).astype(jnp.bfloat16)
    scales = [jnp.sum(p * inv_query, axis=1, keepdims=True) for p in picks]
    blocks = [
        [jnp.sum(p * w, axis=1, keepdims=True) for w in wanted[l]] for l, p in enumerate(picks)
    ]

    for l in range(local_lists):
        rows = picked[l * room : (l + 1) * room, :]
        chosen = [jnp.zeros((room, BLOCK), jnp.float32) for _ in range(cand_count)]
        row = l * list_length
        while row < (l + 1) * list_length:
            if row < staged:
                end = min(row + 512, staged, (l + 1) * list_length)
                values = staged_ref[row:end, :]
            else:
                if row in dict(streams):
                    copy(row, dict(streams)[row]).wait()
                end = min(row + 512, (l + 1) * list_length)
                values = held[row - staged : end - staged, :]
            products = contract(rows, values, ((1,), (1,)))
            first = row - l * list_length
            scaled = products * scales[l] * inv_ref[l : l + 1, first : first + end - row]
            for j in range(0, end - row, BLOCK):
                piece = scaled[:, j : j + BLOCK]
                chosen = [
                    jnp.where(block == (first + j) // BLOCK, piece, old)
                    for block, old in zip(blocks[l], chosen)
                ]
            row = end
        out_ref[:, l * step : (l + 1) * step, :] = jnp.concatenate(
            [c.reshape(owners, capacity, BLOCK) for c in chosen], axis=1
        ).astype(jnp.bfloat16)


def stream_ranges(local_lists, list_length):
    row, end = staged_rows(local_lists, list_length), local_lists * list_length
    ranges = []
    while row < end:
        to = (row // list_length + 1) * list_length
        if to == end and to - row > list_length // 2:
            to = end - list_length // 2
        ranges.append((row, to))
        row = to
    return tuple(ranges)


def block_scores(sizes, me, list_slot, corpus, staged, inv_rows, messages):
    owners, query_count, probe_count, cand_count, capacity = sizes
    local_lists, list_length = inv_rows.shape
    total_rows, features = corpus.shape
    streams = stream_ranges(local_lists, list_length)
    whole = pl.BlockSpec(memory_space=pltpu.VMEM)
    return pl.pallas_call(
        functools.partial(score_kernel, sizes + (streams,)),
        out_shape=jax.ShapeDtypeStruct(
            (owners, local_lists * cand_count * capacity, BLOCK), jnp.bfloat16
        ),
        in_specs=[
            pl.BlockSpec(memory_space=pltpu.SMEM),
            whole,
            pl.BlockSpec(memory_space=pltpu.HBM),
            whole,
            whole,
            whole,
        ],
        out_specs=whole,
        scratch_shapes=[
            pltpu.VMEM((max(total_rows - staged.shape[0], 16), features), corpus.dtype),
            pltpu.VMEM((local_lists * owners * capacity, features), corpus.dtype),
            pltpu.SemaphoreType.DMA((max(len(streams), 1),)),
        ],
        compiler_params=pltpu.CompilerParams(vmem_limit_bytes=40 * MIB),
        cost_estimate=pl.CostEstimate(
            flops=2 * owners * capacity * corpus.size,
            bytes_accessed=2 * corpus.size,
            transcendentals=0,
        ),
    )(me, list_slot, in_hbm(corpus), in_vmem(staged), inv_rows, messages)


def place_kernel(column_ref, returned_ref, out_ref):
    returned = returned_ref[...].reshape(-1, returned_ref.shape[-1])
    each, query_count = column_ref.shape
    column = column_ref[...]
    lanes = lax.broadcasted_iota(jnp.int32, (each, returned.shape[0]), 1)
    pick = jnp.concatenate(
        [(lanes == column[:, i : i + 1]).astype(jnp.float32) for i in range(query_count)], axis=0
    ).astype(jnp.bfloat16)
    out_ref[...] = contract(pick, returned, ((1,), (0,))).astype(jnp.bfloat16)


def place(column, returned):
    whole = pl.BlockSpec(memory_space=pltpu.VMEM)
    return pl.pallas_call(
        place_kernel,
        out_shape=jax.ShapeDtypeStruct((column.size, BLOCK), jnp.bfloat16),
        in_specs=[whole] * 2,
        out_specs=whole,
        compiler_params=pltpu.CompilerParams(vmem_limit_bytes=24 * MIB),
    )(column, returned)


def message_kernel(
    queries_ref, probes_ref, cand_ref, out_ref, queries_vmem, probes_vmem, cand_vmem, sems
):
    owners, height, lanes = out_ref.shape
    query_count, features = queries_ref.shape
    probe_count, cand_count, _ = cand_ref.shape
    pairs = (
        (probes_ref, probes_vmem),
        (cand_ref, cand_vmem),
        (queries_ref, queries_vmem),
    )
    copies = [
        pltpu.make_async_copy(source, target, sems.at[i])
        for i, (source, target) in enumerate(pairs)
    ]
    for c in copies:
        c.start()
    copies[0].wait()
    copies[1].wait()
    pieces = [probes_vmem[...]] + [cand_vmem[:, c, :] for c in range(cand_count)]
    spare = lanes - len(pieces) * query_count
    pieces.append(jnp.zeros((probe_count, spare), jnp.int32))
    indices = jnp.concatenate(pieces, axis=1).astype(jnp.float32).astype(jnp.bfloat16)
    for k in range(owners):
        out_ref[k, height - probe_count :, :] = indices
    copies[2].wait()
    for j in range(features // lanes):
        column = queries_vmem[:, j * lanes : (j + 1) * lanes]
        for k in range(owners):
            out_ref[k, j * query_count : (j + 1) * query_count, :] = column


def make_message(queries, probes, cand, owners):
    query_count, features = queries.shape
    probe_count = probes.shape[1]
    height = query_count * (features // LANES) + probe_count
    whole = pl.BlockSpec(memory_space=pltpu.VMEM)
    return pl.pallas_call(
        message_kernel,
        out_shape=jax.ShapeDtypeStruct((owners, height, LANES), queries.dtype),
        in_specs=[pl.BlockSpec(memory_space=pltpu.HBM)] * 3,
        out_specs=whole,
        scratch_shapes=[
            pltpu.VMEM(queries.shape, queries.dtype),
            pltpu.VMEM(probes.shape[::-1], probes.dtype),
            pltpu.VMEM(cand.transpose(1, 2, 0).shape, cand.dtype),
            pltpu.SemaphoreType.DMA((3,)),
        ],
        compiler_params=pltpu.CompilerParams(vmem_limit_bytes=24 * MIB),
    )(in_hbm(queries), in_hbm(probes.T), in_hbm(cand.transpose(1, 2, 0)))


def on_device(queries, corpus, list_slot, probes, cand):
    owners = lax.axis_size("lists")
    query_count, features = queries.shape
    probe_count = probes.shape[1]
    cand_count = cand.shape[2]
    local_lists = corpus.shape[0]
    corpus = corpus.reshape(-1, features)
    total_lists = list_slot.shape[0]
    pair_count = query_count * probe_count
    capacity = min(query_count, max(2, (2 * pair_count + total_lists - 1) // total_lists))
    sizes = (owners, query_count, probe_count, cand_count, capacity)
    me = lax.axis_index("lists").astype(jnp.int32)

    message = make_message(queries, probes, cand, owners)
    messages = exchange(message, first_order(owners))
    staged, inv_rows, column = row_norms(
        list_slot, probes, corpus, local_lists, cand_count, capacity
    )
    scores = block_scores(sizes, me.reshape(1), list_slot[None, :], corpus, staged, inv_rows, messages)
    returned = exchange(scores, second_order(owners))
    chosen = place(column, returned)
    return chosen.reshape(query_count, probe_count, cand_count, BLOCK)


def solution(mesh):
    placed = (
        P(("groups", "lists", "rep"), None),
        P(("groups", "lists"), None, None),
        P("groups"),
        P(("groups", "lists", "rep"), None),
        P(("groups", "lists", "rep"), None, None),
    )
    return jax.shard_map(
        on_device,
        mesh=mesh,
        in_specs=placed,
        out_specs=P(("groups", "lists", "rep"), None, None, None),
        check_vma=False,
    )
```
